128 devices in a mesh: ctx: 16 (over x_hi, y, core), shard: 8 (over x_lo, z).
Axes of the slice: x: 4 (x_hi: 2, x_lo: 2; x = x_hi * 2 + x_lo), y: 4, z: 4, core: 2. Of those that a mesh axis runs over, the one named last changes fastest.
Arguments:
- tokens: bfloat16 [8, 4096, 1024], P('shard', 'ctx'), may hold values from -6 to 6
- cotangent: bfloat16 [8, 4096, 1024], P('shard', 'ctx'), may hold values from -6 to 6
- segments: int32 [8, 4096], P('shard'), may hold values from 0 to 13, as said below
- positions: int32 [8, 4096], P('shard', 'ctx'), may hold values from 0 to 2303, as said below
- pad_mask: int32 [8, 4096], P('shard'), may hold values from 0 to 1, as said below
- w_in: float32 [1024, 10240], P(('ctx', 'shard')), may hold values from -0.1875 to 0.1875
- w_out: float32 [5120, 1024], P(('ctx', 'shard'))
- gains: float32 [2304], P(('ctx', 'shard')), may hold values from 0.5 to 1.5
- first_in: float32 [1024, 10240], P(('ctx', 'shard'))
- first_out: float32 [5120, 1024], P(('ctx', 'shard'))
- first_gains: float32 [2304], P(('ctx', 'shard'))
- second_in: float32 [1024, 10240], P(('ctx', 'shard')), as said below
- second_out: float32 [5120, 1024], P(('ctx', 'shard')), as said below
- second_gains: float32 [2304], P(('ctx', 'shard')), as said below
Outputs:
- output: float32 [8, 4096, 1024], P('shard', 'ctx')
- input_grad: float32 [8, 4096, 1024], P('shard', 'ctx')
- new_first_in: float32 [1024, 10240], P(('ctx', 'shard'))
- new_first_out: float32 [5120, 1024], P(('ctx', 'shard'))
- new_first_gains: float32 [2304], P(('ctx', 'shard'))
- new_second_in: float32 [1024, 10240], P(('ctx', 'shard'))
- new_second_out: float32 [5120, 1024], P(('ctx', 'shard'))
- new_second_gains: float32 [2304], P(('ctx', 'shard'))
- new_master_in: float32 [1024, 10240], P(('ctx', 'shard'))
- new_master_out: float32 [5120, 1024], P(('ctx', 'shard'))
- new_master_gains: float32 [2304], P(('ctx', 'shard'))
- copy_in: bfloat16 [1024, 10240], P(('ctx', 'shard'))
- copy_out: bfloat16 [5120, 1024], P(('ctx', 'shard'))
The draws below stay inside these ranges and needn't reach their ends.
Inputs may be any that keep to these rules, and one draw needn't show every extreme that they name: `segments`: along the sequence index, segment numbers never fall; the last segment, of one token or more, is padding and has the number 16 / 2 + 5; a segment of 2048 tokens or more begins within the first 128 tokens of the sequence. `positions`: a token's index within its segment. `pad_mask`: 1 exactly on the tokens of all segments but the last. `second_in`: positive. `second_out`: positive. `second_gains`: positive.
All inputs are finite; a program needn't handle non-finite values.
Results may differ from the reference program's by a relative error of at most 0.02.
Values may be sent and summed in bfloat16 or wider, within the bound.
No kernel may reach another device: no remote copies, remote signals or barrier semaphores. Data moves between devices by JAX's collectives and lax.ppermute only.
A program may use at most 320 MiB of HBM per device.

```python
import math
import jax
import jax.numpy as jnp
from jax import lax

D = 1024
H_Q = 16
H_KV = 8
HD = 128
FF = 3072
TOK_DEV = 256
STEP = 5
QD = 2048
CIN = 10240
OUTR = 5120
GN = 2304
NSEQ = 8
LEN = 4096
TOKENS = 32768
N_CTX = 16


def dealt_indices_drawn():
    half_rows = TOK_DEV // 2
    row_ids = jnp.arange(LEN, dtype=jnp.int32)
    block_ids = row_ids // half_rows
    owner_dev = block_ids // 2
    place_ids = jnp.where(block_ids % 2 == 0, owner_dev, 2 * N_CTX - 1 - owner_dev)
    return (place_ids * half_rows + row_ids % half_rows).astype(jnp.int32)


def layout(key):
    doc_count = N_CTX // 2 + 3
    head_len = jax.random.randint(jax.random.fold_in(key, 101), (NSEQ, 1), TOK_DEV // 8, TOK_DEV // 2)
    long_len = jnp.full((NSEQ, 1), LEN // 2 + TOK_DEV, jnp.int32)
    rest_lengths = jax.random.randint(jax.random.fold_in(key, 103), (NSEQ, doc_count), TOK_DEV, 8 * TOK_DEV + 1)
    pad_len = jax.random.randint(jax.random.fold_in(key, 104), (NSEQ,), TOK_DEV // 8, TOK_DEV // 2 + 1)
    doc_lengths = jnp.concatenate([head_len, long_len, rest_lengths], axis=1).astype(jnp.int32)
    doc_ends = jnp.cumsum(doc_lengths, axis=1).astype(jnp.int32)
    doc_starts = doc_ends - doc_lengths
    row_ids = jnp.arange(LEN, dtype=jnp.int32)[None, :]
    doc_ids = jnp.sum((row_ids[:, :, None] >= doc_ends[:, None, :]).astype(jnp.int32), axis=-1).astype(jnp.int32)
    start_of = jnp.take_along_axis(doc_starts, doc_ids, axis=1)
    real_end = (LEN - pad_len).astype(jnp.int32)
    live_rows = row_ids < real_end[:, None]
    segment_ids = jnp.where(live_rows, doc_ids, doc_count + 2).astype(jnp.int32)
    places_in = jnp.where(live_rows, row_ids - start_of, row_ids - real_end[:, None]).astype(jnp.int32)
    live_mask = live_rows.astype(jnp.int32)
    dealt = dealt_indices_drawn()
    return (segment_ids[:, dealt], places_in[:, dealt], live_mask[:, dealt])


def signed_moment(key, dims_shape, magnitude):
    return magnitude * jax.random.truncated_normal(key, -3.0, 3.0, dims_shape, jnp.float32)


def square_moment(key, dims_shape, magnitude):
    return magnitude * magnitude * jnp.exp(jax.random.uniform(key, dims_shape, jnp.float32, 0.0, math.log(4.0)))


def out_magnitude():
    row_ids = jnp.arange(OUTR)[:, None]
    return jnp.where(row_ids < QD, 0.12, 0.6) * math.sqrt(TOKENS)


def draw_segments(key, part):
    shared = layout(key)
    return shared[0]


def draw_positions(key, part):
    shared = layout(key)
    return shared[1]


def draw_pad_mask(key, part):
    shared = layout(key)
    return shared[2]


def draw_w_out(key, part):
    key = jax.random.fold_in(key, 4)
    row_ids = jnp.arange(OUTR)[:, None]
    spread = jnp.where(row_ids < QD, 4.0 / math.sqrt(QD), 1.0 / math.sqrt(FF))
    return spread * jax.random.truncated_normal(key, -4.0, 4.0, (OUTR, D), jnp.float32)


def draw_first_in(key, part):
    key = jax.random.fold_in(key, 11)
    return signed_moment(key, (D, CIN), 0.3 * math.sqrt(TOKENS))


def draw_first_out(key, part):
    key = jax.random.fold_in(key, 12)
    return signed_moment(key, (OUTR, D), out_magnitude())


def draw_first_gains(key, part):
    key = jax.random.fold_in(key, 13)
    return signed_moment(key, (GN,), 0.7 * math.sqrt(TOKENS))


def draw_second_in(key, part):
    key = jax.random.fold_in(key, 21)
    return square_moment(key, (D, CIN), 0.3 * math.sqrt(TOKENS))


def draw_second_out(key, part):
    key = jax.random.fold_in(key, 22)
    return square_moment(key, (OUTR, D), out_magnitude())


def draw_second_gains(key, part):
    key = jax.random.fold_in(key, 23)
    return square_moment(key, (GN,), 0.7 * math.sqrt(TOKENS))


def levels(key, dims, pieces, least, top_value):
    def one(position, parts):
        draws = jax.random.uniform(jax.random.fold_in(jax.random.fold_in(key, 6), position), (parts,), jnp.float32, least / len(pieces), top_value / len(pieces))
        return jnp.repeat(jnp.exp(draws), dims[position] // parts).reshape((-1,) + (1,) * (len(dims) - position - 1))

    factor_of = one(*pieces[0])
    for cut in pieces[1:]:
        factor_of = factor_of * one(*cut)
    return factor_of


def normal_values(rng, extent, scale, most, pieces=(), kind=jnp.bfloat16):
    drawn = scale * jax.random.normal(rng, extent, jnp.float32)
    if pieces:
        drawn = drawn * levels(rng, extent, pieces, -0.22, 0.18)
    return jnp.clip(drawn, -most, most).astype(kind)


def setup_inputs(seed: int = 0) -> dict:
    streams_of = jax.random.split(jax.random.key(seed), 15)
    tokens = normal_values(streams_of[0], (NSEQ, LEN, D), 1.0, 6.0, ((0, 8), (1, 16)))
    cotangent = normal_values(streams_of[1], (NSEQ, LEN, D), 1.0, 6.0, ((0, 8), (1, 16)))
    segments = draw_segments(jax.random.fold_in(streams_of[14], 71), 0)
    positions = draw_positions(jax.random.fold_in(streams_of[14], 71), 0)
    pad_mask = draw_pad_mask(jax.random.fold_in(streams_of[14], 71), 0)
    w_in = normal_values(streams_of[5], (D, CIN), D ** -0.5, 0.1875, ((0, 128),), jnp.float32)
    w_out = draw_w_out(jax.random.fold_in(streams_of[14], 71), 0)
    gains = jnp.clip(1.0 + 0.1 * jax.random.normal(streams_of[7], (GN,), jnp.float32), 0.5, 1.5)
    first_in = draw_first_in(jax.random.fold_in(streams_of[14], 71), 0)
    first_out = draw_first_out(jax.random.fold_in(streams_of[14], 71), 0)
    first_gains = draw_first_gains(jax.random.fold_in(streams_of[14], 71), 0)
    second_in = draw_second_in(jax.random.fold_in(streams_of[14], 71), 0)
    second_out = draw_second_out(jax.random.fold_in(streams_of[14], 71), 0)
    second_gains = draw_second_gains(jax.random.fold_in(streams_of[14], 71), 0)
    return dict(tokens=tokens, cotangent=cotangent, segments=segments, positions=positions, pad_mask=pad_mask, w_in=w_in, w_out=w_out, gains=gains, first_in=first_in, first_out=first_out, first_gains=first_gains, second_in=second_in, second_out=second_out, second_gains=second_gains)


HIGHEST = lax.Precision.HIGHEST
NORM_EPS = 1e-06
ROPE_BASE = 1000000.0
BETA_ONE = 0.5
BETA_TWO = 0.5
ADAM_EPS = 1e-08
WEIGHT_DECAY = 0.1
RATE_MATRIX = 0.03
RATE_GAIN = 0.25
MASKED = -1e+30

@jax.custom_vjp
def low(v):
    return lax.optimization_barrier(v.astype(jnp.bfloat16)).astype(jnp.float32)

@jax.custom_vjp
def low_back(v):
    return v

def low_keep(v):
    return (low(v), None)

def low_pass(kept, grad):
    return (grad,)

def back_keep(v):
    return (v, None)

def back_low(kept, grad):
    return (low(grad),)
low.defvjp(low_keep, low_pass)
low_back.defvjp(back_keep, back_low)

def rms_norm(values, weight):
    return values * lax.rsqrt(lax.optimization_barrier(jnp.mean(values * values, axis=-1, keepdims=True)) + NORM_EPS) * weight

def angles(places):
    halves = jnp.arange(HD // 2, dtype=jnp.float32)
    inverse = ROPE_BASE ** (-2.0 * halves / HD)
    phase_angle = places.astype(jnp.float32)[:, None] * inverse[None, :]
    phase_angle = jnp.concatenate([phase_angle, phase_angle], axis=-1)
    return (jnp.cos(phase_angle)[:, None, :], jnp.sin(phase_angle)[:, None, :])

def rotate(values, cosine_table, sine_table):
    half_width = values.shape[-1] // 2
    turned = jnp.concatenate([-values[..., half_width:], values[..., :half_width]], axis=-1)
    return values * cosine_table + turned * sine_table

def dealt_indices():
    half_rows = TOK_DEV // 2
    row_ids = jnp.arange(LEN, dtype=jnp.int32)
    block_ids = row_ids // half_rows
    owner_dev = block_ids // 2
    place_ids = jnp.where(block_ids % 2 == 0, owner_dev, 2 * N_CTX - 1 - owner_dev)
    return (place_ids * half_rows + row_ids % half_rows).astype(jnp.int32)

def group_attention(block_items, allowed):
    queries, key_rows, value_rows = block_items
    score_scale = 1.0 / math.sqrt(HD)
    scores = low_back(jnp.einsum('tre,ke->trk', queries, key_rows, precision=HIGHEST) * score_scale)
    scores = jnp.where(allowed[:, None, :], scores, MASKED)
    highest = lax.optimization_barrier(jnp.max(scores, axis=-1, keepdims=True))
    expo_vals = jnp.exp(scores - highest)
    probabilities = low(expo_vals / lax.optimization_barrier(jnp.sum(expo_vals, axis=-1, keepdims=True)))
    return jnp.einsum('trk,ke->tre', probabilities, value_rows, precision=HIGHEST)

def layer_forward(inputs, weight_in, weight_out, gain_vals, cosine_table, sine_table, allowed):
    q_width = H_Q * HD
    kv_width = H_KV * HD
    attn_cols = q_width + 2 * kv_width
    repeat = H_Q // H_KV
    gain_one = gain_vals[:D]
    gain_two = gain_vals[D:2 * D]
    gain_query = gain_vals[2 * D:2 * D + HD]
    gain_key = gain_vals[2 * D + HD:]
    normed_in = low(rms_norm(inputs, gain_one))
    projected = low_back(jnp.dot(normed_in, weight_in[:, :attn_cols], precision=HIGHEST))
    query_raw = projected[:, :q_width].reshape(LEN, H_Q, HD)
    key_raw = projected[:, q_width:q_width + kv_width].reshape(LEN, H_KV, HD)
    value_low = low(projected[:, q_width + kv_width:].reshape(LEN, H_KV, HD))
    query_low = low(rotate(rms_norm(query_raw, gain_query), cosine_table, sine_table))
    key_low = low(rotate(rms_norm(key_raw, gain_key), cosine_table, sine_table))
    query_groups = query_low.reshape(LEN, H_KV, repeat, HD).transpose(1, 0, 2, 3)
    key_groups = key_low.transpose(1, 0, 2)
    value_groups = value_low.transpose(1, 0, 2)
    attended = lax.map(jax.checkpoint(lambda block_items: group_attention(block_items, allowed)), (query_groups, key_groups, value_groups))
    attended = attended.transpose(1, 0, 2, 3).reshape(LEN, q_width)
    attended = low_back(low(attended))
    branch_one = low_back(jnp.dot(attended, weight_out[:q_width], precision=HIGHEST))
    residual = inputs + branch_one
    normed_mid = low(rms_norm(residual, gain_two))
    gate_up = low_back(jnp.dot(normed_mid, weight_in[:, attn_cols:], precision=HIGHEST))
    hidden = low(jax.nn.silu(gate_up[:, :FF]) * gate_up[:, FF:])
    return residual + jnp.dot(hidden, weight_out[q_width:], precision=HIGHEST)

def adam_step(master, first_old, second_old, gradient, rate):
    first_new = BETA_ONE * first_old + (1.0 - BETA_ONE) * gradient
    second_new = BETA_TWO * second_old + (1.0 - BETA_TWO) * gradient * gradient
    first_hat = first_new / (1.0 - BETA_ONE ** STEP)
    second_hat = second_new / (1.0 - BETA_TWO ** STEP)
    master_new = master - rate * (first_hat / (jnp.sqrt(second_hat) + ADAM_EPS) + WEIGHT_DECAY * master)
    return (first_new, second_new, master_new)

def reference(tokens, cotangent, segments, positions, pad_mask, w_in, w_out, gains, first_in, first_out, first_gains, second_in, second_out, second_gains):
    used_in = low(w_in)
    used_out = low(w_out)
    used_gains = low(gains)
    indices = dealt_indices()
    row_ids = jnp.arange(LEN, dtype=jnp.int32)

    def per_sequence(running, sequence):
        seq_tokens, seq_cotangent, doc_ids, places, live_mask = sequence
        cosine_table, sine_table = angles(places)
        allowed = (indices[None, :] <= indices[:, None]) & (doc_ids[:, None] == doc_ids[None, :]) & ((live_mask[None, :] == 1) | (row_ids[None, :] == row_ids[:, None]))

        def forward(inputs, weight_in, weight_out, gain_vals):
            return layer_forward(inputs, weight_in, weight_out, gain_vals, cosine_table, sine_table, allowed)
        produced_out, pullback = jax.vjp(forward, seq_tokens.astype(jnp.float32), used_in, used_out, used_gains)
        grad_tokens, grad_in, grad_out, grad_gains = pullback(seq_cotangent.astype(jnp.float32))
        return ((running[0] + grad_in, running[1] + grad_out, running[2] + grad_gains), (produced_out, grad_tokens))
    initial = (jnp.zeros((D, CIN), jnp.float32), jnp.zeros((OUTR, D), jnp.float32), jnp.zeros((GN,), jnp.float32))
    totals, produced = lax.scan(per_sequence, initial, (tokens, cotangent, segments, positions, pad_mask))
    new_first_in, new_second_in, new_master_in = adam_step(w_in, first_in, second_in, totals[0], RATE_MATRIX)
    new_first_out, new_second_out, new_master_out = adam_step(w_out, first_out, second_out, totals[1], RATE_MATRIX)
    new_first_gains, new_second_gains, new_master_gains = adam_step(gains, first_gains, second_gains, totals[2], RATE_GAIN)
    return (produced[0], produced[1], new_first_in, new_first_out, new_first_gains, new_second_in, new_second_out, new_second_gains, new_master_in, new_master_out, new_master_gains, new_master_in.astype(jnp.bfloat16), new_master_out.astype(jnp.bfloat16))
```

```python
import functools
import math

import jax
import jax.numpy as jnp
from jax import lax
from jax.experimental import pallas as pl
from jax.experimental.pallas import tpu as pltpu
from jax.sharding import Mesh
from jax.sharding import PartitionSpec as P

H_Q = 16
H_KV = 8
HD = 128
FF = 3072
STEP = 5

NORM_EPS = 1e-06
ROPE_BASE = 1000000.0
BETA_ONE = 0.5
BETA_TWO = 0.5
ADAM_EPS = 1e-08
WEIGHT_DECAY = 0.1
RATE_MATRIX = 0.03
RATE_GAIN = 0.25

CTX = ("xh", "y", "core")
SHARD = ("xl", "z")
EVERY = CTX + SHARD
AXIS_X = ("xh", "xl")
AXIS_YZ = ("y", "z", "core")
SIZES = {"xh": 2, "y": 4, "core": 2, "xl": 2, "z": 4}

LOG2_E = 1.4426950408889634
SCORE_SCALE = 1.0 / math.sqrt(HD)
BQ = 256
BK = 512
VMEM_BYTES = 48 * 1024 * 1024

bf16 = jnp.bfloat16
f32 = jnp.float32


def rms_norm(values, weight):
    return values * lax.rsqrt(jnp.mean(values * values, axis=-1, keepdims=True) + NORM_EPS) * weight


def rms_back(values, weight, upstream):
    inverse = lax.rsqrt(jnp.mean(values * values, axis=-1, keepdims=True) + NORM_EPS)
    normed = values * inverse
    scaled = upstream * weight
    grad_values = inverse * (scaled - normed * jnp.mean(scaled * normed, axis=-1, keepdims=True))
    return (grad_values, upstream * normed)


def dot_nt(a, b):
    return lax.dot_general(a, b, (((1,), (1,)), ((), ())), preferred_element_type=f32)


def dot_tn(a, b):
    return lax.dot_general(a, b, (((0,), (0,)), ((), ())), preferred_element_type=f32)


def dot_nn(a, b):
    return lax.dot_general(a, b, (((1,), (0,)), ((), ())), preferred_element_type=f32)


def project_kernel(a_ref, w_ref, cos_ref, sin_ref, gq_ref, gk_ref, send_ref, qraw_ref, kraw_ref):
    prod = dot_nn(a_ref[...], w_ref[...])
    cos = cos_ref[...]
    sin = sin_ref[...]

    def roped(raw, gain):
        normed = rms_norm(raw, gain)
        return normed * cos + pltpu.roll(normed, HD // 2, 1) * sin

    key_raw = prod[:, 2 * HD : 3 * HD]
    key = roped(key_raw, gk_ref[...]).astype(bf16)
    value = prod[:, 3 * HD :].astype(bf16)
    kraw_ref[0] = key_raw
    for r in range(2):
        raw = prod[:, r * HD : (r + 1) * HD]
        qraw_ref[r] = raw
        send_ref[r, 0] = (roped(raw, gq_ref[...]) * (SCORE_SCALE * LOG2_E)).astype(bf16)
        send_ref[r, 1] = key
        send_ref[r, 2] = value


def project(a, w, cos, sin, gq, gk):
    rows, width = a.shape
    whole = lambda j: (0, 0)
    return pl.pallas_call(
        project_kernel,
        grid=(H_KV,),
        in_specs=[
            pl.BlockSpec((rows, width), whole),
            pl.BlockSpec((width, 4 * HD), lambda j: (0, j)),
            pl.BlockSpec((rows, HD), whole),
            pl.BlockSpec((rows, HD), whole),
            pl.BlockSpec((1, HD), whole),
            pl.BlockSpec((1, HD), whole),
        ],
        out_specs=[
            pl.BlockSpec((2, 3, rows, HD), lambda j: (j, 0, 0, 0)),
            pl.BlockSpec((2, rows, HD), lambda j: (j, 0, 0)),
            pl.BlockSpec((1, rows, HD), lambda j: (j, 0, 0)),
        ],
        out_shape=[
            jax.ShapeDtypeStruct((H_Q, 3, rows, HD), bf16),
            jax.ShapeDtypeStruct((H_Q, rows, HD), f32),
            jax.ShapeDtypeStruct((H_KV, rows, HD), f32),
        ],
        compiler_params=pltpu.CompilerParams(vmem_limit_bytes=VMEM_BYTES),
        name="project",
    )(a, w, cos, sin, gq, gk)


def project_back_kernel(
    recv_ref, qraw_ref, kraw_ref, cos_ref, sin_ref, gq_ref, gk_ref, w_ref, at_ref, dw_ref, da_ref, dg_ref
):
    step = pl.program_id(0)
    cos = cos_ref[...]
    sin = sin_ref[...]

    def back(raw, gain, grad):
        unrot = grad * cos + pltpu.roll(grad * sin, HD // 2, 1)
        return rms_back(raw, gain, unrot)

    pieces = []
    gq_terms = jnp.zeros((1, HD), f32)
    for r in range(2):
        grad, terms = back(qraw_ref[r], gq_ref[...], recv_ref[r, 0].astype(f32))
        pieces.append(grad.astype(bf16))
        gq_terms = gq_terms + jnp.sum(terms, axis=0, keepdims=True)
    grad_key = recv_ref[0, 1].astype(f32) + recv_ref[1, 1].astype(f32)
    grad, terms = back(kraw_ref[0], gk_ref[...], grad_key)
    gk_terms = jnp.sum(terms, axis=0, keepdims=True)
    pieces.append(grad.astype(bf16))
    pieces.append((recv_ref[0, 2].astype(f32) + recv_ref[1, 2].astype(f32)).astype(bf16))
    dproj = jnp.concatenate(pieces, axis=1)
    dw_ref[...] = dot_nn(at_ref[...], dproj).astype(bf16)
    part = dot_nt(dproj, w_ref[...])
    both = jnp.concatenate([gq_terms, gk_terms, jnp.zeros((6, HD), f32)], axis=0)

    @pl.when(step == 0)
    def _():
        da_ref[...] = part
        dg_ref[...] = both

    @pl.when(step > 0)
    def _():
        da_ref[...] += part
        dg_ref[...] += both


def project_back(recv, qraw, kraw, cos, sin, gq, gk, w, at):
    width, rows = at.shape
    whole = lambda j: (0, 0)
    return pl.pallas_call(
        project_back_kernel,
        grid=(H_KV,),
        in_specs=[
            pl.BlockSpec((2, 3, rows, HD), lambda j: (j, 0, 0, 0)),
            pl.BlockSpec((2, rows, HD), lambda j: (j, 0, 0)),
            pl.BlockSpec((1, rows, HD), lambda j: (j, 0, 0)),
            pl.BlockSpec((rows, HD), whole),
            pl.BlockSpec((rows, HD), whole),
            pl.BlockSpec((1, HD), whole),
            pl.BlockSpec((1, HD), whole),
            pl.BlockSpec((width, 4 * HD), lambda j: (0, j)),
            pl.BlockSpec((width, rows), whole),
        ],
        out_specs=[
            pl.BlockSpec((width, 4 * HD), lambda j: (0, j)),
            pl.BlockSpec((rows, width), whole),
            pl.BlockSpec((8, HD), whole),
        ],
        out_shape=[
            jax.ShapeDtypeStruct((width, 4 * HD * H_KV), bf16),
            jax.ShapeDtypeStruct((rows, width), f32),
            jax.ShapeDtypeStruct((8, HD), f32),
        ],
        compiler_params=pltpu.CompilerParams(vmem_limit_bytes=VMEM_BYTES),
        name="project_back",
    )(recv, qraw, kraw, cos, sin, gq, gk, w, at)


def dealt_slot(place, n_dev):
    if place < n_dev:
        return place, 0
    return 2 * n_dev - 1 - place, 1


def key_mask(len_row, offset):
    ahead = (
        lax.broadcasted_iota(jnp.int32, (BK, BQ), 1)
        - lax.broadcasted_iota(jnp.int32, (BK, BQ), 0)
        + offset
    )
    return (ahead >= 0) & (ahead <= len_row)


def attend_kernel(klo_ref, x_ref, len_ref, osend_ref, onat_ref, linv_ref, qn, kn, vt):
    n_dev = x_ref.shape[0]
    half = x_ref.shape[2] // 2
    span = qn.shape[0]
    for place in range(2 * n_dev):
        dev, side = dealt_slot(place, n_dev)
        rows = slice(side * half, (side + 1) * half)
        to = slice(place * half, (place + 1) * half)
        qn[to, :] = x_ref[dev, 0, rows, :]
        kn[to, :] = x_ref[dev, 1, rows, :]
        vt[:, to] = x_ref[dev, 2, rows, :].astype(f32).T.astype(bf16)

    def q_step(qb, _):
        q_at = pl.multiple_of(qb * BQ, BQ)
        q_blk = qn[pl.ds(q_at, BQ), :]
        len_row = len_ref[pl.ds(qb, 1), :]

        def k_step(kb, carry):
            acc, total = carry
            k_at = pl.multiple_of(kb * BK, BK)
            s = dot_nt(kn[pl.ds(k_at, BK), :], q_blk)
            p = jnp.where(key_mask(len_row, q_at - k_at), jnp.exp2(s), 0.0)
            total = total + jnp.sum(p.reshape(BK // 8, 8, BQ), axis=0)
            acc = acc + dot_nn(vt[:, pl.ds(k_at, BK)], p.astype(bf16))
            return acc, total

        acc, total = lax.fori_loop(
            klo_ref[qb],
            (q_at + BQ - 1) // BK + 1,
            k_step,
            (jnp.zeros((HD, BQ), f32), jnp.zeros((8, BQ), f32)),
        )
        inverse = 1.0 / jnp.sum(total, axis=0, keepdims=True)
        linv_ref[pl.ds(qb, 1), :] = inverse
        out = (acc * inverse).T
        onat_ref[pl.ds(q_at, BQ), :] = out
        return 0

    lax.fori_loop(0, span // BQ, q_step, 0)
    for place in range(2 * n_dev):
        dev, side = dealt_slot(place, n_dev)
        osend_ref[dev, side * half : (side + 1) * half, :] = onat_ref[
            place * half : (place + 1) * half, :
        ].astype(bf16)


def vmem():
    return pl.BlockSpec(memory_space=pltpu.VMEM)


def attend(klo, x, lens):
    n_dev, _, rows, _ = x.shape
    span = n_dev * rows
    return pl.pallas_call(
        attend_kernel,
        in_specs=[pl.BlockSpec(memory_space=pltpu.SMEM), vmem(), vmem()],
        out_specs=[vmem(), vmem(), vmem()],
        out_shape=[
            jax.ShapeDtypeStruct((n_dev, rows, HD), bf16),
            jax.ShapeDtypeStruct((span, HD), f32),
            jax.ShapeDtypeStruct((span // BQ, BQ), f32),
        ],
        scratch_shapes=[
            pltpu.VMEM((span, HD), bf16),
            pltpu.VMEM((span, HD), bf16),
            pltpu.VMEM((HD, span), bf16),
        ],
        compiler_params=pltpu.CompilerParams(vmem_limit_bytes=VMEM_BYTES),
        name="attend",
    )(klo, x, lens)


def attend_back_kernel(
    klo_ref, x_ref, do_ref, onat_ref, linv_ref, len_ref, send_ref, qn, kn, vn, kt, don, dq, dk, dv
):
    n_dev = x_ref.shape[0]
    half = x_ref.shape[2] // 2
    span = qn.shape[0]
    for place in range(2 * n_dev):
        dev, side = dealt_slot(place, n_dev)
        rows = slice(side * half, (side + 1) * half)
        to = slice(place * half, (place + 1) * half)
        qn[to, :] = x_ref[dev, 0, rows, :]
        key = x_ref[dev, 1, rows, :]
        kn[to, :] = key
        kt[:, to] = key.astype(f32).T.astype(bf16)
        vn[to, :] = x_ref[dev, 2, rows, :]
        don[to, :] = do_ref[dev, rows, :]
    dk[...] = jnp.zeros_like(dk)
    dv[...] = jnp.zeros_like(dv)

    def q_step(qb, _):
        q_at = pl.multiple_of(qb * BQ, BQ)
        q_blk = qn[pl.ds(q_at, BQ), :]
        do_blk = don[pl.ds(q_at, BQ), :]
        len_row = len_ref[pl.ds(qb, 1), :]
        inverse = linv_ref[pl.ds(qb, 1), :]
        mixed = (do_blk.astype(f32) * onat_ref[pl.ds(q_at, BQ), :]).T
        delta = jnp.sum(mixed, axis=0, keepdims=True)

        def k_step(kb, acc):
            k_at = pl.multiple_of(kb * BK, BK)
            here = pl.ds(k_at, BK)
            s = dot_nt(kn[here, :], q_blk)
            p = jnp.where(key_mask(len_row, q_at - k_at), jnp.exp2(s) * inverse, 0.0)
            dp = dot_nt(vn[here, :], do_blk)
            ds = (p * (dp - delta)).astype(bf16)
            dv[here, :] += dot_nn(p.astype(bf16), do_blk)
            dk[here, :] += dot_nn(ds, q_blk)
            return acc + dot_nn(kt[:, here], ds)

        acc = lax.fori_loop(
            klo_ref[qb], (q_at + BQ - 1) // BK + 1, k_step, jnp.zeros((HD, BQ), f32)
        )
        dq[pl.ds(q_at, BQ), :] = (acc * SCORE_SCALE).T
        return 0

    lax.fori_loop(0, span // BQ, q_step, 0)
    for place in range(2 * n_dev):
        dev, side = dealt_slot(place, n_dev)
        rows = slice(side * half, (side + 1) * half)
        at = slice(place * half, (place + 1) * half)
        send_ref[dev, 0, rows, :] = dq[at, :].astype(bf16)
        send_ref[dev, 1, rows, :] = (dk[at, :] * (1.0 / LOG2_E)).astype(bf16)
        send_ref[dev, 2, rows, :] = dv[at, :].astype(bf16)


def attend_back(klo, x, do, onat, linv, lens):
    n_dev, _, rows, _ = x.shape
    span = n_dev * rows
    return pl.pallas_call(
        attend_back_kernel,
        in_specs=[pl.BlockSpec(memory_space=pltpu.SMEM)] + [vmem()] * 5,
        out_specs=vmem(),
        out_shape=jax.ShapeDtypeStruct((n_dev, 3, rows, HD), bf16),
        scratch_shapes=[
            pltpu.VMEM((span, HD), bf16),
            pltpu.VMEM((span, HD), bf16),
            pltpu.VMEM((span, HD), bf16),
            pltpu.VMEM((HD, span), bf16),
            pltpu.VMEM((span, HD), bf16),
            pltpu.VMEM((span, HD), f32),
            pltpu.VMEM((span, HD), f32),
            pltpu.VMEM((span, HD), f32),
        ],
        compiler_params=pltpu.CompilerParams(vmem_limit_bytes=VMEM_BYTES),
        name="attend_back",
    )(klo, x, do, onat, linv, lens)


OUT_ROWS = 160
CHUNK_ROWS = 32
N_CHUNKS = 3
CHUNK = FF // N_CHUNKS


def middle_kernel(
    full_ref,
    mixed_ref,
    tok_ref,
    cot_ref,
    gain_ref,
    shuffle_ref,
    gate_ref,
    up_ref,
    out_ref,
    dres_ref,
    dob_ref,
    feat_ref,
    drb_ref,
    grad_ref,
    dgain_ref,
    w_out,
    resid,
    mid_low,
    grad_mid,
    grad_up,
    sems,
):
    step = pl.program_id(0)
    q_width = H_Q * HD
    width = tok_ref.shape[1]

    def fetch(i):
        return pltpu.make_async_copy(
            full_ref.at[i, pl.ds(0, OUT_ROWS), :],
            w_out.at[pl.ds(i * OUT_ROWS, OUT_ROWS), :],
            sems.at[i],
        )

    n_fetch = full_ref.shape[0]
    n_first = -(-q_width // OUT_ROWS)

    @pl.when(step == 0)
    def _():
        for i in range(n_fetch):
            fetch(i).start()
        for h in range(H_Q):
            feat_ref[:, h * HD : (h + 1) * HD] = mixed_ref[h]
        for i in range(n_first):
            fetch(i).wait()
        residual = tok_ref[...].astype(f32) + dot_nn(feat_ref[:, :q_width], w_out[:q_width, :])
        resid[...] = residual
        out_ref[...] = residual
        normed = rms_norm(residual, gain_ref[...]).astype(bf16)
        mid_low[...] = dot_nn(normed, shuffle_ref[...]).astype(bf16)
        grad_mid[...] = jnp.zeros_like(grad_mid)
        for i in range(n_first, n_fetch):
            fetch(i).wait()

    @pl.when((step > 0) & (step < 2 * N_CHUNKS + 1) & (step % 2 == 1))
    def _():
        at = pl.multiple_of(q_width + ((step - 1) // 2) * CHUNK, CHUNK)
        gate_w = gate_ref[...].reshape(width, CHUNK)
        gate = dot_nn(mid_low[...], gate_w)
        up = dot_nn(mid_low[...], up_ref[...].reshape(width, CHUNK))
        sigmoid_gate = 1.0 / (1.0 + jnp.exp(-gate))
        activated = gate * sigmoid_gate
        hidden = (activated * up).astype(bf16)
        feat_ref[:, pl.ds(at, CHUNK)] = hidden
        down_w = w_out[pl.ds(at, CHUNK), :]
        out_ref[...] += dot_nn(hidden, down_w)
        grad_hidden = dot_nt(cot_ref[...], down_w)
        grad_up[...] = (grad_hidden * activated).astype(bf16)
        grad_gate = (
            grad_hidden * up * sigmoid_gate * (1.0 + gate * (1.0 - sigmoid_gate))
        ).astype(bf16)
        grad_mid[...] += dot_nt(grad_gate, gate_w)
        grad_ref[...] = dot_tn(mid_low[...], grad_gate).astype(bf16).reshape(grad_ref.shape)

    @pl.when((step > 0) & (step < 2 * N_CHUNKS + 1) & (step % 2 == 0))
    def _():
        grad_mid[...] += dot_nt(grad_up[...], up_ref[...].reshape(width, CHUNK))
        grad_ref[...] = dot_tn(mid_low[...], grad_up[...]).astype(bf16).reshape(grad_ref.shape)

    @pl.when(step == 2 * N_CHUNKS + 1)
    def _():
        grad = dot_nt(grad_mid[...].astype(bf16), shuffle_ref[...])
        part, terms = rms_back(resid[...], gain_ref[...], grad)
        dgain_ref[...] = jnp.sum(terms, axis=0, keepdims=True)
        dres = cot_ref[...].astype(f32) + part
        dres_ref[...] = dres
        low = dres.astype(bf16)
        drb_ref[...] = low
        for c in range(4):
            piece = dot_nt(low, w_out[c * 4 * HD : (c + 1) * 4 * HD, :]).astype(bf16)
            for h in range(4):
                dob_ref[4 * c + h] = piece[:, h * HD : (h + 1) * HD]


def middle(full, mixed, tok, cot, gain, shuffle):
    rows, width = tok.shape
    n_blocks = full.shape[0]
    first = OUT_ROWS // CHUNK_ROWS
    q_width = H_Q * HD

    def chunk_of(i):
        return jnp.clip((i - 1) // 2, 0, N_CHUNKS - 1)

    def grad_at(i):
        i = jnp.clip(i, 1, 2 * N_CHUNKS)
        return (0, first + N_CHUNKS * ((i - 1) % 2) + (i - 1) // 2, 0)

    def whole(shape):
        return pl.BlockSpec(shape, lambda i: (0,) * len(shape))

    return pl.pallas_call(
        middle_kernel,
        grid=(2 * N_CHUNKS + 2,),
        in_specs=[
            pl.BlockSpec(memory_space=pl.ANY),
            whole((H_Q, rows, HD)),
            whole((rows, width)),
            whole((rows, width)),
            whole((1, width)),
            whole((width, width)),
            pl.BlockSpec((n_blocks, CHUNK_ROWS, CHUNK), lambda i: (0, first + chunk_of(i), 0)),
            pl.BlockSpec(
                (n_blocks, CHUNK_ROWS, CHUNK), lambda i: (0, first + N_CHUNKS + chunk_of(i), 0)
            ),
        ],
        out_specs=[
            whole((rows, width)),
            whole((rows, width)),
            whole((H_Q, rows, HD)),
            whole((rows, q_width + FF)),
            whole((rows, width)),
            pl.BlockSpec((n_blocks, CHUNK_ROWS, CHUNK), grad_at),
            whole((1, width)),
        ],
        out_shape=[
            jax.ShapeDtypeStruct((rows, width), f32),
            jax.ShapeDtypeStruct((rows, width), f32),
            jax.ShapeDtypeStruct((H_Q, rows, HD), bf16),
            jax.ShapeDtypeStruct((rows, q_width + FF), bf16),
            jax.ShapeDtypeStruct((rows, width), bf16),
            jax.ShapeDtypeStruct(full.shape, bf16),
            jax.ShapeDtypeStruct((1, width), f32),
        ],
        scratch_shapes=[
            pltpu.VMEM((q_width + FF, width), bf16),
            pltpu.VMEM((rows, width), f32),
            pltpu.VMEM((rows, width), bf16),
            pltpu.VMEM((rows, width), f32),
            pltpu.VMEM((rows, CHUNK), bf16),
            pltpu.SemaphoreType.DMA((n_blocks,)),
        ],
        compiler_params=pltpu.CompilerParams(vmem_limit_bytes=VMEM_BYTES),
        name="middle",
    )(full, mixed, tok, cot, gain, shuffle, full, full)


def grad_out_kernel(feat_ref, drb_ref, cot_ref, grads_ref, out_ref):
    step = pl.program_id(0)
    q_width = H_Q * HD
    block = feat_ref.shape[1]
    both = q_width // block
    cut = q_width % block

    def store(value):
        out_ref[...] = value.astype(bf16).reshape(out_ref.shape)

    @pl.when(step < both)
    def _():
        store(dot_tn(feat_ref[...], drb_ref[...]))

    @pl.when(step == both)
    def _():
        upper = dot_tn(feat_ref[:, :cut], drb_ref[...])
        lower = dot_tn(feat_ref[:, cut:], cot_ref[...])
        store(jnp.concatenate([upper, lower], axis=0))

    @pl.when(step > both)
    def _():
        store(dot_tn(feat_ref[...], cot_ref[...]))


def grad_out(feat, drb, cot, grads):
    rows, n_features = feat.shape
    width = drb.shape[1]
    blocks = 4
    return pl.pallas_call(
        grad_out_kernel,
        grid=(grads.shape[0] // blocks,),
        in_specs=[
            pl.BlockSpec((rows, blocks * OUT_ROWS), lambda i: (0, i)),
            pl.BlockSpec((rows, width), lambda i: (0, 0)),
            pl.BlockSpec((rows, width), lambda i: (0, 0)),
            pl.BlockSpec(memory_space=pl.ANY),
        ],
        out_specs=pl.BlockSpec((blocks, OUT_ROWS, width), lambda i: (i, 0, 0)),
        out_shape=jax.ShapeDtypeStruct(grads.shape, bf16),
        input_output_aliases={3: 0},
        compiler_params=pltpu.CompilerParams(vmem_limit_bytes=VMEM_BYTES),
        name="grad_out",
    )(feat, drb, cot, grads)


def adam_step(master, first_old, second_old, gradient, rate):
    first_new = BETA_ONE * first_old + (1.0 - BETA_ONE) * gradient
    second_new = BETA_TWO * second_old + (1.0 - BETA_TWO) * gradient * gradient
    first_hat = first_new / (1.0 - BETA_ONE**STEP)
    second_hat = second_new / (1.0 - BETA_TWO**STEP)
    master_new = master - rate * (
        first_hat / (jnp.sqrt(second_hat) + ADAM_EPS) + WEIGHT_DECAY * master
    )
    return (first_new, second_new, master_new)


def gathered(x):
    return lax.all_gather(x, AXIS_YZ, axis=0, tiled=True)


def sum_over_x(blocks):
    me = lax.axis_index(AXIS_X)
    n = blocks.shape[0]

    def block(i):
        return lax.dynamic_index_in_dim(blocks, lax.rem(i, n), 0, keepdims=False)

    total = block(me).astype(f32)
    for shift in range(1, n):
        pairs = [(i, (i + shift) % n) for i in range(n)]
        total = total + lax.ppermute(block(me + shift), AXIS_X, pairs).astype(f32)
    return total


def natural_of_permuted(x):
    tail = x.shape[1:]
    x = x.reshape((4, 4, 2, 2, 2) + tail)
    x = x.transpose((3, 0, 2, 4, 1) + tuple(range(5, 5 + len(tail))))
    return x.reshape((128,) + tail)


def owner_pairs():
    pairs = []
    for n in range(128):
        z = n % 4
        xl = (n // 4) % 2
        core = (n // 8) % 2
        y = (n // 16) % 4
        xh = n // 64
        pairs.append((n, (((y * 4 + z) * 2 + core) * 2 + xh) * 2 + xl))
    return pairs


def body(
    tokens,
    cotangent,
    segments,
    positions,
    pad_mask,
    w_in,
    w_out,
    gains,
    first_in,
    first_out,
    first_gains,
    second_in,
    second_out,
    second_gains,
):
    rows = tokens.shape[1]
    width = tokens.shape[2]
    span = segments.shape[1]
    half = rows // 2
    n_ctx = span // rows
    q_width = H_Q * HD
    kv_width = H_KV * HD
    attn_cols = q_width + 2 * kv_width
    owned = w_in.shape[0]
    owned_gains = gains.shape[0]

    low_in = w_in.astype(bf16)
    own_qkv = jnp.concatenate(
        [
            low_in[:, :q_width].reshape(owned, H_KV, 2 * HD),
            low_in[:, q_width : q_width + kv_width].reshape(owned, H_KV, HD),
            low_in[:, q_width + kv_width : attn_cols].reshape(owned, H_KV, HD),
        ],
        axis=2,
    ).reshape(owned, attn_cols)
    own_gains = jnp.pad(gains.astype(bf16)[None, :], ((0, owned - 1), (0, HD - owned_gains)))
    packed = jnp.concatenate([own_qkv, own_gains, low_in[:, attn_cols:]], axis=1)
    packed = lax.all_gather(packed, AXIS_X, axis=0, tiled=True)
    w_qkv = gathered(packed[:, : attn_cols + HD])
    pairs = owner_pairs()
    own_out = lax.ppermute(w_out.astype(bf16), EVERY, [(p, n) for n, p in pairs])
    own_out = lax.all_gather(own_out, AXIS_X, axis=0, tiled=True)
    own_ffn = packed[:, attn_cols + HD :].reshape(CHUNK_ROWS, 2 * N_CHUNKS, CHUNK)
    own_ffn = own_ffn.transpose(1, 0, 2).reshape(2 * N_CHUNKS * CHUNK_ROWS, CHUNK)
    full = gathered(jnp.concatenate([own_out, own_ffn], axis=0)[None])

    gain_rows = w_qkv[:, attn_cols:].reshape(width // owned, owned, HD)[:, 0, :owned_gains]
    gain_vals = natural_of_permuted(gain_rows).reshape(-1).astype(f32)
    gain_one = gain_vals[:width]
    gain_two = gain_vals[width : 2 * width]
    gain_query = gain_vals[2 * width : 2 * width + HD].reshape(1, HD)
    gain_key = gain_vals[2 * width + HD :].reshape(1, HD)

    order = natural_of_permuted(jnp.arange(width, dtype=jnp.int32).reshape(width // owned, owned)).reshape(-1)
    shuffle = (order[:, None] == jnp.arange(width, dtype=jnp.int32)[None, :]).astype(bf16)

    inputs = tokens[0].astype(f32)
    halves = jnp.arange(HD // 2, dtype=f32)
    inverse = ROPE_BASE ** (-2.0 * halves / HD)
    angle = positions[0].astype(f32)[:, None] * inverse[None, :]
    cos_half = jnp.cos(angle)
    sin_half = jnp.sin(angle)
    cos = jnp.concatenate([cos_half, cos_half], axis=1)
    sin = jnp.concatenate([-sin_half, sin_half], axis=1)

    def natural(x):
        x = x.reshape(n_ctx, 2, half)
        return jnp.concatenate([x[:, 0], x[::-1, 1]], axis=0)

    docs = natural(segments[0])
    live = natural(pad_mask[0])
    at = jnp.arange(span, dtype=jnp.int32).reshape(2 * n_ctx, half)
    start = jnp.zeros_like(docs)
    for number in range(1, 14):
        before = jnp.sum((docs < number).astype(jnp.int32))
        start = jnp.where(docs == number, before, start)
    lens = jnp.where(live == 1, at - start, 0)
    klo = jnp.min((at - lens).reshape(span // BQ, BQ), axis=1) // BK
    lens = lens.reshape(span // BQ, BQ)

    a = rms_norm(inputs, gain_one).astype(bf16)
    a_perm = dot_nn(a, shuffle).astype(bf16)
    send, query_raw, key_raw = project(a_perm, w_qkv, cos, sin, gain_query, gain_key)
    x = lax.all_to_all(send, CTX, 0, 0, tiled=True)
    o_send, o_nat, l_inv = attend(klo, x, lens)
    mixed = lax.all_to_all(o_send, CTX, 0, 0, tiled=True)

    output, grad_residual, do_send, features, resid_low, grads, gain_two_terms = middle(
        full, mixed, tokens[0], cotangent[0], gain_two.reshape(1, width), shuffle
    )
    do = lax.all_to_all(do_send, CTX, 0, 0, tiled=True)
    grads = grad_out(features, resid_low, cotangent[0], grads)
    do, grads = lax.optimization_barrier((do, grads))
    grads = lax.psum_scatter(grads, AXIS_YZ, scatter_dimension=0, tiled=True)[0]
    n_x = 4

    d_send = attend_back(klo, x, do, o_nat, l_inv, lens)
    d_recv = lax.all_to_all(d_send, CTX, 0, 0, tiled=True)
    grad_w_qkv, da_perm, gain_qk = project_back(
        d_recv, query_raw, key_raw, cos, sin, gain_query, gain_key, w_qkv, a_perm.T
    )
    grad_w_qkv, grads = lax.optimization_barrier((grad_w_qkv, grads))
    out_part = grads[:OUT_ROWS].reshape(n_x, OUT_ROWS // n_x, width)
    ffn_part = grads[OUT_ROWS:].reshape(2 * N_CHUNKS, n_x, owned, CHUNK)
    ffn_part = ffn_part.transpose(1, 0, 2, 3).reshape(n_x, 2 * N_CHUNKS * owned, CHUNK)
    grads = sum_over_x(jnp.concatenate([out_part, ffn_part], axis=1))
    owned_out = lax.ppermute(grads[: OUT_ROWS // n_x], EVERY, pairs)
    owned_ffn = grads[OUT_ROWS // n_x :].reshape(2 * N_CHUNKS, owned, CHUNK)
    owned_ffn = owned_ffn.transpose(1, 0, 2).reshape(owned, 2 * FF)
    grad_w_qkv = lax.psum_scatter(grad_w_qkv, AXIS_YZ, scatter_dimension=0, tiled=True)
    grad_a = dot_nt(da_perm.astype(bf16), shuffle)
    grad_in_part, gain_one_terms = rms_back(inputs, gain_one, grad_a)
    input_grad = grad_residual + grad_in_part
    grad_gains = jnp.concatenate(
        [jnp.sum(gain_one_terms, axis=0), gain_two_terms[0], gain_qk[0], gain_qk[1]]
    )
    owned_gain_grad = lax.psum_scatter(grad_gains, EVERY, scatter_dimension=0, tiled=True)
    grad_w_qkv, owned_gain_grad = lax.optimization_barrier((grad_w_qkv, owned_gain_grad))
    owned_qkv = sum_over_x(grad_w_qkv.reshape(n_x, owned, attn_cols)).reshape(owned, H_KV, 4 * HD)
    owned_in = jnp.concatenate(
        [
            owned_qkv[:, :, : 2 * HD].reshape(owned, q_width),
            owned_qkv[:, :, 2 * HD : 3 * HD].reshape(owned, kv_width),
            owned_qkv[:, :, 3 * HD :].reshape(owned, kv_width),
            owned_ffn,
        ],
        axis=1,
    )
    new_first_in, new_second_in, new_master_in = adam_step(
        w_in, first_in, second_in, owned_in, RATE_MATRIX
    )
    new_first_out, new_second_out, new_master_out = adam_step(
        w_out, first_out, second_out, owned_out, RATE_MATRIX
    )
    new_first_gains, new_second_gains, new_master_gains = adam_step(
        gains, first_gains, second_gains, owned_gain_grad, RATE_GAIN
    )
    return (
        output[None],
        input_grad[None],
        new_first_in,
        new_first_out,
        new_first_gains,
        new_second_in,
        new_second_out,
        new_second_gains,
        new_master_in,
        new_master_out,
        new_master_gains,
        new_master_in.astype(bf16),
        new_master_out.astype(bf16),
    )


def solution(mesh):
    cut = Mesh(mesh.devices.reshape(tuple(SIZES[name] for name in EVERY)), EVERY)
    weights = P(EVERY, None)
    vector = P(EVERY)
    acts = P(SHARD, CTX, None)
    in_specs = (
        acts,
        acts,
        P(SHARD, None),
        P(SHARD, CTX),
        P(SHARD, None),
    ) + (weights, weights, vector) * 3
    out_specs = (acts, acts) + (weights, weights, vector) * 3 + (weights, weights)
    return jax.shard_map(body, mesh=cut, in_specs=in_specs, out_specs=out_specs, check_vma=False)
```

```python
import functools
import math

import jax
import jax.numpy as jnp
from jax import lax
from jax.experimental import pallas as pl
from jax.experimental.pallas import tpu as pltpu
from jax.sharding import Mesh
from jax.sharding import PartitionSpec as P

H_Q = 16
H_KV = 8
HD = 128
FF = 3072
STEP = 5

NORM_EPS = 1e-06
ROPE_BASE = 1000000.0
BETA_ONE = 0.5
BETA_TWO = 0.5
ADAM_EPS = 1e-08
WEIGHT_DECAY = 0.1
RATE_MATRIX = 0.03
RATE_GAIN = 0.25

CTX = ("xh", "y", "core")
SHARD = ("xl", "z")
EVERY = CTX + SHARD
AXIS_X = ("xh", "xl")
AXIS_YZ = ("y", "z", "core")
SIZES = {"xh": 2, "y": 4, "core": 2, "xl": 2, "z": 4}

LOG2_E = 1.4426950408889634
SCORE_SCALE = 1.0 / math.sqrt(HD)
BQ = 256
BK = 512
VMEM_BYTES = 48 * 1024 * 1024
BIG_VMEM_BYTES = 60 * 1024 * 1024

bf16 = jnp.bfloat16
f32 = jnp.float32


def rms_norm(values, weight):
    return values * lax.rsqrt(jnp.mean(values * values, axis=-1, keepdims=True) + NORM_EPS) * weight


def rms_back(values, weight, upstream):
    inverse = lax.rsqrt(jnp.mean(values * values, axis=-1, keepdims=True) + NORM_EPS)
    normed = values * inverse
    scaled = upstream * weight
    grad_values = inverse * (scaled - normed * jnp.mean(scaled * normed, axis=-1, keepdims=True))
    return (grad_values, upstream * normed)


def dot_nt(a, b):
    return lax.dot_general(a, b, (((1,), (1,)), ((), ())), preferred_element_type=f32)


def dot_tn(a, b):
    return lax.dot_general(a, b, (((0,), (0,)), ((), ())), preferred_element_type=f32)


def dot_nn(a, b):
    return lax.dot_general(a, b, (((1,), (0,)), ((), ())), preferred_element_type=f32)


N_GROUPS = 4
GROUP = 8
HALF = 128
STEP_BLOCKS = 4
STEPS = GROUP // STEP_BLOCKS
HEAD_COLS = 3 * HD
PAD_COLS = 4 * HD


def block_spec(width, first, count):
    return pl.BlockSpec(
        (STEP_BLOCKS, HALF, width), lambda i, place: (jnp.clip(i - first, 0, count - 1), 0, 0)
    )


def group_specs(width):
    return [block_spec(width, k * STEPS, STEPS) for k in range(N_GROUPS)]


def fixed(shape):
    return pl.BlockSpec(shape, lambda i, place: (0,) * len(shape))


def rows_of(place_ref, step, i):
    return pl.ds(pl.multiple_of(place_ref[step * STEP_BLOCKS + i] * HALF, HALF), HALF)


def project_kernel(
    place_ref, x0, x1, x2, x3, w_ref, cos_ref, sin_ref, gq_ref, gk_ref,
    q_ref, k_ref, v_ref, qraw_ref, kraw_ref, inv_ref,
):
    step = pl.program_id(0)

    def run(x):
        wide = x.astype(f32)
        inverse = lax.rsqrt(jnp.mean(wide * wide, axis=-1, keepdims=True) + NORM_EPS)
        prod = dot_nn(x, w_ref[...]) * inverse
        for i in range(STEP_BLOCKS):
            at = rows_of(place_ref, step, i)
            part = slice(i * HALF, (i + 1) * HALF)
            cos = cos_ref[at, :]
            sin = sin_ref[at, :]

            def roped(raw, gain, cos=cos, sin=sin):
                normed = rms_norm(raw, gain)
                return normed * cos + pltpu.roll(normed, HD // 2, 1) * sin

            query = prod[part, :HD]
            key = prod[part, HD : 2 * HD]
            inv_ref[at, :] = jnp.broadcast_to(inverse[part], (HALF, HD))
            qraw_ref[at, :] = query
            kraw_ref[at, :] = key
            q_ref[at, :] = (roped(query, gq_ref[...]) * (SCORE_SCALE * LOG2_E)).astype(bf16)
            k_ref[at, :] = roped(key, gk_ref[...]).astype(bf16)
            v_ref[at, :] = prod[part, 2 * HD :].astype(bf16)

    for k, x_ref in enumerate((x0, x1, x2, x3)):

        @pl.when(step // STEPS == k)
        def _(x_ref=x_ref):
            run(x_ref[...].reshape(STEP_BLOCKS * HALF, x_ref.shape[2]))


def project(place, groups, w, cos, sin, gq, gk):
    width = w.shape[0]
    span = cos.shape[0]
    low = jax.ShapeDtypeStruct((span, HD), bf16)
    wide = jax.ShapeDtypeStruct((span, HD), f32)
    whole = fixed((span, HD))
    return pl.pallas_call(
        project_kernel,
        grid_spec=pltpu.PrefetchScalarGridSpec(
            num_scalar_prefetch=1,
            grid=(N_GROUPS * STEPS,),
            in_specs=group_specs(width)
            + [fixed((width, HEAD_COLS)), whole, whole, fixed((1, HD)), fixed((1, HD))],
            out_specs=[whole] * 6,
        ),
        out_shape=[low, low, low, wide, wide, wide],
        compiler_params=pltpu.CompilerParams(vmem_limit_bytes=VMEM_BYTES),
        name="project",
    )(place, *groups, w, cos, sin, gq, gk)


def project_back_kernel(
    place_ref, x0, x1, x2, x3, dq_ref, dk_ref, dv_ref, qraw_ref, kraw_ref, inv_ref, cos_ref, sin_ref,
    gq_ref, gk_ref, w_ref, near_ref, far_ref, dw_ref, dg_ref, grads, scaled,
):
    step = pl.program_id(0)

    @pl.when(step == 0)
    def _():
        dw_ref[...] = jnp.zeros_like(dw_ref)
        dg_ref[...] = jnp.zeros_like(dg_ref)

    def run(x, da_ref):
        q_sum = jnp.zeros((1, HD), f32)
        k_sum = jnp.zeros((1, HD), f32)
        for i in range(STEP_BLOCKS):
            at = rows_of(place_ref, step, i)
            part = slice(i * HALF, (i + 1) * HALF)
            cos = cos_ref[at, :]
            sin = sin_ref[at, :]

            def back(raw, gain, grad, cos=cos, sin=sin):
                unrot = grad * cos + pltpu.roll(grad * sin, HD // 2, 1)
                return rms_back(raw, gain, unrot)

            grad_q, q_terms = back(qraw_ref[at, :], gq_ref[...], dq_ref[at, :])
            grad_k, k_terms = back(kraw_ref[at, :], gk_ref[...], dk_ref[at, :])
            inverse = inv_ref[at, :]
            for c, grad in enumerate((grad_q, grad_k, dv_ref[at, :])):
                grads[part, c * HD : (c + 1) * HD] = grad.astype(bf16)
                scaled[part, c * HD : (c + 1) * HD] = (grad * inverse).astype(bf16)
            q_sum = q_sum + jnp.sum(q_terms, axis=0, keepdims=True)
            k_sum = k_sum + jnp.sum(k_terms, axis=0, keepdims=True)
        da_ref[...] = dot_nt(grads[...], w_ref[...]).astype(bf16).reshape(da_ref.shape)
        dw_ref[...] += dot_tn(x, scaled[...])
        dg_ref[0:1, :] += q_sum
        dg_ref[1:2, :] += k_sum

    for k, x_ref in enumerate((x0, x1, x2, x3)):

        @pl.when(step // STEPS == k)
        def _(k=k, x_ref=x_ref):
            da_ref = near_ref if k < N_GROUPS // 2 else far_ref
            run(x_ref[...].reshape(STEP_BLOCKS * HALF, x_ref.shape[2]), da_ref)


def project_back(place, groups, grads, raws, cos, sin, gq, gk, w):
    width = w.shape[0]
    span = cos.shape[0]
    whole = fixed((span, HD))
    n_half = N_GROUPS // 2
    da = jax.ShapeDtypeStruct((n_half * GROUP, HALF, width), bf16)
    return pl.pallas_call(
        project_back_kernel,
        grid_spec=pltpu.PrefetchScalarGridSpec(
            num_scalar_prefetch=1,
            grid=(N_GROUPS * STEPS,),
            in_specs=group_specs(width)
            + [whole] * 8
            + [fixed((1, HD)), fixed((1, HD)), fixed((width, HEAD_COLS))],
            out_specs=[
                block_spec(width, 0, n_half * STEPS),
                block_spec(width, n_half * STEPS, n_half * STEPS),
                fixed((width, HEAD_COLS)),
                fixed((8, HD)),
            ],
            scratch_shapes=[
                pltpu.VMEM((STEP_BLOCKS * HALF, HEAD_COLS), bf16),
                pltpu.VMEM((STEP_BLOCKS * HALF, HEAD_COLS), bf16),
            ],
        ),
        out_shape=[
            da,
            da,
            jax.ShapeDtypeStruct((width, HEAD_COLS), f32),
            jax.ShapeDtypeStruct((8, HD), f32),
        ],
        compiler_params=pltpu.CompilerParams(vmem_limit_bytes=BIG_VMEM_BYTES),
        name="project_back",
    )(place, *groups, *grads, *raws, cos, sin, gq, gk, w)


def dealt_slot(place, n_dev):
    if place < n_dev:
        return place, 0
    return 2 * n_dev - 1 - place, 1


def key_mask(len_row, offset):
    ahead = (
        lax.broadcasted_iota(jnp.int32, (BK, BQ), 1)
        - lax.broadcasted_iota(jnp.int32, (BK, BQ), 0)
        + offset
    )
    return (ahead >= 0) & (ahead <= len_row)


def attend_kernel(klo_ref, q_ref, k_ref, v_ref, len_ref, osend_ref, onat_ref, linv_ref, vt):
    n_dev, rows, _ = osend_ref.shape
    half = rows // 2
    span = q_ref.shape[0]
    for c in range(span // BQ):
        to = slice(c * BQ, (c + 1) * BQ)
        vt[:, to] = v_ref[to, :].astype(f32).T.astype(bf16)

    def q_step(qb, _):
        q_at = pl.multiple_of(qb * BQ, BQ)
        q_blk = q_ref[pl.ds(q_at, BQ), :]
        len_row = len_ref[pl.ds(qb, 1), :]

        def k_step(kb, carry):
            acc, total = carry
            k_at = pl.multiple_of(kb * BK, BK)
            s = dot_nt(k_ref[pl.ds(k_at, BK), :], q_blk)
            p = jnp.where(key_mask(len_row, q_at - k_at), jnp.exp2(s), 0.0)
            total = total + jnp.sum(p.reshape(BK // 8, 8, BQ), axis=0)
            acc = acc + dot_nn(vt[:, pl.ds(k_at, BK)], p.astype(bf16))
            return acc, total

        acc, total = lax.fori_loop(
            klo_ref[qb],
            (q_at + BQ - 1) // BK + 1,
            k_step,
            (jnp.zeros((HD, BQ), f32), jnp.zeros((8, BQ), f32)),
        )
        inverse = 1.0 / jnp.sum(total, axis=0, keepdims=True)
        linv_ref[pl.ds(qb, 1), :] = inverse
        onat_ref[pl.ds(q_at, BQ), :] = (acc * inverse).T
        return 0

    lax.fori_loop(0, span // BQ, q_step, 0)
    for place in range(2 * n_dev):
        dev, side = dealt_slot(place, n_dev)
        osend_ref[dev, side * half : (side + 1) * half, :] = onat_ref[
            place * half : (place + 1) * half, :
        ].astype(bf16)


def vmem():
    return pl.BlockSpec(memory_space=pltpu.VMEM)


def attend(klo, q, k, v, lens, rows):
    span = q.shape[0]
    return pl.pallas_call(
        attend_kernel,
        in_specs=[pl.BlockSpec(memory_space=pltpu.SMEM)] + [vmem()] * 4,
        out_specs=[vmem(), vmem(), vmem()],
        out_shape=[
            jax.ShapeDtypeStruct((span // rows, rows, HD), bf16),
            jax.ShapeDtypeStruct((span, HD), f32),
            jax.ShapeDtypeStruct((span // BQ, BQ), f32),
        ],
        scratch_shapes=[pltpu.VMEM((HD, span), bf16)],
        compiler_params=pltpu.CompilerParams(vmem_limit_bytes=VMEM_BYTES),
        name="attend",
    )(klo, q, k, v, lens)


def attend_back_kernel(
    klo_ref, q_ref, k_ref, v_ref, do_ref, onat_ref, linv_ref, len_ref, dq, dk, dv, kt, don
):
    n_dev, rows, _ = do_ref.shape
    half = rows // 2
    span = q_ref.shape[0]
    for place in range(2 * n_dev):
        dev, side = dealt_slot(place, n_dev)
        to = slice(place * half, (place + 1) * half)
        don[to, :] = do_ref[dev, side * half : (side + 1) * half, :]
        kt[:, to] = k_ref[to, :].astype(f32).T.astype(bf16)
    dk[...] = jnp.zeros_like(dk)
    dv[...] = jnp.zeros_like(dv)

    def q_step(qb, _):
        q_at = pl.multiple_of(qb * BQ, BQ)
        q_blk = q_ref[pl.ds(q_at, BQ), :]
        do_blk = don[pl.ds(q_at, BQ), :]
        len_row = len_ref[pl.ds(qb, 1), :]
        inverse = linv_ref[pl.ds(qb, 1), :]
        mixed = (do_blk.astype(f32) * onat_ref[pl.ds(q_at, BQ), :]).T
        delta = jnp.sum(mixed, axis=0, keepdims=True)

        def k_step(kb, acc):
            k_at = pl.multiple_of(kb * BK, BK)
            here = pl.ds(k_at, BK)
            s = dot_nt(k_ref[here, :], q_blk)
            p = jnp.where(key_mask(len_row, q_at - k_at), jnp.exp2(s) * inverse, 0.0)
            dp = dot_nt(v_ref[here, :], do_blk)
            ds = (p * (dp - delta)).astype(bf16)
            dv[here, :] += dot_nn(p.astype(bf16), do_blk)
            dk[here, :] += dot_nn(ds, q_blk)
            return acc + dot_nn(kt[:, here], ds)

        acc = lax.fori_loop(
            klo_ref[qb], (q_at + BQ - 1) // BK + 1, k_step, jnp.zeros((HD, BQ), f32)
        )
        dq[pl.ds(q_at, BQ), :] = (acc * SCORE_SCALE).T
        return 0

    lax.fori_loop(0, span // BQ, q_step, 0)
    dk[...] = dk[...] * (1.0 / LOG2_E)


def attend_back(klo, q, k, v, do, onat, linv, lens):
    span = q.shape[0]
    return pl.pallas_call(
        attend_back_kernel,
        in_specs=[pl.BlockSpec(memory_space=pltpu.SMEM)] + [vmem()] * 7,
        out_specs=[vmem()] * 3,
        out_shape=[jax.ShapeDtypeStruct((span, HD), f32)] * 3,
        scratch_shapes=[pltpu.VMEM((HD, span), bf16), pltpu.VMEM((span, HD), bf16)],
        compiler_params=pltpu.CompilerParams(vmem_limit_bytes=VMEM_BYTES),
        name="attend_back",
    )(klo, q, k, v, do, onat, linv, lens)


OUT_ROWS = 160
CHUNK_ROWS = 32
N_CHUNKS = 3
CHUNK = FF // N_CHUNKS


def middle_kernel(
    full_ref,
    mixed_ref,
    tok_ref,
    cot_ref,
    gain_ref,
    shuffle_ref,
    gate_ref,
    up_ref,
    out_ref,
    dres_ref,
    dob_ref,
    feat_ref,
    drb_ref,
    grad_ref,
    dgain_ref,
    w_out,
    resid,
    mid_low,
    grad_mid,
    grad_up,
    sems,
):
    step = pl.program_id(0)
    q_width = H_Q * HD
    width = tok_ref.shape[1]

    def fetch(i):
        return pltpu.make_async_copy(
            full_ref.at[i, pl.ds(0, OUT_ROWS), :],
            w_out.at[pl.ds(i * OUT_ROWS, OUT_ROWS), :],
            sems.at[i],
        )

    n_fetch = full_ref.shape[0]
    n_first = -(-q_width // OUT_ROWS)

    @pl.when(step == 0)
    def _():
        for i in range(n_fetch):
            fetch(i).start()
        for h in range(H_Q):
            feat_ref[:, h * HD : (h + 1) * HD] = mixed_ref[h]
        for i in range(n_first):
            fetch(i).wait()
        residual = tok_ref[...].astype(f32) + dot_nn(feat_ref[:, :q_width], w_out[:q_width, :])
        resid[...] = residual
        out_ref[...] = residual
        normed = rms_norm(residual, gain_ref[...]).astype(bf16)
        mid_low[...] = dot_nn(normed, shuffle_ref[...]).astype(bf16)
        grad_mid[...] = jnp.zeros_like(grad_mid)
        for i in range(n_first, n_fetch):
            fetch(i).wait()

    @pl.when((step > 0) & (step < 2 * N_CHUNKS + 1) & (step % 2 == 1))
    def _():
        at = pl.multiple_of(q_width + ((step - 1) // 2) * CHUNK, CHUNK)
        gate_w = gate_ref[...].reshape(width, CHUNK)
        gate = dot_nn(mid_low[...], gate_w)
        up = dot_nn(mid_low[...], up_ref[...].reshape(width, CHUNK))
        sigmoid_gate = 1.0 / (1.0 + jnp.exp(-gate))
        activated = gate * sigmoid_gate
        hidden = (activated * up).astype(bf16)
        feat_ref[:, pl.ds(at, CHUNK)] = hidden
        down_w = w_out[pl.ds(at, CHUNK), :]
        out_ref[...] += dot_nn(hidden, down_w)
        grad_hidden = dot_nt(cot_ref[...], down_w)
        grad_up[...] = (grad_hidden * activated).astype(bf16)
        grad_gate = (
            grad_hidden * up * sigmoid_gate * (1.0 + gate * (1.0 - sigmoid_gate))
        ).astype(bf16)
        grad_mid[...] += dot_nt(grad_gate, gate_w)
        grad_ref[...] = dot_tn(mid_low[...], grad_gate).astype(bf16).reshape(grad_ref.shape)

    @pl.when((step > 0) & (step < 2 * N_CHUNKS + 1) & (step % 2 == 0))
    def _():
        grad_mid[...] += dot_nt(grad_up[...], up_ref[...].reshape(width, CHUNK))
        grad_ref[...] = dot_tn(mid_low[...], grad_up[...]).astype(bf16).reshape(grad_ref.shape)

    @pl.when(step == 2 * N_CHUNKS + 1)
    def _():
        grad = dot_nt(grad_mid[...].astype(bf16), shuffle_ref[...])
        part, terms = rms_back(resid[...], gain_ref[...], grad)
        dgain_ref[...] = jnp.sum(terms, axis=0, keepdims=True)
        dres = cot_ref[...].astype(f32) + part
        dres_ref[...] = dres
        low = dres.astype(bf16)
        drb_ref[...] = low
        for c in range(4):
            piece = dot_nt(low, w_out[c * 4 * HD : (c + 1) * 4 * HD, :]).astype(bf16)
            for h in range(4):
                dob_ref[4 * c + h] = piece[:, h * HD : (h + 1) * HD]


def middle(full, mixed, tok, cot, gain, shuffle):
    rows, width = tok.shape
    n_blocks = full.shape[0]
    first = OUT_ROWS // CHUNK_ROWS
    q_width = H_Q * HD

    def chunk_of(i):
        return jnp.clip((i - 1) // 2, 0, N_CHUNKS - 1)

    def grad_at(i):
        i = jnp.clip(i, 1, 2 * N_CHUNKS)
        return (0, first + N_CHUNKS * ((i - 1) % 2) + (i - 1) // 2, 0)

    def whole(shape):
        return pl.BlockSpec(shape, lambda i: (0,) * len(shape))

    return pl.pallas_call(
        middle_kernel,
        grid=(2 * N_CHUNKS + 2,),
        in_specs=[
            pl.BlockSpec(memory_space=pl.ANY),
            whole((H_Q, rows, HD)),
            whole((rows, width)),
            whole((rows, width)),
            whole((1, width)),
            whole((width, width)),
            pl.BlockSpec((n_blocks, CHUNK_ROWS, CHUNK), lambda i: (0, first + chunk_of(i), 0)),
            pl.BlockSpec(
                (n_blocks, CHUNK_ROWS, CHUNK), lambda i: (0, first + N_CHUNKS + chunk_of(i), 0)
            ),
        ],
        out_specs=[
            whole((rows, width)),
            whole((rows, width)),
            whole((H_Q, rows, HD)),
            whole((rows, q_width + FF)),
            whole((rows, width)),
            pl.BlockSpec((n_blocks, CHUNK_ROWS, CHUNK), grad_at),
            whole((1, width)),
        ],
        out_shape=[
            jax.ShapeDtypeStruct((rows, width), f32),
            jax.ShapeDtypeStruct((rows, width), f32),
            jax.ShapeDtypeStruct((H_Q, rows, HD), bf16),
            jax.ShapeDtypeStruct((rows, q_width + FF), bf16),
            jax.ShapeDtypeStruct((rows, width), bf16),
            jax.ShapeDtypeStruct(full.shape, bf16),
            jax.ShapeDtypeStruct((1, width), f32),
        ],
        scratch_shapes=[
            pltpu.VMEM((q_width + FF, width), bf16),
            pltpu.VMEM((rows, width), f32),
            pltpu.VMEM((rows, width), bf16),
            pltpu.VMEM((rows, width), f32),
            pltpu.VMEM((rows, CHUNK), bf16),
            pltpu.SemaphoreType.DMA((n_blocks,)),
        ],
        compiler_params=pltpu.CompilerParams(vmem_limit_bytes=VMEM_BYTES),
        name="middle",
    )(full, mixed, tok, cot, gain, shuffle, full, full)


def grad_out_kernel(feat_ref, drb_ref, cot_ref, grads_ref, out_ref):
    step = pl.program_id(0)
    q_width = H_Q * HD
    block = feat_ref.shape[1]
    both = q_width // block
    cut = q_width % block

    def store(value):
        out_ref[...] = value.astype(bf16).reshape(out_ref.shape)

    @pl.when(step < both)
    def _():
        store(dot_tn(feat_ref[...], drb_ref[...]))

    @pl.when(step == both)
    def _():
        upper = dot_tn(feat_ref[:, :cut], drb_ref[...])
        lower = dot_tn(feat_ref[:, cut:], cot_ref[...])
        store(jnp.concatenate([upper, lower], axis=0))

    @pl.when(step > both)
    def _():
        store(dot_tn(feat_ref[...], cot_ref[...]))


def grad_out(feat, drb, cot, grads):
    rows, n_features = feat.shape
    width = drb.shape[1]
    blocks = 4
    return pl.pallas_call(
        grad_out_kernel,
        grid=(grads.shape[0] // blocks,),
        in_specs=[
            pl.BlockSpec((rows, blocks * OUT_ROWS), lambda i: (0, i)),
            pl.BlockSpec((rows, width), lambda i: (0, 0)),
            pl.BlockSpec((rows, width), lambda i: (0, 0)),
            pl.BlockSpec(memory_space=pl.ANY),
        ],
        out_specs=pl.BlockSpec((blocks, OUT_ROWS, width), lambda i: (i, 0, 0)),
        out_shape=jax.ShapeDtypeStruct(grads.shape, bf16),
        input_output_aliases={3: 0},
        compiler_params=pltpu.CompilerParams(vmem_limit_bytes=VMEM_BYTES),
        name="grad_out",
    )(feat, drb, cot, grads)


def adam_step(master, first_old, second_old, gradient, rate):
    first_new = BETA_ONE * first_old + (1.0 - BETA_ONE) * gradient
    second_new = BETA_TWO * second_old + (1.0 - BETA_TWO) * gradient * gradient
    first_hat = first_new / (1.0 - BETA_ONE**STEP)
    second_hat = second_new / (1.0 - BETA_TWO**STEP)
    master_new = master - rate * (
        first_hat / (jnp.sqrt(second_hat) + ADAM_EPS) + WEIGHT_DECAY * master
    )
    return (first_new, second_new, master_new)


def gathered(x):
    return lax.all_gather(x, AXIS_YZ, axis=0, tiled=True)


def sum_over_x(blocks):
    me = lax.axis_index(AXIS_X)
    n = blocks.shape[0]

    def block(i):
        return lax.dynamic_index_in_dim(blocks, lax.rem(i, n), 0, keepdims=False)

    total = block(me).astype(f32)
    for shift in range(1, n):
        pairs = [(i, (i + shift) % n) for i in range(n)]
        total = total + lax.ppermute(block(me + shift), AXIS_X, pairs).astype(f32)
    return total


def shift(x, axis, step):
    n = SIZES[axis]
    return lax.ppermute(x, axis, [(i, (i + step) % n) for i in range(n)])


def first_moves(x):
    first, second = x[None, :HALF], x[None, HALF:]
    pair = jnp.concatenate([first, shift(first, "xh", 1)], axis=0)
    ring = jnp.concatenate([second] + [shift(second, "y", b) for b in (1, 2, 3)], axis=0)
    return pair, ring


def second_moves(pair, ring):
    one = jnp.concatenate([pair] + [shift(pair, "y", b) for b in (1, 2, 3)], axis=0)
    two = jnp.concatenate([ring, shift(ring, "xh", 1)], axis=0)
    return [one, two, shift(one, "core", 1), shift(two, "core", 1)]


def places_of_groups():
    xh, y, core = (lax.axis_index(name) for name in CTX)
    places = []
    for other in range(2):
        for side in range(2):
            for i in range(GROUP):
                b, a = (i // 2, i % 2) if side == 0 else (i % 4, i // 4)
                dev = (((xh + a) % 2) * 4 + (y - b) % 4) * 2 + (core + other) % 2
                places.append(dev if side == 0 else 31 - dev)
    return jnp.stack(places).astype(jnp.int32)


def sum_over_core(near, far):
    return (near.astype(f32) + shift(far, "core", 1).astype(f32)).astype(bf16)


def first_sums(plane):
    one = plane[:GROUP].reshape((4, 2) + plane.shape[1:])
    two = plane[GROUP:].reshape((2, 4) + plane.shape[1:])
    two = (two[0].astype(f32) + shift(two[1], "xh", 1).astype(f32)).astype(bf16)
    one = sum((shift(one[b], "y", -b).astype(f32) for b in (1, 2, 3)), one[0].astype(f32))
    return one.astype(bf16), two


def second_sums(one, two):
    two = sum((shift(two[b], "y", -b).astype(f32) for b in (1, 2, 3)), two[0].astype(f32))
    one = one[0].astype(f32) + shift(one[1], "xh", 1).astype(f32)
    return jnp.concatenate([one, two], axis=0)


def pick(v, i, n, axis):
    return lax.dynamic_index_in_dim(v, lax.rem(i, n), axis, keepdims=False)


def sum_over_xl(x):
    xl = lax.axis_index("xl")
    return pick(x, xl, 2, 1).astype(f32) + shift(pick(x, xl + 1, 2, 1), "xl", 1).astype(f32)


def sum_over_z(x):
    z = lax.axis_index("z")
    low = x.astype(bf16)
    total = pick(x, z, 4, 1)
    for step in (1, 2, 3):
        total = total + shift(pick(low, z + step, 4, 1), "z", step).astype(f32)
    return total


def gather_shard(x):
    z = lax.axis_index("z")
    xl = lax.axis_index("xl")
    ring = [x] + [shift(x, "z", -step) for step in (1, 2, 3)]
    ring = lax.dynamic_slice_in_dim(jnp.stack(ring + ring[:3]), lax.rem(4 - z, 4), 4, 0)
    other = shift(ring, "xl", 1)
    return jnp.stack([jnp.where(xl == 0, ring, other), jnp.where(xl == 0, other, ring)])


def natural_of_permuted(x):
    tail = x.shape[1:]
    x = x.reshape((4, 4, 2, 2, 2) + tail)
    x = x.transpose((3, 0, 2, 4, 1) + tuple(range(5, 5 + len(tail))))
    return x.reshape((128,) + tail)


def owner_pairs():
    pairs = []
    for n in range(128):
        z = n % 4
        xl = (n // 4) % 2
        core = (n // 8) % 2
        y = (n // 16) % 4
        xh = n // 64
        pairs.append((n, (((y * 4 + z) * 2 + core) * 2 + xh) * 2 + xl))
    return pairs


def body(
    tokens,
    cotangent,
    segments,
    positions,
    pad_mask,
    w_in,
    w_out,
    gains,
    first_in,
    first_out,
    first_gains,
    second_in,
    second_out,
    second_gains,
):
    rows = tokens.shape[1]
    width = tokens.shape[2]
    span = segments.shape[1]
    half = rows // 2
    n_ctx = span // rows
    q_width = H_Q * HD
    kv_width = H_KV * HD
    attn_cols = q_width + 2 * kv_width
    owned = w_in.shape[0]
    owned_gains = gains.shape[0]

    n_x = 4
    low_in = w_in.astype(bf16)
    n_dev = width // owned

    own_head = jnp.concatenate(
        [
            low_in[:, :q_width].reshape(owned, H_Q, HD),
            jnp.repeat(low_in[:, q_width : q_width + kv_width].reshape(owned, H_KV, HD), 2, axis=1),
            jnp.repeat(low_in[:, q_width + kv_width : attn_cols].reshape(owned, H_KV, HD), 2, axis=1),
            jnp.broadcast_to(
                jnp.pad(gains.astype(bf16)[None, None], ((0, owned - 1), (0, 0), (0, HD - owned_gains))),
                (owned, H_Q, HD),
            ),
        ],
        axis=2,
    ).transpose(1, 0, 2)
    pair, ring = first_moves(tokens[0])
    pairs = owner_pairs()
    own_out = lax.ppermute(w_out.astype(bf16), EVERY, [(p, n) for n, p in pairs])
    own_ffn = low_in[:, attn_cols:].reshape(owned, 2 * N_CHUNKS, CHUNK)
    own_ffn = own_ffn.transpose(1, 0, 2).reshape(2 * N_CHUNKS * owned, CHUNK)
    own_rest = jnp.concatenate([own_out, own_ffn], axis=0)
    own_rest = lax.all_gather(own_rest, AXIS_X, axis=0, tiled=False)
    own_head, own_rest, pair, ring = lax.optimization_barrier((own_head, own_rest, pair, ring))
    head = gather_shard(lax.all_to_all(own_head, CTX, 0, 0, tiled=True))
    head = head.transpose(2, 0, 1, 3, 4)
    gain_vals = head[:, :, :, 0, HEAD_COLS : HEAD_COLS + owned_gains].reshape(-1).astype(f32)
    w_head = head[..., :HEAD_COLS].reshape(width, HEAD_COLS)
    gain_one = gain_vals[:width]
    gain_two = gain_vals[width : 2 * width]
    gain_query = gain_vals[2 * width : 2 * width + HD].reshape(1, HD)
    gain_key = gain_vals[2 * width + HD :].reshape(1, HD)
    w_scaled = (w_head.astype(f32) * gain_one[:, None]).astype(bf16)

    n_out = w_out.shape[0]
    part_out = own_rest[:, :n_out].reshape(n_x * n_out, width)
    part_ffn = own_rest[:, n_out:].reshape(n_x, 2 * N_CHUNKS, owned, CHUNK).transpose(1, 0, 2, 3)
    part_ffn = part_ffn.reshape(2 * N_CHUNKS * CHUNK_ROWS, CHUNK)
    full = gathered(jnp.concatenate([part_out, part_ffn], axis=0)[None])

    order = natural_of_permuted(jnp.arange(width, dtype=jnp.int32).reshape(n_dev, owned)).reshape(-1)
    shuffle = (order[:, None] == jnp.arange(width, dtype=jnp.int32)[None, :]).astype(bf16)

    def natural(x):
        x = x.reshape(n_ctx, 2, half)
        return jnp.concatenate([x[:, 0], x[::-1, 1]], axis=0)

    docs = natural(segments[0])
    live = natural(pad_mask[0])
    at = jnp.arange(span, dtype=jnp.int32).reshape(2 * n_ctx, half)
    start = jnp.zeros_like(docs)
    for number in range(1, 14):
        before = jnp.sum((docs < number).astype(jnp.int32))
        start = jnp.where(docs == number, before, start)
    place_in = at - start
    lens = jnp.where(live == 1, place_in, 0)
    klo = jnp.min((at - lens).reshape(span // BQ, BQ), axis=1) // BK
    lens = lens.reshape(span // BQ, BQ)
    halves = jnp.arange(HD // 2, dtype=f32)
    inverse = ROPE_BASE ** (-2.0 * halves / HD)
    angle = place_in.reshape(span, 1).astype(f32) * inverse[None, :]
    cos_half = jnp.cos(angle)
    sin_half = jnp.sin(angle)
    cos = jnp.concatenate([cos_half, cos_half], axis=1)
    sin = jnp.concatenate([-sin_half, sin_half], axis=1)

    groups = second_moves(pair, ring)
    place = places_of_groups()
    q, k, v, query_raw, key_raw, inv = project(
        place, groups, w_scaled, cos, sin, gain_query, gain_key
    )
    o_send, o_nat, l_inv = attend(klo, q, k, v, lens, rows)
    mixed = lax.all_to_all(o_send, CTX, 0, 0, tiled=True)

    output, grad_residual, do_send, features, resid_low, grads, gain_two_terms = middle(
        full, mixed, tokens[0], cotangent[0], gain_two.reshape(1, width), shuffle
    )
    do = lax.all_to_all(do_send, CTX, 0, 0, tiled=True)
    grads = grad_out(features, resid_low, cotangent[0], grads)
    do, grads = lax.optimization_barrier((do, grads))
    grads = lax.psum_scatter(grads, AXIS_YZ, scatter_dimension=0, tiled=True)[0]

    head_grads = attend_back(klo, q, k, v, do, o_nat, l_inv, lens)
    da_near, da_far, dw_head, gain_qk = project_back(
        place, groups, head_grads, (query_raw, key_raw, inv), cos, sin, gain_query, gain_key, w_head
    )

    gain_one_grad = jnp.sum(dw_head * w_head.astype(f32), axis=1)
    grad_gains = jnp.concatenate([gain_one_grad, gain_two_terms[0], gain_qk[0], gain_qk[1]])
    grad_gains = jnp.pad(
        grad_gains.reshape(n_dev, 1, owned_gains), ((0, 0), (0, owned - 1), (0, HD - owned_gains))
    )
    dw_head = (dw_head * gain_one[:, None]).reshape(n_dev, owned, HEAD_COLS)
    dw_head = jnp.concatenate([dw_head, grad_gains], axis=2).astype(bf16)
    dw_head = sum_over_xl(dw_head.reshape(n_ctx, 2, 4, owned, PAD_COLS))
    plane = sum_over_core(da_near, da_far)
    dw_head, plane = lax.optimization_barrier((dw_head, plane))
    dw_head = sum_over_z(dw_head).astype(bf16)
    one, two = first_sums(plane)
    dw_head, one, two = lax.optimization_barrier((dw_head, one, two))
    dw_head = lax.all_to_all(dw_head, CTX, 0, 0, tiled=True).astype(f32)

    grad_a = second_sums(one, two)
    inputs = tokens[0].astype(f32)
    input_grad = grad_residual + rms_back(inputs, gain_one, grad_a)[0]
    owned_gain_grad = jnp.sum(dw_head[:, 0, HEAD_COLS : HEAD_COLS + owned_gains], axis=0)

    def columns(x):
        return x.transpose(1, 0, 2).reshape(owned, -1)

    def over_pair(x):
        return columns(jnp.sum(x.reshape(H_KV, 2, owned, HD), axis=1))

    out_part = grads[:OUT_ROWS].reshape(n_x, OUT_ROWS // n_x, width)
    ffn_part = grads[OUT_ROWS:].reshape(2 * N_CHUNKS, n_x, owned, CHUNK)
    ffn_part = ffn_part.transpose(1, 0, 2, 3).reshape(n_x, 2 * N_CHUNKS * owned, CHUNK)
    grads = sum_over_x(jnp.concatenate([out_part, ffn_part], axis=1))
    owned_out = lax.ppermute(grads[: OUT_ROWS // n_x], EVERY, pairs)
    owned_ffn = grads[OUT_ROWS // n_x :].reshape(2 * N_CHUNKS, owned, CHUNK)
    owned_in = jnp.concatenate(
        [
            columns(dw_head[:, :, :HD]),
            over_pair(dw_head[:, :, HD : 2 * HD]),
            over_pair(dw_head[:, :, 2 * HD : HEAD_COLS]),
            columns(owned_ffn),
        ],
        axis=1,
    )
    new_first_in, new_second_in, new_master_in = adam_step(
        w_in, first_in, second_in, owned_in, RATE_MATRIX
    )
    new_first_out, new_second_out, new_master_out = adam_step(
        w_out, first_out, second_out, owned_out, RATE_MATRIX
    )
    new_first_gains, new_second_gains, new_master_gains = adam_step(
        gains, first_gains, second_gains, owned_gain_grad, RATE_GAIN
    )
    return (
        output[None],
        input_grad[None],
        new_first_in,
        new_first_out,
        new_first_gains,
        new_second_in,
        new_second_out,
        new_second_gains,
        new_master_in,
        new_master_out,
        new_master_gains,
        new_master_in.astype(bf16),
        new_master_out.astype(bf16),
    )


def solution(mesh):
    cut = Mesh(mesh.devices.reshape(tuple(SIZES[name] for name in EVERY)), EVERY)
    weights = P(EVERY, None)
    vector = P(EVERY)
    acts = P(SHARD, CTX, None)
    in_specs = (
        acts,
        acts,
        P(SHARD, None),
        P(SHARD, CTX),
        P(SHARD, None),
    ) + (weights, weights, vector) * 3
    out_specs = (acts, acts) + (weights, weights, vector) * 3 + (weights, weights)
    return jax.shard_map(body, mesh=cut, in_specs=in_specs, out_specs=out_specs, check_vma=False)
```

```python
import functools
import math

import jax
import jax.numpy as jnp
from jax import lax
from jax.experimental import pallas as pl
from jax.experimental.pallas import tpu as pltpu
from jax.sharding import Mesh
from jax.sharding import PartitionSpec as P

H_Q = 16
H_KV = 8
HD = 128
FF = 3072
STEP = 5

NORM_EPS = 1e-06
ROPE_BASE = 1000000.0
BETA_ONE = 0.5
BETA_TWO = 0.5
ADAM_EPS = 1e-08
WEIGHT_DECAY = 0.1
RATE_MATRIX = 0.03
RATE_GAIN = 0.25

CTX = ("xh", "y", "core")
SHARD = ("xl", "z")
EVERY = CTX + SHARD
AXIS_X = ("xh", "xl")
AXIS_YZ = ("y", "z")
AXIS_CYZ = ("core", "y", "z")
SIZES = {"xh": 2, "y": 4, "core": 2, "xl": 2, "z": 4}

LOG2_E = 1.4426950408889634
SCORE_SCALE = 1.0 / math.sqrt(HD)
BQ = 256
BK = 512
VMEM_BYTES = 48 * 1024 * 1024
BIG_VMEM_BYTES = 60 * 1024 * 1024

bf16 = jnp.bfloat16
f32 = jnp.float32


def rms_norm(values, weight):
    return values * lax.rsqrt(jnp.mean(values * values, axis=-1, keepdims=True) + NORM_EPS) * weight


def rms_back(values, weight, upstream):
    inverse = lax.rsqrt(jnp.mean(values * values, axis=-1, keepdims=True) + NORM_EPS)
    normed = values * inverse
    scaled = upstream * weight
    grad_values = inverse * (scaled - normed * jnp.mean(scaled * normed, axis=-1, keepdims=True))
    return (grad_values, upstream * normed)


def dot_nt(a, b):
    return lax.dot_general(a, b, (((1,), (1,)), ((), ())), preferred_element_type=f32)


def dot_tn(a, b):
    return lax.dot_general(a, b, (((0,), (0,)), ((), ())), preferred_element_type=f32)


def dot_nn(a, b):
    return lax.dot_general(a, b, (((1,), (0,)), ((), ())), preferred_element_type=f32)


N_GROUPS = 4
GROUP = 8
HALF = 128
STEP_BLOCKS = 4
STEPS = GROUP // STEP_BLOCKS
HEAD_COLS = 3 * HD
PAD_COLS = 4 * HD


def block_spec(width, first, count):
    return pl.BlockSpec(
        (STEP_BLOCKS, HALF, width), lambda i, place: (jnp.clip(i - first, 0, count - 1), 0, 0)
    )


def group_specs(width):
    return [block_spec(width, k * STEPS, STEPS) for k in range(N_GROUPS)]


def fixed(shape):
    return pl.BlockSpec(shape, lambda i, place: (0,) * len(shape))


def rows_of(place_ref, step, i):
    return pl.ds(pl.multiple_of(place_ref[step * STEP_BLOCKS + i] * HALF, HALF), HALF)


def project_kernel(
    place_ref, x0, x1, x2, x3, w_ref, cos_ref, sin_ref, gq_ref, gk_ref,
    q_ref, k_ref, v_ref, qraw_ref, kraw_ref, inv_ref,
):
    step = pl.program_id(0)

    def run(x):
        wide = x.astype(f32)
        inverse = lax.rsqrt(jnp.mean(wide * wide, axis=-1, keepdims=True) + NORM_EPS)
        prod = dot_nn(x, w_ref[...]) * inverse
        for i in range(STEP_BLOCKS):
            at = rows_of(place_ref, step, i)
            part = slice(i * HALF, (i + 1) * HALF)
            cos = cos_ref[at, :]
            sin = sin_ref[at, :]

            def roped(raw, gain, cos=cos, sin=sin):
                normed = rms_norm(raw, gain)
                return normed * cos + pltpu.roll(normed, HD // 2, 1) * sin

            query = prod[part, :HD]
            key = prod[part, HD : 2 * HD]
            inv_ref[at, :] = jnp.broadcast_to(inverse[part], (HALF, HD))
            qraw_ref[at, :] = query
            kraw_ref[at, :] = key
            q_ref[at, :] = (roped(query, gq_ref[...]) * (SCORE_SCALE * LOG2_E)).astype(bf16)
            k_ref[at, :] = roped(key, gk_ref[...]).astype(bf16)
            v_ref[at, :] = prod[part, 2 * HD :].astype(bf16)

    for k, x_ref in enumerate((x0, x1, x2, x3)):

        @pl.when(step // STEPS == k)
        def _(x_ref=x_ref):
            run(x_ref[...].reshape(STEP_BLOCKS * HALF, x_ref.shape[2]))


def project(place, groups, w, cos, sin, gq, gk):
    width = w.shape[0]
    span = cos.shape[0]
    low = jax.ShapeDtypeStruct((span, HD), bf16)
    wide = jax.ShapeDtypeStruct((span, HD), f32)
    whole = fixed((span, HD))
    return pl.pallas_call(
        project_kernel,
        grid_spec=pltpu.PrefetchScalarGridSpec(
            num_scalar_prefetch=1,
            grid=(N_GROUPS * STEPS,),
            in_specs=group_specs(width)
            + [fixed((width, HEAD_COLS)), whole, whole, fixed((1, HD)), fixed((1, HD))],
            out_specs=[whole] * 6,
        ),
        out_shape=[low, low, low, wide, wide, wide],
        compiler_params=pltpu.CompilerParams(vmem_limit_bytes=VMEM_BYTES),
        name="project",
    )(place, *groups, w, cos, sin, gq, gk)


def project_back_kernel(
    place_ref, x0, x1, x2, x3, dq_ref, dk_ref, dv_ref, qraw_ref, kraw_ref, inv_ref, cos_ref, sin_ref,
    gq_ref, gk_ref, w_ref, near_ref, far_ref, dw_ref, dg_ref, grads, scaled,
):
    step = pl.program_id(0)

    @pl.when(step == 0)
    def _():
        dw_ref[...] = jnp.zeros_like(dw_ref)
        dg_ref[...] = jnp.zeros_like(dg_ref)

    def run(x, da_ref):
        q_sum = jnp.zeros((1, HD), f32)
        k_sum = jnp.zeros((1, HD), f32)
        for i in range(STEP_BLOCKS):
            at = rows_of(place_ref, step, i)
            part = slice(i * HALF, (i + 1) * HALF)
            cos = cos_ref[at, :]
            sin = sin_ref[at, :]

            def back(raw, gain, grad, cos=cos, sin=sin):
                unrot = grad * cos + pltpu.roll(grad * sin, HD // 2, 1)
                return rms_back(raw, gain, unrot)

            grad_q, q_terms = back(qraw_ref[at, :], gq_ref[...], dq_ref[at, :])
            grad_k, k_terms = back(kraw_ref[at, :], gk_ref[...], dk_ref[at, :])
            inverse = inv_ref[at, :]
            for c, grad in enumerate((grad_q, grad_k, dv_ref[at, :])):
                grads[part, c * HD : (c + 1) * HD] = grad.astype(bf16)
                scaled[part, c * HD : (c + 1) * HD] = (grad * inverse).astype(bf16)
            q_sum = q_sum + jnp.sum(q_terms, axis=0, keepdims=True)
            k_sum = k_sum + jnp.sum(k_terms, axis=0, keepdims=True)
        da_ref[...] = dot_nt(grads[...], w_ref[...]).astype(bf16).reshape(da_ref.shape)
        dw_ref[...] += dot_tn(x, scaled[...])
        dg_ref[0:1, :] += q_sum
        dg_ref[1:2, :] += k_sum

    for k, x_ref in enumerate((x0, x1, x2, x3)):

        @pl.when(step // STEPS == k)
        def _(k=k, x_ref=x_ref):
            da_ref = near_ref if k < N_GROUPS // 2 else far_ref
            run(x_ref[...].reshape(STEP_BLOCKS * HALF, x_ref.shape[2]), da_ref)


def project_back(place, groups, grads, raws, cos, sin, gq, gk, w):
    width = w.shape[0]
    span = cos.shape[0]
    whole = fixed((span, HD))
    n_half = N_GROUPS // 2
    da = jax.ShapeDtypeStruct((n_half * GROUP, HALF, width), bf16)
    return pl.pallas_call(
        project_back_kernel,
        grid_spec=pltpu.PrefetchScalarGridSpec(
            num_scalar_prefetch=1,
            grid=(N_GROUPS * STEPS,),
            in_specs=group_specs(width)
            + [whole] * 8
            + [fixed((1, HD)), fixed((1, HD)), fixed((width, HEAD_COLS))],
            out_specs=[
                block_spec(width, 0, n_half * STEPS),
                block_spec(width, n_half * STEPS, n_half * STEPS),
                fixed((width, HEAD_COLS)),
                fixed((8, HD)),
            ],
            scratch_shapes=[
                pltpu.VMEM((STEP_BLOCKS * HALF, HEAD_COLS), bf16),
                pltpu.VMEM((STEP_BLOCKS * HALF, HEAD_COLS), bf16),
            ],
        ),
        out_shape=[
            da,
            da,
            jax.ShapeDtypeStruct((width, HEAD_COLS), f32),
            jax.ShapeDtypeStruct((8, HD), f32),
        ],
        compiler_params=pltpu.CompilerParams(vmem_limit_bytes=BIG_VMEM_BYTES),
        name="project_back",
    )(place, *groups, *grads, *raws, cos, sin, gq, gk, w)


def dealt_slot(place, n_dev):
    if place < n_dev:
        return place, 0
    return 2 * n_dev - 1 - place, 1


def key_mask(len_row, offset):
    ahead = (
        lax.broadcasted_iota(jnp.int32, (BK, BQ), 1)
        - lax.broadcasted_iota(jnp.int32, (BK, BQ), 0)
        + offset
    )
    return (ahead >= 0) & (ahead <= len_row)


def attend_kernel(klo_ref, q_ref, k_ref, v_ref, len_ref, osend_ref, onat_ref, linv_ref, vt):
    n_dev, rows, _ = osend_ref.shape
    half = rows // 2
    span = q_ref.shape[0]
    for c in range(span // BQ):
        to = slice(c * BQ, (c + 1) * BQ)
        vt[:, to] = v_ref[to, :].astype(f32).T.astype(bf16)

    def q_step(qb, _):
        q_at = pl.multiple_of(qb * BQ, BQ)
        q_blk = q_ref[pl.ds(q_at, BQ), :]
        len_row = len_ref[pl.ds(qb, 1), :]

        def k_step(kb, carry):
            acc, total = carry
            k_at = pl.multiple_of(kb * BK, BK)
            s = dot_nt(k_ref[pl.ds(k_at, BK), :], q_blk)
            p = jnp.where(key_mask(len_row, q_at - k_at), jnp.exp2(s), 0.0)
            total = total + jnp.sum(p.reshape(BK // 8, 8, BQ), axis=0)
            acc = acc + dot_nn(vt[:, pl.ds(k_at, BK)], p.astype(bf16))
            return acc, total

        acc, total = lax.fori_loop(
            klo_ref[qb],
            (q_at + BQ - 1) // BK + 1,
            k_step,
            (jnp.zeros((HD, BQ), f32), jnp.zeros((8, BQ), f32)),
        )
        inverse = 1.0 / jnp.sum(total, axis=0, keepdims=True)
        linv_ref[pl.ds(qb, 1), :] = inverse
        onat_ref[pl.ds(q_at, BQ), :] = (acc * inverse).T
        return 0

    lax.fori_loop(0, span // BQ, q_step, 0)
    for place in range(2 * n_dev):
        dev, side = dealt_slot(place, n_dev)
        osend_ref[dev, side * half : (side + 1) * half, :] = onat_ref[
            place * half : (place + 1) * half, :
        ].astype(bf16)


def vmem():
    return pl.BlockSpec(memory_space=pltpu.VMEM)


def attend(klo, q, k, v, lens, rows):
    span = q.shape[0]
    return pl.pallas_call(
        attend_kernel,
        in_specs=[pl.BlockSpec(memory_space=pltpu.SMEM)] + [vmem()] * 4,
        out_specs=[vmem(), vmem(), vmem()],
        out_shape=[
            jax.ShapeDtypeStruct((span // rows, rows, HD), bf16),
            jax.ShapeDtypeStruct((span, HD), f32),
            jax.ShapeDtypeStruct((span // BQ, BQ), f32),
        ],
        scratch_shapes=[pltpu.VMEM((HD, span), bf16)],
        compiler_params=pltpu.CompilerParams(vmem_limit_bytes=VMEM_BYTES),
        name="attend",
    )(klo, q, k, v, lens)


def attend_back_kernel(
    klo_ref, q_ref, k_ref, v_ref, do_ref, onat_ref, linv_ref, len_ref, dq, dk, dv, kt, don
):
    n_dev, rows, _ = do_ref.shape
    half = rows // 2
    span = q_ref.shape[0]
    for place in range(2 * n_dev):
        dev, side = dealt_slot(place, n_dev)
        to = slice(place * half, (place + 1) * half)
        don[to, :] = do_ref[dev, side * half : (side + 1) * half, :]
        kt[:, to] = k_ref[to, :].astype(f32).T.astype(bf16)
    dk[...] = jnp.zeros_like(dk)
    dv[...] = jnp.zeros_like(dv)

    def q_step(qb, _):
        q_at = pl.multiple_of(qb * BQ, BQ)
        q_blk = q_ref[pl.ds(q_at, BQ), :]
        do_blk = don[pl.ds(q_at, BQ), :]
        len_row = len_ref[pl.ds(qb, 1), :]
        inverse = linv_ref[pl.ds(qb, 1), :]
        mixed = (do_blk.astype(f32) * onat_ref[pl.ds(q_at, BQ), :]).T
        delta = jnp.sum(mixed, axis=0, keepdims=True)

        def k_step(kb, acc):
            k_at = pl.multiple_of(kb * BK, BK)
            here = pl.ds(k_at, BK)
            s = dot_nt(k_ref[here, :], q_blk)
            p = jnp.where(key_mask(len_row, q_at - k_at), jnp.exp2(s) * inverse, 0.0)
            dp = dot_nt(v_ref[here, :], do_blk)
            ds = (p * (dp - delta)).astype(bf16)
            dv[here, :] += dot_nn(p.astype(bf16), do_blk)
            dk[here, :] += dot_nn(ds, q_blk)
            return acc + dot_nn(kt[:, here], ds)

        acc = lax.fori_loop(
            klo_ref[qb], (q_at + BQ - 1) // BK + 1, k_step, jnp.zeros((HD, BQ), f32)
        )
        dq[pl.ds(q_at, BQ), :] = (acc * SCORE_SCALE).T
        return 0

    lax.fori_loop(0, span // BQ, q_step, 0)
    dk[...] = dk[...] * (1.0 / LOG2_E)


def attend_back(klo, q, k, v, do, onat, linv, lens):
    span = q.shape[0]
    return pl.pallas_call(
        attend_back_kernel,
        in_specs=[pl.BlockSpec(memory_space=pltpu.SMEM)] + [vmem()] * 7,
        out_specs=[vmem()] * 3,
        out_shape=[jax.ShapeDtypeStruct((span, HD), f32)] * 3,
        scratch_shapes=[pltpu.VMEM((HD, span), bf16), pltpu.VMEM((span, HD), bf16)],
        compiler_params=pltpu.CompilerParams(vmem_limit_bytes=VMEM_BYTES),
        name="attend_back",
    )(klo, q, k, v, do, onat, linv, lens)


OUT_ROWS = 160
CHUNK_ROWS = 32
N_CHUNKS = 3
CHUNK = FF // N_CHUNKS
Q_WIDTH = H_Q * HD
HALF_OUT = (Q_WIDTH + FF) // 2
HALF_MID = 512
LEFT = HALF_OUT + HALF_MID


def middle_kernel(
    full_ref, mixed_ref, tok_ref, cot_ref, gain_ref, shuffle_ref, gate_ref, up_ref,
    out_ref, dres_ref, dob_ref, left_ref, wide_ref, dgain_ref,
    w_out, resid, mid_low, grad_mid, sems,
):
    step = pl.program_id(0)
    width = tok_ref.shape[1]

    def fetch(i):
        return pltpu.make_async_copy(
            full_ref.at[i, pl.ds(0, OUT_ROWS), :],
            w_out.at[pl.ds(i * OUT_ROWS, OUT_ROWS), :],
            sems.at[i],
        )

    n_fetch = full_ref.shape[0]
    n_first = -(-Q_WIDTH // OUT_ROWS)

    @pl.when(step == 0)
    def _():
        for i in range(n_fetch):
            fetch(i).start()
        for h in range(H_Q):
            left_ref[0, :, h * HD : (h + 1) * HD] = mixed_ref[h]
        for i in range(n_first):
            fetch(i).wait()
        residual = tok_ref[...].astype(f32) + dot_nn(
            left_ref[0, :, :Q_WIDTH], w_out[:Q_WIDTH, :]
        )
        resid[...] = residual
        out_ref[...] = residual
        normed = rms_norm(residual, gain_ref[...]).astype(bf16)
        low = dot_nn(normed, shuffle_ref[...]).astype(bf16)
        mid_low[...] = low
        for side in range(2):
            left_ref[side, :, HALF_OUT:] = low[:, side * HALF_MID : (side + 1) * HALF_MID]
        grad_mid[...] = jnp.zeros_like(grad_mid)
        for i in range(n_first, n_fetch):
            fetch(i).wait()

    for f in range(N_CHUNKS):

        @pl.when(step == f + 1)
        def _(f=f):
            at = Q_WIDTH + f * CHUNK
            gate_w = gate_ref[...].reshape(width, CHUNK)
            up_w = up_ref[...].reshape(width, CHUNK)
            gate = dot_nn(mid_low[...], gate_w)
            up = dot_nn(mid_low[...], up_w)
            sigmoid_gate = 1.0 / (1.0 + jnp.exp(-gate))
            activated = gate * sigmoid_gate
            hidden = (activated * up).astype(bf16)
            cut = min(max(HALF_OUT - at, 0), CHUNK)
            if cut > 0:
                left_ref[0, :, at : at + cut] = hidden[:, :cut]
            if cut < CHUNK:
                left_ref[1, :, at + cut - HALF_OUT : at + CHUNK - HALF_OUT] = hidden[:, cut:]
            down_w = w_out[at : at + CHUNK, :]
            out_ref[...] += dot_nn(hidden, down_w)
            grad_hidden = dot_nt(cot_ref[...], down_w)
            grad_up = (grad_hidden * activated).astype(bf16)
            grad_gate = (
                grad_hidden * up * sigmoid_gate * (1.0 + gate * (1.0 - sigmoid_gate))
            ).astype(bf16)
            wide_ref[:, f * CHUNK : (f + 1) * CHUNK] = grad_gate
            wide_ref[:, FF + f * CHUNK : FF + (f + 1) * CHUNK] = grad_up
            grad_mid[...] += dot_nt(grad_gate, gate_w) + dot_nt(grad_up, up_w)

    @pl.when(step == N_CHUNKS + 1)
    def _():
        grad = dot_nt(grad_mid[...].astype(bf16), shuffle_ref[...])
        part, terms = rms_back(resid[...], gain_ref[...], grad)
        dgain_ref[...] = jnp.sum(terms, axis=0, keepdims=True)
        dres = cot_ref[...].astype(f32) + part
        dres_ref[...] = dres
        low = dres.astype(bf16)
        wide_ref[:, 2 * FF :] = low
        for c in range(4):
            piece = dot_nt(low, w_out[c * 4 * HD : (c + 1) * 4 * HD, :]).astype(bf16)
            for h in range(4):
                dob_ref[4 * c + h] = piece[:, h * HD : (h + 1) * HD]


def middle(full, mixed, tok, cot, gain, shuffle):
    rows, width = tok.shape
    n_blocks = full.shape[0]
    first = OUT_ROWS // CHUNK_ROWS

    def chunk_of(i):
        return jnp.clip(i - 1, 0, N_CHUNKS - 1)

    def whole(shape):
        return pl.BlockSpec(shape, lambda i: (0,) * len(shape))

    chunk = (n_blocks, CHUNK_ROWS, CHUNK)
    return pl.pallas_call(
        middle_kernel,
        grid=(N_CHUNKS + 2,),
        in_specs=[
            pl.BlockSpec(memory_space=pl.ANY),
            whole((H_Q, rows, HD)),
            whole((rows, width)),
            whole((rows, width)),
            whole((1, width)),
            whole((width, width)),
            pl.BlockSpec(chunk, lambda i: (0, first + chunk_of(i), 0)),
            pl.BlockSpec(chunk, lambda i: (0, first + N_CHUNKS + chunk_of(i), 0)),
        ],
        out_specs=[
            whole((rows, width)),
            whole((rows, width)),
            whole((H_Q, rows, HD)),
            whole((2, rows, LEFT)),
            whole((rows, 2 * FF + width)),
            whole((1, width)),
        ],
        out_shape=[
            jax.ShapeDtypeStruct((rows, width), f32),
            jax.ShapeDtypeStruct((rows, width), f32),
            jax.ShapeDtypeStruct((H_Q, rows, HD), bf16),
            jax.ShapeDtypeStruct((2, rows, LEFT), bf16),
            jax.ShapeDtypeStruct((rows, 2 * FF + width), bf16),
            jax.ShapeDtypeStruct((1, width), f32),
        ],
        scratch_shapes=[
            pltpu.VMEM((Q_WIDTH + FF, width), bf16),
            pltpu.VMEM((rows, width), f32),
            pltpu.VMEM((rows, width), bf16),
            pltpu.VMEM((rows, width), f32),
            pltpu.SemaphoreType.DMA((n_blocks,)),
        ],
        compiler_params=pltpu.CompilerParams(vmem_limit_bytes=BIG_VMEM_BYTES),
        name="middle",
    )(full, mixed, tok, cot, gain, shuffle, full, full)


def grad_ffn_kernel(left_a, left_b, right_a, right_b, out_ref):
    total = dot_tn(left_a[...], right_a[...]) + dot_tn(left_b[...], right_b[...])
    out_ref[...] = total.astype(bf16).reshape(out_ref.shape)


def grad_ffn(lefts, wides, n_blocks):
    rows = lefts[0].shape[0]
    left = pl.BlockSpec((rows, HALF_MID), lambda i: (0, HALF_OUT // HALF_MID))
    right = pl.BlockSpec((rows, CHUNK), lambda i: (0, i))
    first = OUT_ROWS // CHUNK_ROWS
    height = OUT_ROWS + 2 * N_CHUNKS * CHUNK_ROWS
    return pl.pallas_call(
        grad_ffn_kernel,
        grid=(2 * N_CHUNKS,),
        in_specs=[left, left, right, right],
        out_specs=pl.BlockSpec((n_blocks, CHUNK_ROWS, CHUNK), lambda i: (0, first + i, 0)),
        out_shape=jax.ShapeDtypeStruct((n_blocks, height, CHUNK), bf16),
        compiler_params=pltpu.CompilerParams(vmem_limit_bytes=VMEM_BYTES),
        name="grad_ffn",
    )(*lefts, *wides)


def grad_out_kernel(core_ref, left_a, left_b, drb_a, drb_b, cot_a, cot_b, grads_ref, out_ref):
    step = pl.program_id(0)
    block = left_a.shape[1]
    both = Q_WIDTH // block
    cut = Q_WIDTH % block
    lower = core_ref[0] == 0

    def store(value):
        out_ref[...] = value.astype(bf16).reshape(out_ref.shape)

    @pl.when(lower & (step < both))
    def _():
        store(dot_tn(left_a[...], drb_a[...]) + dot_tn(left_b[...], drb_b[...]))

    @pl.when(lower & (step == both))
    def _():
        top = dot_tn(left_a[:, :cut], drb_a[...]) + dot_tn(left_b[:, :cut], drb_b[...])
        rest = dot_tn(left_a[:, cut:], cot_a[...]) + dot_tn(left_b[:, cut:], cot_b[...])
        store(jnp.concatenate([top, rest], axis=0))

    @pl.when(core_ref[0] == 1)
    def _():
        store(dot_tn(left_a[...], cot_a[...]) + dot_tn(left_b[...], cot_b[...]))


def grad_out(core, lefts, wides, cots, grads):
    rows, width = cots[0].shape
    blocks = 4
    left = pl.BlockSpec((rows, blocks * OUT_ROWS), lambda i, core: (0, i))
    drb = pl.BlockSpec((rows, width), lambda i, core: (0, 2 * N_CHUNKS))
    cot = pl.BlockSpec((rows, width), lambda i, core: (0, 0))
    return pl.pallas_call(
        grad_out_kernel,
        grid_spec=pltpu.PrefetchScalarGridSpec(
            num_scalar_prefetch=1,
            grid=(grads.shape[0] // blocks,),
            in_specs=[left, left, drb, drb, cot, cot, pl.BlockSpec(memory_space=pl.ANY)],
            out_specs=pl.BlockSpec((blocks, OUT_ROWS, width), lambda i, core: (i, 0, 0)),
        ),
        out_shape=jax.ShapeDtypeStruct(grads.shape, bf16),
        input_output_aliases={7: 0},
        compiler_params=pltpu.CompilerParams(vmem_limit_bytes=VMEM_BYTES),
        name="grad_out",
    )(core, *lefts, *wides, *cots, grads)


def adam_step(master, first_old, second_old, gradient, rate):
    first_new = BETA_ONE * first_old + (1.0 - BETA_ONE) * gradient
    second_new = BETA_TWO * second_old + (1.0 - BETA_TWO) * gradient * gradient
    first_hat = first_new / (1.0 - BETA_ONE**STEP)
    second_hat = second_new / (1.0 - BETA_TWO**STEP)
    master_new = master - rate * (
        first_hat / (jnp.sqrt(second_hat) + ADAM_EPS) + WEIGHT_DECAY * master
    )
    return (first_new, second_new, master_new)


def gathered(x):
    return lax.all_gather(x, AXIS_CYZ, axis=0, tiled=True)


def sum_over_x(blocks):
    me = lax.axis_index(AXIS_X)
    n = blocks.shape[0]

    def block(i):
        return lax.dynamic_index_in_dim(blocks, lax.rem(i, n), 0, keepdims=False)

    total = block(me).astype(f32)
    for shift in range(1, n):
        pairs = [(i, (i + shift) % n) for i in range(n)]
        total = total + lax.ppermute(block(me + shift), AXIS_X, pairs).astype(f32)
    return total


def shift(x, axis, step):
    n = SIZES[axis]
    return lax.ppermute(x, axis, [(i, (i + step) % n) for i in range(n)])


def first_moves(x):
    first, second = x[None, :HALF], x[None, HALF:]
    pair = jnp.concatenate([first, shift(first, "xh", 1)], axis=0)
    ring = jnp.concatenate([second] + [shift(second, "y", b) for b in (1, 2, 3)], axis=0)
    return pair, ring


def second_moves(pair, ring):
    one = jnp.concatenate([pair] + [shift(pair, "y", b) for b in (1, 2, 3)], axis=0)
    two = jnp.concatenate([ring, shift(ring, "xh", 1)], axis=0)
    return [one, two, shift(one, "core", 1), shift(two, "core", 1)]


def places_of_groups():
    xh, y, core = (lax.axis_index(name) for name in CTX)
    places = []
    for other in range(2):
        for side in range(2):
            for i in range(GROUP):
                b, a = (i // 2, i % 2) if side == 0 else (i % 4, i // 4)
                dev = (((xh + a) % 2) * 4 + (y - b) % 4) * 2 + (core + other) % 2
                places.append(dev if side == 0 else 31 - dev)
    return jnp.stack(places).astype(jnp.int32)


def sum_over_core(near, far):
    return (near.astype(f32) + shift(far, "core", 1).astype(f32)).astype(bf16)


def first_sums(plane):
    one = plane[:GROUP].reshape((4, 2) + plane.shape[1:])
    two = plane[GROUP:].reshape((2, 4) + plane.shape[1:])
    two = (two[0].astype(f32) + shift(two[1], "xh", 1).astype(f32)).astype(bf16)
    one = sum((shift(one[b], "y", -b).astype(f32) for b in (1, 2, 3)), one[0].astype(f32))
    return one.astype(bf16), two


def second_sums(one, two):
    two = sum((shift(two[b], "y", -b).astype(f32) for b in (1, 2, 3)), two[0].astype(f32))
    one = one[0].astype(f32) + shift(one[1], "xh", 1).astype(f32)
    return jnp.concatenate([one, two], axis=0)


def pick(v, i, n, axis):
    return lax.dynamic_index_in_dim(v, lax.rem(i, n), axis, keepdims=False)


def sum_over_xl(x):
    xl = lax.axis_index("xl")
    return pick(x, xl, 2, 1).astype(f32) + shift(pick(x, xl + 1, 2, 1), "xl", 1).astype(f32)


def sum_over_z(x):
    z = lax.axis_index("z")
    low = x.astype(bf16)
    total = pick(x, z, 4, 1)
    for step in (1, 2, 3):
        total = total + shift(pick(low, z + step, 4, 1), "z", step).astype(f32)
    return total


def gather_shard(x):
    xl = lax.axis_index("xl")
    ring = lax.all_gather(x, "z", axis=0, tiled=False)
    other = shift(ring, "xl", 1)
    return jnp.stack([jnp.where(xl == 0, ring, other), jnp.where(xl == 0, other, ring)])


def natural_of_permuted(x):
    tail = x.shape[1:]
    x = x.reshape((2, 4, 4, 2, 2) + tail)
    x = x.transpose((3, 1, 0, 4, 2) + tuple(range(5, 5 + len(tail))))
    return x.reshape((128,) + tail)


def owner_pairs():
    pairs = []
    for n in range(128):
        z = n % 4
        xl = (n // 4) % 2
        core = (n // 8) % 2
        y = (n // 16) % 4
        xh = n // 64
        pairs.append((n, (((core * 4 + y) * 4 + z) * 2 + xh) * 2 + xl))
    return pairs


def body(
    tokens,
    cotangent,
    segments,
    positions,
    pad_mask,
    w_in,
    w_out,
    gains,
    first_in,
    first_out,
    first_gains,
    second_in,
    second_out,
    second_gains,
):
    rows = tokens.shape[1]
    width = tokens.shape[2]
    span = segments.shape[1]
    half = rows // 2
    n_ctx = span // rows
    q_width = H_Q * HD
    kv_width = H_KV * HD
    attn_cols = q_width + 2 * kv_width
    owned = w_in.shape[0]
    owned_gains = gains.shape[0]

    n_x = 4
    low_in = w_in.astype(bf16)
    n_dev = width // owned

    own_head = jnp.concatenate(
        [
            low_in[:, :q_width].reshape(owned, H_Q, HD),
            jnp.repeat(low_in[:, q_width : q_width + kv_width].reshape(owned, H_KV, HD), 2, axis=1),
            jnp.repeat(low_in[:, q_width + kv_width : attn_cols].reshape(owned, H_KV, HD), 2, axis=1),
            jnp.broadcast_to(
                jnp.pad(gains.astype(bf16)[None, None], ((0, owned - 1), (0, 0), (0, HD - owned_gains))),
                (owned, H_Q, HD),
            ),
        ],
        axis=2,
    ).transpose(1, 0, 2)
    pair, ring = first_moves(tokens[0])
    pairs = owner_pairs()
    own_out = lax.ppermute(w_out.astype(bf16), EVERY, [(p, n) for n, p in pairs])
    own_ffn = low_in[:, attn_cols:].reshape(owned, 2 * N_CHUNKS, CHUNK)
    own_ffn = own_ffn.transpose(1, 0, 2).reshape(2 * N_CHUNKS * owned, CHUNK)
    own_rest = jnp.concatenate([own_out, own_ffn], axis=0)
    own_rest = lax.all_gather(own_rest, AXIS_X, axis=0, tiled=False)
    own_head, own_rest, pair, ring = lax.optimization_barrier((own_head, own_rest, pair, ring))
    head = lax.all_to_all(own_head, CTX, 0, 0, tiled=True)
    head, segments, pad_mask = lax.optimization_barrier((head, segments, pad_mask))
    head = gather_shard(head)
    head = head.transpose(2, 0, 1, 3, 4)
    gain_vals = head[:, :, :, 0, HEAD_COLS : HEAD_COLS + owned_gains].reshape(-1).astype(f32)
    w_head = head[..., :HEAD_COLS].reshape(width, HEAD_COLS)
    gain_one = gain_vals[:width]
    gain_two = gain_vals[width : 2 * width]
    gain_query = gain_vals[2 * width : 2 * width + HD].reshape(1, HD)
    gain_key = gain_vals[2 * width + HD :].reshape(1, HD)
    w_scaled = (w_head.astype(f32) * gain_one[:, None]).astype(bf16)

    n_out = w_out.shape[0]
    part_out = own_rest[:, :n_out].reshape(n_x * n_out, width)
    part_ffn = own_rest[:, n_out:].reshape(n_x, 2 * N_CHUNKS, owned, CHUNK).transpose(1, 0, 2, 3)
    part_ffn = part_ffn.reshape(2 * N_CHUNKS * CHUNK_ROWS, CHUNK)
    full = gathered(jnp.concatenate([part_out, part_ffn], axis=0)[None])

    order = natural_of_permuted(jnp.arange(width, dtype=jnp.int32).reshape(n_dev, owned)).reshape(-1)
    shuffle = (order[:, None] == jnp.arange(width, dtype=jnp.int32)[None, :]).astype(bf16)

    def natural(x):
        x = x.reshape(n_ctx, 2, half)
        return jnp.concatenate([x[:, 0], x[::-1, 1]], axis=0)

    docs = natural(segments[0])
    live = natural(pad_mask[0])
    at = jnp.arange(span, dtype=jnp.int32).reshape(2 * n_ctx, half)
    start = jnp.zeros_like(docs)
    for number in range(1, 14):
        before = jnp.sum((docs < number).astype(jnp.int32))
        start = jnp.where(docs == number, before, start)
    place_in = at - start
    lens = jnp.where(live == 1, place_in, 0)
    klo = jnp.min((at - lens).reshape(span // BQ, BQ), axis=1) // BK
    lens = lens.reshape(span // BQ, BQ)
    halves = jnp.arange(HD // 2, dtype=f32)
    inverse = ROPE_BASE ** (-2.0 * halves / HD)
    angle = place_in.reshape(span, 1).astype(f32) * inverse[None, :]
    cos_half = jnp.cos(angle)
    sin_half = jnp.sin(angle)
    cos = jnp.concatenate([cos_half, cos_half], axis=1)
    sin = jnp.concatenate([-sin_half, sin_half], axis=1)

    groups = second_moves(pair, ring)
    place = places_of_groups()
    q, k, v, query_raw, key_raw, inv = project(
        place, groups, w_scaled, cos, sin, gain_query, gain_key
    )
    o_send, o_nat, l_inv = attend(klo, q, k, v, lens, rows)
    mixed = lax.all_to_all(o_send, CTX, 0, 0, tiled=True)

    output, grad_residual, do_send, left, wide, gain_two_terms = middle(
        full, mixed, tokens[0], cotangent[0], gain_two.reshape(1, width), shuffle
    )
    core = lax.axis_index("core")
    lefts = (pick(left, core, 2, 0), shift(pick(left, core + 1, 2, 0), "core", 1))
    wides = (wide, shift(wide, "core", 1))
    cots = (cotangent[0], shift(cotangent[0], "core", 1))
    grads = grad_ffn(lefts, wides, full.shape[0] // 2)
    grads = grad_out(core.astype(jnp.int32).reshape(1), lefts, wides, cots, grads)
    do = lax.all_to_all(do_send, CTX, 0, 0, tiled=True)
    do, grads = lax.optimization_barrier((do, grads))
    grads = grads.reshape(-1, width)
    grads = lax.psum_scatter(grads, AXIS_YZ, scatter_dimension=0, tiled=True)

    head_grads = attend_back(klo, q, k, v, do, o_nat, l_inv, lens)
    da_near, da_far, dw_head, gain_qk = project_back(
        place, groups, head_grads, (query_raw, key_raw, inv), cos, sin, gain_query, gain_key, w_head
    )

    gain_one_grad = jnp.sum(dw_head * w_head.astype(f32), axis=1)
    grad_gains = jnp.concatenate([gain_one_grad, gain_two_terms[0], gain_qk[0], gain_qk[1]])
    grad_gains = jnp.pad(
        grad_gains.reshape(n_dev, 1, owned_gains), ((0, 0), (0, owned - 1), (0, HD - owned_gains))
    )
    dw_head = (dw_head * gain_one[:, None]).reshape(n_dev, owned, HEAD_COLS)
    dw_head = jnp.concatenate([dw_head, grad_gains], axis=2).astype(bf16)
    dw_head = sum_over_xl(dw_head.reshape(n_ctx, 2, 4, owned, PAD_COLS))
    plane = sum_over_core(da_near, da_far)
    dw_head, plane = lax.optimization_barrier((dw_head, plane))
    dw_head = sum_over_z(dw_head).astype(bf16)
    one, two = first_sums(plane)
    dw_head, one, two = lax.optimization_barrier((dw_head, one, two))
    dw_head = lax.all_to_all(dw_head, CTX, 0, 0, tiled=True).astype(f32)

    grad_a = second_sums(one, two)
    inputs = tokens[0].astype(f32)
    input_grad = grad_residual + rms_back(inputs, gain_one, grad_a)[0]
    owned_gain_grad = jnp.sum(dw_head[:, 0, HEAD_COLS : HEAD_COLS + owned_gains], axis=0)

    def columns(x):
        return x.transpose(1, 0, 2).reshape(owned, -1)

    def over_pair(x):
        return columns(jnp.sum(x.reshape(H_KV, 2, owned, HD), axis=1))

    out_part = grads[:OUT_ROWS].reshape(n_x, OUT_ROWS // n_x, width)
    ffn_part = grads[OUT_ROWS:].reshape(2 * N_CHUNKS, n_x, owned, CHUNK)
    ffn_part = ffn_part.transpose(1, 0, 2, 3).reshape(n_x, 2 * N_CHUNKS * owned, CHUNK)
    grads = sum_over_x(jnp.concatenate([out_part, ffn_part], axis=1))
    owned_out = lax.ppermute(grads[: OUT_ROWS // n_x], EVERY, pairs)
    owned_ffn = grads[OUT_ROWS // n_x :].reshape(2 * N_CHUNKS, owned, CHUNK)
    owned_in = jnp.concatenate(
        [
            columns(dw_head[:, :, :HD]),
            over_pair(dw_head[:, :, HD : 2 * HD]),
            over_pair(dw_head[:, :, 2 * HD : HEAD_COLS]),
            columns(owned_ffn),
        ],
        axis=1,
    )
    new_first_in, new_second_in, new_master_in = adam_step(
        w_in, first_in, second_in, owned_in, RATE_MATRIX
    )
    new_first_out, new_second_out, new_master_out = adam_step(
        w_out, first_out, second_out, owned_out, RATE_MATRIX
    )
    new_first_gains, new_second_gains, new_master_gains = adam_step(
        gains, first_gains, second_gains, owned_gain_grad, RATE_GAIN
    )
    return (
        output[None],
        input_grad[None],
        new_first_in,
        new_first_out,
        new_first_gains,
        new_second_in,
        new_second_out,
        new_second_gains,
        new_master_in,
        new_master_out,
        new_master_gains,
        new_master_in.astype(bf16),
        new_master_out.astype(bf16),
    )


def solution(mesh):
    cut = Mesh(mesh.devices.reshape(tuple(SIZES[name] for name in EVERY)), EVERY)
    weights = P(EVERY, None)
    vector = P(EVERY)
    acts = P(SHARD, CTX, None)
    in_specs = (
        acts,
        acts,
        P(SHARD, None),
        P(SHARD, CTX),
        P(SHARD, None),
    ) + (weights, weights, vector) * 3
    out_specs = (acts, acts) + (weights, weights, vector) * 3 + (weights, weights)
    return jax.shard_map(body, mesh=cut, in_specs=in_specs, out_specs=out_specs, check_vma=False)
```

```python
import functools
import math

import jax
import jax.numpy as jnp
from jax import lax
from jax.experimental import pallas as pl
from jax.experimental.pallas import tpu as pltpu
from jax.sharding import Mesh
from jax.sharding import PartitionSpec as P

H_Q = 16
H_KV = 8
HD = 128
FF = 3072
STEP = 5

NORM_EPS = 1e-06
ROPE_BASE = 1000000.0
BETA_ONE = 0.5
BETA_TWO = 0.5
ADAM_EPS = 1e-08
WEIGHT_DECAY = 0.1
RATE_MATRIX = 0.03
RATE_GAIN = 0.25

CTX = ("xh", "y", "core")
SHARD = ("xl", "z")
EVERY = CTX + SHARD
AXIS_X = ("xh", "xl")
AXIS_YZ = ("y", "z")
AXIS_CYZ = ("core", "y", "z")
SIZES = {"xh": 2, "y": 4, "core": 2, "xl": 2, "z": 4}

LOG2_E = 1.4426950408889634
SCORE_SCALE = 1.0 / math.sqrt(HD)
BQ = 512
BK = 512
SUB = 256
VMEM_BYTES = 48 * 1024 * 1024
BIG_VMEM_BYTES = 60 * 1024 * 1024

bf16 = jnp.bfloat16
f32 = jnp.float32


def rms_norm(values, weight):
    return values * lax.rsqrt(jnp.mean(values * values, axis=-1, keepdims=True) + NORM_EPS) * weight


def rms_back(values, weight, upstream):
    inverse = lax.rsqrt(jnp.mean(values * values, axis=-1, keepdims=True) + NORM_EPS)
    normed = values * inverse
    scaled = upstream * weight
    grad_values = inverse * (scaled - normed * jnp.mean(scaled * normed, axis=-1, keepdims=True))
    return (grad_values, upstream * normed)


def dot_nt(a, b):
    return lax.dot_general(a, b, (((1,), (1,)), ((), ())), preferred_element_type=f32)


def dot_tn(a, b):
    return lax.dot_general(a, b, (((0,), (0,)), ((), ())), preferred_element_type=f32)


def dot_nn(a, b):
    return lax.dot_general(a, b, (((1,), (0,)), ((), ())), preferred_element_type=f32)


N_GROUPS = 4
GROUP = 8
HALF = 128
STEP_BLOCKS = 4
STEPS = GROUP // STEP_BLOCKS
HEAD_COLS = 3 * HD
PAD_COLS = 4 * HD


def block_spec(width, first, count):
    return pl.BlockSpec(
        (STEP_BLOCKS, HALF, width), lambda i, place: (jnp.clip(i - first, 0, count - 1), 0, 0)
    )


def group_specs(width):
    return [block_spec(width, k * STEPS, STEPS) for k in range(N_GROUPS)]


def fixed(shape):
    return pl.BlockSpec(shape, lambda i, place: (0,) * len(shape))


def rows_of(place_ref, step, i):
    return pl.ds(pl.multiple_of(place_ref[step * STEP_BLOCKS + i] * HALF, HALF), HALF)


def head_mean(x):
    return lax.dot_general(
        x.astype(bf16),
        jnp.full((HD, HD), 1.0 / HD, bf16),
        (((1,), (0,)), ((), ())),
        preferred_element_type=f32,
    )


def project_kernel(
    place_ref, x0, x1, x2, x3, w_ref, cos_ref, sin_ref, gq_ref, gk_ref,
    q_ref, k_ref, v_ref, qraw_ref, kraw_ref, inv_ref,
):
    step = pl.program_id(0)

    def run(x):
        wide = x.astype(f32)
        inverse = lax.rsqrt(jnp.mean(wide * wide, axis=-1, keepdims=True) + NORM_EPS)
        prod = dot_nn(x, w_ref[...]) * inverse
        for i in range(STEP_BLOCKS):
            at = rows_of(place_ref, step, i)
            part = slice(i * HALF, (i + 1) * HALF)
            cos = cos_ref[at, :]
            sin = sin_ref[at, :]

            def roped(raw, gain, cos=cos, sin=sin):
                normed = raw * lax.rsqrt(head_mean(raw * raw) + NORM_EPS) * gain
                return normed * cos + pltpu.roll(normed, HD // 2, 1) * sin

            query = prod[part, :HD]
            key = prod[part, HD : 2 * HD]
            inv_ref[at, :] = jnp.broadcast_to(inverse[part], (HALF, HD)).astype(bf16)
            qraw_ref[at, :] = query.astype(bf16)
            kraw_ref[at, :] = key.astype(bf16)
            q_ref[at, :] = (roped(query, gq_ref[...]) * (SCORE_SCALE * LOG2_E)).astype(bf16)
            k_ref[at, :] = roped(key, gk_ref[...]).astype(bf16)
            v_ref[at, :] = prod[part, 2 * HD :].astype(bf16)

    for k, x_ref in enumerate((x0, x1, x2, x3)):

        @pl.when(step // STEPS == k)
        def _(x_ref=x_ref):
            run(x_ref[...].reshape(STEP_BLOCKS * HALF, x_ref.shape[2]))


def project(place, groups, w, cos, sin, gq, gk):
    width = w.shape[0]
    span = cos.shape[0]
    low = jax.ShapeDtypeStruct((span, HD), bf16)
    whole = fixed((span, HD))
    return pl.pallas_call(
        project_kernel,
        grid_spec=pltpu.PrefetchScalarGridSpec(
            num_scalar_prefetch=1,
            grid=(N_GROUPS * STEPS,),
            in_specs=group_specs(width)
            + [fixed((width, HEAD_COLS)), whole, whole, fixed((1, HD)), fixed((1, HD))],
            out_specs=[whole] * 6,
        ),
        out_shape=[low] * 6,
        compiler_params=pltpu.CompilerParams(vmem_limit_bytes=VMEM_BYTES),
        name="project",
    )(place, *groups, w, cos, sin, gq, gk)


def project_back_kernel(
    place_ref, x0, x1, x2, x3, dq_ref, dk_ref, dv_ref, qraw_ref, kraw_ref, inv_ref, cos_ref, sin_ref,
    gq_ref, gk_ref, w_ref, near_ref, far_ref, dw_ref, dg_ref, grads, scaled,
):
    step = pl.program_id(0)

    @pl.when(step == 0)
    def _():
        dw_ref[...] = jnp.zeros_like(dw_ref)
        dg_ref[...] = jnp.zeros_like(dg_ref)

    def run(x, da_ref):
        q_sum = jnp.zeros((1, HD), f32)
        k_sum = jnp.zeros((1, HD), f32)
        for i in range(STEP_BLOCKS):
            at = rows_of(place_ref, step, i)
            part = slice(i * HALF, (i + 1) * HALF)
            cos = cos_ref[at, :]
            sin = sin_ref[at, :]

            def back(raw, gain, grad, cos=cos, sin=sin):
                unrot = grad * cos + pltpu.roll(grad * sin, HD // 2, 1)
                inv_rms = lax.rsqrt(head_mean(raw * raw) + NORM_EPS)
                normed = raw * inv_rms
                scaled_up = unrot * gain
                grad = inv_rms * (scaled_up - normed * head_mean(scaled_up * normed))
                return grad, unrot * normed

            grad_q, q_terms = back(qraw_ref[at, :].astype(f32), gq_ref[...], dq_ref[at, :])
            grad_k, k_terms = back(kraw_ref[at, :].astype(f32), gk_ref[...], dk_ref[at, :])
            inverse = inv_ref[at, :].astype(f32)
            for c, grad in enumerate((grad_q, grad_k, dv_ref[at, :])):
                grads[part, c * HD : (c + 1) * HD] = grad.astype(bf16)
                scaled[part, c * HD : (c + 1) * HD] = (grad * inverse).astype(bf16)
            q_sum = q_sum + jnp.sum(q_terms, axis=0, keepdims=True)
            k_sum = k_sum + jnp.sum(k_terms, axis=0, keepdims=True)
        da_ref[...] = dot_nt(grads[...], w_ref[...]).astype(bf16).reshape(da_ref.shape)
        dw_ref[...] += dot_tn(x, scaled[...])
        dg_ref[0:1, :] += q_sum
        dg_ref[1:2, :] += k_sum

    for k, x_ref in enumerate((x0, x1, x2, x3)):

        @pl.when(step // STEPS == k)
        def _(k=k, x_ref=x_ref):
            da_ref = near_ref if k < N_GROUPS // 2 else far_ref
            run(x_ref[...].reshape(STEP_BLOCKS * HALF, x_ref.shape[2]), da_ref)


def project_back(place, groups, grads, raws, cos, sin, gq, gk, w):
    width = w.shape[0]
    span = cos.shape[0]
    whole = fixed((span, HD))
    n_half = N_GROUPS // 2
    da = jax.ShapeDtypeStruct((n_half * GROUP, HALF, width), bf16)
    return pl.pallas_call(
        project_back_kernel,
        grid_spec=pltpu.PrefetchScalarGridSpec(
            num_scalar_prefetch=1,
            grid=(N_GROUPS * STEPS,),
            in_specs=group_specs(width)
            + [whole] * 8
            + [fixed((1, HD)), fixed((1, HD)), fixed((width, HEAD_COLS))],
            out_specs=[
                block_spec(width, 0, n_half * STEPS),
                block_spec(width, n_half * STEPS, n_half * STEPS),
                fixed((width, HEAD_COLS)),
                fixed((8, HD)),
            ],
            scratch_shapes=[
                pltpu.VMEM((STEP_BLOCKS * HALF, HEAD_COLS), bf16),
                pltpu.VMEM((STEP_BLOCKS * HALF, HEAD_COLS), bf16),
            ],
        ),
        out_shape=[
            da,
            da,
            jax.ShapeDtypeStruct((width, HEAD_COLS), f32),
            jax.ShapeDtypeStruct((8, HD), f32),
        ],
        compiler_params=pltpu.CompilerParams(vmem_limit_bytes=BIG_VMEM_BYTES),
        name="project_back",
    )(place, *groups, *grads, *raws, cos, sin, gq, gk, w)


def dealt_slot(place, n_dev):
    if place < n_dev:
        return place, 0
    return 2 * n_dev - 1 - place, 1


def key_mask(len_row, offset):
    ahead = (
        lax.broadcasted_iota(jnp.int32, (SUB, BQ), 1)
        - lax.broadcasted_iota(jnp.int32, (SUB, BQ), 0)
        + offset
    )
    return (ahead >= 0) & (ahead <= len_row)


def key_loops(bounds_ref, qb, q_at, tile):
    low = bounds_ref[0, qb]
    high = (q_at + BQ - 1) // BK + 1
    first = jnp.minimum(bounds_ref[1, qb], high)
    last = jnp.maximum((q_at + 1) // BK, first)

    def run(masked):
        def step(kb, _):
            tile(kb, masked)
            return 0

        return step

    lax.fori_loop(low, first, run(True), 0)
    lax.fori_loop(first, last, run(False), 0)
    lax.fori_loop(last, high, run(True), 0)


def attend_kernel(
    bounds_ref, q_ref, k_ref, v_ref, len_ref, osend_ref, onat_ref, linv_ref, acc, total
):
    n_dev, rows, _ = osend_ref.shape
    half = rows // 2
    span = q_ref.shape[0]
    def q_step(qb, _):
        q_at = pl.multiple_of(qb * BQ, BQ)
        q_blk = q_ref[pl.ds(q_at, BQ), :]
        len_row = len_ref[pl.ds(qb, 1), :]
        acc[...] = jnp.zeros_like(acc)
        total[...] = jnp.zeros_like(total)

        def tile(kb, masked):
            mixed = None
            summed = None
            for c in range(BK // SUB):
                k_at = pl.multiple_of(kb * BK + c * SUB, SUB)
                p = jnp.exp2(dot_nt(k_ref[pl.ds(k_at, SUB), :], q_blk))
                if masked:
                    p = jnp.where(key_mask(len_row, q_at - k_at), p, 0.0)
                part = jnp.sum(p.reshape(SUB // 8, 8, BQ), axis=0)
                more = dot_tn(v_ref[pl.ds(k_at, SUB), :], p.astype(bf16))
                summed = part if summed is None else summed + part
                mixed = more if mixed is None else mixed + more
            acc[...] += mixed
            total[...] += summed

        key_loops(bounds_ref, qb, q_at, tile)
        inverse = 1.0 / jnp.sum(total[...], axis=0, keepdims=True)
        linv_ref[pl.ds(qb, 1), :] = inverse
        onat_ref[pl.ds(q_at, BQ), :] = (acc[...] * inverse).T
        return 0

    lax.fori_loop(0, span // BQ, q_step, 0)
    for place in range(2 * n_dev):
        dev, side = dealt_slot(place, n_dev)
        osend_ref[dev, side * half : (side + 1) * half, :] = onat_ref[
            place * half : (place + 1) * half, :
        ].astype(bf16)


def vmem():
    return pl.BlockSpec(memory_space=pltpu.VMEM)


def attend(klo, q, k, v, lens, rows):
    span = q.shape[0]
    return pl.pallas_call(
        attend_kernel,
        in_specs=[pl.BlockSpec(memory_space=pltpu.SMEM)] + [vmem()] * 4,
        out_specs=[vmem(), vmem(), vmem()],
        out_shape=[
            jax.ShapeDtypeStruct((span // rows, rows, HD), bf16),
            jax.ShapeDtypeStruct((span, HD), f32),
            jax.ShapeDtypeStruct((span // BQ, BQ), f32),
        ],
        scratch_shapes=[
            pltpu.VMEM((HD, BQ), f32),
            pltpu.VMEM((8, BQ), f32),
        ],
        compiler_params=pltpu.CompilerParams(vmem_limit_bytes=VMEM_BYTES),
        name="attend",
    )(klo, q, k, v, lens)


def attend_back_kernel(
    bounds_ref, q_ref, k_ref, v_ref, do_ref, onat_ref, linv_ref, len_ref, dq, dk, dv, don, acc
):
    n_dev, rows, _ = do_ref.shape
    half = rows // 2
    span = q_ref.shape[0]
    for place in range(2 * n_dev):
        dev, side = dealt_slot(place, n_dev)
        to = slice(place * half, (place + 1) * half)
        don[to, :] = do_ref[dev, side * half : (side + 1) * half, :]
    dk[...] = jnp.zeros_like(dk)
    dv[...] = jnp.zeros_like(dv)

    def q_step(qb, _):
        q_at = pl.multiple_of(qb * BQ, BQ)
        q_blk = q_ref[pl.ds(q_at, BQ), :]
        do_blk = don[pl.ds(q_at, BQ), :]
        len_row = len_ref[pl.ds(qb, 1), :]
        inverse = linv_ref[pl.ds(qb, 1), :]
        mixed = (do_blk.astype(f32) * onat_ref[pl.ds(q_at, BQ), :]).T
        delta = jnp.sum(mixed, axis=0, keepdims=True)
        acc[...] = jnp.zeros_like(acc)

        def tile(kb, masked):
            total = None
            for c in range(BK // SUB):
                k_at = pl.multiple_of(kb * BK + c * SUB, SUB)
                here = pl.ds(k_at, SUB)
                p = jnp.exp2(dot_nt(k_ref[here, :], q_blk)) * inverse
                if masked:
                    p = jnp.where(key_mask(len_row, q_at - k_at), p, 0.0)
                dp = dot_nt(v_ref[here, :], do_blk)
                ds = (p * (dp - delta)).astype(bf16)
                dv[here, :] += dot_nn(p.astype(bf16), do_blk)
                dk[here, :] += dot_nn(ds, q_blk)
                more = dot_tn(k_ref[here, :], ds)
                total = more if total is None else total + more
            acc[...] += total

        key_loops(bounds_ref, qb, q_at, tile)
        dq[pl.ds(q_at, BQ), :] = (acc[...] * SCORE_SCALE).T
        return 0

    lax.fori_loop(0, span // BQ, q_step, 0)
    dk[...] = dk[...] * (1.0 / LOG2_E)


def attend_back(klo, q, k, v, do, onat, linv, lens):
    span = q.shape[0]
    return pl.pallas_call(
        attend_back_kernel,
        in_specs=[pl.BlockSpec(memory_space=pltpu.SMEM)] + [vmem()] * 7,
        out_specs=[vmem()] * 3,
        out_shape=[jax.ShapeDtypeStruct((span, HD), f32)] * 3,
        scratch_shapes=[
            pltpu.VMEM((span, HD), bf16),
            pltpu.VMEM((HD, BQ), f32),
        ],
        compiler_params=pltpu.CompilerParams(vmem_limit_bytes=VMEM_BYTES),
        name="attend_back",
    )(klo, q, k, v, do, onat, linv, lens)


OUT_ROWS = 160
CHUNK_ROWS = 32
N_CHUNKS = 3
CHUNK = FF // N_CHUNKS
Q_WIDTH = H_Q * HD
HALF_OUT = (Q_WIDTH + FF) // 2
HALF_MID = 512
LEFT = HALF_OUT + HALF_MID


def middle_kernel(
    full_ref, mixed_ref, tok_ref, cot_ref, gain_ref, shuffle_ref, gate_ref, up_ref,
    out_ref, dres_ref, dob_ref, left_ref, wide_ref, dgain_ref,
    w_out, resid, mid_low, grad_mid, sems,
):
    step = pl.program_id(0)
    width = tok_ref.shape[1]

    def fetch(i):
        return pltpu.make_async_copy(
            full_ref.at[i, pl.ds(0, OUT_ROWS), :],
            w_out.at[pl.ds(i * OUT_ROWS, OUT_ROWS), :],
            sems.at[i],
        )

    n_fetch = full_ref.shape[0]
    n_first = -(-Q_WIDTH // OUT_ROWS)

    @pl.when(step == 0)
    def _():
        for i in range(n_fetch):
            fetch(i).start()
        for h in range(H_Q):
            left_ref[0, :, h * HD : (h + 1) * HD] = mixed_ref[h]
        for i in range(n_first):
            fetch(i).wait()
        residual = tok_ref[...].astype(f32) + dot_nn(
            left_ref[0, :, :Q_WIDTH], w_out[:Q_WIDTH, :]
        )
        resid[...] = residual
        out_ref[...] = residual
        normed = rms_norm(residual, gain_ref[...]).astype(bf16)
        low = dot_nn(normed, shuffle_ref[...]).astype(bf16)
        mid_low[...] = low
        for side in range(2):
            left_ref[side, :, HALF_OUT:] = low[:, side * HALF_MID : (side + 1) * HALF_MID]
        grad_mid[...] = jnp.zeros_like(grad_mid)
        for i in range(n_first, n_fetch):
            fetch(i).wait()

    for f in range(N_CHUNKS):

        @pl.when(step == f + 1)
        def _(f=f):
            at = Q_WIDTH + f * CHUNK
            gate_w = gate_ref[...].reshape(width, CHUNK)
            up_w = up_ref[...].reshape(width, CHUNK)
            gate = dot_nn(mid_low[...], gate_w)
            up = dot_nn(mid_low[...], up_w)
            sigmoid_gate = 1.0 / (1.0 + jnp.exp(-gate))
            activated = gate * sigmoid_gate
            hidden = (activated * up).astype(bf16)
            cut = min(max(HALF_OUT - at, 0), CHUNK)
            if cut > 0:
                left_ref[0, :, at : at + cut] = hidden[:, :cut]
            if cut < CHUNK:
                left_ref[1, :, at + cut - HALF_OUT : at + CHUNK - HALF_OUT] = hidden[:, cut:]
            down_w = w_out[at : at + CHUNK, :]
            out_ref[...] += dot_nn(hidden, down_w)
            grad_hidden = dot_nt(cot_ref[...], down_w)
            grad_up = (grad_hidden * activated).astype(bf16)
            grad_gate = (
                grad_hidden * up * sigmoid_gate * (1.0 + gate * (1.0 - sigmoid_gate))
            ).astype(bf16)
            wide_ref[:, f * CHUNK : (f + 1) * CHUNK] = grad_gate
            wide_ref[:, FF + f * CHUNK : FF + (f + 1) * CHUNK] = grad_up
            grad_mid[...] += dot_nt(grad_gate, gate_w) + dot_nt(grad_up, up_w)

    @pl.when(step == N_CHUNKS + 1)
    def _():
        grad = dot_nt(grad_mid[...].astype(bf16), shuffle_ref[...])
        part, terms = rms_back(resid[...], gain_ref[...], grad)
        dgain_ref[...] = jnp.sum(terms, axis=0, keepdims=True)
        dres = cot_ref[...].astype(f32) + part
        dres_ref[...] = dres
        low = dres.astype(bf16)
        wide_ref[:, 2 * FF :] = low
        for c in range(4):
            piece = dot_nt(low, w_out[c * 4 * HD : (c + 1) * 4 * HD, :]).astype(bf16)
            for h in range(4):
                dob_ref[4 * c + h] = piece[:, h * HD : (h + 1) * HD]


def middle(full, mixed, tok, cot, gain, shuffle):
    rows, width = tok.shape
    n_blocks = full.shape[0]
    first = OUT_ROWS // CHUNK_ROWS

    def chunk_of(i):
        return jnp.clip(i - 1, 0, N_CHUNKS - 1)

    def whole(shape):
        return pl.BlockSpec(shape, lambda i: (0,) * len(shape))

    chunk = (n_blocks, CHUNK_ROWS, CHUNK)
    return pl.pallas_call(
        middle_kernel,
        grid=(N_CHUNKS + 2,),
        in_specs=[
            pl.BlockSpec(memory_space=pl.ANY),
            whole((H_Q, rows, HD)),
            whole((rows, width)),
            whole((rows, width)),
            whole((1, width)),
            whole((width, width)),
            pl.BlockSpec(chunk, lambda i: (0, first + chunk_of(i), 0)),
            pl.BlockSpec(chunk, lambda i: (0, first + N_CHUNKS + chunk_of(i), 0)),
        ],
        out_specs=[
            whole((rows, width)),
            whole((rows, width)),
            whole((H_Q, rows, HD)),
            whole((2, rows, LEFT)),
            whole((rows, 2 * FF + width)),
            whole((1, width)),
        ],
        out_shape=[
            jax.ShapeDtypeStruct((rows, width), f32),
            jax.ShapeDtypeStruct((rows, width), f32),
            jax.ShapeDtypeStruct((H_Q, rows, HD), bf16),
            jax.ShapeDtypeStruct((2, rows, LEFT), bf16),
            jax.ShapeDtypeStruct((rows, 2 * FF + width), bf16),
            jax.ShapeDtypeStruct((1, width), f32),
        ],
        scratch_shapes=[
            pltpu.VMEM((Q_WIDTH + FF, width), bf16),
            pltpu.VMEM((rows, width), f32),
            pltpu.VMEM((rows, width), bf16),
            pltpu.VMEM((rows, width), f32),
            pltpu.SemaphoreType.DMA((n_blocks,)),
        ],
        compiler_params=pltpu.CompilerParams(vmem_limit_bytes=BIG_VMEM_BYTES),
        name="middle",
    )(full, mixed, tok, cot, gain, shuffle, full, full)


def grad_ffn_kernel(left_a, left_b, right_a, right_b, out_ref):
    total = dot_tn(left_a[...], right_a[...]) + dot_tn(left_b[...], right_b[...])
    out_ref[...] = total.astype(bf16).reshape(out_ref.shape)


def grad_ffn(lefts, wides, n_blocks):
    rows = lefts[0].shape[0]
    left = pl.BlockSpec((rows, HALF_MID), lambda i: (0, HALF_OUT // HALF_MID))
    right = pl.BlockSpec((rows, CHUNK), lambda i: (0, i))
    first = OUT_ROWS // CHUNK_ROWS
    height = OUT_ROWS + 2 * N_CHUNKS * CHUNK_ROWS
    return pl.pallas_call(
        grad_ffn_kernel,
        grid=(2 * N_CHUNKS,),
        in_specs=[left, left, right, right],
        out_specs=pl.BlockSpec((n_blocks, CHUNK_ROWS, CHUNK), lambda i: (0, first + i, 0)),
        out_shape=jax.ShapeDtypeStruct((n_blocks, height, CHUNK), bf16),
        compiler_params=pltpu.CompilerParams(vmem_limit_bytes=VMEM_BYTES),
        name="grad_ffn",
    )(*lefts, *wides)


def grad_out_kernel(core_ref, left_a, left_b, drb_a, drb_b, cot_a, cot_b, grads_ref, out_ref):
    step = pl.program_id(0)
    block = left_a.shape[1]
    both = Q_WIDTH // block
    cut = Q_WIDTH % block
    lower = core_ref[0] == 0

    def store(value):
        out_ref[...] = value.astype(bf16).reshape(out_ref.shape)

    @pl.when(lower & (step < both))
    def _():
        store(dot_tn(left_a[...], drb_a[...]) + dot_tn(left_b[...], drb_b[...]))

    @pl.when(lower & (step == both))
    def _():
        top = dot_tn(left_a[:, :cut], drb_a[...]) + dot_tn(left_b[:, :cut], drb_b[...])
        rest = dot_tn(left_a[:, cut:], cot_a[...]) + dot_tn(left_b[:, cut:], cot_b[...])
        store(jnp.concatenate([top, rest], axis=0))

    @pl.when(core_ref[0] == 1)
    def _():
        store(dot_tn(left_a[...], cot_a[...]) + dot_tn(left_b[...], cot_b[...]))


def grad_out(core, lefts, wides, cots, grads):
    rows, width = cots[0].shape
    blocks = 4
    left = pl.BlockSpec((rows, blocks * OUT_ROWS), lambda i, core: (0, i))
    drb = pl.BlockSpec((rows, width), lambda i, core: (0, 2 * N_CHUNKS))
    cot = pl.BlockSpec((rows, width), lambda i, core: (0, 0))
    return pl.pallas_call(
        grad_out_kernel,
        grid_spec=pltpu.PrefetchScalarGridSpec(
            num_scalar_prefetch=1,
            grid=(grads.shape[0] // blocks,),
            in_specs=[left, left, drb, drb, cot, cot, pl.BlockSpec(memory_space=pl.ANY)],
            out_specs=pl.BlockSpec((blocks, OUT_ROWS, width), lambda i, core: (i, 0, 0)),
        ),
        out_shape=jax.ShapeDtypeStruct(grads.shape, bf16),
        input_output_aliases={7: 0},
        compiler_params=pltpu.CompilerParams(vmem_limit_bytes=VMEM_BYTES),
        name="grad_out",
    )(core, *lefts, *wides, *cots, grads)


def adam_step(master, first_old, second_old, gradient, rate):
    first_new = BETA_ONE * first_old + (1.0 - BETA_ONE) * gradient
    second_new = BETA_TWO * second_old + (1.0 - BETA_TWO) * gradient * gradient
    first_hat = first_new / (1.0 - BETA_ONE**STEP)
    second_hat = second_new / (1.0 - BETA_TWO**STEP)
    master_new = master - rate * (
        first_hat / (jnp.sqrt(second_hat) + ADAM_EPS) + WEIGHT_DECAY * master
    )
    return (first_new, second_new, master_new)


def gathered(x):
    return lax.all_gather(x, AXIS_CYZ, axis=0, tiled=True)


def shift(x, axis, step):
    n = SIZES[axis]
    return lax.ppermute(x, axis, [(i, (i + step) % n) for i in range(n)])


def first_moves(x):
    first, second = x[None, :HALF], x[None, HALF:]
    pair = jnp.concatenate([first, shift(first, "xh", 1)], axis=0)
    ring = jnp.concatenate([second] + [shift(second, "y", b) for b in (1, 2, 3)], axis=0)
    return pair, ring


def second_moves(pair, ring):
    one = jnp.concatenate([pair] + [shift(pair, "y", b) for b in (1, 2, 3)], axis=0)
    two = jnp.concatenate([ring, shift(ring, "xh", 1)], axis=0)
    return [one, two, shift(one, "core", 1), shift(two, "core", 1)]


def places_of_groups():
    xh, y, core = (lax.axis_index(name) for name in CTX)
    places = []
    for other in range(2):
        for side in range(2):
            for i in range(GROUP):
                b, a = (i // 2, i % 2) if side == 0 else (i % 4, i // 4)
                dev = (((xh + a) % 2) * 4 + (y - b) % 4) * 2 + (core + other) % 2
                places.append(dev if side == 0 else 31 - dev)
    return jnp.stack(places).astype(jnp.int32)


def sum_over_core(near, far):
    return (near.astype(f32) + shift(far, "core", 1).astype(f32)).astype(bf16)


def first_sums(plane):
    one = plane[:GROUP].reshape((4, 2) + plane.shape[1:])
    two = plane[GROUP:].reshape((2, 4) + plane.shape[1:])
    two = (two[0].astype(f32) + shift(two[1], "xh", 1).astype(f32)).astype(bf16)
    one = sum((shift(one[b], "y", -b).astype(f32) for b in (1, 2, 3)), one[0].astype(f32))
    return one.astype(bf16), two


def second_sums(one, two):
    two = sum((shift(two[b], "y", -b).astype(f32) for b in (1, 2, 3)), two[0].astype(f32))
    one = one[0].astype(f32) + shift(one[1], "xh", 1).astype(f32)
    return jnp.concatenate([one, two], axis=0)


def pick(v, i, n, axis):
    return lax.dynamic_index_in_dim(v, lax.rem(i, n), axis, keepdims=False)


def natural_of_permuted(x):
    tail = x.shape[1:]
    x = x.reshape((2, 4, 4, 2, 2) + tail)
    x = x.transpose((3, 1, 0, 4, 2) + tuple(range(5, 5 + len(tail))))
    return x.reshape((128,) + tail)


def owner_pairs():
    pairs = []
    for n in range(128):
        z = n % 4
        xl = (n // 4) % 2
        core = (n // 8) % 2
        y = (n // 16) % 4
        xh = n // 64
        pairs.append((n, (((core * 4 + y) * 4 + z) * 2 + xh) * 2 + xl))
    return pairs


def body(
    tokens,
    cotangent,
    segments,
    positions,
    pad_mask,
    w_in,
    w_out,
    gains,
    first_in,
    first_out,
    first_gains,
    second_in,
    second_out,
    second_gains,
):
    rows = tokens.shape[1]
    width = tokens.shape[2]
    span = segments.shape[1]
    half = rows // 2
    n_ctx = span // rows
    q_width = H_Q * HD
    kv_width = H_KV * HD
    attn_cols = q_width + 2 * kv_width
    owned = w_in.shape[0]
    owned_gains = gains.shape[0]

    n_x = 4
    low_in = w_in.astype(bf16)
    n_dev = width // owned

    own_head = jnp.concatenate(
        [
            low_in[:, :q_width].reshape(owned, H_Q, HD),
            jnp.repeat(low_in[:, q_width : q_width + kv_width].reshape(owned, H_KV, HD), 2, axis=1),
            jnp.repeat(low_in[:, q_width + kv_width : attn_cols].reshape(owned, H_KV, HD), 2, axis=1),
            jnp.broadcast_to(
                jnp.pad(gains.astype(bf16)[None, None], ((0, owned - 1), (0, 0), (0, HD - owned_gains))),
                (owned, H_Q, HD),
            ),
        ],
        axis=2,
    ).transpose(1, 0, 2)
    pair, ring = first_moves(tokens[0])
    head = lax.all_to_all(own_head, CTX, 0, 0, tiled=True)
    head = lax.all_gather(head, SHARD, axis=0, tiled=False)
    pairs = owner_pairs()
    own_out = lax.ppermute(w_out.astype(bf16), EVERY, [(p, n) for n, p in pairs])
    own_ffn = low_in[:, attn_cols:].reshape(owned, 2 * N_CHUNKS, CHUNK)
    own_ffn = own_ffn.transpose(1, 0, 2).reshape(2 * N_CHUNKS * owned, CHUNK)
    own_rest = jnp.concatenate([own_out, own_ffn], axis=0)
    own_rest = lax.all_gather(own_rest, AXIS_X, axis=0, tiled=False)
    segments, pad_mask, own_rest, pair, ring = lax.optimization_barrier(
        (segments, pad_mask, own_rest, pair, ring)
    )
    head = head.reshape((2, 4) + own_head.shape).transpose(2, 0, 1, 3, 4)
    gain_vals = head[:, :, :, 0, HEAD_COLS : HEAD_COLS + owned_gains].reshape(-1).astype(f32)
    w_head = head[..., :HEAD_COLS].reshape(width, HEAD_COLS)
    gain_one = gain_vals[:width]
    gain_two = gain_vals[width : 2 * width]
    gain_query = gain_vals[2 * width : 2 * width + HD].reshape(1, HD)
    gain_key = gain_vals[2 * width + HD :].reshape(1, HD)
    w_scaled = (w_head.astype(f32) * gain_one[:, None]).astype(bf16)

    n_out = w_out.shape[0]
    part_out = own_rest[:, :n_out].reshape(n_x * n_out, width)
    part_ffn = own_rest[:, n_out:].reshape(n_x, 2 * N_CHUNKS, owned, CHUNK).transpose(1, 0, 2, 3)
    part_ffn = part_ffn.reshape(2 * N_CHUNKS * CHUNK_ROWS, CHUNK)
    full = gathered(jnp.concatenate([part_out, part_ffn], axis=0)[None])

    order = natural_of_permuted(jnp.arange(width, dtype=jnp.int32).reshape(n_dev, owned)).reshape(-1)
    shuffle = (order[:, None] == jnp.arange(width, dtype=jnp.int32)[None, :]).astype(bf16)

    def natural(x):
        x = x.reshape(n_ctx, 2, half)
        return jnp.concatenate([x[:, 0], x[::-1, 1]], axis=0)

    docs = natural(segments[0])
    live = natural(pad_mask[0])
    at = jnp.arange(span, dtype=jnp.int32).reshape(2 * n_ctx, half)
    start = jnp.zeros_like(docs)
    for number in range(1, 14):
        before = jnp.sum((docs < number).astype(jnp.int32))
        start = jnp.where(docs == number, before, start)
    place_in = at - start
    lens = jnp.where(live == 1, place_in, 0)
    first_key = (at - lens).reshape(span // BQ, BQ)
    klo = jnp.stack(
        [jnp.min(first_key, axis=1) // BK, (jnp.max(first_key, axis=1) + BK - 1) // BK]
    )
    lens = lens.reshape(span // BQ, BQ)
    halves = jnp.arange(HD // 2, dtype=f32)
    inverse = ROPE_BASE ** (-2.0 * halves / HD)
    angle = place_in.reshape(span, 1).astype(f32) * inverse[None, :]
    cos_half = jnp.cos(angle)
    sin_half = jnp.sin(angle)
    cos = jnp.concatenate([cos_half, cos_half], axis=1)
    sin = jnp.concatenate([-sin_half, sin_half], axis=1)

    groups = second_moves(pair, ring)
    place = places_of_groups()
    q, k, v, query_raw, key_raw, inv = project(
        place, groups, w_scaled, cos, sin, gain_query, gain_key
    )
    o_send, o_nat, l_inv = attend(klo, q, k, v, lens, rows)
    mixed = lax.all_to_all(o_send, CTX, 0, 0, tiled=True)

    output, grad_residual, do_send, left, wide, gain_two_terms = middle(
        full, mixed, tokens[0], cotangent[0], gain_two.reshape(1, width), shuffle
    )
    core = lax.axis_index("core")
    lefts = (pick(left, core, 2, 0), shift(pick(left, core + 1, 2, 0), "core", 1))
    wides = (wide, shift(wide, "core", 1))
    cots = (cotangent[0], shift(cotangent[0], "core", 1))
    grads = grad_ffn(lefts, wides, full.shape[0] // 2)
    grads = grad_out(core.astype(jnp.int32).reshape(1), lefts, wides, cots, grads)
    do = lax.all_to_all(do_send, CTX, 0, 0, tiled=True)
    do, grads = lax.optimization_barrier((do, grads))
    grads = grads.reshape(-1, width)
    grads = lax.psum_scatter(grads, AXIS_YZ, scatter_dimension=0, tiled=True)

    head_grads = attend_back(klo, q, k, v, do, o_nat, l_inv, lens)
    da_near, da_far, dw_head, gain_qk = project_back(
        place, groups, head_grads, (query_raw, key_raw, inv), cos, sin, gain_query, gain_key, w_head
    )

    gain_one_grad = jnp.sum(dw_head * w_head.astype(f32), axis=1)
    grad_gains = jnp.concatenate([gain_one_grad, gain_two_terms[0], gain_qk[0], gain_qk[1]])
    grad_gains = jnp.pad(
        grad_gains.reshape(n_dev, 1, owned_gains), ((0, 0), (0, owned - 1), (0, HD - owned_gains))
    )
    dw_head = (dw_head * gain_one[:, None]).reshape(n_dev, owned, HEAD_COLS)
    dw_head = jnp.concatenate([dw_head, grad_gains], axis=2).astype(bf16)
    dw_head = dw_head.reshape(n_ctx, n_dev // n_ctx, owned, PAD_COLS).transpose(1, 0, 2, 3)
    plane = sum_over_core(da_near, da_far)
    dw_head, _, _ = lax.optimization_barrier((dw_head, grads, plane))
    dw_head = lax.psum_scatter(
        dw_head.reshape(-1, PAD_COLS), SHARD, scatter_dimension=0, tiled=True
    )
    grads, dw_head = lax.optimization_barrier((grads, dw_head))
    dw_head = lax.all_to_all(
        dw_head.reshape(n_ctx, owned, PAD_COLS), CTX, 0, 0, tiled=True
    ).astype(f32)
    owned_gain_grad = jnp.sum(dw_head[:, 0, HEAD_COLS : HEAD_COLS + owned_gains], axis=0)

    grad_a = second_sums(*first_sums(plane))
    inputs = tokens[0].astype(f32)
    input_grad = grad_residual + rms_back(inputs, gain_one, grad_a)[0]

    def columns(x):
        return x.transpose(1, 0, 2).reshape(owned, -1)

    def over_pair(x):
        return columns(jnp.sum(x.reshape(H_KV, 2, owned, HD), axis=1))

    out_part = grads[:OUT_ROWS].reshape(n_x, OUT_ROWS // n_x, width)
    ffn_part = grads[OUT_ROWS:].reshape(2 * N_CHUNKS, n_x, owned, CHUNK)
    ffn_part = ffn_part.transpose(1, 0, 2, 3).reshape(n_x, 2 * N_CHUNKS * owned, CHUNK)
    grads = jnp.concatenate([out_part, ffn_part], axis=1).reshape(-1, width)
    grads = lax.psum_scatter(grads, AXIS_X, scatter_dimension=0, tiled=True).astype(f32)
    owned_out = lax.ppermute(grads[: OUT_ROWS // n_x], EVERY, pairs)
    owned_ffn = grads[OUT_ROWS // n_x :].reshape(2 * N_CHUNKS, owned, CHUNK)
    owned_in = jnp.concatenate(
        [
            columns(dw_head[:, :, :HD]),
            over_pair(dw_head[:, :, HD : 2 * HD]),
            over_pair(dw_head[:, :, 2 * HD : HEAD_COLS]),
            columns(owned_ffn),
        ],
        axis=1,
    )
    new_first_in, new_second_in, new_master_in = adam_step(
        w_in, first_in, second_in, owned_in, RATE_MATRIX
    )
    new_first_out, new_second_out, new_master_out = adam_step(
        w_out, first_out, second_out, owned_out, RATE_MATRIX
    )
    new_first_gains, new_second_gains, new_master_gains = adam_step(
        gains, first_gains, second_gains, owned_gain_grad, RATE_GAIN
    )
    return (
        output[None],
        input_grad[None],
        new_first_in,
        new_first_out,
        new_first_gains,
        new_second_in,
        new_second_out,
        new_second_gains,
        new_master_in,
        new_master_out,
        new_master_gains,
        new_master_in.astype(bf16),
        new_master_out.astype(bf16),
    )


def solution(mesh):
    cut = Mesh(mesh.devices.reshape(tuple(SIZES[name] for name in EVERY)), EVERY)
    weights = P(EVERY, None)
    vector = P(EVERY)
    acts = P(SHARD, CTX, None)
    in_specs = (
        acts,
        acts,
        P(SHARD, None),
        P(SHARD, CTX),
        P(SHARD, None),
    ) + (weights, weights, vector) * 3
    out_specs = (acts, acts) + (weights, weights, vector) * 3 + (weights, weights)
    return jax.shard_map(body, mesh=cut, in_specs=in_specs, out_specs=out_specs, check_vma=False)
```

```python
import functools
import math

import jax
import jax.numpy as jnp
from jax import lax
from jax.experimental import pallas as pl
from jax.experimental.pallas import tpu as pltpu
from jax.sharding import Mesh
from jax.sharding import PartitionSpec as P

H_Q = 16
H_KV = 8
HD = 128
FF = 3072
STEP = 5

NORM_EPS = 1e-06
ROPE_BASE = 1000000.0
BETA_ONE = 0.5
BETA_TWO = 0.5
ADAM_EPS = 1e-08
WEIGHT_DECAY = 0.1
RATE_MATRIX = 0.03
RATE_GAIN = 0.25

CTX = ("xh", "y", "core")
SHARD = ("xl", "z")
EVERY = CTX + SHARD
AXIS_X = ("xh", "xl")
AXIS_YZ = ("y", "z")
AXIS_CYZ = ("core", "y", "z")
SIZES = {"xh": 2, "y": 4, "core": 2, "xl": 2, "z": 4}

LOG2_E = 1.4426950408889634
SCORE_SCALE = 1.0 / math.sqrt(HD)
BQ = 512
BK = 512
SUB = 256
VMEM_BYTES = 48 * 1024 * 1024
BIG_VMEM_BYTES = 60 * 1024 * 1024

bf16 = jnp.bfloat16
f32 = jnp.float32


def rms_norm(values, weight):
    return values * lax.rsqrt(jnp.mean(values * values, axis=-1, keepdims=True) + NORM_EPS) * weight


def rms_back(values, weight, upstream):
    inverse = lax.rsqrt(jnp.mean(values * values, axis=-1, keepdims=True) + NORM_EPS)
    normed = values * inverse
    scaled = upstream * weight
    grad_values = inverse * (scaled - normed * jnp.mean(scaled * normed, axis=-1, keepdims=True))
    return (grad_values, upstream * normed)


def dot_nt(a, b):
    return lax.dot_general(a, b, (((1,), (1,)), ((), ())), preferred_element_type=f32)


def dot_tn(a, b):
    return lax.dot_general(a, b, (((0,), (0,)), ((), ())), preferred_element_type=f32)


def dot_nn(a, b):
    return lax.dot_general(a, b, (((1,), (0,)), ((), ())), preferred_element_type=f32)


LAST_DOC = 13


def tables_kernel(docs_ref, live_ref, freq_ref, cos_ref, sin_ref, lens_ref):
    docs = docs_ref[...]
    shape = docs.shape
    start = jnp.zeros(shape, f32)
    for number in range(1, LAST_DOC + 1):
        before = jnp.sum(jnp.where(docs < number, 1.0, 0.0))
        start = jnp.where(docs == number, before, start)
    at = lax.broadcasted_iota(jnp.int32, shape, 0) * shape[1] + lax.broadcasted_iota(
        jnp.int32, shape, 1
    )
    within = at.astype(f32) - start
    lens_ref[...] = jnp.where(live_ref[...] == 1, within.astype(jnp.int32), 0)

    left = lax.broadcasted_iota(jnp.int32, (HD, HD), 1) < HD // 2
    for i in range(0, shape[0], 2):
        cols = [jnp.broadcast_to(within[i + n : i + n + 1, :], (HD, HD)).T for n in range(2)]
        angle = jnp.where(left, cols[0], cols[1]) * freq_ref[...]
        for ref, values, flip in ((cos_ref, jnp.cos(angle), False), (sin_ref, jnp.sin(angle), True)):
            turned = pltpu.roll(values, HD // 2, 1)
            for n in range(2):
                lower, upper = (values, turned) if n == 0 else (turned, values)
                ref[(i + n) * HD : (i + n + 1) * HD, :] = jnp.where(
                    left, -lower if flip else lower, upper
                )


def tables(docs, live, freq):
    span = docs.size
    table = jax.ShapeDtypeStruct((span, HD), f32)
    return pl.pallas_call(
        tables_kernel,
        in_specs=[vmem()] * 3,
        out_specs=[vmem()] * 3,
        out_shape=[table, table, jax.ShapeDtypeStruct(docs.shape, jnp.int32)],
        compiler_params=pltpu.CompilerParams(vmem_limit_bytes=VMEM_BYTES),
        cost_estimate=pl.CostEstimate(
            flops=100 * span * HD, bytes_accessed=3 * span * HD * 4, transcendentals=span * HD
        ),
        name="tables",
    )(docs, live, freq)


N_GROUPS = 4
GROUP = 8
HALF = 128
STEP_BLOCKS = 4
STEPS = GROUP // STEP_BLOCKS
HEAD_COLS = 3 * HD
PAD_COLS = 4 * HD


def block_spec(width, first, count):
    return pl.BlockSpec(
        (STEP_BLOCKS, HALF, width), lambda i, place: (jnp.clip(i - first, 0, count - 1), 0, 0)
    )


def group_specs(width):
    return [block_spec(width, k * STEPS, STEPS) for k in range(N_GROUPS)]


def fixed(shape):
    return pl.BlockSpec(shape, lambda i, place: (0,) * len(shape))


def rows_of(place_ref, step, i):
    return pl.ds(pl.multiple_of(place_ref[step * STEP_BLOCKS + i] * HALF, HALF), HALF)


def head_mean(x):
    return lax.dot_general(
        x.astype(bf16),
        jnp.full((HD, HD), 1.0 / HD, bf16),
        (((1,), (0,)), ((), ())),
        preferred_element_type=f32,
    )


def project_kernel(
    place_ref, x0, x1, x2, x3, w_ref, cos_ref, sin_ref, gq_ref, gk_ref,
    q_ref, k_ref, v_ref, qraw_ref, kraw_ref, inv_ref,
):
    step = pl.program_id(0)

    def run(x):
        wide = x.astype(f32)
        inverse = lax.rsqrt(jnp.mean(wide * wide, axis=-1, keepdims=True) + NORM_EPS)
        prod = dot_nn(x, w_ref[...]) * inverse
        for i in range(STEP_BLOCKS):
            at = rows_of(place_ref, step, i)
            part = slice(i * HALF, (i + 1) * HALF)
            cos = cos_ref[at, :]
            sin = sin_ref[at, :]

            def roped(raw, gain, cos=cos, sin=sin):
                normed = raw * lax.rsqrt(head_mean(raw * raw) + NORM_EPS) * gain
                return normed * cos + pltpu.roll(normed, HD // 2, 1) * sin

            query = prod[part, :HD]
            key = prod[part, HD : 2 * HD]
            inv_ref[at, :] = jnp.broadcast_to(inverse[part], (HALF, HD)).astype(bf16)
            qraw_ref[at, :] = query.astype(bf16)
            kraw_ref[at, :] = key.astype(bf16)
            q_ref[at, :] = (roped(query, gq_ref[...]) * (SCORE_SCALE * LOG2_E)).astype(bf16)
            k_ref[at, :] = roped(key, gk_ref[...]).astype(bf16)
            v_ref[at, :] = prod[part, 2 * HD :].astype(bf16)

    for k, x_ref in enumerate((x0, x1, x2, x3)):

        @pl.when(step // STEPS == k)
        def _(x_ref=x_ref):
            run(x_ref[...].reshape(STEP_BLOCKS * HALF, x_ref.shape[2]))


def project(place, groups, w, cos, sin, gq, gk):
    width = w.shape[0]
    span = cos.shape[0]
    low = jax.ShapeDtypeStruct((span, HD), bf16)
    whole = fixed((span, HD))
    return pl.pallas_call(
        project_kernel,
        grid_spec=pltpu.PrefetchScalarGridSpec(
            num_scalar_prefetch=1,
            grid=(N_GROUPS * STEPS,),
            in_specs=group_specs(width)
            + [fixed((width, HEAD_COLS)), whole, whole, fixed((1, HD)), fixed((1, HD))],
            out_specs=[whole] * 6,
        ),
        out_shape=[low] * 6,
        compiler_params=pltpu.CompilerParams(vmem_limit_bytes=VMEM_BYTES),
        name="project",
    )(place, *groups, w, cos, sin, gq, gk)


def project_back_kernel(
    place_ref, x0, x1, x2, x3, dq_ref, dk_ref, dv_ref, qraw_ref, kraw_ref, inv_ref, cos_ref, sin_ref,
    gq_ref, gk_ref, w_ref, near_ref, far_ref, dw_ref, dg_ref, grads, scaled,
):
    step = pl.program_id(0)

    @pl.when(step == 0)
    def _():
        dw_ref[...] = jnp.zeros_like(dw_ref)
        dg_ref[...] = jnp.zeros_like(dg_ref)

    def run(x, da_ref):
        q_sum = jnp.zeros((1, HD), f32)
        k_sum = jnp.zeros((1, HD), f32)
        for i in range(STEP_BLOCKS):
            at = rows_of(place_ref, step, i)
            part = slice(i * HALF, (i + 1) * HALF)
            cos = cos_ref[at, :]
            sin = sin_ref[at, :]

            def back(raw, gain, grad, cos=cos, sin=sin):
                unrot = grad * cos + pltpu.roll(grad * sin, HD // 2, 1)
                inv_rms = lax.rsqrt(head_mean(raw * raw) + NORM_EPS)
                normed = raw * inv_rms
                scaled_up = unrot * gain
                grad = inv_rms * (scaled_up - normed * head_mean(scaled_up * normed))
                return grad, unrot * normed

            grad_q, q_terms = back(qraw_ref[at, :].astype(f32), gq_ref[...], dq_ref[at, :])
            grad_k, k_terms = back(kraw_ref[at, :].astype(f32), gk_ref[...], dk_ref[at, :])
            inverse = inv_ref[at, :].astype(f32)
            for c, grad in enumerate((grad_q, grad_k, dv_ref[at, :])):
                grads[part, c * HD : (c + 1) * HD] = grad.astype(bf16)
                scaled[part, c * HD : (c + 1) * HD] = (grad * inverse).astype(bf16)
            q_sum = q_sum + jnp.sum(q_terms, axis=0, keepdims=True)
            k_sum = k_sum + jnp.sum(k_terms, axis=0, keepdims=True)
        da_ref[...] = dot_nt(grads[...], w_ref[...]).astype(bf16).reshape(da_ref.shape)
        dw_ref[...] += dot_tn(x, scaled[...])
        dg_ref[0:1, :] += q_sum
        dg_ref[1:2, :] += k_sum

    for k, x_ref in enumerate((x0, x1, x2, x3)):

        @pl.when(step // STEPS == k)
        def _(k=k, x_ref=x_ref):
            da_ref = near_ref if k < N_GROUPS // 2 else far_ref
            run(x_ref[...].reshape(STEP_BLOCKS * HALF, x_ref.shape[2]), da_ref)


def project_back(place, groups, grads, raws, cos, sin, gq, gk, w):
    width = w.shape[0]
    span = cos.shape[0]
    whole = fixed((span, HD))
    n_half = N_GROUPS // 2
    da = jax.ShapeDtypeStruct((n_half * GROUP, HALF, width), bf16)
    return pl.pallas_call(
        project_back_kernel,
        grid_spec=pltpu.PrefetchScalarGridSpec(
            num_scalar_prefetch=1,
            grid=(N_GROUPS * STEPS,),
            in_specs=group_specs(width)
            + [whole] * 8
            + [fixed((1, HD)), fixed((1, HD)), fixed((width, HEAD_COLS))],
            out_specs=[
                block_spec(width, 0, n_half * STEPS),
                block_spec(width, n_half * STEPS, n_half * STEPS),
                fixed((width, HEAD_COLS)),
                fixed((8, HD)),
            ],
            scratch_shapes=[
                pltpu.VMEM((STEP_BLOCKS * HALF, HEAD_COLS), bf16),
                pltpu.VMEM((STEP_BLOCKS * HALF, HEAD_COLS), bf16),
            ],
        ),
        out_shape=[
            da,
            da,
            jax.ShapeDtypeStruct((width, HEAD_COLS), f32),
            jax.ShapeDtypeStruct((8, HD), f32),
        ],
        compiler_params=pltpu.CompilerParams(vmem_limit_bytes=BIG_VMEM_BYTES),
        name="project_back",
    )(place, *groups, *grads, *raws, cos, sin, gq, gk, w)


def dealt_slot(place, n_dev):
    if place < n_dev:
        return place, 0
    return 2 * n_dev - 1 - place, 1


def key_mask(len_row, offset):
    ahead = (
        lax.broadcasted_iota(jnp.int32, (SUB, BQ), 1)
        - lax.broadcasted_iota(jnp.int32, (SUB, BQ), 0)
        + offset
    )
    return (ahead >= 0) & (ahead <= len_row)


def key_loops(bounds_ref, qb, q_at, tile):
    low = bounds_ref[0, qb]
    high = (q_at + BQ - 1) // BK + 1
    first = jnp.minimum(bounds_ref[1, qb], high)
    last = jnp.maximum((q_at + 1) // BK, first)

    def run(masked):
        def step(kb, _):
            tile(kb, masked)
            return 0

        return step

    lax.fori_loop(low, first, run(True), 0)
    lax.fori_loop(first, last, run(False), 0)
    lax.fori_loop(last, high, run(True), 0)


def attend_kernel(
    bounds_ref, q_ref, k_ref, v_ref, len_ref, osend_ref, onat_ref, linv_ref, acc, total
):
    n_dev, rows, _ = osend_ref.shape
    half = rows // 2
    span = q_ref.shape[0]
    def q_step(qb, _):
        q_at = pl.multiple_of(qb * BQ, BQ)
        q_blk = q_ref[pl.ds(q_at, BQ), :]
        len_row = len_ref[pl.ds(qb, 1), :]
        acc[...] = jnp.zeros_like(acc)
        total[...] = jnp.zeros_like(total)

        def tile(kb, masked):
            mixed = None
            summed = None
            for c in range(BK // SUB):
                k_at = pl.multiple_of(kb * BK + c * SUB, SUB)
                p = jnp.exp2(dot_nt(k_ref[pl.ds(k_at, SUB), :], q_blk))
                if masked:
                    p = jnp.where(key_mask(len_row, q_at - k_at), p, 0.0)
                part = jnp.sum(p.reshape(SUB // 8, 8, BQ), axis=0)
                more = dot_tn(v_ref[pl.ds(k_at, SUB), :], p.astype(bf16))
                summed = part if summed is None else summed + part
                mixed = more if mixed is None else mixed + more
            acc[...] += mixed
            total[...] += summed

        key_loops(bounds_ref, qb, q_at, tile)
        inverse = 1.0 / jnp.sum(total[...], axis=0, keepdims=True)
        linv_ref[pl.ds(qb, 1), :] = inverse
        onat_ref[pl.ds(q_at, BQ), :] = (acc[...] * inverse).T
        return 0

    lax.fori_loop(0, span // BQ, q_step, 0)
    for place in range(2 * n_dev):
        dev, side = dealt_slot(place, n_dev)
        osend_ref[dev, side * half : (side + 1) * half, :] = onat_ref[
            place * half : (place + 1) * half, :
        ].astype(bf16)


def vmem():
    return pl.BlockSpec(memory_space=pltpu.VMEM)


def attend(klo, q, k, v, lens, rows):
    span = q.shape[0]
    return pl.pallas_call(
        attend_kernel,
        in_specs=[pl.BlockSpec(memory_space=pltpu.SMEM)] + [vmem()] * 4,
        out_specs=[vmem(), vmem(), vmem()],
        out_shape=[
            jax.ShapeDtypeStruct((span // rows, rows, HD), bf16),
            jax.ShapeDtypeStruct((span, HD), f32),
            jax.ShapeDtypeStruct((span // BQ, BQ), f32),
        ],
        scratch_shapes=[
            pltpu.VMEM((HD, BQ), f32),
            pltpu.VMEM((8, BQ), f32),
        ],
        compiler_params=pltpu.CompilerParams(vmem_limit_bytes=VMEM_BYTES),
        name="attend",
    )(klo, q, k, v, lens)


def attend_back_kernel(
    bounds_ref, q_ref, k_ref, v_ref, do_ref, onat_ref, linv_ref, len_ref, dq, dk, dv, don, acc
):
    n_dev, rows, _ = do_ref.shape
    half = rows // 2
    span = q_ref.shape[0]
    for place in range(2 * n_dev):
        dev, side = dealt_slot(place, n_dev)
        to = slice(place * half, (place + 1) * half)
        don[to, :] = do_ref[dev, side * half : (side + 1) * half, :]
    dk[...] = jnp.zeros_like(dk)
    dv[...] = jnp.zeros_like(dv)

    def q_step(qb, _):
        q_at = pl.multiple_of(qb * BQ, BQ)
        q_blk = q_ref[pl.ds(q_at, BQ), :]
        do_blk = don[pl.ds(q_at, BQ), :]
        len_row = len_ref[pl.ds(qb, 1), :]
        inverse = linv_ref[pl.ds(qb, 1), :]
        mixed = (do_blk.astype(f32) * onat_ref[pl.ds(q_at, BQ), :]).T
        delta = jnp.sum(mixed, axis=0, keepdims=True)
        acc[...] = jnp.zeros_like(acc)

        def tile(kb, masked):
            total = None
            for c in range(BK // SUB):
                k_at = pl.multiple_of(kb * BK + c * SUB, SUB)
                here = pl.ds(k_at, SUB)
                p = jnp.exp2(dot_nt(k_ref[here, :], q_blk)) * inverse
                if masked:
                    p = jnp.where(key_mask(len_row, q_at - k_at), p, 0.0)
                dp = dot_nt(v_ref[here, :], do_blk)
                ds = (p * (dp - delta)).astype(bf16)
                dv[here, :] += dot_nn(p.astype(bf16), do_blk)
                dk[here, :] += dot_nn(ds, q_blk)
                more = dot_tn(k_ref[here, :], ds)
                total = more if total is None else total + more
            acc[...] += total

        key_loops(bounds_ref, qb, q_at, tile)
        dq[pl.ds(q_at, BQ), :] = (acc[...] * SCORE_SCALE).T
        return 0

    lax.fori_loop(0, span // BQ, q_step, 0)
    dk[...] = dk[...] * (1.0 / LOG2_E)


def attend_back(klo, q, k, v, do, onat, linv, lens):
    span = q.shape[0]
    return pl.pallas_call(
        attend_back_kernel,
        in_specs=[pl.BlockSpec(memory_space=pltpu.SMEM)] + [vmem()] * 7,
        out_specs=[vmem()] * 3,
        out_shape=[jax.ShapeDtypeStruct((span, HD), f32)] * 3,
        scratch_shapes=[
            pltpu.VMEM((span, HD), bf16),
            pltpu.VMEM((HD, BQ), f32),
        ],
        compiler_params=pltpu.CompilerParams(vmem_limit_bytes=VMEM_BYTES),
        name="attend_back",
    )(klo, q, k, v, do, onat, linv, lens)


OUT_ROWS = 160
CHUNK_ROWS = 32
N_CHUNKS = 3
CHUNK = FF // N_CHUNKS
Q_WIDTH = H_Q * HD
HALF_OUT = (Q_WIDTH + FF) // 2
HALF_MID = 512
LEFT = HALF_OUT + HALF_MID


def middle_kernel(
    full_ref, mixed_ref, tok_ref, cot_ref, gain_ref, shuffle_ref, gate_ref, up_ref,
    out_ref, dres_ref, dob_ref, left_ref, wide_ref, dgain_ref,
    w_out, resid, mid_low, grad_mid, sems,
):
    step = pl.program_id(0)
    width = tok_ref.shape[1]

    def fetch(i):
        return pltpu.make_async_copy(
            full_ref.at[i, pl.ds(0, OUT_ROWS), :],
            w_out.at[pl.ds(i * OUT_ROWS, OUT_ROWS), :],
            sems.at[i],
        )

    n_fetch = full_ref.shape[0]
    n_first = -(-Q_WIDTH // OUT_ROWS)

    @pl.when(step == 0)
    def _():
        for i in range(n_fetch):
            fetch(i).start()
        for h in range(H_Q):
            left_ref[0, :, h * HD : (h + 1) * HD] = mixed_ref[h]
        for i in range(n_first):
            fetch(i).wait()
        residual = tok_ref[...].astype(f32) + dot_nn(
            left_ref[0, :, :Q_WIDTH], w_out[:Q_WIDTH, :]
        )
        resid[...] = residual
        out_ref[...] = residual
        normed = rms_norm(residual, gain_ref[...]).astype(bf16)
        low = dot_nn(normed, shuffle_ref[...]).astype(bf16)
        mid_low[...] = low
        for side in range(2):
            left_ref[side, :, HALF_OUT:] = low[:, side * HALF_MID : (side + 1) * HALF_MID]
        grad_mid[...] = jnp.zeros_like(grad_mid)
        for i in range(n_first, n_fetch):
            fetch(i).wait()

    for f in range(N_CHUNKS):

        @pl.when(step == f + 1)
        def _(f=f):
            at = Q_WIDTH + f * CHUNK
            gate_w = gate_ref[...].reshape(width, CHUNK)
            up_w = up_ref[...].reshape(width, CHUNK)
            gate = dot_nn(mid_low[...], gate_w)
            up = dot_nn(mid_low[...], up_w)
            sigmoid_gate = 1.0 / (1.0 + jnp.exp(-gate))
            activated = gate * sigmoid_gate
            hidden = (activated * up).astype(bf16)
            cut = min(max(HALF_OUT - at, 0), CHUNK)
            if cut > 0:
                left_ref[0, :, at : at + cut] = hidden[:, :cut]
            if cut < CHUNK:
                left_ref[1, :, at + cut - HALF_OUT : at + CHUNK - HALF_OUT] = hidden[:, cut:]
            down_w = w_out[at : at + CHUNK, :]
            out_ref[...] += dot_nn(hidden, down_w)
            grad_hidden = dot_nt(cot_ref[...], down_w)
            grad_up = (grad_hidden * activated).astype(bf16)
            grad_gate = (
                grad_hidden * up * sigmoid_gate * (1.0 + gate * (1.0 - sigmoid_gate))
            ).astype(bf16)
            wide_ref[:, f * CHUNK : (f + 1) * CHUNK] = grad_gate
            wide_ref[:, FF + f * CHUNK : FF + (f + 1) * CHUNK] = grad_up
            grad_mid[...] += dot_nt(grad_gate, gate_w) + dot_nt(grad_up, up_w)

    @pl.when(step == N_CHUNKS + 1)
    def _():
        grad = dot_nt(grad_mid[...].astype(bf16), shuffle_ref[...])
        part, terms = rms_back(resid[...], gain_ref[...], grad)
        dgain_ref[...] = jnp.sum(terms, axis=0, keepdims=True)
        dres = cot_ref[...].astype(f32) + part
        dres_ref[...] = dres
        low = dres.astype(bf16)
        wide_ref[:, 2 * FF :] = low
        for c in range(4):
            piece = dot_nt(low, w_out[c * 4 * HD : (c + 1) * 4 * HD, :]).astype(bf16)
            for h in range(4):
                dob_ref[4 * c + h] = piece[:, h * HD : (h + 1) * HD]


def middle(full, mixed, tok, cot, gain, shuffle):
    rows, width = tok.shape
    n_blocks = full.shape[0]
    first = OUT_ROWS // CHUNK_ROWS

    def chunk_of(i):
        return jnp.clip(i - 1, 0, N_CHUNKS - 1)

    def whole(shape):
        return pl.BlockSpec(shape, lambda i: (0,) * len(shape))

    chunk = (n_blocks, CHUNK_ROWS, CHUNK)
    return pl.pallas_call(
        middle_kernel,
        grid=(N_CHUNKS + 2,),
        in_specs=[
            pl.BlockSpec(memory_space=pl.ANY),
            whole((H_Q, rows, HD)),
            whole((rows, width)),
            whole((rows, width)),
            whole((1, width)),
            whole((width, width)),
            pl.BlockSpec(chunk, lambda i: (0, first + chunk_of(i), 0)),
            pl.BlockSpec(chunk, lambda i: (0, first + N_CHUNKS + chunk_of(i), 0)),
        ],
        out_specs=[
            whole((rows, width)),
            whole((rows, width)),
            whole((H_Q, rows, HD)),
            whole((2, rows, LEFT)),
            whole((rows, 2 * FF + width)),
            whole((1, width)),
        ],
        out_shape=[
            jax.ShapeDtypeStruct((rows, width), f32),
            jax.ShapeDtypeStruct((rows, width), f32),
            jax.ShapeDtypeStruct((H_Q, rows, HD), bf16),
            jax.ShapeDtypeStruct((2, rows, LEFT), bf16),
            jax.ShapeDtypeStruct((rows, 2 * FF + width), bf16),
            jax.ShapeDtypeStruct((1, width), f32),
        ],
        scratch_shapes=[
            pltpu.VMEM((Q_WIDTH + FF, width), bf16),
            pltpu.VMEM((rows, width), f32),
            pltpu.VMEM((rows, width), bf16),
            pltpu.VMEM((rows, width), f32),
            pltpu.SemaphoreType.DMA((n_blocks,)),
        ],
        compiler_params=pltpu.CompilerParams(vmem_limit_bytes=BIG_VMEM_BYTES),
        name="middle",
    )(full, mixed, tok, cot, gain, shuffle, full, full)


def grad_ffn_kernel(left_a, left_b, right_a, right_b, out_ref):
    total = dot_tn(left_a[...], right_a[...]) + dot_tn(left_b[...], right_b[...])
    out_ref[...] = total.astype(bf16).reshape(out_ref.shape)


def grad_ffn(lefts, wides, n_blocks):
    rows = lefts[0].shape[0]
    left = pl.BlockSpec((rows, HALF_MID), lambda i: (0, HALF_OUT // HALF_MID))
    right = pl.BlockSpec((rows, CHUNK), lambda i: (0, i))
    first = OUT_ROWS // CHUNK_ROWS
    height = OUT_ROWS + 2 * N_CHUNKS * CHUNK_ROWS
    return pl.pallas_call(
        grad_ffn_kernel,
        grid=(2 * N_CHUNKS,),
        in_specs=[left, left, right, right],
        out_specs=pl.BlockSpec((n_blocks, CHUNK_ROWS, CHUNK), lambda i: (0, first + i, 0)),
        out_shape=jax.ShapeDtypeStruct((n_blocks, height, CHUNK), bf16),
        compiler_params=pltpu.CompilerParams(vmem_limit_bytes=VMEM_BYTES),
        name="grad_ffn",
    )(*lefts, *wides)


def grad_out_kernel(core_ref, left_a, left_b, drb_a, drb_b, cot_a, cot_b, grads_ref, out_ref):
    step = pl.program_id(0)
    block = left_a.shape[1]
    both = Q_WIDTH // block
    cut = Q_WIDTH % block
    lower = core_ref[0] == 0

    def store(value):
        out_ref[...] = value.astype(bf16).reshape(out_ref.shape)

    @pl.when(lower & (step < both))
    def _():
        store(dot_tn(left_a[...], drb_a[...]) + dot_tn(left_b[...], drb_b[...]))

    @pl.when(lower & (step == both))
    def _():
        top = dot_tn(left_a[:, :cut], drb_a[...]) + dot_tn(left_b[:, :cut], drb_b[...])
        rest = dot_tn(left_a[:, cut:], cot_a[...]) + dot_tn(left_b[:, cut:], cot_b[...])
        store(jnp.concatenate([top, rest], axis=0))

    @pl.when(core_ref[0] == 1)
    def _():
        store(dot_tn(left_a[...], cot_a[...]) + dot_tn(left_b[...], cot_b[...]))


def grad_out(core, lefts, wides, cots, grads):
    rows, width = cots[0].shape
    blocks = 4
    left = pl.BlockSpec((rows, blocks * OUT_ROWS), lambda i, core: (0, i))
    drb = pl.BlockSpec((rows, width), lambda i, core: (0, 2 * N_CHUNKS))
    cot = pl.BlockSpec((rows, width), lambda i, core: (0, 0))
    return pl.pallas_call(
        grad_out_kernel,
        grid_spec=pltpu.PrefetchScalarGridSpec(
            num_scalar_prefetch=1,
            grid=(grads.shape[0] // blocks,),
            in_specs=[left, left, drb, drb, cot, cot, pl.BlockSpec(memory_space=pl.ANY)],
            out_specs=pl.BlockSpec((blocks, OUT_ROWS, width), lambda i, core: (i, 0, 0)),
        ),
        out_shape=jax.ShapeDtypeStruct(grads.shape, bf16),
        input_output_aliases={7: 0},
        compiler_params=pltpu.CompilerParams(vmem_limit_bytes=VMEM_BYTES),
        name="grad_out",
    )(core, *lefts, *wides, *cots, grads)


def adam_step(master, first_old, second_old, gradient, rate):
    first_new = BETA_ONE * first_old + (1.0 - BETA_ONE) * gradient
    second_new = BETA_TWO * second_old + (1.0 - BETA_TWO) * gradient * gradient
    first_hat = first_new / (1.0 - BETA_ONE**STEP)
    second_hat = second_new / (1.0 - BETA_TWO**STEP)
    master_new = master - rate * (
        first_hat / (jnp.sqrt(second_hat) + ADAM_EPS) + WEIGHT_DECAY * master
    )
    return (first_new, second_new, master_new)


def gathered(x):
    return lax.all_gather(x, AXIS_CYZ, axis=0, tiled=True)


def shift(x, axis, step):
    n = SIZES[axis]
    return lax.ppermute(x, axis, [(i, (i + step) % n) for i in range(n)])


def first_moves(x):
    first, second = x[None, :HALF], x[None, HALF:]
    pair = jnp.concatenate([first, shift(first, "xh", 1)], axis=0)
    ring = jnp.concatenate([second] + [shift(second, "y", b) for b in (1, 2, 3)], axis=0)
    return pair, ring


def second_moves(pair, ring, after):
    one = jnp.concatenate([pair] + [shift(pair, "y", b) for b in (1, 2, 3)], axis=0)
    two = jnp.concatenate([ring, shift(ring, "xh", 1)], axis=0)
    one, two, _ = lax.optimization_barrier((one, two, after))
    return [one, two, shift(one, "core", 1), shift(two, "core", 1)]


def places_of_groups():
    xh, y, core = (lax.axis_index(name) for name in CTX)
    places = []
    for other in range(2):
        for side in range(2):
            for i in range(GROUP):
                b, a = (i // 2, i % 2) if side == 0 else (i % 4, i // 4)
                dev = (((xh + a) % 2) * 4 + (y - b) % 4) * 2 + (core + other) % 2
                places.append(dev if side == 0 else 31 - dev)
    return jnp.stack(places).astype(jnp.int32)


def sum_over_core(near, far):
    return (near.astype(f32) + shift(far, "core", 1).astype(f32)).astype(bf16)


def first_sums(plane):
    one = plane[:GROUP].reshape((4, 2) + plane.shape[1:])
    two = plane[GROUP:].reshape((2, 4) + plane.shape[1:])
    two = (two[0].astype(f32) + shift(two[1], "xh", 1).astype(f32)).astype(bf16)
    one = sum((shift(one[b], "y", -b).astype(f32) for b in (1, 2, 3)), one[0].astype(f32))
    return one.astype(bf16), two


def second_sums(one, two):
    two = sum((shift(two[b], "y", -b).astype(f32) for b in (1, 2, 3)), two[0].astype(f32))
    one = one[0].astype(f32) + shift(one[1], "xh", 1).astype(f32)
    return jnp.concatenate([one, two], axis=0)


def pick(v, i, n, axis):
    return lax.dynamic_index_in_dim(v, lax.rem(i, n), axis, keepdims=False)


def natural_of_permuted(x):
    tail = x.shape[1:]
    x = x.reshape((2, 4, 4, 2, 2) + tail)
    x = x.transpose((3, 1, 0, 4, 2) + tuple(range(5, 5 + len(tail))))
    return x.reshape((128,) + tail)


def owner_pairs():
    pairs = []
    for n in range(128):
        z = n % 4
        xl = (n // 4) % 2
        core = (n // 8) % 2
        y = (n // 16) % 4
        xh = n // 64
        pairs.append((n, (((core * 4 + y) * 4 + z) * 2 + xh) * 2 + xl))
    return pairs


def body(
    tokens,
    cotangent,
    segments,
    positions,
    pad_mask,
    w_in,
    w_out,
    gains,
    first_in,
    first_out,
    first_gains,
    second_in,
    second_out,
    second_gains,
):
    rows = tokens.shape[1]
    width = tokens.shape[2]
    span = segments.shape[1]
    half = rows // 2
    n_ctx = span // rows
    q_width = H_Q * HD
    kv_width = H_KV * HD
    attn_cols = q_width + 2 * kv_width
    owned = w_in.shape[0]
    owned_gains = gains.shape[0]

    n_x = 4
    low_in = w_in.astype(bf16)
    n_dev = width // owned

    own_head = jnp.concatenate(
        [
            low_in[:, :q_width].reshape(owned, H_Q, HD),
            jnp.repeat(low_in[:, q_width : q_width + kv_width].reshape(owned, H_KV, HD), 2, axis=1),
            jnp.repeat(low_in[:, q_width + kv_width : attn_cols].reshape(owned, H_KV, HD), 2, axis=1),
            jnp.broadcast_to(
                jnp.pad(gains.astype(bf16)[None, None], ((0, owned - 1), (0, 0), (0, HD - owned_gains))),
                (owned, H_Q, HD),
            ),
        ],
        axis=2,
    ).transpose(1, 0, 2)
    pair, ring = first_moves(tokens[0])
    head = lax.all_to_all(own_head, CTX, 0, 0, tiled=True)
    head = lax.all_gather(head, SHARD, axis=0, tiled=False)
    pairs = owner_pairs()
    own_out = lax.ppermute(w_out.astype(bf16), EVERY, [(p, n) for n, p in pairs])
    own_ffn = low_in[:, attn_cols:].reshape(owned, 2 * N_CHUNKS, CHUNK)
    own_ffn = own_ffn.transpose(1, 0, 2).reshape(2 * N_CHUNKS * owned, CHUNK)
    own_rest = jnp.concatenate([own_out, own_ffn], axis=0)
    own_rest = lax.all_gather(own_rest, AXIS_X, axis=0, tiled=False)
    segments, pad_mask, own_rest, pair, ring = lax.optimization_barrier(
        (segments, pad_mask, own_rest, pair, ring)
    )
    head = head.reshape((2, 4) + own_head.shape).transpose(2, 0, 1, 3, 4)
    gain_vals = head[:, :, :, 0, HEAD_COLS : HEAD_COLS + owned_gains].reshape(-1).astype(f32)
    w_head = head[..., :HEAD_COLS].reshape(width, HEAD_COLS)
    gain_one = gain_vals[:width]
    gain_two = gain_vals[width : 2 * width]
    gain_query = gain_vals[2 * width : 2 * width + HD].reshape(1, HD)
    gain_key = gain_vals[2 * width + HD :].reshape(1, HD)
    w_scaled = (w_head.astype(f32) * gain_one[:, None]).astype(bf16)

    n_out = w_out.shape[0]
    part_out = own_rest[:, :n_out].reshape(n_x * n_out, width)
    part_ffn = own_rest[:, n_out:].reshape(n_x, 2 * N_CHUNKS, owned, CHUNK).transpose(1, 0, 2, 3)
    part_ffn = part_ffn.reshape(2 * N_CHUNKS * CHUNK_ROWS, CHUNK)
    full = gathered(jnp.concatenate([part_out, part_ffn], axis=0)[None])

    order = natural_of_permuted(jnp.arange(width, dtype=jnp.int32).reshape(n_dev, owned)).reshape(-1)
    shuffle = (order[:, None] == jnp.arange(width, dtype=jnp.int32)[None, :]).astype(bf16)

    def natural(x):
        x = x.reshape(n_ctx, 2, half)
        return jnp.concatenate([x[:, 0], x[::-1, 1]], axis=0)

    halves = jnp.arange(HD // 2, dtype=f32)
    inverse = ROPE_BASE ** (-2.0 * halves / HD)
    cos, sin, lens = tables(
        natural(segments[0]), natural(pad_mask[0]), jnp.concatenate([inverse, inverse])[None]
    )
    first_key = (jnp.arange(span, dtype=jnp.int32).reshape(lens.shape) - lens).reshape(span // BQ, BQ)
    klo = jnp.stack(
        [jnp.min(first_key, axis=1) // BK, (jnp.max(first_key, axis=1) + BK - 1) // BK]
    )
    lens = lens.reshape(span // BQ, BQ)

    groups = second_moves(pair, ring, (cos, klo, lens))
    place = places_of_groups()
    q, k, v, query_raw, key_raw, inv = project(
        place, groups, w_scaled, cos, sin, gain_query, gain_key
    )
    o_send, o_nat, l_inv = attend(klo, q, k, v, lens, rows)
    mixed = lax.all_to_all(o_send, CTX, 0, 0, tiled=True)

    output, grad_residual, do_send, left, wide, gain_two_terms = middle(
        full, mixed, tokens[0], cotangent[0], gain_two.reshape(1, width), shuffle
    )
    core = lax.axis_index("core")
    lefts = (pick(left, core, 2, 0), shift(pick(left, core + 1, 2, 0), "core", 1))
    wides = (wide, shift(wide, "core", 1))
    cots = (cotangent[0], shift(cotangent[0], "core", 1))
    grads = grad_ffn(lefts, wides, full.shape[0] // 2)
    grads = grad_out(core.astype(jnp.int32).reshape(1), lefts, wides, cots, grads)
    do = lax.all_to_all(do_send, CTX, 0, 0, tiled=True)
    do, grads = lax.optimization_barrier((do, grads))
    grads = grads.reshape(-1, width)
    grads = lax.psum_scatter(grads, AXIS_YZ, scatter_dimension=0, tiled=True)

    head_grads = attend_back(klo, q, k, v, do, o_nat, l_inv, lens)
    da_near, da_far, dw_head, gain_qk = project_back(
        place, groups, head_grads, (query_raw, key_raw, inv), cos, sin, gain_query, gain_key, w_head
    )

    gain_one_grad = jnp.sum(dw_head * w_head.astype(f32), axis=1)
    grad_gains = jnp.concatenate([gain_one_grad, gain_two_terms[0], gain_qk[0], gain_qk[1]])
    grad_gains = jnp.pad(
        grad_gains.reshape(n_dev, 1, owned_gains), ((0, 0), (0, owned - 1), (0, HD - owned_gains))
    )
    dw_head = (dw_head * gain_one[:, None]).reshape(n_dev, owned, HEAD_COLS)
    dw_head = jnp.concatenate([dw_head, grad_gains], axis=2).astype(bf16)
    dw_head = dw_head.reshape(n_ctx, n_dev // n_ctx, owned, PAD_COLS).transpose(1, 0, 2, 3)
    plane = sum_over_core(da_near, da_far)
    dw_head, _ = lax.optimization_barrier((dw_head, plane))
    dw_head = lax.all_to_all(dw_head, SHARD, 0, 0, tiled=True)
    dw_head = jnp.sum(dw_head.astype(f32), axis=0).astype(bf16)
    one, two = first_sums(plane)
    dw_head, _, _ = lax.optimization_barrier((dw_head, one, two))
    dw_head = lax.all_to_all(dw_head, CTX, 0, 0, tiled=True).astype(f32)
    owned_gain_grad = jnp.sum(dw_head[:, 0, HEAD_COLS : HEAD_COLS + owned_gains], axis=0)

    grad_a = second_sums(one, two)
    inputs = tokens[0].astype(f32)
    input_grad = grad_residual + rms_back(inputs, gain_one, grad_a)[0]

    def columns(x):
        return x.transpose(1, 0, 2).reshape(owned, -1)

    def over_pair(x):
        return columns(jnp.sum(x.reshape(H_KV, 2, owned, HD), axis=1))

    out_part = grads[:OUT_ROWS].reshape(n_x, OUT_ROWS // n_x, width)
    ffn_part = grads[OUT_ROWS:].reshape(2 * N_CHUNKS, n_x, owned, CHUNK)
    ffn_part = ffn_part.transpose(1, 0, 2, 3).reshape(n_x, 2 * N_CHUNKS * owned, CHUNK)
    grads = jnp.concatenate([out_part, ffn_part], axis=1).reshape(-1, width)
    grads = lax.psum_scatter(grads, AXIS_X, scatter_dimension=0, tiled=True).astype(f32)
    owned_out = lax.ppermute(grads[: OUT_ROWS // n_x], EVERY, pairs)
    owned_ffn = grads[OUT_ROWS // n_x :].reshape(2 * N_CHUNKS, owned, CHUNK)
    owned_in = jnp.concatenate(
        [
            columns(dw_head[:, :, :HD]),
            over_pair(dw_head[:, :, HD : 2 * HD]),
            over_pair(dw_head[:, :, 2 * HD : HEAD_COLS]),
            columns(owned_ffn),
        ],
        axis=1,
    )
    new_first_in, new_second_in, new_master_in = adam_step(
        w_in, first_in, second_in, owned_in, RATE_MATRIX
    )
    new_first_out, new_second_out, new_master_out = adam_step(
        w_out, first_out, second_out, owned_out, RATE_MATRIX
    )
    new_first_gains, new_second_gains, new_master_gains = adam_step(
        gains, first_gains, second_gains, owned_gain_grad, RATE_GAIN
    )
    return (
        output[None],
        input_grad[None],
        new_first_in,
        new_first_out,
        new_first_gains,
        new_second_in,
        new_second_out,
        new_second_gains,
        new_master_in,
        new_master_out,
        new_master_gains,
        new_master_in.astype(bf16),
        new_master_out.astype(bf16),
    )


def solution(mesh):
    cut = Mesh(mesh.devices.reshape(tuple(SIZES[name] for name in EVERY)), EVERY)
    weights = P(EVERY, None)
    vector = P(EVERY)
    acts = P(SHARD, CTX, None)
    in_specs = (
        acts,
        acts,
        P(SHARD, None),
        P(SHARD, CTX),
        P(SHARD, None),
    ) + (weights, weights, vector) * 3
    out_specs = (acts, acts) + (weights, weights, vector) * 3 + (weights, weights)
    return jax.shard_map(body, mesh=cut, in_specs=in_specs, out_specs=out_specs, check_vma=False)
```

```python
import functools
import math

import jax
import jax.numpy as jnp
from jax import lax
from jax.experimental import pallas as pl
from jax.experimental.pallas import tpu as pltpu
from jax.sharding import Mesh
from jax.sharding import PartitionSpec as P

H_Q = 16
H_KV = 8
HD = 128
FF = 3072
STEP = 5

NORM_EPS = 1e-06
ROPE_BASE = 1000000.0
BETA_ONE = 0.5
BETA_TWO = 0.5
ADAM_EPS = 1e-08
WEIGHT_DECAY = 0.1
RATE_MATRIX = 0.03
RATE_GAIN = 0.25

CTX = ("xh", "y", "core")
SHARD = ("xl", "z")
EVERY = CTX + SHARD
AXIS_X = ("xh", "xl")
AXIS_YZ = ("y", "z")
AXIS_CYZ = ("core", "y", "z")
SIZES = {"xh": 2, "y": 4, "core": 2, "xl": 2, "z": 4}

LOG2_E = 1.4426950408889634
SCORE_SCALE = 1.0 / math.sqrt(HD)
BQ = 512
BK = 512
SUB = 256
VMEM_BYTES = 48 * 1024 * 1024
BIG_VMEM_BYTES = 60 * 1024 * 1024

bf16 = jnp.bfloat16
f32 = jnp.float32


def rms_norm(values, weight):
    return values * lax.rsqrt(jnp.mean(values * values, axis=-1, keepdims=True) + NORM_EPS) * weight


def rms_back(values, weight, upstream):
    inverse = lax.rsqrt(jnp.mean(values * values, axis=-1, keepdims=True) + NORM_EPS)
    normed = values * inverse
    scaled = upstream * weight
    grad_values = inverse * (scaled - normed * jnp.mean(scaled * normed, axis=-1, keepdims=True))
    return (grad_values, upstream * normed)


def dot_nt(a, b):
    return lax.dot_general(a, b, (((1,), (1,)), ((), ())), preferred_element_type=f32)


def dot_tn(a, b):
    return lax.dot_general(a, b, (((0,), (0,)), ((), ())), preferred_element_type=f32)


def dot_nn(a, b):
    return lax.dot_general(a, b, (((1,), (0,)), ((), ())), preferred_element_type=f32)


LAST_DOC = 13


def tables_kernel(docs_ref, live_ref, freq_ref, cos_ref, sin_ref, lens_ref):
    docs = docs_ref[...]
    shape = docs.shape
    start = jnp.zeros(shape, f32)
    for number in range(1, LAST_DOC + 1):
        before = jnp.sum(jnp.where(docs < number, 1.0, 0.0))
        start = jnp.where(docs == number, before, start)
    at = lax.broadcasted_iota(jnp.int32, shape, 0) * shape[1] + lax.broadcasted_iota(
        jnp.int32, shape, 1
    )
    within = at.astype(f32) - start
    lens_ref[...] = jnp.where(live_ref[...] == 1, within.astype(jnp.int32), 0)

    left = lax.broadcasted_iota(jnp.int32, (HD, HD), 1) < HD // 2
    for i in range(0, shape[0], 2):
        cols = [jnp.broadcast_to(within[i + n : i + n + 1, :], (HD, HD)).T for n in range(2)]
        angle = jnp.where(left, cols[0], cols[1]) * freq_ref[...]
        for ref, values, flip in ((cos_ref, jnp.cos(angle), False), (sin_ref, jnp.sin(angle), True)):
            turned = pltpu.roll(values, HD // 2, 1)
            for n in range(2):
                lower, upper = (values, turned) if n == 0 else (turned, values)
                ref[(i + n) * HD : (i + n + 1) * HD, :] = jnp.where(
                    left, -lower if flip else lower, upper
                )


def tables(docs, live, freq):
    span = docs.size
    table = jax.ShapeDtypeStruct((span, HD), f32)
    return pl.pallas_call(
        tables_kernel,
        in_specs=[vmem()] * 3,
        out_specs=[vmem()] * 3,
        out_shape=[table, table, jax.ShapeDtypeStruct(docs.shape, jnp.int32)],
        compiler_params=pltpu.CompilerParams(vmem_limit_bytes=VMEM_BYTES),
        cost_estimate=pl.CostEstimate(
            flops=100 * span * HD, bytes_accessed=3 * span * HD * 4, transcendentals=span * HD
        ),
        name="tables",
    )(docs, live, freq)


N_GROUPS = 4
GROUP = 8
HALF = 128
STEP_BLOCKS = 4
STEPS = GROUP // STEP_BLOCKS
HEAD_COLS = 3 * HD
PAD_COLS = 4 * HD


def block_spec(width, first, count):
    return pl.BlockSpec(
        (STEP_BLOCKS, HALF, width), lambda i, place: (jnp.clip(i - first, 0, count - 1), 0, 0)
    )


def group_specs(width):
    return [block_spec(width, k * STEPS, STEPS) for k in range(N_GROUPS)]


def fixed(shape):
    return pl.BlockSpec(shape, lambda i, place: (0,) * len(shape))


def rows_of(place_ref, step, i):
    return pl.ds(pl.multiple_of(place_ref[step * STEP_BLOCKS + i] * HALF, HALF), HALF)


def head_mean(x):
    return lax.dot_general(
        x.astype(bf16),
        jnp.full((HD, HD), 1.0 / HD, bf16),
        (((1,), (0,)), ((), ())),
        preferred_element_type=f32,
    )


def project_kernel(
    place_ref, x0, x1, x2, x3, w_ref, cos_ref, sin_ref, gq_ref, gk_ref,
    q_ref, k_ref, v_ref, qraw_ref, kraw_ref, inv_ref,
):
    step = pl.program_id(0)

    def run(x):
        wide = x.astype(f32)
        inverse = lax.rsqrt(jnp.mean(wide * wide, axis=-1, keepdims=True) + NORM_EPS)
        prod = dot_nn(x, w_ref[...]) * inverse
        for i in range(STEP_BLOCKS):
            at = rows_of(place_ref, step, i)
            part = slice(i * HALF, (i + 1) * HALF)
            cos = cos_ref[at, :]
            sin = sin_ref[at, :]

            def roped(raw, gain, cos=cos, sin=sin):
                normed = raw * lax.rsqrt(head_mean(raw * raw) + NORM_EPS) * gain
                return normed * cos + pltpu.roll(normed, HD // 2, 1) * sin

            query = prod[part, :HD]
            key = prod[part, HD : 2 * HD]
            inv_ref[at, :] = jnp.broadcast_to(inverse[part], (HALF, HD)).astype(bf16)
            qraw_ref[at, :] = query.astype(bf16)
            kraw_ref[at, :] = key.astype(bf16)
            q_ref[at, :] = (roped(query, gq_ref[...]) * (SCORE_SCALE * LOG2_E)).astype(bf16)
            k_ref[at, :] = roped(key, gk_ref[...]).astype(bf16)
            v_ref[at, :] = prod[part, 2 * HD :].astype(bf16)

    for k, x_ref in enumerate((x0, x1, x2, x3)):

        @pl.when(step // STEPS == k)
        def _(x_ref=x_ref):
            run(x_ref[...].reshape(STEP_BLOCKS * HALF, x_ref.shape[2]))


def project(place, groups, w, cos, sin, gq, gk):
    width = w.shape[0]
    span = cos.shape[0]
    low = jax.ShapeDtypeStruct((span, HD), bf16)
    whole = fixed((span, HD))
    return pl.pallas_call(
        project_kernel,
        grid_spec=pltpu.PrefetchScalarGridSpec(
            num_scalar_prefetch=1,
            grid=(N_GROUPS * STEPS,),
            in_specs=group_specs(width)
            + [fixed((width, HEAD_COLS)), whole, whole, fixed((1, HD)), fixed((1, HD))],
            out_specs=[whole] * 6,
        ),
        out_shape=[low] * 6,
        compiler_params=pltpu.CompilerParams(vmem_limit_bytes=VMEM_BYTES),
        name="project",
    )(place, *groups, w, cos, sin, gq, gk)


def project_back_kernel(
    place_ref, x0, x1, x2, x3, dq_ref, dk_ref, dv_ref, qraw_ref, kraw_ref, inv_ref, cos_ref, sin_ref,
    gq_ref, gk_ref, send_ref, dw_ref, dg_ref, scaled,
):
    step = pl.program_id(0)
    n_dev = send_ref.shape[0]

    @pl.when(step == 0)
    def _():
        dw_ref[...] = jnp.zeros_like(dw_ref)
        dg_ref[...] = jnp.zeros_like(dg_ref)

    def run(x):
        q_sum = jnp.zeros((1, HD), f32)
        k_sum = jnp.zeros((1, HD), f32)
        for i in range(STEP_BLOCKS):
            place = place_ref[step * STEP_BLOCKS + i]
            dev = jnp.where(place < n_dev, place, 2 * n_dev - 1 - place)
            to = pl.ds(pl.multiple_of(jnp.where(place < n_dev, 0, HALF), HALF), HALF)
            at = rows_of(place_ref, step, i)
            part = slice(i * HALF, (i + 1) * HALF)
            cos = cos_ref[at, :]
            sin = sin_ref[at, :]

            def back(raw, gain, grad, cos=cos, sin=sin):
                unrot = grad * cos + pltpu.roll(grad * sin, HD // 2, 1)
                inv_rms = lax.rsqrt(head_mean(raw * raw) + NORM_EPS)
                normed = raw * inv_rms
                scaled_up = unrot * gain
                grad = inv_rms * (scaled_up - normed * head_mean(scaled_up * normed))
                return grad, unrot * normed

            grad_q, q_terms = back(qraw_ref[at, :].astype(f32), gq_ref[...], dq_ref[at, :])
            grad_k, k_terms = back(kraw_ref[at, :].astype(f32), gk_ref[...], dk_ref[at, :])
            inverse = inv_ref[at, :].astype(f32)
            for c, grad in enumerate((grad_q, grad_k, dv_ref[at, :])):
                send_ref[dev, c, to, :] = grad.astype(bf16)
                scaled[part, c * HD : (c + 1) * HD] = (grad * inverse).astype(bf16)
            q_sum = q_sum + jnp.sum(q_terms, axis=0, keepdims=True)
            k_sum = k_sum + jnp.sum(k_terms, axis=0, keepdims=True)
        dw_ref[...] += dot_tn(x, scaled[...])
        dg_ref[0:1, :] += q_sum
        dg_ref[1:2, :] += k_sum

    for k, x_ref in enumerate((x0, x1, x2, x3)):

        @pl.when(step // STEPS == k)
        def _(x_ref=x_ref):
            run(x_ref[...].reshape(STEP_BLOCKS * HALF, x_ref.shape[2]))


def project_back(place, groups, grads, raws, cos, sin, gq, gk):
    width = groups[0].shape[2]
    span = cos.shape[0]
    whole = fixed((span, HD))
    rows = 2 * HALF
    send = (span // rows, 3, rows, HD)
    return pl.pallas_call(
        project_back_kernel,
        grid_spec=pltpu.PrefetchScalarGridSpec(
            num_scalar_prefetch=1,
            grid=(N_GROUPS * STEPS,),
            in_specs=group_specs(width) + [whole] * 8 + [fixed((1, HD)), fixed((1, HD))],
            out_specs=[fixed(send), fixed((width, HEAD_COLS)), fixed((8, HD))],
            scratch_shapes=[pltpu.VMEM((STEP_BLOCKS * HALF, HEAD_COLS), bf16)],
        ),
        out_shape=[
            jax.ShapeDtypeStruct(send, bf16),
            jax.ShapeDtypeStruct((width, HEAD_COLS), f32),
            jax.ShapeDtypeStruct((8, HD), f32),
        ],
        compiler_params=pltpu.CompilerParams(vmem_limit_bytes=BIG_VMEM_BYTES),
        name="project_back",
    )(place, *groups, *grads, *raws, cos, sin, gq, gk)


def tokens_back_kernel(
    recv_ref, w_ref, shuffle_ref, tok_ref, dres_ref, gain_ref, out_ref, cols, grad
):
    step = pl.program_id(0)
    per = cols.shape[1] // HD

    for s in range(2):

        @pl.when(step == s)
        def _(s=s):
            for h in range(per):
                cols[:, h * HD : (h + 1) * HD] = recv_ref[s * per + h, 0]

    for s in range(2):

        @pl.when(step == 2 + s)
        def _(s=s):
            for j in range(per):
                both = recv_ref[2 * j, 1 + s].astype(f32) + recv_ref[2 * j + 1, 1 + s].astype(f32)
                cols[:, j * HD : (j + 1) * HD] = both.astype(bf16)

    part = dot_nt(cols[...], w_ref[...].reshape(shuffle_ref.shape[0], cols.shape[1]))

    @pl.when(step == 0)
    def _():
        grad[...] = part

    @pl.when(step > 0)
    def _():
        grad[...] += part

    @pl.when(step == pl.num_programs(0) - 1)
    def _():
        natural = dot_nt(grad[...].astype(bf16), shuffle_ref[...])
        back, _ = rms_back(tok_ref[...].astype(f32), gain_ref[...], natural)
        out_ref[...] = dres_ref[...] + back


def tokens_back(recv, w, shuffle, tok, dres, gain):
    rows, width = tok.shape
    n_blocks, height, chunk = w.shape
    n_chunks = height // CHUNK_ROWS

    def whole(shape):
        return pl.BlockSpec(shape, lambda i: (0,) * len(shape))

    return pl.pallas_call(
        tokens_back_kernel,
        grid=(n_chunks,),
        in_specs=[
            whole(recv.shape),
            pl.BlockSpec((n_blocks, CHUNK_ROWS, chunk), lambda i: (0, i, 0)),
            whole((width, width)),
            whole((rows, width)),
            whole((rows, width)),
            whole((1, width)),
        ],
        out_specs=whole((rows, width)),
        out_shape=jax.ShapeDtypeStruct((rows, width), f32),
        scratch_shapes=[pltpu.VMEM((rows, chunk), bf16), pltpu.VMEM((rows, width), f32)],
        compiler_params=pltpu.CompilerParams(vmem_limit_bytes=VMEM_BYTES),
        name="tokens_back",
    )(recv, w, shuffle, tok, dres, gain)


def dealt_slot(place, n_dev):
    if place < n_dev:
        return place, 0
    return 2 * n_dev - 1 - place, 1


def key_mask(len_row, offset):
    ahead = (
        lax.broadcasted_iota(jnp.int32, (SUB, BQ), 1)
        - lax.broadcasted_iota(jnp.int32, (SUB, BQ), 0)
        + offset
    )
    return (ahead >= 0) & (ahead <= len_row)


def key_loops(bounds_ref, qb, q_at, tile):
    low = bounds_ref[0, qb]
    high = (q_at + BQ - 1) // BK + 1
    first = jnp.minimum(bounds_ref[1, qb], high)
    last = jnp.maximum((q_at + 1) // BK, first)

    def run(masked):
        def step(kb, _):
            tile(kb, masked)
            return 0

        return step

    lax.fori_loop(low, first, run(True), 0)
    lax.fori_loop(first, last, run(False), 0)
    lax.fori_loop(last, high, run(True), 0)


def attend_kernel(
    bounds_ref, q_ref, k_ref, v_ref, len_ref, osend_ref, onat_ref, linv_ref, acc, total
):
    n_dev, rows, _ = osend_ref.shape
    half = rows // 2
    span = q_ref.shape[0]
    def q_step(qb, _):
        q_at = pl.multiple_of(qb * BQ, BQ)
        q_blk = q_ref[pl.ds(q_at, BQ), :]
        len_row = len_ref[pl.ds(qb, 1), :]
        acc[...] = jnp.zeros_like(acc)
        total[...] = jnp.zeros_like(total)

        def tile(kb, masked):
            mixed = None
            summed = None
            for c in range(BK // SUB):
                k_at = pl.multiple_of(kb * BK + c * SUB, SUB)
                p = jnp.exp2(dot_nt(k_ref[pl.ds(k_at, SUB), :], q_blk))
                if masked:
                    p = jnp.where(key_mask(len_row, q_at - k_at), p, 0.0)
                part = jnp.sum(p.reshape(SUB // 8, 8, BQ), axis=0)
                more = dot_tn(v_ref[pl.ds(k_at, SUB), :], p.astype(bf16))
                summed = part if summed is None else summed + part
                mixed = more if mixed is None else mixed + more
            acc[...] += mixed
            total[...] += summed

        key_loops(bounds_ref, qb, q_at, tile)
        inverse = 1.0 / jnp.sum(total[...], axis=0, keepdims=True)
        linv_ref[pl.ds(qb, 1), :] = inverse
        onat_ref[pl.ds(q_at, BQ), :] = (acc[...] * inverse).T
        return 0

    lax.fori_loop(0, span // BQ, q_step, 0)
    for place in range(2 * n_dev):
        dev, side = dealt_slot(place, n_dev)
        osend_ref[dev, side * half : (side + 1) * half, :] = onat_ref[
            place * half : (place + 1) * half, :
        ].astype(bf16)


def vmem():
    return pl.BlockSpec(memory_space=pltpu.VMEM)


def attend(klo, q, k, v, lens, rows):
    span = q.shape[0]
    return pl.pallas_call(
        attend_kernel,
        in_specs=[pl.BlockSpec(memory_space=pltpu.SMEM)] + [vmem()] * 4,
        out_specs=[vmem(), vmem(), vmem()],
        out_shape=[
            jax.ShapeDtypeStruct((span // rows, rows, HD), bf16),
            jax.ShapeDtypeStruct((span, HD), f32),
            jax.ShapeDtypeStruct((span // BQ, BQ), f32),
        ],
        scratch_shapes=[
            pltpu.VMEM((HD, BQ), f32),
            pltpu.VMEM((8, BQ), f32),
        ],
        compiler_params=pltpu.CompilerParams(vmem_limit_bytes=VMEM_BYTES),
        name="attend",
    )(klo, q, k, v, lens)


def attend_back_kernel(
    bounds_ref, q_ref, k_ref, v_ref, do_ref, onat_ref, linv_ref, len_ref, dq, dk, dv, don, acc
):
    n_dev, rows, _ = do_ref.shape
    half = rows // 2
    span = q_ref.shape[0]
    for place in range(2 * n_dev):
        dev, side = dealt_slot(place, n_dev)
        to = slice(place * half, (place + 1) * half)
        don[to, :] = do_ref[dev, side * half : (side + 1) * half, :]
    dk[...] = jnp.zeros_like(dk)
    dv[...] = jnp.zeros_like(dv)

    def q_step(qb, _):
        q_at = pl.multiple_of(qb * BQ, BQ)
        q_blk = q_ref[pl.ds(q_at, BQ), :]
        do_blk = don[pl.ds(q_at, BQ), :]
        len_row = len_ref[pl.ds(qb, 1), :]
        inverse = linv_ref[pl.ds(qb, 1), :]
        mixed = (do_blk.astype(f32) * onat_ref[pl.ds(q_at, BQ), :]).T
        delta = jnp.sum(mixed, axis=0, keepdims=True)
        acc[...] = jnp.zeros_like(acc)

        def tile(kb, masked):
            total = None
            for c in range(BK // SUB):
                k_at = pl.multiple_of(kb * BK + c * SUB, SUB)
                here = pl.ds(k_at, SUB)
                p = jnp.exp2(dot_nt(k_ref[here, :], q_blk)) * inverse
                if masked:
                    p = jnp.where(key_mask(len_row, q_at - k_at), p, 0.0)
                dp = dot_nt(v_ref[here, :], do_blk)
                ds = (p * (dp - delta)).astype(bf16)
                dv[here, :] += dot_nn(p.astype(bf16), do_blk)
                dk[here, :] += dot_nn(ds, q_blk)
                more = dot_tn(k_ref[here, :], ds)
                total = more if total is None else total + more
            acc[...] += total

        key_loops(bounds_ref, qb, q_at, tile)
        dq[pl.ds(q_at, BQ), :] = (acc[...] * SCORE_SCALE).T
        return 0

    lax.fori_loop(0, span // BQ, q_step, 0)
    dk[...] = dk[...] * (1.0 / LOG2_E)


def attend_back(klo, q, k, v, do, onat, linv, lens):
    span = q.shape[0]
    return pl.pallas_call(
        attend_back_kernel,
        in_specs=[pl.BlockSpec(memory_space=pltpu.SMEM)] + [vmem()] * 7,
        out_specs=[vmem()] * 3,
        out_shape=[jax.ShapeDtypeStruct((span, HD), f32)] * 3,
        scratch_shapes=[
            pltpu.VMEM((span, HD), bf16),
            pltpu.VMEM((HD, BQ), f32),
        ],
        compiler_params=pltpu.CompilerParams(vmem_limit_bytes=VMEM_BYTES),
        name="attend_back",
    )(klo, q, k, v, do, onat, linv, lens)


OUT_ROWS = 160
CHUNK_ROWS = 32
N_CHUNKS = 3
CHUNK = FF // N_CHUNKS
Q_WIDTH = H_Q * HD
HALF_OUT = (Q_WIDTH + FF) // 2
HALF_MID = 512
LEFT = HALF_OUT + HALF_MID


def middle_kernel(
    full_ref, mixed_ref, tok_ref, cot_ref, gain_ref, shuffle_ref, gate_ref, up_ref,
    out_ref, dres_ref, dob_ref, left_ref, wide_ref, dgain_ref,
    w_out, resid, mid_low, grad_mid, sems,
):
    step = pl.program_id(0)
    width = tok_ref.shape[1]

    def fetch(i):
        return pltpu.make_async_copy(
            full_ref.at[i, pl.ds(0, OUT_ROWS), :],
            w_out.at[pl.ds(i * OUT_ROWS, OUT_ROWS), :],
            sems.at[i],
        )

    n_fetch = full_ref.shape[0]
    n_first = -(-Q_WIDTH // OUT_ROWS)

    @pl.when(step == 0)
    def _():
        for i in range(n_fetch):
            fetch(i).start()
        for h in range(H_Q):
            left_ref[0, :, h * HD : (h + 1) * HD] = mixed_ref[h]
        for i in range(n_first):
            fetch(i).wait()
        residual = tok_ref[...].astype(f32) + dot_nn(
            left_ref[0, :, :Q_WIDTH], w_out[:Q_WIDTH, :]
        )
        resid[...] = residual
        out_ref[...] = residual
        normed = rms_norm(residual, gain_ref[...]).astype(bf16)
        low = dot_nn(normed, shuffle_ref[...]).astype(bf16)
        mid_low[...] = low
        for side in range(2):
            left_ref[side, :, HALF_OUT:] = low[:, side * HALF_MID : (side + 1) * HALF_MID]
        grad_mid[...] = jnp.zeros_like(grad_mid)
        for i in range(n_first, n_fetch):
            fetch(i).wait()

    for f in range(N_CHUNKS):

        @pl.when(step == f + 1)
        def _(f=f):
            at = Q_WIDTH + f * CHUNK
            gate_w = gate_ref[...].reshape(width, CHUNK)
            up_w = up_ref[...].reshape(width, CHUNK)
            gate = dot_nn(mid_low[...], gate_w)
            up = dot_nn(mid_low[...], up_w)
            sigmoid_gate = 1.0 / (1.0 + jnp.exp(-gate))
            activated = gate * sigmoid_gate
            hidden = (activated * up).astype(bf16)
            cut = min(max(HALF_OUT - at, 0), CHUNK)
            if cut > 0:
                left_ref[0, :, at : at + cut] = hidden[:, :cut]
            if cut < CHUNK:
                left_ref[1, :, at + cut - HALF_OUT : at + CHUNK - HALF_OUT] = hidden[:, cut:]
            down_w = w_out[at : at + CHUNK, :]
            out_ref[...] += dot_nn(hidden, down_w)
            grad_hidden = dot_nt(cot_ref[...], down_w)
            grad_up = (grad_hidden * activated).astype(bf16)
            grad_gate = (
                grad_hidden * up * sigmoid_gate * (1.0 + gate * (1.0 - sigmoid_gate))
            ).astype(bf16)
            wide_ref[:, f * CHUNK : (f + 1) * CHUNK] = grad_gate
            wide_ref[:, FF + f * CHUNK : FF + (f + 1) * CHUNK] = grad_up
            grad_mid[...] += dot_nt(grad_gate, gate_w) + dot_nt(grad_up, up_w)

    @pl.when(step == N_CHUNKS + 1)
    def _():
        grad = dot_nt(grad_mid[...].astype(bf16), shuffle_ref[...])
        part, terms = rms_back(resid[...], gain_ref[...], grad)
        dgain_ref[...] = jnp.sum(terms, axis=0, keepdims=True)
        dres = cot_ref[...].astype(f32) + part
        dres_ref[...] = dres
        low = dres.astype(bf16)
        wide_ref[:, 2 * FF :] = low
        for c in range(4):
            piece = dot_nt(low, w_out[c * 4 * HD : (c + 1) * 4 * HD, :]).astype(bf16)
            for h in range(4):
                dob_ref[4 * c + h] = piece[:, h * HD : (h + 1) * HD]


def middle(full, mixed, tok, cot, gain, shuffle):
    rows, width = tok.shape
    n_blocks = full.shape[0]
    first = OUT_ROWS // CHUNK_ROWS

    def chunk_of(i):
        return jnp.clip(i - 1, 0, N_CHUNKS - 1)

    def whole(shape):
        return pl.BlockSpec(shape, lambda i: (0,) * len(shape))

    chunk = (n_blocks, CHUNK_ROWS, CHUNK)
    return pl.pallas_call(
        middle_kernel,
        grid=(N_CHUNKS + 2,),
        in_specs=[
            pl.BlockSpec(memory_space=pl.ANY),
            whole((H_Q, rows, HD)),
            whole((rows, width)),
            whole((rows, width)),
            whole((1, width)),
            whole((width, width)),
            pl.BlockSpec(chunk, lambda i: (0, first + chunk_of(i), 0)),
            pl.BlockSpec(chunk, lambda i: (0, first + N_CHUNKS + chunk_of(i), 0)),
        ],
        out_specs=[
            whole((rows, width)),
            whole((rows, width)),
            whole((H_Q, rows, HD)),
            whole((2, rows, LEFT)),
            whole((rows, 2 * FF + width)),
            whole((1, width)),
        ],
        out_shape=[
            jax.ShapeDtypeStruct((rows, width), f32),
            jax.ShapeDtypeStruct((rows, width), f32),
            jax.ShapeDtypeStruct((H_Q, rows, HD), bf16),
            jax.ShapeDtypeStruct((2, rows, LEFT), bf16),
            jax.ShapeDtypeStruct((rows, 2 * FF + width), bf16),
            jax.ShapeDtypeStruct((1, width), f32),
        ],
        scratch_shapes=[
            pltpu.VMEM((Q_WIDTH + FF, width), bf16),
            pltpu.VMEM((rows, width), f32),
            pltpu.VMEM((rows, width), bf16),
            pltpu.VMEM((rows, width), f32),
            pltpu.SemaphoreType.DMA((n_blocks,)),
        ],
        compiler_params=pltpu.CompilerParams(vmem_limit_bytes=BIG_VMEM_BYTES),
        name="middle",
    )(full, mixed, tok, cot, gain, shuffle, full, full)


def grad_ffn_kernel(left_a, left_b, right_a, right_b, out_ref):
    total = dot_tn(left_a[...], right_a[...]) + dot_tn(left_b[...], right_b[...])
    out_ref[...] = total.astype(bf16).reshape(out_ref.shape)


def grad_ffn(lefts, wides, n_blocks):
    rows = lefts[0].shape[0]
    left = pl.BlockSpec((rows, HALF_MID), lambda i: (0, HALF_OUT // HALF_MID))
    right = pl.BlockSpec((rows, CHUNK), lambda i: (0, i))
    first = OUT_ROWS // CHUNK_ROWS
    height = OUT_ROWS + 2 * N_CHUNKS * CHUNK_ROWS
    return pl.pallas_call(
        grad_ffn_kernel,
        grid=(2 * N_CHUNKS,),
        in_specs=[left, left, right, right],
        out_specs=pl.BlockSpec((n_blocks, CHUNK_ROWS, CHUNK), lambda i: (0, first + i, 0)),
        out_shape=jax.ShapeDtypeStruct((n_blocks, height, CHUNK), bf16),
        compiler_params=pltpu.CompilerParams(vmem_limit_bytes=VMEM_BYTES),
        name="grad_ffn",
    )(*lefts, *wides)


def grad_out_kernel(core_ref, left_a, left_b, drb_a, drb_b, cot_a, cot_b, grads_ref, out_ref):
    step = pl.program_id(0)
    block = left_a.shape[1]
    both = Q_WIDTH // block
    cut = Q_WIDTH % block
    lower = core_ref[0] == 0

    def store(value):
        out_ref[...] = value.astype(bf16).reshape(out_ref.shape)

    @pl.when(lower & (step < both))
    def _():
        store(dot_tn(left_a[...], drb_a[...]) + dot_tn(left_b[...], drb_b[...]))

    @pl.when(lower & (step == both))
    def _():
        top = dot_tn(left_a[:, :cut], drb_a[...]) + dot_tn(left_b[:, :cut], drb_b[...])
        rest = dot_tn(left_a[:, cut:], cot_a[...]) + dot_tn(left_b[:, cut:], cot_b[...])
        store(jnp.concatenate([top, rest], axis=0))

    @pl.when(core_ref[0] == 1)
    def _():
        store(dot_tn(left_a[...], cot_a[...]) + dot_tn(left_b[...], cot_b[...]))


def grad_out(core, lefts, wides, cots, grads):
    rows, width = cots[0].shape
    blocks = 4
    left = pl.BlockSpec((rows, blocks * OUT_ROWS), lambda i, core: (0, i))
    drb = pl.BlockSpec((rows, width), lambda i, core: (0, 2 * N_CHUNKS))
    cot = pl.BlockSpec((rows, width), lambda i, core: (0, 0))
    return pl.pallas_call(
        grad_out_kernel,
        grid_spec=pltpu.PrefetchScalarGridSpec(
            num_scalar_prefetch=1,
            grid=(grads.shape[0] // blocks,),
            in_specs=[left, left, drb, drb, cot, cot, pl.BlockSpec(memory_space=pl.ANY)],
            out_specs=pl.BlockSpec((blocks, OUT_ROWS, width), lambda i, core: (i, 0, 0)),
        ),
        out_shape=jax.ShapeDtypeStruct(grads.shape, bf16),
        input_output_aliases={7: 0},
        compiler_params=pltpu.CompilerParams(vmem_limit_bytes=VMEM_BYTES),
        name="grad_out",
    )(core, *lefts, *wides, *cots, grads)


def adam_step(master, first_old, second_old, gradient, rate):
    first_new = BETA_ONE * first_old + (1.0 - BETA_ONE) * gradient
    second_new = BETA_TWO * second_old + (1.0 - BETA_TWO) * gradient * gradient
    first_hat = first_new / (1.0 - BETA_ONE**STEP)
    second_hat = second_new / (1.0 - BETA_TWO**STEP)
    master_new = master - rate * (
        first_hat / (jnp.sqrt(second_hat) + ADAM_EPS) + WEIGHT_DECAY * master
    )
    return (first_new, second_new, master_new)


def gathered(x):
    return lax.all_gather(x, AXIS_CYZ, axis=0, tiled=True)


def shift(x, axis, step):
    n = SIZES[axis]
    return lax.ppermute(x, axis, [(i, (i + step) % n) for i in range(n)])


def first_moves(x):
    first, second = x[None, :HALF], x[None, HALF:]
    pair = jnp.concatenate([first, shift(first, "xh", 1)], axis=0)
    ring = jnp.concatenate([second] + [shift(second, "y", b) for b in (1, 2, 3)], axis=0)
    return pair, ring


def second_moves(pair, ring, after):
    one = jnp.concatenate([pair] + [shift(pair, "y", b) for b in (1, 2, 3)], axis=0)
    two = jnp.concatenate([ring, shift(ring, "xh", 1)], axis=0)
    one, two, _ = lax.optimization_barrier((one, two, after))
    return [one, two, shift(one, "core", 1), shift(two, "core", 1)]


def places_of_groups():
    xh, y, core = (lax.axis_index(name) for name in CTX)
    places = []
    for other in range(2):
        for side in range(2):
            for i in range(GROUP):
                b, a = (i // 2, i % 2) if side == 0 else (i % 4, i // 4)
                dev = (((xh + a) % 2) * 4 + (y - b) % 4) * 2 + (core + other) % 2
                places.append(dev if side == 0 else 31 - dev)
    return jnp.stack(places).astype(jnp.int32)


def sum_over_shard(x):
    xl, z = lax.axis_index("xl"), lax.axis_index("z")
    x = pick(x, xl, 2).astype(f32) + shift(pick(x, xl + 1, 2), "xl", 1).astype(f32)
    low = x.astype(bf16)
    total = pick(x, z, 4)
    for step in (1, 2, 3):
        total = total + shift(pick(low, z + step, 4), "z", step).astype(f32)
    return total


def pick(v, i, n):
    return lax.dynamic_index_in_dim(v, lax.rem(i, n), 0, keepdims=False)


def sum_over_x(blocks):
    me = lax.axis_index(AXIS_X)
    n = blocks.shape[0]
    total = pick(blocks, me, n).astype(f32)
    for step in range(1, n):
        moves = [(i, (i + step) % n) for i in range(n)]
        total = total + lax.ppermute(pick(blocks, me + step, n), AXIS_X, moves).astype(f32)
    return total


def sum_at_owners(blocks):
    me = lax.axis_index(AXIS_X)
    n = blocks.shape[0]
    total = 0.0
    for step in range(n):
        moves = []
        for source, place in owner_pairs():
            moves.append((source, place - place % n + (place % n + step) % n))
        total = total + lax.ppermute(pick(blocks, me + step, n), EVERY, moves).astype(f32)
    return total


def natural_of_permuted(x):
    tail = x.shape[1:]
    x = x.reshape((2, 4, 4, 2, 2) + tail)
    x = x.transpose((3, 1, 0, 4, 2) + tuple(range(5, 5 + len(tail))))
    return x.reshape((128,) + tail)


def owner_pairs():
    pairs = []
    for n in range(128):
        z = n % 4
        xl = (n // 4) % 2
        core = (n // 8) % 2
        y = (n // 16) % 4
        xh = n // 64
        pairs.append((n, (((core * 4 + y) * 4 + z) * 2 + xh) * 2 + xl))
    return pairs


def body(
    tokens,
    cotangent,
    segments,
    positions,
    pad_mask,
    w_in,
    w_out,
    gains,
    first_in,
    first_out,
    first_gains,
    second_in,
    second_out,
    second_gains,
):
    rows = tokens.shape[1]
    width = tokens.shape[2]
    span = segments.shape[1]
    half = rows // 2
    n_ctx = span // rows
    q_width = H_Q * HD
    kv_width = H_KV * HD
    attn_cols = q_width + 2 * kv_width
    owned = w_in.shape[0]
    owned_gains = gains.shape[0]

    n_x = 4
    low_in = w_in.astype(bf16)
    n_dev = width // owned

    own_head = jnp.concatenate(
        [
            low_in[:, :q_width].reshape(owned, H_Q, HD),
            jnp.repeat(low_in[:, q_width : q_width + kv_width].reshape(owned, H_KV, HD), 2, axis=1),
            jnp.repeat(low_in[:, q_width + kv_width : attn_cols].reshape(owned, H_KV, HD), 2, axis=1),
            jnp.broadcast_to(
                jnp.pad(gains.astype(bf16)[None, None], ((0, owned - 1), (0, 0), (0, HD - owned_gains))),
                (owned, H_Q, HD),
            ),
        ],
        axis=2,
    ).transpose(1, 0, 2)
    pair, ring = first_moves(tokens[0])
    head = lax.all_to_all(own_head, CTX, 0, 0, tiled=True)
    head = lax.all_gather(head, SHARD, axis=0, tiled=False)
    pairs = owner_pairs()
    own_out = lax.ppermute(w_out.astype(bf16), EVERY, [(p, n) for n, p in pairs])
    own_ffn = low_in[:, attn_cols:].reshape(owned, 2 * N_CHUNKS, CHUNK)
    own_ffn = own_ffn.transpose(1, 0, 2).reshape(2 * N_CHUNKS * owned, CHUNK)
    own_qkv = low_in[:, :attn_cols].reshape(owned, attn_cols // width, width)
    own_qkv = own_qkv.transpose(1, 0, 2).reshape(-1, width)
    own_rest = jnp.concatenate([own_out, own_ffn, own_qkv], axis=0)
    own_rest = lax.all_gather(own_rest, AXIS_X, axis=0, tiled=False)
    segments, pad_mask, own_rest, pair, ring = lax.optimization_barrier(
        (segments, pad_mask, own_rest, pair, ring)
    )
    head = head.reshape((2, 4) + own_head.shape).transpose(2, 0, 1, 3, 4)
    gain_vals = head[:, :, :, 0, HEAD_COLS : HEAD_COLS + owned_gains].reshape(-1).astype(f32)
    w_head = head[..., :HEAD_COLS].reshape(width, HEAD_COLS)
    gain_one = gain_vals[:width]
    gain_two = gain_vals[width : 2 * width]
    gain_query = gain_vals[2 * width : 2 * width + HD].reshape(1, HD)
    gain_key = gain_vals[2 * width + HD :].reshape(1, HD)
    w_scaled = (w_head.astype(f32) * gain_one[:, None]).astype(bf16)

    n_out = w_out.shape[0]
    part_out = own_rest[:, :n_out].reshape(n_x * n_out, width)
    n_ffn = n_out + 2 * N_CHUNKS * owned
    part_qkv = own_rest[:, n_ffn:].reshape(n_x, attn_cols // width, owned, width)
    part_qkv = part_qkv.transpose(1, 0, 2, 3).reshape(-1, width)
    part_ffn = own_rest[:, n_out:n_ffn].reshape(n_x, 2 * N_CHUNKS, owned, CHUNK)
    part_ffn = part_ffn.transpose(1, 0, 2, 3)
    part_ffn = part_ffn.reshape(2 * N_CHUNKS * CHUNK_ROWS, CHUNK)
    full = gathered(jnp.concatenate([part_out, part_ffn], axis=0)[None])

    order = natural_of_permuted(jnp.arange(width, dtype=jnp.int32).reshape(n_dev, owned)).reshape(-1)
    shuffle = (order[:, None] == jnp.arange(width, dtype=jnp.int32)[None, :]).astype(bf16)

    def natural(x):
        x = x.reshape(n_ctx, 2, half)
        return jnp.concatenate([x[:, 0], x[::-1, 1]], axis=0)

    halves = jnp.arange(HD // 2, dtype=f32)
    inverse = ROPE_BASE ** (-2.0 * halves / HD)
    cos, sin, lens = tables(
        natural(segments[0]), natural(pad_mask[0]), jnp.concatenate([inverse, inverse])[None]
    )
    first_key = (jnp.arange(span, dtype=jnp.int32).reshape(lens.shape) - lens).reshape(span // BQ, BQ)
    klo = jnp.stack(
        [jnp.min(first_key, axis=1) // BK, (jnp.max(first_key, axis=1) + BK - 1) // BK]
    )
    lens = lens.reshape(span // BQ, BQ)

    groups = second_moves(pair, ring, (cos, klo, lens))
    place = places_of_groups()
    q, k, v, query_raw, key_raw, inv = project(
        place, groups, w_scaled, cos, sin, gain_query, gain_key
    )
    part_qkv, _ = lax.optimization_barrier((part_qkv, k))
    full_qkv = gathered(part_qkv[None])
    o_send, o_nat, l_inv = attend(klo, q, k, v, lens, rows)
    mixed = lax.all_to_all(o_send, CTX, 0, 0, tiled=True)

    output, grad_residual, do_send, left, wide, gain_two_terms = middle(
        full, mixed, tokens[0], cotangent[0], gain_two.reshape(1, width), shuffle
    )
    core = lax.axis_index("core")
    lefts = (pick(left, core, 2), shift(pick(left, core + 1, 2), "core", 1))
    wides = (wide, shift(wide, "core", 1))
    cots = (cotangent[0], shift(cotangent[0], "core", 1))
    grads = grad_ffn(lefts, wides, full.shape[0] // 2)
    grads = grad_out(core.astype(jnp.int32).reshape(1), lefts, wides, cots, grads)
    do = lax.all_to_all(do_send, CTX, 0, 0, tiled=True)
    do, grads = lax.optimization_barrier((do, grads))
    grads = grads.reshape(-1, width)
    grads = lax.psum_scatter(grads, AXIS_YZ, scatter_dimension=0, tiled=True)

    head_grads = attend_back(klo, q, k, v, do, o_nat, l_inv, lens)
    d_send, dw_head, gain_qk = project_back(
        place, groups, head_grads, (query_raw, key_raw, inv), cos, sin, gain_query, gain_key
    )
    d_recv = lax.all_to_all(d_send, CTX, 0, 0, tiled=True)
    input_grad = tokens_back(
        d_recv, full_qkv, shuffle, tokens[0], grad_residual, gain_one.reshape(1, width)
    )

    gain_one_grad = jnp.sum(dw_head * w_head.astype(f32), axis=1)
    grad_gains = jnp.concatenate([gain_one_grad, gain_two_terms[0], gain_qk[0], gain_qk[1]])
    grad_gains = jnp.pad(
        grad_gains.reshape(n_dev, 1, owned_gains), ((0, 0), (0, owned - 1), (0, HD - owned_gains))
    )
    dw_head = (dw_head * gain_one[:, None]).reshape(n_dev, owned, HEAD_COLS)
    dw_head = jnp.concatenate([dw_head, grad_gains], axis=2).astype(bf16)
    dw_head = dw_head.reshape(n_ctx, n_dev // n_ctx, owned, PAD_COLS).transpose(1, 0, 2, 3)
    dw_head = sum_over_shard(dw_head.reshape((2, 4) + dw_head.shape[1:])).astype(bf16)
    dw_head, _ = lax.optimization_barrier((dw_head, d_recv))
    dw_head = lax.all_to_all(dw_head, CTX, 0, 0, tiled=True).astype(f32)
    owned_gain_grad = jnp.sum(dw_head[:, 0, HEAD_COLS : HEAD_COLS + owned_gains], axis=0)

    def columns(x):
        return x.transpose(1, 0, 2).reshape(owned, -1)

    def over_pair(x):
        return columns(jnp.sum(x.reshape(H_KV, 2, owned, HD), axis=1))

    out_part = grads[:OUT_ROWS].reshape(n_x, OUT_ROWS // n_x, width)
    ffn_part = grads[OUT_ROWS:].reshape(2 * N_CHUNKS, n_x, owned, CHUNK)
    ffn_part = ffn_part.transpose(1, 0, 2, 3).reshape(n_x, 2 * N_CHUNKS * owned, CHUNK)
    owned_out = sum_at_owners(out_part)
    owned_ffn = sum_over_x(ffn_part).reshape(2 * N_CHUNKS, owned, CHUNK)
    owned_in = jnp.concatenate(
        [
            columns(dw_head[:, :, :HD]),
            over_pair(dw_head[:, :, HD : 2 * HD]),
            over_pair(dw_head[:, :, 2 * HD : HEAD_COLS]),
            columns(owned_ffn),
        ],
        axis=1,
    )
    new_first_in, new_second_in, new_master_in = adam_step(
        w_in, first_in, second_in, owned_in, RATE_MATRIX
    )
    new_first_out, new_second_out, new_master_out = adam_step(
        w_out, first_out, second_out, owned_out, RATE_MATRIX
    )
    new_first_gains, new_second_gains, new_master_gains = adam_step(
        gains, first_gains, second_gains, owned_gain_grad, RATE_GAIN
    )
    return (
        output[None],
        input_grad[None],
        new_first_in,
        new_first_out,
        new_first_gains,
        new_second_in,
        new_second_out,
        new_second_gains,
        new_master_in,
        new_master_out,
        new_master_gains,
        new_master_in.astype(bf16),
        new_master_out.astype(bf16),
    )


def solution(mesh):
    cut = Mesh(mesh.devices.reshape(tuple(SIZES[name] for name in EVERY)), EVERY)
    weights = P(EVERY, None)
    vector = P(EVERY)
    acts = P(SHARD, CTX, None)
    in_specs = (
        acts,
        acts,
        P(SHARD, None),
        P(SHARD, CTX),
        P(SHARD, None),
    ) + (weights, weights, vector) * 3
    out_specs = (acts, acts) + (weights, weights, vector) * 3 + (weights, weights)
    return jax.shard_map(body, mesh=cut, in_specs=in_specs, out_specs=out_specs, check_vma=False)
```

```python
import functools
import math

import jax
import jax.numpy as jnp
from jax import lax
from jax.experimental import pallas as pl
from jax.experimental.pallas import tpu as pltpu
from jax.sharding import Mesh
from jax.sharding import PartitionSpec as P

H_Q = 16
H_KV = 8
HD = 128
FF = 3072
STEP = 5

NORM_EPS = 1e-06
ROPE_BASE = 1000000.0
BETA_ONE = 0.5
BETA_TWO = 0.5
ADAM_EPS = 1e-08
WEIGHT_DECAY = 0.1
RATE_MATRIX = 0.03
RATE_GAIN = 0.25

CTX = ("xh", "y", "core")
SHARD = ("xl", "z")
EVERY = CTX + SHARD
AXIS_X = ("xh", "xl")
AXIS_YZ = ("y", "z")
AXIS_CYZ = ("core", "y", "z")
SIZES = {"xh": 2, "y": 4, "core": 2, "xl": 2, "z": 4}

LOG2_E = 1.4426950408889634
SCORE_SCALE = 1.0 / math.sqrt(HD)
BQ = 512
BK = 512
SUB = 256
VMEM_BYTES = 48 * 1024 * 1024
BIG_VMEM_BYTES = 60 * 1024 * 1024

bf16 = jnp.bfloat16
f32 = jnp.float32


def rms_norm(values, weight):
    return values * lax.rsqrt(jnp.mean(values * values, axis=-1, keepdims=True) + NORM_EPS) * weight


def rms_back(values, weight, upstream):
    inverse = lax.rsqrt(jnp.mean(values * values, axis=-1, keepdims=True) + NORM_EPS)
    normed = values * inverse
    scaled = upstream * weight
    grad_values = inverse * (scaled - normed * jnp.mean(scaled * normed, axis=-1, keepdims=True))
    return (grad_values, upstream * normed)


def dot_nt(a, b):
    return lax.dot_general(a, b, (((1,), (1,)), ((), ())), preferred_element_type=f32)


def dot_tn(a, b):
    return lax.dot_general(a, b, (((0,), (0,)), ((), ())), preferred_element_type=f32)


def dot_nn(a, b):
    return lax.dot_general(a, b, (((1,), (0,)), ((), ())), preferred_element_type=f32)


LAST_DOC = 13


def tables_kernel(docs_ref, live_ref, freq_ref, cos_ref, sin_ref, lens_ref):
    docs = docs_ref[...]
    shape = docs.shape
    start = jnp.zeros(shape, f32)
    for number in range(1, LAST_DOC + 1):
        before = jnp.sum(jnp.where(docs < number, 1.0, 0.0))
        start = jnp.where(docs == number, before, start)
    at = lax.broadcasted_iota(jnp.int32, shape, 0) * shape[1] + lax.broadcasted_iota(
        jnp.int32, shape, 1
    )
    within = at.astype(f32) - start
    lens_ref[...] = jnp.where(live_ref[...] == 1, within.astype(jnp.int32), 0)

    left = lax.broadcasted_iota(jnp.int32, (HD, HD), 1) < HD // 2
    for i in range(0, shape[0], 2):
        cols = [jnp.broadcast_to(within[i + n : i + n + 1, :], (HD, HD)).T for n in range(2)]
        angle = jnp.where(left, cols[0], cols[1]) * freq_ref[...]
        for ref, values, flip in ((cos_ref, jnp.cos(angle), False), (sin_ref, jnp.sin(angle), True)):
            turned = pltpu.roll(values, HD // 2, 1)
            for n in range(2):
                lower, upper = (values, turned) if n == 0 else (turned, values)
                ref[(i + n) * HD : (i + n + 1) * HD, :] = jnp.where(
                    left, -lower if flip else lower, upper
                )


def tables(docs, live, freq):
    span = docs.size
    table = jax.ShapeDtypeStruct((span, HD), f32)
    return pl.pallas_call(
        tables_kernel,
        in_specs=[vmem()] * 3,
        out_specs=[vmem()] * 3,
        out_shape=[table, table, jax.ShapeDtypeStruct(docs.shape, jnp.int32)],
        compiler_params=pltpu.CompilerParams(vmem_limit_bytes=VMEM_BYTES),
        cost_estimate=pl.CostEstimate(
            flops=100 * span * HD, bytes_accessed=3 * span * HD * 4, transcendentals=span * HD
        ),
        name="tables",
    )(docs, live, freq)


N_GROUPS = 4
GROUP = 8
HALF = 128
STEP_BLOCKS = 4
STEPS = GROUP // STEP_BLOCKS
HEAD_COLS = 3 * HD
PAD_COLS = 4 * HD


def block_spec(width, first, count):
    return pl.BlockSpec(
        (STEP_BLOCKS, HALF, width), lambda i, place: (jnp.clip(i - first, 0, count - 1), 0, 0)
    )


def group_specs(width):
    return [block_spec(width, k * STEPS, STEPS) for k in range(N_GROUPS)]


def fixed(shape):
    return pl.BlockSpec(shape, lambda i, place: (0,) * len(shape))


def rows_of(place_ref, step, i):
    return pl.ds(pl.multiple_of(place_ref[step * STEP_BLOCKS + i] * HALF, HALF), HALF)


def head_mean(x):
    return lax.dot_general(
        x.astype(bf16),
        jnp.full((HD, HD), 1.0 / HD, bf16),
        (((1,), (0,)), ((), ())),
        preferred_element_type=f32,
    )


def project_kernel(
    place_ref, x0, x1, x2, x3, w_ref, cos_ref, sin_ref, gq_ref, gk_ref,
    q_ref, k_ref, v_ref, qraw_ref, kraw_ref, inv_ref,
):
    step = pl.program_id(0)

    def run(x):
        wide = x.astype(f32)
        inverse = lax.rsqrt(jnp.mean(wide * wide, axis=-1, keepdims=True) + NORM_EPS)
        prod = dot_nn(x, w_ref[...]) * inverse
        for i in range(STEP_BLOCKS):
            at = rows_of(place_ref, step, i)
            part = slice(i * HALF, (i + 1) * HALF)
            cos = cos_ref[at, :]
            sin = sin_ref[at, :]

            def roped(raw, gain, cos=cos, sin=sin):
                normed = raw * lax.rsqrt(head_mean(raw * raw) + NORM_EPS) * gain
                return normed * cos + pltpu.roll(normed, HD // 2, 1) * sin

            query = prod[part, :HD]
            key = prod[part, HD : 2 * HD]
            inv_ref[at, :] = jnp.broadcast_to(inverse[part], (HALF, HD)).astype(bf16)
            qraw_ref[at, :] = query.astype(bf16)
            kraw_ref[at, :] = key.astype(bf16)
            q_ref[at, :] = (roped(query, gq_ref[...]) * (SCORE_SCALE * LOG2_E)).astype(bf16)
            k_ref[at, :] = roped(key, gk_ref[...]).astype(bf16)
            v_ref[at, :] = prod[part, 2 * HD :].astype(bf16)

    for k, x_ref in enumerate((x0, x1, x2, x3)):

        @pl.when(step // STEPS == k)
        def _(x_ref=x_ref):
            run(x_ref[...].reshape(STEP_BLOCKS * HALF, x_ref.shape[2]))


def project(place, groups, w, cos, sin, gq, gk):
    width = w.shape[0]
    span = cos.shape[0]
    low = jax.ShapeDtypeStruct((span, HD), bf16)
    whole = fixed((span, HD))
    return pl.pallas_call(
        project_kernel,
        grid_spec=pltpu.PrefetchScalarGridSpec(
            num_scalar_prefetch=1,
            grid=(N_GROUPS * STEPS,),
            in_specs=group_specs(width)
            + [fixed((width, HEAD_COLS)), whole, whole, fixed((1, HD)), fixed((1, HD))],
            out_specs=[whole] * 6,
        ),
        out_shape=[low] * 6,
        compiler_params=pltpu.CompilerParams(vmem_limit_bytes=VMEM_BYTES),
        name="project",
    )(place, *groups, w, cos, sin, gq, gk)


def project_back_kernel(
    place_ref, x0, x1, x2, x3, dq_ref, dk_ref, dv_ref, qraw_ref, kraw_ref, inv_ref, cos_ref, sin_ref,
    gq_ref, gk_ref, w_ref, near_ref, far_ref, dw_ref, dg_ref, grads, scaled,
):
    step = pl.program_id(0)

    @pl.when(step == 0)
    def _():
        dw_ref[...] = jnp.zeros_like(dw_ref)
        dg_ref[...] = jnp.zeros_like(dg_ref)

    def run(x, da_ref):
        q_sum = jnp.zeros((1, HD), f32)
        k_sum = jnp.zeros((1, HD), f32)
        for i in range(STEP_BLOCKS):
            at = rows_of(place_ref, step, i)
            part = slice(i * HALF, (i + 1) * HALF)
            cos = cos_ref[at, :]
            sin = sin_ref[at, :]

            def back(raw, gain, grad, cos=cos, sin=sin):
                unrot = grad * cos + pltpu.roll(grad * sin, HD // 2, 1)
                inv_rms = lax.rsqrt(head_mean(raw * raw) + NORM_EPS)
                normed = raw * inv_rms
                scaled_up = unrot * gain
                grad = inv_rms * (scaled_up - normed * head_mean(scaled_up * normed))
                return grad, unrot * normed

            grad_q, q_terms = back(qraw_ref[at, :].astype(f32), gq_ref[...], dq_ref[at, :])
            grad_k, k_terms = back(kraw_ref[at, :].astype(f32), gk_ref[...], dk_ref[at, :])
            inverse = inv_ref[at, :].astype(f32)
            for c, grad in enumerate((grad_q, grad_k, dv_ref[at, :])):
                grads[part, c * HD : (c + 1) * HD] = grad.astype(bf16)
                scaled[part, c * HD : (c + 1) * HD] = (grad * inverse).astype(bf16)
            q_sum = q_sum + jnp.sum(q_terms, axis=0, keepdims=True)
            k_sum = k_sum + jnp.sum(k_terms, axis=0, keepdims=True)
        da_ref[...] = dot_nt(grads[...], w_ref[...]).astype(bf16).reshape(da_ref.shape)
        dw_ref[...] += dot_tn(x, scaled[...])
        dg_ref[0:1, :] += q_sum
        dg_ref[1:2, :] += k_sum

    for k, x_ref in enumerate((x0, x1, x2, x3)):

        @pl.when(step // STEPS == k)
        def _(k=k, x_ref=x_ref):
            da_ref = near_ref if k < N_GROUPS // 2 else far_ref
            run(x_ref[...].reshape(STEP_BLOCKS * HALF, x_ref.shape[2]), da_ref)


def project_back(place, groups, grads, raws, cos, sin, gq, gk, w):
    width = w.shape[0]
    span = cos.shape[0]
    whole = fixed((span, HD))
    n_half = N_GROUPS // 2
    da = jax.ShapeDtypeStruct((n_half * GROUP, HALF, width), bf16)
    return pl.pallas_call(
        project_back_kernel,
        grid_spec=pltpu.PrefetchScalarGridSpec(
            num_scalar_prefetch=1,
            grid=(N_GROUPS * STEPS,),
            in_specs=group_specs(width)
            + [whole] * 8
            + [fixed((1, HD)), fixed((1, HD)), fixed((width, HEAD_COLS))],
            out_specs=[
                block_spec(width, 0, n_half * STEPS),
                block_spec(width, n_half * STEPS, n_half * STEPS),
                fixed((width, HEAD_COLS)),
                fixed((8, HD)),
            ],
            scratch_shapes=[
                pltpu.VMEM((STEP_BLOCKS * HALF, HEAD_COLS), bf16),
                pltpu.VMEM((STEP_BLOCKS * HALF, HEAD_COLS), bf16),
            ],
        ),
        out_shape=[
            da,
            da,
            jax.ShapeDtypeStruct((width, HEAD_COLS), f32),
            jax.ShapeDtypeStruct((8, HD), f32),
        ],
        compiler_params=pltpu.CompilerParams(vmem_limit_bytes=BIG_VMEM_BYTES),
        name="project_back",
    )(place, *groups, *grads, *raws, cos, sin, gq, gk, w)


def dealt_slot(place, n_dev):
    if place < n_dev:
        return place, 0
    return 2 * n_dev - 1 - place, 1


def key_mask(len_row, offset):
    ahead = (
        lax.broadcasted_iota(jnp.int32, (SUB, BQ), 1)
        - lax.broadcasted_iota(jnp.int32, (SUB, BQ), 0)
        + offset
    )
    return (ahead >= 0) & (ahead <= len_row)


def key_loops(bounds_ref, qb, q_at, tile):
    low = bounds_ref[0, qb]
    high = (q_at + BQ - 1) // BK + 1
    first = jnp.minimum(bounds_ref[1, qb], high)
    last = jnp.maximum((q_at + 1) // BK, first)

    def run(masked):
        def step(kb, _):
            tile(kb, masked)
            return 0

        return step

    lax.fori_loop(low, first, run(True), 0)
    lax.fori_loop(first, last, run(False), 0)
    lax.fori_loop(last, high, run(True), 0)


def attend_kernel(
    bounds_ref, q_ref, k_ref, v_ref, len_ref, osend_ref, onat_ref, linv_ref, acc, total
):
    n_dev, rows, _ = osend_ref.shape
    half = rows // 2
    span = q_ref.shape[0]
    def q_step(qb, _):
        q_at = pl.multiple_of(qb * BQ, BQ)
        q_blk = q_ref[pl.ds(q_at, BQ), :]
        len_row = len_ref[pl.ds(qb, 1), :]
        acc[...] = jnp.zeros_like(acc)
        total[...] = jnp.zeros_like(total)

        def tile(kb, masked):
            mixed = None
            summed = None
            for c in range(BK // SUB):
                k_at = pl.multiple_of(kb * BK + c * SUB, SUB)
                p = jnp.exp2(dot_nt(k_ref[pl.ds(k_at, SUB), :], q_blk))
                if masked:
                    p = jnp.where(key_mask(len_row, q_at - k_at), p, 0.0)
                part = jnp.sum(p.reshape(SUB // 8, 8, BQ), axis=0)
                more = dot_tn(v_ref[pl.ds(k_at, SUB), :], p.astype(bf16))
                summed = part if summed is None else summed + part
                mixed = more if mixed is None else mixed + more
            acc[...] += mixed
            total[...] += summed

        key_loops(bounds_ref, qb, q_at, tile)
        inverse = 1.0 / jnp.sum(total[...], axis=0, keepdims=True)
        linv_ref[pl.ds(qb, 1), :] = inverse
        onat_ref[pl.ds(q_at, BQ), :] = (acc[...] * inverse).T
        return 0

    lax.fori_loop(0, span // BQ, q_step, 0)
    for place in range(2 * n_dev):
        dev, side = dealt_slot(place, n_dev)
        osend_ref[dev, side * half : (side + 1) * half, :] = onat_ref[
            place * half : (place + 1) * half, :
        ].astype(bf16)


def vmem():
    return pl.BlockSpec(memory_space=pltpu.VMEM)


def attend(klo, q, k, v, lens, rows):
    span = q.shape[0]
    return pl.pallas_call(
        attend_kernel,
        in_specs=[pl.BlockSpec(memory_space=pltpu.SMEM)] + [vmem()] * 4,
        out_specs=[vmem(), vmem(), vmem()],
        out_shape=[
            jax.ShapeDtypeStruct((span // rows, rows, HD), bf16),
            jax.ShapeDtypeStruct((span, HD), f32),
            jax.ShapeDtypeStruct((span // BQ, BQ), f32),
        ],
        scratch_shapes=[
            pltpu.VMEM((HD, BQ), f32),
            pltpu.VMEM((8, BQ), f32),
        ],
        compiler_params=pltpu.CompilerParams(vmem_limit_bytes=VMEM_BYTES),
        name="attend",
    )(klo, q, k, v, lens)


def attend_back_kernel(
    bounds_ref, q_ref, k_ref, v_ref, do_ref, onat_ref, linv_ref, len_ref, dq, dk, dv, don, acc
):
    n_dev, rows, _ = do_ref.shape
    half = rows // 2
    span = q_ref.shape[0]
    for place in range(2 * n_dev):
        dev, side = dealt_slot(place, n_dev)
        to = slice(place * half, (place + 1) * half)
        don[to, :] = do_ref[dev, side * half : (side + 1) * half, :]
    dk[...] = jnp.zeros_like(dk)
    dv[...] = jnp.zeros_like(dv)

    def q_step(qb, _):
        q_at = pl.multiple_of(qb * BQ, BQ)
        q_blk = q_ref[pl.ds(q_at, BQ), :]
        do_blk = don[pl.ds(q_at, BQ), :]
        len_row = len_ref[pl.ds(qb, 1), :]
        inverse = linv_ref[pl.ds(qb, 1), :]
        mixed = (do_blk.astype(f32) * onat_ref[pl.ds(q_at, BQ), :]).T
        delta = jnp.sum(mixed, axis=0, keepdims=True)
        acc[...] = jnp.zeros_like(acc)

        def tile(kb, masked):
            total = None
            for c in range(BK // SUB):
                k_at = pl.multiple_of(kb * BK + c * SUB, SUB)
                here = pl.ds(k_at, SUB)
                p = jnp.exp2(dot_nt(k_ref[here, :], q_blk)) * inverse
                if masked:
                    p = jnp.where(key_mask(len_row, q_at - k_at), p, 0.0)
                dp = dot_nt(v_ref[here, :], do_blk)
                ds = (p * (dp - delta)).astype(bf16)
                dv[here, :] += dot_nn(p.astype(bf16), do_blk)
                dk[here, :] += dot_nn(ds, q_blk)
                more = dot_tn(k_ref[here, :], ds)
                total = more if total is None else total + more
            acc[...] += total

        key_loops(bounds_ref, qb, q_at, tile)
        dq[pl.ds(q_at, BQ), :] = (acc[...] * SCORE_SCALE).T
        return 0

    lax.fori_loop(0, span // BQ, q_step, 0)
    dk[...] = dk[...] * (1.0 / LOG2_E)


def attend_back(klo, q, k, v, do, onat, linv, lens):
    span = q.shape[0]
    return pl.pallas_call(
        attend_back_kernel,
        in_specs=[pl.BlockSpec(memory_space=pltpu.SMEM)] + [vmem()] * 7,
        out_specs=[vmem()] * 3,
        out_shape=[jax.ShapeDtypeStruct((span, HD), f32)] * 3,
        scratch_shapes=[
            pltpu.VMEM((span, HD), bf16),
            pltpu.VMEM((HD, BQ), f32),
        ],
        compiler_params=pltpu.CompilerParams(vmem_limit_bytes=VMEM_BYTES),
        name="attend_back",
    )(klo, q, k, v, do, onat, linv, lens)


OUT_ROWS = 160
CHUNK_ROWS = 32
N_CHUNKS = 3
CHUNK = FF // N_CHUNKS
Q_WIDTH = H_Q * HD
HALF_OUT = (Q_WIDTH + FF) // 2
HALF_MID = 512
LEFT = HALF_OUT + HALF_MID


def middle_kernel(
    full_ref, mixed_ref, tok_ref, cot_ref, gain_ref, shuffle_ref, gate_ref, up_ref,
    out_ref, dres_ref, dob_ref, left_ref, wide_ref, dgain_ref,
    w_out, resid, mid_low, grad_mid, sems,
):
    step = pl.program_id(0)
    width = tok_ref.shape[1]

    def fetch(i):
        return pltpu.make_async_copy(
            full_ref.at[i, pl.ds(0, OUT_ROWS), :],
            w_out.at[pl.ds(i * OUT_ROWS, OUT_ROWS), :],
            sems.at[i],
        )

    n_fetch = full_ref.shape[0]
    n_first = -(-Q_WIDTH // OUT_ROWS)

    @pl.when(step == 0)
    def _():
        for i in range(n_fetch):
            fetch(i).start()
        for h in range(H_Q):
            left_ref[0, :, h * HD : (h + 1) * HD] = mixed_ref[h]
        for i in range(n_first):
            fetch(i).wait()
        residual = tok_ref[...].astype(f32) + dot_nn(
            left_ref[0, :, :Q_WIDTH], w_out[:Q_WIDTH, :]
        )
        resid[...] = residual
        out_ref[...] = residual
        normed = rms_norm(residual, gain_ref[...]).astype(bf16)
        low = dot_nn(normed, shuffle_ref[...]).astype(bf16)
        mid_low[...] = low
        for side in range(2):
            left_ref[side, :, HALF_OUT:] = low[:, side * HALF_MID : (side + 1) * HALF_MID]
        grad_mid[...] = jnp.zeros_like(grad_mid)
        for i in range(n_first, n_fetch):
            fetch(i).wait()

    for f in range(N_CHUNKS):

        @pl.when(step == f + 1)
        def _(f=f):
            at = Q_WIDTH + f * CHUNK
            gate_w = gate_ref[...].reshape(width, CHUNK)
            up_w = up_ref[...].reshape(width, CHUNK)
            gate = dot_nn(mid_low[...], gate_w)
            up = dot_nn(mid_low[...], up_w)
            sigmoid_gate = 1.0 / (1.0 + jnp.exp(-gate))
            activated = gate * sigmoid_gate
            hidden = (activated * up).astype(bf16)
            cut = min(max(HALF_OUT - at, 0), CHUNK)
            if cut > 0:
                left_ref[0, :, at : at + cut] = hidden[:, :cut]
            if cut < CHUNK:
                left_ref[1, :, at + cut - HALF_OUT : at + CHUNK - HALF_OUT] = hidden[:, cut:]
            down_w = w_out[at : at + CHUNK, :]
            out_ref[...] += dot_nn(hidden, down_w)
            grad_hidden = dot_nt(cot_ref[...], down_w)
            grad_up = (grad_hidden * activated).astype(bf16)
            grad_gate = (
                grad_hidden * up * sigmoid_gate * (1.0 + gate * (1.0 - sigmoid_gate))
            ).astype(bf16)
            wide_ref[:, f * CHUNK : (f + 1) * CHUNK] = grad_gate
            wide_ref[:, FF + f * CHUNK : FF + (f + 1) * CHUNK] = grad_up
            grad_mid[...] += dot_nt(grad_gate, gate_w) + dot_nt(grad_up, up_w)

    @pl.when(step == N_CHUNKS + 1)
    def _():
        grad = dot_nt(grad_mid[...].astype(bf16), shuffle_ref[...])
        part, terms = rms_back(resid[...], gain_ref[...], grad)
        dgain_ref[...] = jnp.sum(terms, axis=0, keepdims=True)
        dres = cot_ref[...].astype(f32) + part
        dres_ref[...] = dres
        low = dres.astype(bf16)
        wide_ref[:, 2 * FF :] = low
        for c in range(4):
            piece = dot_nt(low, w_out[c * 4 * HD : (c + 1) * 4 * HD, :]).astype(bf16)
            for h in range(4):
                dob_ref[4 * c + h] = piece[:, h * HD : (h + 1) * HD]


def middle(full, mixed, tok, cot, gain, shuffle):
    rows, width = tok.shape
    n_blocks = full.shape[0]
    first = OUT_ROWS // CHUNK_ROWS

    def chunk_of(i):
        return jnp.clip(i - 1, 0, N_CHUNKS - 1)

    def whole(shape):
        return pl.BlockSpec(shape, lambda i: (0,) * len(shape))

    chunk = (n_blocks, CHUNK_ROWS, CHUNK)
    return pl.pallas_call(
        middle_kernel,
        grid=(N_CHUNKS + 2,),
        in_specs=[
            pl.BlockSpec(memory_space=pl.ANY),
            whole((H_Q, rows, HD)),
            whole((rows, width)),
            whole((rows, width)),
            whole((1, width)),
            whole((width, width)),
            pl.BlockSpec(chunk, lambda i: (0, first + chunk_of(i), 0)),
            pl.BlockSpec(chunk, lambda i: (0, first + N_CHUNKS + chunk_of(i), 0)),
        ],
        out_specs=[
            whole((rows, width)),
            whole((rows, width)),
            whole((H_Q, rows, HD)),
            whole((2, rows, LEFT)),
            whole((rows, 2 * FF + width)),
            whole((1, width)),
        ],
        out_shape=[
            jax.ShapeDtypeStruct((rows, width), f32),
            jax.ShapeDtypeStruct((rows, width), f32),
            jax.ShapeDtypeStruct((H_Q, rows, HD), bf16),
            jax.ShapeDtypeStruct((2, rows, LEFT), bf16),
            jax.ShapeDtypeStruct((rows, 2 * FF + width), bf16),
            jax.ShapeDtypeStruct((1, width), f32),
        ],
        scratch_shapes=[
            pltpu.VMEM((Q_WIDTH + FF, width), bf16),
            pltpu.VMEM((rows, width), f32),
            pltpu.VMEM((rows, width), bf16),
            pltpu.VMEM((rows, width), f32),
            pltpu.SemaphoreType.DMA((n_blocks,)),
        ],
        compiler_params=pltpu.CompilerParams(vmem_limit_bytes=BIG_VMEM_BYTES),
        name="middle",
    )(full, mixed, tok, cot, gain, shuffle, full, full)


def grad_ffn_kernel(left_a, left_b, right_a, right_b, out_ref):
    total = dot_tn(left_a[...], right_a[...]) + dot_tn(left_b[...], right_b[...])
    out_ref[...] = total.astype(bf16).reshape(out_ref.shape)


def grad_ffn(lefts, wides, n_blocks):
    rows = lefts[0].shape[0]
    left = pl.BlockSpec((rows, HALF_MID), lambda i: (0, HALF_OUT // HALF_MID))
    right = pl.BlockSpec((rows, CHUNK), lambda i: (0, i))
    first = OUT_ROWS // CHUNK_ROWS
    height = OUT_ROWS + 2 * N_CHUNKS * CHUNK_ROWS
    return pl.pallas_call(
        grad_ffn_kernel,
        grid=(2 * N_CHUNKS,),
        in_specs=[left, left, right, right],
        out_specs=pl.BlockSpec((n_blocks, CHUNK_ROWS, CHUNK), lambda i: (0, first + i, 0)),
        out_shape=jax.ShapeDtypeStruct((n_blocks, height, CHUNK), bf16),
        compiler_params=pltpu.CompilerParams(vmem_limit_bytes=VMEM_BYTES),
        name="grad_ffn",
    )(*lefts, *wides)


def grad_out_kernel(core_ref, left_a, left_b, drb_a, drb_b, cot_a, cot_b, grads_ref, out_ref):
    step = pl.program_id(0)
    block = left_a.shape[1]
    both = Q_WIDTH // block
    cut = Q_WIDTH % block
    lower = core_ref[0] == 0

    def store(value):
        out_ref[...] = value.astype(bf16).reshape(out_ref.shape)

    @pl.when(lower & (step < both))
    def _():
        store(dot_tn(left_a[...], drb_a[...]) + dot_tn(left_b[...], drb_b[...]))

    @pl.when(lower & (step == both))
    def _():
        top = dot_tn(left_a[:, :cut], drb_a[...]) + dot_tn(left_b[:, :cut], drb_b[...])
        rest = dot_tn(left_a[:, cut:], cot_a[...]) + dot_tn(left_b[:, cut:], cot_b[...])
        store(jnp.concatenate([top, rest], axis=0))

    @pl.when(core_ref[0] == 1)
    def _():
        store(dot_tn(left_a[...], cot_a[...]) + dot_tn(left_b[...], cot_b[...]))


def grad_out(core, lefts, wides, cots, grads):
    rows, width = cots[0].shape
    blocks = 4
    left = pl.BlockSpec((rows, blocks * OUT_ROWS), lambda i, core: (0, i))
    drb = pl.BlockSpec((rows, width), lambda i, core: (0, 2 * N_CHUNKS))
    cot = pl.BlockSpec((rows, width), lambda i, core: (0, 0))
    return pl.pallas_call(
        grad_out_kernel,
        grid_spec=pltpu.PrefetchScalarGridSpec(
            num_scalar_prefetch=1,
            grid=(grads.shape[0] // blocks,),
            in_specs=[left, left, drb, drb, cot, cot, pl.BlockSpec(memory_space=pl.ANY)],
            out_specs=pl.BlockSpec((blocks, OUT_ROWS, width), lambda i, core: (i, 0, 0)),
        ),
        out_shape=jax.ShapeDtypeStruct(grads.shape, bf16),
        input_output_aliases={7: 0},
        compiler_params=pltpu.CompilerParams(vmem_limit_bytes=VMEM_BYTES),
        name="grad_out",
    )(core, *lefts, *wides, *cots, grads)


def adam_step(master, first_old, second_old, gradient, rate):
    first_new = BETA_ONE * first_old + (1.0 - BETA_ONE) * gradient
    second_new = BETA_TWO * second_old + (1.0 - BETA_TWO) * gradient * gradient
    first_hat = first_new / (1.0 - BETA_ONE**STEP)
    second_hat = second_new / (1.0 - BETA_TWO**STEP)
    master_new = master - rate * (
        first_hat / (jnp.sqrt(second_hat) + ADAM_EPS) + WEIGHT_DECAY * master
    )
    return (first_new, second_new, master_new)


def gathered(x):
    return lax.all_gather(x, AXIS_CYZ, axis=0, tiled=True)


def shift(x, axis, step):
    n = SIZES[axis]
    return lax.ppermute(x, axis, [(i, (i + step) % n) for i in range(n)])


def first_moves(x):
    first, second = x[None, :HALF], x[None, HALF:]
    pair = jnp.concatenate([first, shift(first, "xh", 1)], axis=0)
    ring = jnp.concatenate([second] + [shift(second, "y", b) for b in (1, 2, 3)], axis=0)
    return pair, ring


def second_moves(pair, ring, after):
    one = jnp.concatenate([pair] + [shift(pair, "y", b) for b in (1, 2, 3)], axis=0)
    two = jnp.concatenate([ring, shift(ring, "xh", 1)], axis=0)
    one, two, _ = lax.optimization_barrier((one, two, after))
    return [one, two, shift(one, "core", 1), shift(two, "core", 1)]


def places_of_groups():
    xh, y, core = (lax.axis_index(name) for name in CTX)
    places = []
    for other in range(2):
        for side in range(2):
            for i in range(GROUP):
                b, a = (i // 2, i % 2) if side == 0 else (i % 4, i // 4)
                dev = (((xh + a) % 2) * 4 + (y - b) % 4) * 2 + (core + other) % 2
                places.append(dev if side == 0 else 31 - dev)
    return jnp.stack(places).astype(jnp.int32)


def sum_over_core(near, far):
    return (near.astype(f32) + shift(far, "core", 1).astype(f32)).astype(bf16)


def first_sums(plane):
    one = plane[:GROUP].reshape((4, 2) + plane.shape[1:])
    two = plane[GROUP:].reshape((2, 4) + plane.shape[1:])
    two = (two[0].astype(f32) + shift(two[1], "xh", 1).astype(f32)).astype(bf16)
    one = sum((shift(one[b], "y", -b).astype(f32) for b in (1, 2, 3)), one[0].astype(f32))
    return one.astype(bf16), two


def second_sums(one, two):
    two = sum((shift(two[b], "y", -b).astype(f32) for b in (1, 2, 3)), two[0].astype(f32))
    one = one[0].astype(f32) + shift(one[1], "xh", 1).astype(f32)
    return jnp.concatenate([one, two], axis=0)


def pick(v, i, n):
    return lax.dynamic_index_in_dim(v, lax.rem(i, n), 0, keepdims=False)


def sum_over_x(blocks):
    me = lax.axis_index(AXIS_X)
    n = blocks.shape[0]
    total = pick(blocks, me, n).astype(f32)
    for step in range(1, n):
        moves = [(i, (i + step) % n) for i in range(n)]
        total = total + lax.ppermute(pick(blocks, me + step, n), AXIS_X, moves).astype(f32)
    return total


def sum_at_owners(blocks):
    me = lax.axis_index(AXIS_X)
    n = blocks.shape[0]
    total = 0.0
    for step in range(n):
        moves = []
        for source, place in owner_pairs():
            moves.append((source, place - place % n + (place % n + step) % n))
        total = total + lax.ppermute(pick(blocks, me + step, n), EVERY, moves).astype(f32)
    return total


def natural_of_permuted(x):
    tail = x.shape[1:]
    x = x.reshape((2, 4, 4, 2, 2) + tail)
    x = x.transpose((3, 1, 0, 4, 2) + tuple(range(5, 5 + len(tail))))
    return x.reshape((128,) + tail)


def owner_pairs():
    pairs = []
    for n in range(128):
        z = n % 4
        xl = (n // 4) % 2
        core = (n // 8) % 2
        y = (n // 16) % 4
        xh = n // 64
        pairs.append((n, (((core * 4 + y) * 4 + z) * 2 + xh) * 2 + xl))
    return pairs


def body(
    tokens,
    cotangent,
    segments,
    positions,
    pad_mask,
    w_in,
    w_out,
    gains,
    first_in,
    first_out,
    first_gains,
    second_in,
    second_out,
    second_gains,
):
    rows = tokens.shape[1]
    width = tokens.shape[2]
    span = segments.shape[1]
    half = rows // 2
    n_ctx = span // rows
    q_width = H_Q * HD
    kv_width = H_KV * HD
    attn_cols = q_width + 2 * kv_width
    owned = w_in.shape[0]
    owned_gains = gains.shape[0]

    n_x = 4
    low_in = w_in.astype(bf16)
    n_dev = width // owned

    own_head = jnp.concatenate(
        [
            low_in[:, :q_width].reshape(owned, H_Q, HD),
            jnp.repeat(low_in[:, q_width : q_width + kv_width].reshape(owned, H_KV, HD), 2, axis=1),
            jnp.repeat(low_in[:, q_width + kv_width : attn_cols].reshape(owned, H_KV, HD), 2, axis=1),
            jnp.broadcast_to(
                jnp.pad(gains.astype(bf16)[None, None], ((0, owned - 1), (0, 0), (0, HD - owned_gains))),
                (owned, H_Q, HD),
            ),
        ],
        axis=2,
    ).transpose(1, 0, 2)
    pair, ring = first_moves(tokens[0])
    head = lax.all_to_all(own_head, CTX, 0, 0, tiled=True)
    head = lax.all_gather(head, SHARD, axis=0, tiled=False)
    pairs = owner_pairs()
    own_out = lax.ppermute(w_out.astype(bf16), EVERY, [(p, n) for n, p in pairs])
    own_ffn = low_in[:, attn_cols:].reshape(owned, 2 * N_CHUNKS, CHUNK)
    own_ffn = own_ffn.transpose(1, 0, 2).reshape(2 * N_CHUNKS * owned, CHUNK)
    own_rest = jnp.concatenate([own_out, own_ffn], axis=0)
    own_rest = lax.all_gather(own_rest, AXIS_X, axis=0, tiled=False)
    segments, pad_mask, own_rest, pair, ring = lax.optimization_barrier(
        (segments, pad_mask, own_rest, pair, ring)
    )
    head = head.reshape((2, 4) + own_head.shape).transpose(2, 0, 1, 3, 4)
    gain_vals = head[:, :, :, 0, HEAD_COLS : HEAD_COLS + owned_gains].reshape(-1).astype(f32)
    w_head = head[..., :HEAD_COLS].reshape(width, HEAD_COLS)
    gain_one = gain_vals[:width]
    gain_two = gain_vals[width : 2 * width]
    gain_query = gain_vals[2 * width : 2 * width + HD].reshape(1, HD)
    gain_key = gain_vals[2 * width + HD :].reshape(1, HD)
    w_scaled = (w_head.astype(f32) * gain_one[:, None]).astype(bf16)

    n_out = w_out.shape[0]
    part_out = own_rest[:, :n_out].reshape(n_x * n_out, width)
    part_ffn = own_rest[:, n_out:].reshape(n_x, 2 * N_CHUNKS, owned, CHUNK).transpose(1, 0, 2, 3)
    part_ffn = part_ffn.reshape(2 * N_CHUNKS * CHUNK_ROWS, CHUNK)
    full = gathered(jnp.concatenate([part_out, part_ffn], axis=0)[None])

    order = natural_of_permuted(jnp.arange(width, dtype=jnp.int32).reshape(n_dev, owned)).reshape(-1)
    shuffle = (order[:, None] == jnp.arange(width, dtype=jnp.int32)[None, :]).astype(bf16)

    def natural(x):
        x = x.reshape(n_ctx, 2, half)
        return jnp.concatenate([x[:, 0], x[::-1, 1]], axis=0)

    halves = jnp.arange(HD // 2, dtype=f32)
    inverse = ROPE_BASE ** (-2.0 * halves / HD)
    cos, sin, lens = tables(
        natural(segments[0]), natural(pad_mask[0]), jnp.concatenate([inverse, inverse])[None]
    )
    first_key = (jnp.arange(span, dtype=jnp.int32).reshape(lens.shape) - lens).reshape(span // BQ, BQ)
    klo = jnp.stack(
        [jnp.min(first_key, axis=1) // BK, (jnp.max(first_key, axis=1) + BK - 1) // BK]
    )
    lens = lens.reshape(span // BQ, BQ)

    groups = second_moves(pair, ring, (cos, klo, lens))
    place = places_of_groups()
    q, k, v, query_raw, key_raw, inv = project(
        place, groups, w_scaled, cos, sin, gain_query, gain_key
    )
    o_send, o_nat, l_inv = attend(klo, q, k, v, lens, rows)
    mixed = lax.all_to_all(o_send, CTX, 0, 0, tiled=True)

    output, grad_residual, do_send, left, wide, gain_two_terms = middle(
        full, mixed, tokens[0], cotangent[0], gain_two.reshape(1, width), shuffle
    )
    core = lax.axis_index("core")
    lefts = (pick(left, core, 2), shift(pick(left, core + 1, 2), "core", 1))
    wides = (wide, shift(wide, "core", 1))
    cots = (cotangent[0], shift(cotangent[0], "core", 1))
    grads = grad_ffn(lefts, wides, full.shape[0] // 2)
    grads = grad_out(core.astype(jnp.int32).reshape(1), lefts, wides, cots, grads)
    do = lax.all_to_all(do_send, CTX, 0, 0, tiled=True)
    do, grads = lax.optimization_barrier((do, grads))
    grads = grads.reshape(-1, width)
    grads = lax.psum_scatter(grads, AXIS_YZ, scatter_dimension=0, tiled=True)

    head_grads = attend_back(klo, q, k, v, do, o_nat, l_inv, lens)
    da_near, da_far, dw_head, gain_qk = project_back(
        place, groups, head_grads, (query_raw, key_raw, inv), cos, sin, gain_query, gain_key, w_head
    )

    gain_one_grad = jnp.sum(dw_head * w_head.astype(f32), axis=1)
    grad_gains = jnp.concatenate([gain_one_grad, gain_two_terms[0], gain_qk[0], gain_qk[1]])
    grad_gains = jnp.pad(
        grad_gains.reshape(n_dev, 1, owned_gains), ((0, 0), (0, owned - 1), (0, HD - owned_gains))
    )
    dw_head = (dw_head * gain_one[:, None]).reshape(n_dev, owned, HEAD_COLS)
    dw_head = jnp.concatenate([dw_head, grad_gains], axis=2).astype(bf16)
    dw_head = dw_head.reshape(n_ctx, n_dev // n_ctx, owned, PAD_COLS).transpose(1, 0, 2, 3)
    plane = sum_over_core(da_near, da_far)
    dw_head, _ = lax.optimization_barrier((dw_head, plane))
    dw_head = lax.all_to_all(dw_head, SHARD, 0, 0, tiled=True)
    dw_head = jnp.sum(dw_head.astype(f32), axis=0).astype(bf16)
    one, two = first_sums(plane)

    out_part = grads[:OUT_ROWS].reshape(n_x, OUT_ROWS // n_x, width)
    ffn_part = grads[OUT_ROWS:].reshape(2 * N_CHUNKS, n_x, owned, CHUNK)
    ffn_part = ffn_part.transpose(1, 0, 2, 3).reshape(n_x, 2 * N_CHUNKS * owned, CHUNK)
    owned_out = sum_at_owners(out_part)
    owned_ffn = sum_over_x(ffn_part).reshape(2 * N_CHUNKS, owned, CHUNK)
    one, two, owned_out, owned_ffn = lax.optimization_barrier((one, two, owned_out, owned_ffn))

    dw_head, _, _ = lax.optimization_barrier((dw_head, one, two))
    dw_head = lax.all_to_all(dw_head, CTX, 0, 0, tiled=True).astype(f32)
    owned_gain_grad = jnp.sum(dw_head[:, 0, HEAD_COLS : HEAD_COLS + owned_gains], axis=0)

    grad_a = second_sums(one, two)
    inputs = tokens[0].astype(f32)
    input_grad = grad_residual + rms_back(inputs, gain_one, grad_a)[0]

    def columns(x):
        return x.transpose(1, 0, 2).reshape(owned, -1)

    def over_pair(x):
        return columns(jnp.sum(x.reshape(H_KV, 2, owned, HD), axis=1))

    owned_in = jnp.concatenate(
        [
            columns(dw_head[:, :, :HD]),
            over_pair(dw_head[:, :, HD : 2 * HD]),
            over_pair(dw_head[:, :, 2 * HD : HEAD_COLS]),
            columns(owned_ffn),
        ],
        axis=1,
    )
    new_first_in, new_second_in, new_master_in = adam_step(
        w_in, first_in, second_in, owned_in, RATE_MATRIX
    )
    new_first_out, new_second_out, new_master_out = adam_step(
        w_out, first_out, second_out, owned_out, RATE_MATRIX
    )
    new_first_gains, new_second_gains, new_master_gains = adam_step(
        gains, first_gains, second_gains, owned_gain_grad, RATE_GAIN
    )
    return (
        output[None],
        input_grad[None],
        new_first_in,
        new_first_out,
        new_first_gains,
        new_second_in,
        new_second_out,
        new_second_gains,
        new_master_in,
        new_master_out,
        new_master_gains,
        new_master_in.astype(bf16),
        new_master_out.astype(bf16),
    )


def solution(mesh):
    cut = Mesh(mesh.devices.reshape(tuple(SIZES[name] for name in EVERY)), EVERY)
    weights = P(EVERY, None)
    vector = P(EVERY)
    acts = P(SHARD, CTX, None)
    in_specs = (
        acts,
        acts,
        P(SHARD, None),
        P(SHARD, CTX),
        P(SHARD, None),
    ) + (weights, weights, vector) * 3
    out_specs = (acts, acts) + (weights, weights, vector) * 3 + (weights, weights)
    return jax.shard_map(body, mesh=cut, in_specs=in_specs, out_specs=out_specs, check_vma=False)
```

```python
import functools
import math

import jax
import jax.numpy as jnp
from jax import lax
from jax.experimental import pallas as pl
from jax.experimental.pallas import tpu as pltpu
from jax.sharding import Mesh
from jax.sharding import PartitionSpec as P

H_Q = 16
H_KV = 8
HD = 128
FF = 3072
STEP = 5

NORM_EPS = 1e-06
ROPE_BASE = 1000000.0
BETA_ONE = 0.5
BETA_TWO = 0.5
ADAM_EPS = 1e-08
WEIGHT_DECAY = 0.1
RATE_MATRIX = 0.03
RATE_GAIN = 0.25

CTX = ("xh", "y", "core")
SHARD = ("xl", "z")
EVERY = CTX + SHARD
AXIS_X = ("xh", "xl")
AXIS_YZ = ("y", "z")
AXIS_CYZ = ("core", "y", "z")
SIZES = {"xh": 2, "y": 4, "core": 2, "xl": 2, "z": 4}

LOG2_E = 1.4426950408889634
SCORE_SCALE = 1.0 / math.sqrt(HD)
BQ = 512
BK = 512
SUB = 256
VMEM_BYTES = 48 * 1024 * 1024
BIG_VMEM_BYTES = 60 * 1024 * 1024

bf16 = jnp.bfloat16
f32 = jnp.float32


def rms_norm(values, weight):
    return values * lax.rsqrt(jnp.mean(values * values, axis=-1, keepdims=True) + NORM_EPS) * weight


def rms_back(values, weight, upstream):
    inverse = lax.rsqrt(jnp.mean(values * values, axis=-1, keepdims=True) + NORM_EPS)
    normed = values * inverse
    scaled = upstream * weight
    grad_values = inverse * (scaled - normed * jnp.mean(scaled * normed, axis=-1, keepdims=True))
    return (grad_values, upstream * normed)


def dot_nt(a, b):
    return lax.dot_general(a, b, (((1,), (1,)), ((), ())), preferred_element_type=f32)


def dot_tn(a, b):
    return lax.dot_general(a, b, (((0,), (0,)), ((), ())), preferred_element_type=f32)


def dot_nn(a, b):
    return lax.dot_general(a, b, (((1,), (0,)), ((), ())), preferred_element_type=f32)


LAST_DOC = 13


def tables_kernel(docs_ref, live_ref, freq_ref, cos_ref, sin_ref, lens_ref):
    docs = docs_ref[...]
    shape = docs.shape
    start = jnp.zeros(shape, f32)
    for number in range(1, LAST_DOC + 1):
        before = jnp.sum(jnp.where(docs < number, 1.0, 0.0))
        start = jnp.where(docs == number, before, start)
    at = lax.broadcasted_iota(jnp.int32, shape, 0) * shape[1] + lax.broadcasted_iota(
        jnp.int32, shape, 1
    )
    within = at.astype(f32) - start
    lens_ref[...] = jnp.where(live_ref[...] == 1, within.astype(jnp.int32), 0)

    left = lax.broadcasted_iota(jnp.int32, (HD, HD), 1) < HD // 2
    for i in range(0, shape[0], 2):
        cols = [jnp.broadcast_to(within[i + n : i + n + 1, :], (HD, HD)).T for n in range(2)]
        angle = jnp.where(left, cols[0], cols[1]) * freq_ref[...]
        for ref, values, flip in ((cos_ref, jnp.cos(angle), False), (sin_ref, jnp.sin(angle), True)):
            turned = pltpu.roll(values, HD // 2, 1)
            for n in range(2):
                lower, upper = (values, turned) if n == 0 else (turned, values)
                ref[(i + n) * HD : (i + n + 1) * HD, :] = jnp.where(
                    left, -lower if flip else lower, upper
                )


def tables(docs, live, freq):
    span = docs.size
    table = jax.ShapeDtypeStruct((span, HD), f32)
    return pl.pallas_call(
        tables_kernel,
        in_specs=[vmem()] * 3,
        out_specs=[vmem()] * 3,
        out_shape=[table, table, jax.ShapeDtypeStruct(docs.shape, jnp.int32)],
        compiler_params=pltpu.CompilerParams(vmem_limit_bytes=VMEM_BYTES),
        cost_estimate=pl.CostEstimate(
            flops=100 * span * HD, bytes_accessed=3 * span * HD * 4, transcendentals=span * HD
        ),
        name="tables",
    )(docs, live, freq)


N_GROUPS = 4
GROUP = 8
HALF = 128
STEP_BLOCKS = 4
STEPS = GROUP // STEP_BLOCKS
HEAD_COLS = 3 * HD
PAD_COLS = 4 * HD


def block_spec(width, first, count):
    return pl.BlockSpec(
        (STEP_BLOCKS, HALF, width), lambda i, place: (jnp.clip(i - first, 0, count - 1), 0, 0)
    )


def group_specs(width):
    return [block_spec(width, k * STEPS, STEPS) for k in range(N_GROUPS)]


def fixed(shape):
    return pl.BlockSpec(shape, lambda i, place: (0,) * len(shape))


def rows_of(place_ref, step, i):
    return pl.ds(pl.multiple_of(place_ref[step * STEP_BLOCKS + i] * HALF, HALF), HALF)


def head_mean(x):
    return lax.dot_general(
        x.astype(bf16),
        jnp.full((HD, HD), 1.0 / HD, bf16),
        (((1,), (0,)), ((), ())),
        preferred_element_type=f32,
    )


def project_kernel(
    place_ref, x0, x1, x2, x3, w_ref, cos_ref, sin_ref, gq_ref, gk_ref,
    q_ref, k_ref, v_ref, qraw_ref, kraw_ref, inv_ref,
):
    step = pl.program_id(0)

    def run(x):
        wide = x.astype(f32)
        inverse = lax.rsqrt(jnp.mean(wide * wide, axis=-1, keepdims=True) + NORM_EPS)
        prod = dot_nn(x, w_ref[...]) * inverse
        for i in range(STEP_BLOCKS):
            at = rows_of(place_ref, step, i)
            part = slice(i * HALF, (i + 1) * HALF)
            cos = cos_ref[at, :]
            sin = sin_ref[at, :]

            def roped(raw, gain, cos=cos, sin=sin):
                normed = raw * lax.rsqrt(head_mean(raw * raw) + NORM_EPS) * gain
                return normed * cos + pltpu.roll(normed, HD // 2, 1) * sin

            query = prod[part, :HD]
            key = prod[part, HD : 2 * HD]
            inv_ref[at, :] = jnp.broadcast_to(inverse[part], (HALF, HD)).astype(bf16)
            qraw_ref[at, :] = query.astype(bf16)
            kraw_ref[at, :] = key.astype(bf16)
            q_ref[at, :] = (roped(query, gq_ref[...]) * (SCORE_SCALE * LOG2_E)).astype(bf16)
            k_ref[at, :] = roped(key, gk_ref[...]).astype(bf16)
            v_ref[at, :] = prod[part, 2 * HD :].astype(bf16)

    for k, x_ref in enumerate((x0, x1, x2, x3)):

        @pl.when(step // STEPS == k)
        def _(x_ref=x_ref):
            run(x_ref[...].reshape(STEP_BLOCKS * HALF, x_ref.shape[2]))


def project(place, groups, w, cos, sin, gq, gk):
    width = w.shape[0]
    span = cos.shape[0]
    low = jax.ShapeDtypeStruct((span, HD), bf16)
    whole = fixed((span, HD))
    return pl.pallas_call(
        project_kernel,
        grid_spec=pltpu.PrefetchScalarGridSpec(
            num_scalar_prefetch=1,
            grid=(N_GROUPS * STEPS,),
            in_specs=group_specs(width)
            + [fixed((width, HEAD_COLS)), whole, whole, fixed((1, HD)), fixed((1, HD))],
            out_specs=[whole] * 6,
        ),
        out_shape=[low] * 6,
        compiler_params=pltpu.CompilerParams(vmem_limit_bytes=VMEM_BYTES),
        name="project",
    )(place, *groups, w, cos, sin, gq, gk)


def project_back_kernel(
    place_ref, x0, x1, x2, x3, dq_ref, dk_ref, dv_ref, qraw_ref, kraw_ref, inv_ref, cos_ref, sin_ref,
    gq_ref, gk_ref, w_ref, near_ref, far_ref, dw_ref, dg_ref, grads, scaled,
):
    step = pl.program_id(0)

    @pl.when(step == 0)
    def _():
        dw_ref[...] = jnp.zeros_like(dw_ref)
        dg_ref[...] = jnp.zeros_like(dg_ref)

    def run(x, da_ref):
        q_sum = jnp.zeros((1, HD), f32)
        k_sum = jnp.zeros((1, HD), f32)
        for i in range(STEP_BLOCKS):
            at = rows_of(place_ref, step, i)
            part = slice(i * HALF, (i + 1) * HALF)
            cos = cos_ref[at, :]
            sin = sin_ref[at, :]

            def back(raw, gain, grad, cos=cos, sin=sin):
                unrot = grad * cos + pltpu.roll(grad * sin, HD // 2, 1)
                inv_rms = lax.rsqrt(head_mean(raw * raw) + NORM_EPS)
                normed = raw * inv_rms
                scaled_up = unrot * gain
                grad = inv_rms * (scaled_up - normed * head_mean(scaled_up * normed))
                return grad, unrot * normed

            grad_q, q_terms = back(qraw_ref[at, :].astype(f32), gq_ref[...], dq_ref[at, :])
            grad_k, k_terms = back(kraw_ref[at, :].astype(f32), gk_ref[...], dk_ref[at, :])
            inverse = inv_ref[at, :].astype(f32)
            for c, grad in enumerate((grad_q, grad_k, dv_ref[at, :])):
                grads[part, c * HD : (c + 1) * HD] = grad.astype(bf16)
                scaled[part, c * HD : (c + 1) * HD] = (grad * inverse).astype(bf16)
            q_sum = q_sum + jnp.sum(q_terms, axis=0, keepdims=True)
            k_sum = k_sum + jnp.sum(k_terms, axis=0, keepdims=True)
        da_ref[...] = dot_nt(grads[...], w_ref[...]).astype(bf16).reshape(da_ref.shape)
        dw_ref[...] += dot_tn(x, scaled[...])
        dg_ref[0:1, :] += q_sum
        dg_ref[1:2, :] += k_sum

    for k, x_ref in enumerate((x0, x1, x2, x3)):

        @pl.when(step // STEPS == k)
        def _(k=k, x_ref=x_ref):
            da_ref = near_ref if k < N_GROUPS // 2 else far_ref
            run(x_ref[...].reshape(STEP_BLOCKS * HALF, x_ref.shape[2]), da_ref)


def project_back(place, groups, grads, raws, cos, sin, gq, gk, w):
    width = w.shape[0]
    span = cos.shape[0]
    whole = fixed((span, HD))
    n_half = N_GROUPS // 2
    da = jax.ShapeDtypeStruct((n_half * GROUP, HALF, width), bf16)
    return pl.pallas_call(
        project_back_kernel,
        grid_spec=pltpu.PrefetchScalarGridSpec(
            num_scalar_prefetch=1,
            grid=(N_GROUPS * STEPS,),
            in_specs=group_specs(width)
            + [whole] * 8
            + [fixed((1, HD)), fixed((1, HD)), fixed((width, HEAD_COLS))],
            out_specs=[
                block_spec(width, 0, n_half * STEPS),
                block_spec(width, n_half * STEPS, n_half * STEPS),
                fixed((width, HEAD_COLS)),
                fixed((8, HD)),
            ],
            scratch_shapes=[
                pltpu.VMEM((STEP_BLOCKS * HALF, HEAD_COLS), bf16),
                pltpu.VMEM((STEP_BLOCKS * HALF, HEAD_COLS), bf16),
            ],
        ),
        out_shape=[
            da,
            da,
            jax.ShapeDtypeStruct((width, HEAD_COLS), f32),
            jax.ShapeDtypeStruct((8, HD), f32),
        ],
        compiler_params=pltpu.CompilerParams(vmem_limit_bytes=BIG_VMEM_BYTES),
        name="project_back",
    )(place, *groups, *grads, *raws, cos, sin, gq, gk, w)


def dealt_slot(place, n_dev):
    if place < n_dev:
        return place, 0
    return 2 * n_dev - 1 - place, 1


def key_mask(len_row, offset):
    ahead = (
        lax.broadcasted_iota(jnp.int32, (SUB, BQ), 1)
        - lax.broadcasted_iota(jnp.int32, (SUB, BQ), 0)
        + offset
    )
    return (ahead >= 0) & (ahead <= len_row)


def key_loops(bounds_ref, qb, q_at, tile):
    low = bounds_ref[0, qb]
    high = (q_at + BQ - 1) // BK + 1
    first = jnp.minimum(bounds_ref[1, qb], high)
    last = jnp.maximum((q_at + 1) // BK, first)

    def run(masked):
        def step(kb, _):
            tile(kb, masked)
            return 0

        return step

    lax.fori_loop(low, first, run(True), 0)
    lax.fori_loop(first, last, run(False), 0)
    lax.fori_loop(last, high, run(True), 0)


def attend_kernel(
    bounds_ref, q_ref, k_ref, v_ref, len_ref, osend_ref, onat_ref, linv_ref, acc, total
):
    n_dev, rows, _ = osend_ref.shape
    half = rows // 2
    span = q_ref.shape[0]
    def q_step(qb, _):
        q_at = pl.multiple_of(qb * BQ, BQ)
        q_blk = q_ref[pl.ds(q_at, BQ), :]
        len_row = len_ref[pl.ds(qb, 1), :]
        acc[...] = jnp.zeros_like(acc)
        total[...] = jnp.zeros_like(total)

        def tile(kb, masked):
            mixed = None
            summed = None
            for c in range(BK // SUB):
                k_at = pl.multiple_of(kb * BK + c * SUB, SUB)
                p = jnp.exp2(dot_nt(k_ref[pl.ds(k_at, SUB), :], q_blk))
                if masked:
                    p = jnp.where(key_mask(len_row, q_at - k_at), p, 0.0)
                part = jnp.sum(p.reshape(SUB // 8, 8, BQ), axis=0)
                more = dot_tn(v_ref[pl.ds(k_at, SUB), :], p.astype(bf16))
                summed = part if summed is None else summed + part
                mixed = more if mixed is None else mixed + more
            acc[...] += mixed
            total[...] += summed

        key_loops(bounds_ref, qb, q_at, tile)
        inverse = 1.0 / jnp.sum(total[...], axis=0, keepdims=True)
        linv_ref[pl.ds(qb, 1), :] = inverse
        onat_ref[pl.ds(q_at, BQ), :] = (acc[...] * inverse).T
        return 0

    lax.fori_loop(0, span // BQ, q_step, 0)
    for place in range(2 * n_dev):
        dev, side = dealt_slot(place, n_dev)
        osend_ref[dev, side * half : (side + 1) * half, :] = onat_ref[
            place * half : (place + 1) * half, :
        ].astype(bf16)


def vmem():
    return pl.BlockSpec(memory_space=pltpu.VMEM)


def attend(klo, q, k, v, lens, rows):
    span = q.shape[0]
    return pl.pallas_call(
        attend_kernel,
        in_specs=[pl.BlockSpec(memory_space=pltpu.SMEM)] + [vmem()] * 4,
        out_specs=[vmem(), vmem(), vmem()],
        out_shape=[
            jax.ShapeDtypeStruct((span // rows, rows, HD), bf16),
            jax.ShapeDtypeStruct((span, HD), f32),
            jax.ShapeDtypeStruct((span // BQ, BQ), f32),
        ],
        scratch_shapes=[
            pltpu.VMEM((HD, BQ), f32),
            pltpu.VMEM((8, BQ), f32),
        ],
        compiler_params=pltpu.CompilerParams(vmem_limit_bytes=VMEM_BYTES),
        name="attend",
    )(klo, q, k, v, lens)


def attend_back_kernel(
    bounds_ref, q_ref, k_ref, v_ref, do_ref, onat_ref, linv_ref, len_ref, dq, dk, dv, don, acc
):
    n_dev, rows, _ = do_ref.shape
    half = rows // 2
    span = q_ref.shape[0]
    for place in range(2 * n_dev):
        dev, side = dealt_slot(place, n_dev)
        to = slice(place * half, (place + 1) * half)
        don[to, :] = do_ref[dev, side * half : (side + 1) * half, :]
    dk[...] = jnp.zeros_like(dk)
    dv[...] = jnp.zeros_like(dv)

    def q_step(qb, _):
        q_at = pl.multiple_of(qb * BQ, BQ)
        q_blk = q_ref[pl.ds(q_at, BQ), :]
        do_blk = don[pl.ds(q_at, BQ), :]
        len_row = len_ref[pl.ds(qb, 1), :]
        inverse = linv_ref[pl.ds(qb, 1), :]
        mixed = (do_blk.astype(f32) * onat_ref[pl.ds(q_at, BQ), :]).T
        delta = jnp.sum(mixed, axis=0, keepdims=True)
        acc[...] = jnp.zeros_like(acc)

        def tile(kb, masked):
            total = None
            for c in range(BK // SUB):
                k_at = pl.multiple_of(kb * BK + c * SUB, SUB)
                here = pl.ds(k_at, SUB)
                p = jnp.exp2(dot_nt(k_ref[here, :], q_blk)) * inverse
                if masked:
                    p = jnp.where(key_mask(len_row, q_at - k_at), p, 0.0)
                dp = dot_nt(v_ref[here, :], do_blk)
                ds = (p * (dp - delta)).astype(bf16)
                dv[here, :] += dot_nn(p.astype(bf16), do_blk)
                dk[here, :] += dot_nn(ds, q_blk)
                more = dot_tn(k_ref[here, :], ds)
                total = more if total is None else total + more
            acc[...] += total

        key_loops(bounds_ref, qb, q_at, tile)
        dq[pl.ds(q_at, BQ), :] = (acc[...] * SCORE_SCALE).T
        return 0

    lax.fori_loop(0, span // BQ, q_step, 0)
    dk[...] = dk[...] * (1.0 / LOG2_E)


def attend_back(klo, q, k, v, do, onat, linv, lens):
    span = q.shape[0]
    return pl.pallas_call(
        attend_back_kernel,
        in_specs=[pl.BlockSpec(memory_space=pltpu.SMEM)] + [vmem()] * 7,
        out_specs=[vmem()] * 3,
        out_shape=[jax.ShapeDtypeStruct((span, HD), f32)] * 3,
        scratch_shapes=[
            pltpu.VMEM((span, HD), bf16),
            pltpu.VMEM((HD, BQ), f32),
        ],
        compiler_params=pltpu.CompilerParams(vmem_limit_bytes=VMEM_BYTES),
        name="attend_back",
    )(klo, q, k, v, do, onat, linv, lens)


OUT_ROWS = 160
CHUNK_ROWS = 32
N_CHUNKS = 3
CHUNK = FF // N_CHUNKS
Q_WIDTH = H_Q * HD
HALF_OUT = (Q_WIDTH + FF) // 2
HALF_MID = 512
LEFT = HALF_OUT + HALF_MID


def middle_kernel(
    full_ref, mixed_ref, tok_ref, cot_ref, gain_ref, shuffle_ref, gate_ref, up_ref,
    out_ref, dres_ref, dob_ref, left_ref, wide_ref, dgain_ref,
    w_out, resid, mid_low, grad_mid, sems,
):
    step = pl.program_id(0)
    width = tok_ref.shape[1]

    def fetch(i):
        return pltpu.make_async_copy(
            full_ref.at[i, pl.ds(0, OUT_ROWS), :],
            w_out.at[pl.ds(i * OUT_ROWS, OUT_ROWS), :],
            sems.at[i],
        )

    n_fetch = full_ref.shape[0]
    n_first = -(-Q_WIDTH // OUT_ROWS)

    @pl.when(step == 0)
    def _():
        for i in range(n_fetch):
            fetch(i).start()
        for h in range(H_Q):
            left_ref[0, :, h * HD : (h + 1) * HD] = mixed_ref[h]
        for i in range(n_first):
            fetch(i).wait()
        residual = tok_ref[...].astype(f32) + dot_nn(
            left_ref[0, :, :Q_WIDTH], w_out[:Q_WIDTH, :]
        )
        resid[...] = residual
        out_ref[...] = residual
        normed = rms_norm(residual, gain_ref[...]).astype(bf16)
        low = dot_nn(normed, shuffle_ref[...]).astype(bf16)
        mid_low[...] = low
        for side in range(2):
            left_ref[side, :, HALF_OUT:] = low[:, side * HALF_MID : (side + 1) * HALF_MID]
        grad_mid[...] = jnp.zeros_like(grad_mid)
        for i in range(n_first, n_fetch):
            fetch(i).wait()

    for f in range(N_CHUNKS):

        @pl.when(step == f + 1)
        def _(f=f):
            at = Q_WIDTH + f * CHUNK
            gate_w = gate_ref[...].reshape(width, CHUNK)
            up_w = up_ref[...].reshape(width, CHUNK)
            gate = dot_nn(mid_low[...], gate_w)
            up = dot_nn(mid_low[...], up_w)
            sigmoid_gate = 1.0 / (1.0 + jnp.exp(-gate))
            activated = gate * sigmoid_gate
            hidden = (activated * up).astype(bf16)
            cut = min(max(HALF_OUT - at, 0), CHUNK)
            if cut > 0:
                left_ref[0, :, at : at + cut] = hidden[:, :cut]
            if cut < CHUNK:
                left_ref[1, :, at + cut - HALF_OUT : at + CHUNK - HALF_OUT] = hidden[:, cut:]
            down_w = w_out[at : at + CHUNK, :]
            out_ref[...] += dot_nn(hidden, down_w)
            grad_hidden = dot_nt(cot_ref[...], down_w)
            grad_up = (grad_hidden * activated).astype(bf16)
            grad_gate = (
                grad_hidden * up * sigmoid_gate * (1.0 + gate * (1.0 - sigmoid_gate))
            ).astype(bf16)
            wide_ref[:, f * CHUNK : (f + 1) * CHUNK] = grad_gate
            wide_ref[:, FF + f * CHUNK : FF + (f + 1) * CHUNK] = grad_up
            grad_mid[...] += dot_nt(grad_gate, gate_w) + dot_nt(grad_up, up_w)

    @pl.when(step == N_CHUNKS + 1)
    def _():
        grad = dot_nt(grad_mid[...].astype(bf16), shuffle_ref[...])
        part, terms = rms_back(resid[...], gain_ref[...], grad)
        dgain_ref[...] = jnp.sum(terms, axis=0, keepdims=True)
        dres = cot_ref[...].astype(f32) + part
        dres_ref[...] = dres
        low = dres.astype(bf16)
        wide_ref[:, 2 * FF :] = low
        for c in range(4):
            piece = dot_nt(low, w_out[c * 4 * HD : (c + 1) * 4 * HD, :]).astype(bf16)
            for h in range(4):
                dob_ref[4 * c + h] = piece[:, h * HD : (h + 1) * HD]


def middle(full, mixed, tok, cot, gain, shuffle):
    rows, width = tok.shape
    n_blocks = full.shape[0]
    first = OUT_ROWS // CHUNK_ROWS

    def chunk_of(i):
        return jnp.clip(i - 1, 0, N_CHUNKS - 1)

    def whole(shape):
        return pl.BlockSpec(shape, lambda i: (0,) * len(shape))

    chunk = (n_blocks, CHUNK_ROWS, CHUNK)
    return pl.pallas_call(
        middle_kernel,
        grid=(N_CHUNKS + 2,),
        in_specs=[
            pl.BlockSpec(memory_space=pl.ANY),
            whole((H_Q, rows, HD)),
            whole((rows, width)),
            whole((rows, width)),
            whole((1, width)),
            whole((width, width)),
            pl.BlockSpec(chunk, lambda i: (0, first + chunk_of(i), 0)),
            pl.BlockSpec(chunk, lambda i: (0, first + N_CHUNKS + chunk_of(i), 0)),
        ],
        out_specs=[
            whole((rows, width)),
            whole((rows, width)),
            whole((H_Q, rows, HD)),
            whole((2, rows, LEFT)),
            whole((rows, 2 * FF + width)),
            whole((1, width)),
        ],
        out_shape=[
            jax.ShapeDtypeStruct((rows, width), f32),
            jax.ShapeDtypeStruct((rows, width), f32),
            jax.ShapeDtypeStruct((H_Q, rows, HD), bf16),
            jax.ShapeDtypeStruct((2, rows, LEFT), bf16),
            jax.ShapeDtypeStruct((rows, 2 * FF + width), bf16),
            jax.ShapeDtypeStruct((1, width), f32),
        ],
        scratch_shapes=[
            pltpu.VMEM((Q_WIDTH + FF, width), bf16),
            pltpu.VMEM((rows, width), f32),
            pltpu.VMEM((rows, width), bf16),
            pltpu.VMEM((rows, width), f32),
            pltpu.SemaphoreType.DMA((n_blocks,)),
        ],
        compiler_params=pltpu.CompilerParams(vmem_limit_bytes=BIG_VMEM_BYTES),
        name="middle",
    )(full, mixed, tok, cot, gain, shuffle, full, full)


def grad_ffn_kernel(left_a, left_b, right_a, right_b, out_ref):
    total = dot_tn(left_a[...], right_a[...]) + dot_tn(left_b[...], right_b[...])
    out_ref[...] = total.astype(bf16).reshape(out_ref.shape)


def grad_ffn(lefts, wides, n_blocks):
    rows = lefts[0].shape[0]
    left = pl.BlockSpec((rows, HALF_MID), lambda i: (0, HALF_OUT // HALF_MID))
    right = pl.BlockSpec((rows, CHUNK), lambda i: (0, i))
    first = OUT_ROWS // CHUNK_ROWS
    height = OUT_ROWS + 2 * N_CHUNKS * CHUNK_ROWS
    return pl.pallas_call(
        grad_ffn_kernel,
        grid=(2 * N_CHUNKS,),
        in_specs=[left, left, right, right],
        out_specs=pl.BlockSpec((n_blocks, CHUNK_ROWS, CHUNK), lambda i: (0, first + i, 0)),
        out_shape=jax.ShapeDtypeStruct((n_blocks, height, CHUNK), bf16),
        compiler_params=pltpu.CompilerParams(vmem_limit_bytes=VMEM_BYTES),
        name="grad_ffn",
    )(*lefts, *wides)


def grad_out_kernel(core_ref, left_a, left_b, drb_a, drb_b, cot_a, cot_b, grads_ref, out_ref):
    step = pl.program_id(0)
    block = left_a.shape[1]
    both = Q_WIDTH // block
    cut = Q_WIDTH % block
    lower = core_ref[0] == 0

    def store(value):
        out_ref[...] = value.astype(bf16).reshape(out_ref.shape)

    @pl.when(lower & (step < both))
    def _():
        store(dot_tn(left_a[...], drb_a[...]) + dot_tn(left_b[...], drb_b[...]))

    @pl.when(lower & (step == both))
    def _():
        top = dot_tn(left_a[:, :cut], drb_a[...]) + dot_tn(left_b[:, :cut], drb_b[...])
        rest = dot_tn(left_a[:, cut:], cot_a[...]) + dot_tn(left_b[:, cut:], cot_b[...])
        store(jnp.concatenate([top, rest], axis=0))

    @pl.when(core_ref[0] == 1)
    def _():
        store(dot_tn(left_a[...], cot_a[...]) + dot_tn(left_b[...], cot_b[...]))


def grad_out(core, lefts, wides, cots, grads):
    rows, width = cots[0].shape
    blocks = 4
    left = pl.BlockSpec((rows, blocks * OUT_ROWS), lambda i, core: (0, i))
    drb = pl.BlockSpec((rows, width), lambda i, core: (0, 2 * N_CHUNKS))
    cot = pl.BlockSpec((rows, width), lambda i, core: (0, 0))
    return pl.pallas_call(
        grad_out_kernel,
        grid_spec=pltpu.PrefetchScalarGridSpec(
            num_scalar_prefetch=1,
            grid=(grads.shape[0] // blocks,),
            in_specs=[left, left, drb, drb, cot, cot, pl.BlockSpec(memory_space=pl.ANY)],
            out_specs=pl.BlockSpec((blocks, OUT_ROWS, width), lambda i, core: (i, 0, 0)),
        ),
        out_shape=jax.ShapeDtypeStruct(grads.shape, bf16),
        input_output_aliases={7: 0},
        compiler_params=pltpu.CompilerParams(vmem_limit_bytes=VMEM_BYTES),
        name="grad_out",
    )(core, *lefts, *wides, *cots, grads)


def adam_step(master, first_old, second_old, gradient, rate):
    first_new = BETA_ONE * first_old + (1.0 - BETA_ONE) * gradient
    second_new = BETA_TWO * second_old + (1.0 - BETA_TWO) * gradient * gradient
    first_hat = first_new / (1.0 - BETA_ONE**STEP)
    second_hat = second_new / (1.0 - BETA_TWO**STEP)
    master_new = master - rate * (
        first_hat / (jnp.sqrt(second_hat) + ADAM_EPS) + WEIGHT_DECAY * master
    )
    return (first_new, second_new, master_new)


def gathered(x):
    return lax.all_gather(x, AXIS_CYZ, axis=0, tiled=True)


def shift(x, axis, step):
    n = SIZES[axis]
    return lax.ppermute(x, axis, [(i, (i + step) % n) for i in range(n)])


def first_moves(x):
    first, second = x[None, :HALF], x[None, HALF:]
    pair = jnp.concatenate([first, shift(first, "xh", 1)], axis=0)
    ring = jnp.concatenate([second] + [shift(second, "y", b) for b in (1, 2, 3)], axis=0)
    return pair, ring


def second_moves(pair, ring, after):
    one = jnp.concatenate([pair] + [shift(pair, "y", b) for b in (1, 2, 3)], axis=0)
    two = jnp.concatenate([ring, shift(ring, "xh", 1)], axis=0)
    one, two, _ = lax.optimization_barrier((one, two, after))
    return [one, two, shift(one, "core", 1), shift(two, "core", 1)]


def places_of_groups():
    xh, y, core = (lax.axis_index(name) for name in CTX)
    places = []
    for other in range(2):
        for side in range(2):
            for i in range(GROUP):
                b, a = (i // 2, i % 2) if side == 0 else (i % 4, i // 4)
                dev = (((xh + a) % 2) * 4 + (y - b) % 4) * 2 + (core + other) % 2
                places.append(dev if side == 0 else 31 - dev)
    return jnp.stack(places).astype(jnp.int32)


def sum_over_core(near, far):
    return (near.astype(f32) + shift(far, "core", 1).astype(f32)).astype(bf16)


def first_sums(plane):
    one = plane[:GROUP].reshape((4, 2) + plane.shape[1:])
    two = plane[GROUP:].reshape((2, 4) + plane.shape[1:])
    two = (two[0].astype(f32) + shift(two[1], "xh", 1).astype(f32)).astype(bf16)
    one = sum((shift(one[b], "y", -b).astype(f32) for b in (1, 2, 3)), one[0].astype(f32))
    return one.astype(bf16), two


def second_sums(one, two):
    two = sum((shift(two[b], "y", -b).astype(f32) for b in (1, 2, 3)), two[0].astype(f32))
    one = one[0].astype(f32) + shift(one[1], "xh", 1).astype(f32)
    return jnp.concatenate([one, two], axis=0)


def pick(v, i, n):
    return lax.dynamic_index_in_dim(v, lax.rem(i, n), 0, keepdims=False)


def sum_over_x(blocks):
    me = lax.axis_index(AXIS_X)
    n = blocks.shape[0]
    total = pick(blocks, me, n).astype(f32)
    for step in range(1, n):
        moves = [(i, (i + step) % n) for i in range(n)]
        total = total + lax.ppermute(pick(blocks, me + step, n), AXIS_X, moves).astype(f32)
    return total


def sum_at_owners(blocks):
    me = lax.axis_index(AXIS_X)
    n = blocks.shape[0]
    total = 0.0
    for step in range(n):
        moves = []
        for source, place in owner_pairs():
            moves.append((source, place - place % n + (place % n + step) % n))
        total = total + lax.ppermute(pick(blocks, me + step, n), EVERY, moves).astype(f32)
    return total


def natural_of_permuted(x):
    tail = x.shape[1:]
    x = x.reshape((2, 4, 4, 2, 2) + tail)
    x = x.transpose((3, 1, 0, 4, 2) + tuple(range(5, 5 + len(tail))))
    return x.reshape((128,) + tail)


def owner_pairs():
    pairs = []
    for n in range(128):
        z = n % 4
        xl = (n // 4) % 2
        core = (n // 8) % 2
        y = (n // 16) % 4
        xh = n // 64
        pairs.append((n, (((core * 4 + y) * 4 + z) * 2 + xh) * 2 + xl))
    return pairs


def body(
    tokens,
    cotangent,
    segments,
    positions,
    pad_mask,
    w_in,
    w_out,
    gains,
    first_in,
    first_out,
    first_gains,
    second_in,
    second_out,
    second_gains,
):
    rows = tokens.shape[1]
    width = tokens.shape[2]
    span = segments.shape[1]
    half = rows // 2
    n_ctx = span // rows
    q_width = H_Q * HD
    kv_width = H_KV * HD
    attn_cols = q_width + 2 * kv_width
    owned = w_in.shape[0]
    owned_gains = gains.shape[0]

    n_x = 4
    low_in = w_in.astype(bf16)
    n_dev = width // owned

    own_head = jnp.concatenate(
        [
            low_in[:, :q_width].reshape(owned, H_Q, HD),
            jnp.repeat(low_in[:, q_width : q_width + kv_width].reshape(owned, H_KV, HD), 2, axis=1),
            jnp.repeat(low_in[:, q_width + kv_width : attn_cols].reshape(owned, H_KV, HD), 2, axis=1),
            jnp.broadcast_to(
                jnp.pad(gains.astype(bf16)[None, None], ((0, owned - 1), (0, 0), (0, HD - owned_gains))),
                (owned, H_Q, HD),
            ),
        ],
        axis=2,
    ).transpose(1, 0, 2)
    pair, ring = first_moves(tokens[0])
    head = lax.all_to_all(own_head, CTX, 0, 0, tiled=True)
    pairs = owner_pairs()
    own_out = lax.ppermute(w_out.astype(bf16), EVERY, [(p, n) for n, p in pairs])
    head, pair, ring, own_out = lax.optimization_barrier((head, pair, ring, own_out))
    head = lax.all_gather(head, SHARD, axis=0, tiled=False)
    own_ffn = low_in[:, attn_cols:].reshape(owned, 2 * N_CHUNKS, CHUNK)
    own_ffn = own_ffn.transpose(1, 0, 2).reshape(2 * N_CHUNKS * owned, CHUNK)
    own_rest = jnp.concatenate([own_out, own_ffn], axis=0)
    own_rest = lax.all_gather(own_rest, AXIS_X, axis=0, tiled=False)
    segments, pad_mask, own_rest, pair, ring = lax.optimization_barrier(
        (segments, pad_mask, own_rest, pair, ring)
    )
    head = head.reshape((2, 4) + own_head.shape).transpose(2, 0, 1, 3, 4)
    gain_vals = head[:, :, :, 0, HEAD_COLS : HEAD_COLS + owned_gains].reshape(-1).astype(f32)
    w_head = head[..., :HEAD_COLS].reshape(width, HEAD_COLS)
    gain_one = gain_vals[:width]
    gain_two = gain_vals[width : 2 * width]
    gain_query = gain_vals[2 * width : 2 * width + HD].reshape(1, HD)
    gain_key = gain_vals[2 * width + HD :].reshape(1, HD)
    w_scaled = (w_head.astype(f32) * gain_one[:, None]).astype(bf16)

    n_out = w_out.shape[0]
    part_out = own_rest[:, :n_out].reshape(n_x * n_out, width)
    part_ffn = own_rest[:, n_out:].reshape(n_x, 2 * N_CHUNKS, owned, CHUNK).transpose(1, 0, 2, 3)
    part_ffn = part_ffn.reshape(2 * N_CHUNKS * CHUNK_ROWS, CHUNK)
    full = gathered(jnp.concatenate([part_out, part_ffn], axis=0)[None])

    order = natural_of_permuted(jnp.arange(width, dtype=jnp.int32).reshape(n_dev, owned)).reshape(-1)
    shuffle = (order[:, None] == jnp.arange(width, dtype=jnp.int32)[None, :]).astype(bf16)

    def natural(x):
        x = x.reshape(n_ctx, 2, half)
        return jnp.concatenate([x[:, 0], x[::-1, 1]], axis=0)

    halves = jnp.arange(HD // 2, dtype=f32)
    inverse = ROPE_BASE ** (-2.0 * halves / HD)
    cos, sin, lens = tables(
        natural(segments[0]), natural(pad_mask[0]), jnp.concatenate([inverse, inverse])[None]
    )
    first_key = (jnp.arange(span, dtype=jnp.int32).reshape(lens.shape) - lens).reshape(span // BQ, BQ)
    klo = jnp.stack(
        [jnp.min(first_key, axis=1) // BK, (jnp.max(first_key, axis=1) + BK - 1) // BK]
    )
    lens = lens.reshape(span // BQ, BQ)

    groups = second_moves(pair, ring, (cos, klo, lens))
    place = places_of_groups()
    q, k, v, query_raw, key_raw, inv = project(
        place, groups, w_scaled, cos, sin, gain_query, gain_key
    )
    o_send, o_nat, l_inv = attend(klo, q, k, v, lens, rows)
    mixed = lax.all_to_all(o_send, CTX, 0, 0, tiled=True)

    output, grad_residual, do_send, left, wide, gain_two_terms = middle(
        full, mixed, tokens[0], cotangent[0], gain_two.reshape(1, width), shuffle
    )
    core = lax.axis_index("core")
    lefts = (pick(left, core, 2), shift(pick(left, core + 1, 2), "core", 1))
    wides = (wide, shift(wide, "core", 1))
    cots = (cotangent[0], shift(cotangent[0], "core", 1))
    grads = grad_ffn(lefts, wides, full.shape[0] // 2)
    grads = grad_out(core.astype(jnp.int32).reshape(1), lefts, wides, cots, grads)
    do = lax.all_to_all(do_send, CTX, 0, 0, tiled=True)
    do, grads = lax.optimization_barrier((do, grads))
    grads = grads.reshape(-1, width)
    grads = lax.psum_scatter(grads, AXIS_YZ, scatter_dimension=0, tiled=True)

    head_grads = attend_back(klo, q, k, v, do, o_nat, l_inv, lens)
    da_near, da_far, dw_head, gain_qk = project_back(
        place, groups, head_grads, (query_raw, key_raw, inv), cos, sin, gain_query, gain_key, w_head
    )

    gain_one_grad = jnp.sum(dw_head * w_head.astype(f32), axis=1)
    grad_gains = jnp.concatenate([gain_one_grad, gain_two_terms[0], gain_qk[0], gain_qk[1]])
    grad_gains = jnp.pad(
        grad_gains.reshape(n_dev, 1, owned_gains), ((0, 0), (0, owned - 1), (0, HD - owned_gains))
    )
    dw_head = (dw_head * gain_one[:, None]).reshape(n_dev, owned, HEAD_COLS)
    dw_head = jnp.concatenate([dw_head, grad_gains], axis=2).astype(bf16)
    dw_head = dw_head.reshape(n_ctx, n_dev // n_ctx, owned, PAD_COLS).transpose(1, 0, 2, 3)
    plane = sum_over_core(da_near, da_far)
    one, two = first_sums(plane)
    dw_head = lax.all_to_all(dw_head, SHARD, 0, 0, tiled=True)
    dw_head = jnp.sum(dw_head.astype(f32), axis=0).astype(bf16)

    out_part = grads[:OUT_ROWS].reshape(n_x, OUT_ROWS // n_x, width)
    ffn_part = grads[OUT_ROWS:].reshape(2 * N_CHUNKS, n_x, owned, CHUNK)
    ffn_part = ffn_part.transpose(1, 0, 2, 3).reshape(n_x, 2 * N_CHUNKS * owned, CHUNK)
    owned_out = sum_at_owners(out_part)
    owned_ffn = sum_over_x(ffn_part).reshape(2 * N_CHUNKS, owned, CHUNK)
    one, two, owned_out, owned_ffn = lax.optimization_barrier((one, two, owned_out, owned_ffn))

    dw_head, _, _ = lax.optimization_barrier((dw_head, one, two))
    dw_head = lax.all_to_all(dw_head, CTX, 0, 0, tiled=True).astype(f32)
    owned_gain_grad = jnp.sum(dw_head[:, 0, HEAD_COLS : HEAD_COLS + owned_gains], axis=0)

    grad_a = second_sums(one, two)
    inputs = tokens[0].astype(f32)
    input_grad = grad_residual + rms_back(inputs, gain_one, grad_a)[0]

    def columns(x):
        return x.transpose(1, 0, 2).reshape(owned, -1)

    def over_pair(x):
        return columns(jnp.sum(x.reshape(H_KV, 2, owned, HD), axis=1))

    owned_in = jnp.concatenate(
        [
            columns(dw_head[:, :, :HD]),
            over_pair(dw_head[:, :, HD : 2 * HD]),
            over_pair(dw_head[:, :, 2 * HD : HEAD_COLS]),
            columns(owned_ffn),
        ],
        axis=1,
    )
    new_first_in, new_second_in, new_master_in = adam_step(
        w_in, first_in, second_in, owned_in, RATE_MATRIX
    )
    new_first_out, new_second_out, new_master_out = adam_step(
        w_out, first_out, second_out, owned_out, RATE_MATRIX
    )
    new_first_gains, new_second_gains, new_master_gains = adam_step(
        gains, first_gains, second_gains, owned_gain_grad, RATE_GAIN
    )
    return (
        output[None],
        input_grad[None],
        new_first_in,
        new_first_out,
        new_first_gains,
        new_second_in,
        new_second_out,
        new_second_gains,
        new_master_in,
        new_master_out,
        new_master_gains,
        new_master_in.astype(bf16),
        new_master_out.astype(bf16),
    )


def solution(mesh):
    cut = Mesh(mesh.devices.reshape(tuple(SIZES[name] for name in EVERY)), EVERY)
    weights = P(EVERY, None)
    vector = P(EVERY)
    acts = P(SHARD, CTX, None)
    in_specs = (
        acts,
        acts,
        P(SHARD, None),
        P(SHARD, CTX),
        P(SHARD, None),
    ) + (weights, weights, vector) * 3
    out_specs = (acts, acts) + (weights, weights, vector) * 3 + (weights, weights)
    return jax.shard_map(body, mesh=cut, in_specs=in_specs, out_specs=out_specs, check_vma=False)
```

```python
import functools
import math

import jax
import jax.numpy as jnp
from jax import lax
from jax.experimental import pallas as pl
from jax.experimental.pallas import tpu as pltpu
from jax.sharding import Mesh
from jax.sharding import PartitionSpec as P

H_Q = 16
H_KV = 8
HD = 128
FF = 3072
STEP = 5

NORM_EPS = 1e-06
ROPE_BASE = 1000000.0
BETA_ONE = 0.5
BETA_TWO = 0.5
ADAM_EPS = 1e-08
WEIGHT_DECAY = 0.1
RATE_MATRIX = 0.03
RATE_GAIN = 0.25

CTX = ("xh", "y", "core")
SHARD = ("xl", "z")
EVERY = CTX + SHARD
AXIS_X = ("xh", "xl")
AXIS_YZ = ("y", "z")
AXIS_CYZ = ("core", "y", "z")
SIZES = {"xh": 2, "y": 4, "core": 2, "xl": 2, "z": 4}

LOG2_E = 1.4426950408889634
SCORE_SCALE = 1.0 / math.sqrt(HD)
BQ = 512
BK = 512
SUB = 256
VMEM_BYTES = 48 * 1024 * 1024
BIG_VMEM_BYTES = 60 * 1024 * 1024

bf16 = jnp.bfloat16
f32 = jnp.float32


def rms_norm(values, weight):
    return values * lax.rsqrt(jnp.mean(values * values, axis=-1, keepdims=True) + NORM_EPS) * weight


def rms_back(values, weight, upstream):
    inverse = lax.rsqrt(jnp.mean(values * values, axis=-1, keepdims=True) + NORM_EPS)
    normed = values * inverse
    scaled = upstream * weight
    grad_values = inverse * (scaled - normed * jnp.mean(scaled * normed, axis=-1, keepdims=True))
    return (grad_values, upstream * normed)


def dot_nt(a, b):
    return lax.dot_general(a, b, (((1,), (1,)), ((), ())), preferred_element_type=f32)


def dot_tn(a, b):
    return lax.dot_general(a, b, (((0,), (0,)), ((), ())), preferred_element_type=f32)


def dot_nn(a, b):
    return lax.dot_general(a, b, (((1,), (0,)), ((), ())), preferred_element_type=f32)


LAST_DOC = 13


def tables_kernel(docs_ref, live_ref, freq_ref, cos_ref, sin_ref, lens_ref):
    docs = docs_ref[...]
    shape = docs.shape
    start = jnp.zeros(shape, f32)
    for number in range(1, LAST_DOC + 1):
        before = jnp.sum(jnp.where(docs < number, 1.0, 0.0))
        start = jnp.where(docs == number, before, start)
    at = lax.broadcasted_iota(jnp.int32, shape, 0) * shape[1] + lax.broadcasted_iota(
        jnp.int32, shape, 1
    )
    within = at.astype(f32) - start
    lens_ref[...] = jnp.where(live_ref[...] == 1, within.astype(jnp.int32), 0)

    left = lax.broadcasted_iota(jnp.int32, (HD, HD), 1) < HD // 2
    for i in range(0, shape[0], 2):
        cols = [jnp.broadcast_to(within[i + n : i + n + 1, :], (HD, HD)).T for n in range(2)]
        angle = jnp.where(left, cols[0], cols[1]) * freq_ref[...]
        for ref, values, flip in ((cos_ref, jnp.cos(angle), False), (sin_ref, jnp.sin(angle), True)):
            turned = pltpu.roll(values, HD // 2, 1)
            for n in range(2):
                lower, upper = (values, turned) if n == 0 else (turned, values)
                ref[(i + n) * HD : (i + n + 1) * HD, :] = jnp.where(
                    left, -lower if flip else lower, upper
                )


def tables(docs, live, freq):
    span = docs.size
    table = jax.ShapeDtypeStruct((span, HD), f32)
    return pl.pallas_call(
        tables_kernel,
        in_specs=[vmem()] * 3,
        out_specs=[vmem()] * 3,
        out_shape=[table, table, jax.ShapeDtypeStruct(docs.shape, jnp.int32)],
        compiler_params=pltpu.CompilerParams(vmem_limit_bytes=VMEM_BYTES),
        cost_estimate=pl.CostEstimate(
            flops=100 * span * HD, bytes_accessed=3 * span * HD * 4, transcendentals=span * HD
        ),
        name="tables",
    )(docs, live, freq)


N_GROUPS = 4
GROUP = 8
HALF = 128
STEP_BLOCKS = 4
STEPS = GROUP // STEP_BLOCKS
HEAD_COLS = 3 * HD
PAD_COLS = 4 * HD


def block_spec(width, first, count):
    return pl.BlockSpec(
        (STEP_BLOCKS, HALF, width), lambda i, place: (jnp.clip(i - first, 0, count - 1), 0, 0)
    )


def group_specs(width):
    return [block_spec(width, k * STEPS, STEPS) for k in range(N_GROUPS)]


def fixed(shape):
    return pl.BlockSpec(shape, lambda i, place: (0,) * len(shape))


def rows_of(place_ref, step, i):
    return pl.ds(pl.multiple_of(place_ref[step * STEP_BLOCKS + i] * HALF, HALF), HALF)


def head_mean(x):
    return lax.dot_general(
        x.astype(bf16),
        jnp.full((HD, HD), 1.0 / HD, bf16),
        (((1,), (0,)), ((), ())),
        preferred_element_type=f32,
    )


def project_kernel(
    place_ref, x0, x1, x2, x3, w_ref, cos_ref, sin_ref, gq_ref, gk_ref,
    q_ref, k_ref, v_ref, qraw_ref, kraw_ref, inv_ref,
):
    step = pl.program_id(0)

    def run(x):
        wide = x.astype(f32)
        inverse = lax.rsqrt(jnp.mean(wide * wide, axis=-1, keepdims=True) + NORM_EPS)
        prod = dot_nn(x, w_ref[...]) * inverse
        for i in range(STEP_BLOCKS):
            at = rows_of(place_ref, step, i)
            part = slice(i * HALF, (i + 1) * HALF)
            cos = cos_ref[at, :]
            sin = sin_ref[at, :]

            def roped(raw, gain, cos=cos, sin=sin):
                normed = raw * lax.rsqrt(head_mean(raw * raw) + NORM_EPS) * gain
                return normed * cos + pltpu.roll(normed, HD // 2, 1) * sin

            query = prod[part, :HD]
            key = prod[part, HD : 2 * HD]
            inv_ref[at, :] = jnp.broadcast_to(inverse[part], (HALF, HD)).astype(bf16)
            qraw_ref[at, :] = query.astype(bf16)
            kraw_ref[at, :] = key.astype(bf16)
            q_ref[at, :] = (roped(query, gq_ref[...]) * (SCORE_SCALE * LOG2_E)).astype(bf16)
            k_ref[at, :] = roped(key, gk_ref[...]).astype(bf16)
            v_ref[at, :] = prod[part, 2 * HD :].astype(bf16)

    for k, x_ref in enumerate((x0, x1, x2, x3)):

        @pl.when(step // STEPS == k)
        def _(x_ref=x_ref):
            run(x_ref[...].reshape(STEP_BLOCKS * HALF, x_ref.shape[2]))


def project(place, groups, w, cos, sin, gq, gk):
    width = w.shape[0]
    span = cos.shape[0]
    low = jax.ShapeDtypeStruct((span, HD), bf16)
    whole = fixed((span, HD))
    return pl.pallas_call(
        project_kernel,
        grid_spec=pltpu.PrefetchScalarGridSpec(
            num_scalar_prefetch=1,
            grid=(N_GROUPS * STEPS,),
            in_specs=group_specs(width)
            + [fixed((width, HEAD_COLS)), whole, whole, fixed((1, HD)), fixed((1, HD))],
            out_specs=[whole] * 6,
        ),
        out_shape=[low] * 6,
        compiler_params=pltpu.CompilerParams(vmem_limit_bytes=VMEM_BYTES),
        name="project",
    )(place, *groups, w, cos, sin, gq, gk)


def project_back_kernel(
    place_ref, x0, x1, x2, x3, dq_ref, dk_ref, dv_ref, qraw_ref, kraw_ref, inv_ref, cos_ref, sin_ref,
    gq_ref, gk_ref, w_ref, near_ref, far_ref, dw_ref, dg_ref, grads, scaled,
):
    step = pl.program_id(0)

    @pl.when(step == 0)
    def _():
        dw_ref[...] = jnp.zeros_like(dw_ref)
        dg_ref[...] = jnp.zeros_like(dg_ref)

    def run(x, da_ref):
        q_sum = jnp.zeros((1, HD), f32)
        k_sum = jnp.zeros((1, HD), f32)
        for i in range(STEP_BLOCKS):
            at = rows_of(place_ref, step, i)
            part = slice(i * HALF, (i + 1) * HALF)
            cos = cos_ref[at, :]
            sin = sin_ref[at, :]

            def back(raw, gain, grad, cos=cos, sin=sin):
                unrot = grad * cos + pltpu.roll(grad * sin, HD // 2, 1)
                inv_rms = lax.rsqrt(head_mean(raw * raw) + NORM_EPS)
                normed = raw * inv_rms
                scaled_up = unrot * gain
                grad = inv_rms * (scaled_up - normed * head_mean(scaled_up * normed))
                return grad, unrot * normed

            grad_q, q_terms = back(qraw_ref[at, :].astype(f32), gq_ref[...], dq_ref[at, :])
            grad_k, k_terms = back(kraw_ref[at, :].astype(f32), gk_ref[...], dk_ref[at, :])
            inverse = inv_ref[at, :].astype(f32)
            for c, grad in enumerate((grad_q, grad_k, dv_ref[at, :])):
                grads[part, c * HD : (c + 1) * HD] = grad.astype(bf16)
                scaled[part, c * HD : (c + 1) * HD] = (grad * inverse).astype(bf16)
            q_sum = q_sum + jnp.sum(q_terms, axis=0, keepdims=True)
            k_sum = k_sum + jnp.sum(k_terms, axis=0, keepdims=True)
        da_ref[...] = dot_nt(grads[...], w_ref[...]).astype(bf16).reshape(da_ref.shape)
        dw_ref[...] += dot_tn(x, scaled[...])
        dg_ref[0:1, :] += q_sum
        dg_ref[1:2, :] += k_sum

    for k, x_ref in enumerate((x0, x1, x2, x3)):

        @pl.when(step // STEPS == k)
        def _(k=k, x_ref=x_ref):
            da_ref = near_ref if k < N_GROUPS // 2 else far_ref
            run(x_ref[...].reshape(STEP_BLOCKS * HALF, x_ref.shape[2]), da_ref)


def project_back(place, groups, grads, raws, cos, sin, gq, gk, w):
    width = w.shape[0]
    span = cos.shape[0]
    whole = fixed((span, HD))
    n_half = N_GROUPS // 2
    da = jax.ShapeDtypeStruct((n_half * GROUP, HALF, width), bf16)
    return pl.pallas_call(
        project_back_kernel,
        grid_spec=pltpu.PrefetchScalarGridSpec(
            num_scalar_prefetch=1,
            grid=(N_GROUPS * STEPS,),
            in_specs=group_specs(width)
            + [whole] * 8
            + [fixed((1, HD)), fixed((1, HD)), fixed((width, HEAD_COLS))],
            out_specs=[
                block_spec(width, 0, n_half * STEPS),
                block_spec(width, n_half * STEPS, n_half * STEPS),
                fixed((width, HEAD_COLS)),
                fixed((8, HD)),
            ],
            scratch_shapes=[
                pltpu.VMEM((STEP_BLOCKS * HALF, HEAD_COLS), bf16),
                pltpu.VMEM((STEP_BLOCKS * HALF, HEAD_COLS), bf16),
            ],
        ),
        out_shape=[
            da,
            da,
            jax.ShapeDtypeStruct((width, HEAD_COLS), f32),
            jax.ShapeDtypeStruct((8, HD), f32),
        ],
        compiler_params=pltpu.CompilerParams(vmem_limit_bytes=BIG_VMEM_BYTES),
        name="project_back",
    )(place, *groups, *grads, *raws, cos, sin, gq, gk, w)


def dealt_slot(place, n_dev):
    if place < n_dev:
        return place, 0
    return 2 * n_dev - 1 - place, 1


def key_mask(len_row, offset):
    ahead = (
        lax.broadcasted_iota(jnp.int32, (SUB, BQ), 1)
        - lax.broadcasted_iota(jnp.int32, (SUB, BQ), 0)
        + offset
    )
    return (ahead >= 0) & (ahead <= len_row)


def key_loops(bounds_ref, qb, q_at, tile):
    low = bounds_ref[0, qb]
    high = (q_at + BQ - 1) // BK + 1
    first = jnp.minimum(bounds_ref[1, qb], high)
    last = jnp.maximum((q_at + 1) // BK, first)

    def run(masked):
        def step(kb, _):
            tile(kb, masked)
            return 0

        return step

    lax.fori_loop(low, first, run(True), 0)
    lax.fori_loop(first, last, run(False), 0)
    lax.fori_loop(last, high, run(True), 0)


def attend_kernel(
    bounds_ref, q_ref, k_ref, v_ref, len_ref, osend_ref, onat_ref, linv_ref, acc, total
):
    n_dev, rows, _ = osend_ref.shape
    half = rows // 2
    span = q_ref.shape[0]
    def q_step(qb, _):
        q_at = pl.multiple_of(qb * BQ, BQ)
        q_blk = q_ref[pl.ds(q_at, BQ), :]
        len_row = len_ref[pl.ds(qb, 1), :]
        acc[...] = jnp.zeros_like(acc)
        total[...] = jnp.zeros_like(total)

        def tile(kb, masked):
            mixed = None
            summed = None
            for c in range(BK // SUB):
                k_at = pl.multiple_of(kb * BK + c * SUB, SUB)
                p = jnp.exp2(dot_nt(k_ref[pl.ds(k_at, SUB), :], q_blk))
                if masked:
                    p = jnp.where(key_mask(len_row, q_at - k_at), p, 0.0)
                part = jnp.sum(p.reshape(SUB // 8, 8, BQ), axis=0)
                more = dot_tn(v_ref[pl.ds(k_at, SUB), :], p.astype(bf16))
                summed = part if summed is None else summed + part
                mixed = more if mixed is None else mixed + more
            acc[...] += mixed
            total[...] += summed

        key_loops(bounds_ref, qb, q_at, tile)
        inverse = 1.0 / jnp.sum(total[...], axis=0, keepdims=True)
        linv_ref[pl.ds(qb, 1), :] = inverse
        onat_ref[pl.ds(q_at, BQ), :] = (acc[...] * inverse).T
        return 0

    lax.fori_loop(0, span // BQ, q_step, 0)
    for place in range(2 * n_dev):
        dev, side = dealt_slot(place, n_dev)
        osend_ref[dev, side * half : (side + 1) * half, :] = onat_ref[
            place * half : (place + 1) * half, :
        ].astype(bf16)


def vmem():
    return pl.BlockSpec(memory_space=pltpu.VMEM)


def attend(klo, q, k, v, lens, rows):
    span = q.shape[0]
    return pl.pallas_call(
        attend_kernel,
        in_specs=[pl.BlockSpec(memory_space=pltpu.SMEM)] + [vmem()] * 4,
        out_specs=[vmem(), vmem(), vmem()],
        out_shape=[
            jax.ShapeDtypeStruct((span // rows, rows, HD), bf16),
            jax.ShapeDtypeStruct((span, HD), f32),
            jax.ShapeDtypeStruct((span // BQ, BQ), f32),
        ],
        scratch_shapes=[
            pltpu.VMEM((HD, BQ), f32),
            pltpu.VMEM((8, BQ), f32),
        ],
        compiler_params=pltpu.CompilerParams(vmem_limit_bytes=VMEM_BYTES),
        name="attend",
    )(klo, q, k, v, lens)


def attend_back_kernel(
    bounds_ref, q_ref, k_ref, v_ref, do_ref, onat_ref, linv_ref, len_ref, dq, dk, dv, don, acc
):
    n_dev, rows, _ = do_ref.shape
    half = rows // 2
    span = q_ref.shape[0]
    for place in range(2 * n_dev):
        dev, side = dealt_slot(place, n_dev)
        to = slice(place * half, (place + 1) * half)
        don[to, :] = do_ref[dev, side * half : (side + 1) * half, :]
    dk[...] = jnp.zeros_like(dk)
    dv[...] = jnp.zeros_like(dv)

    def q_step(qb, _):
        q_at = pl.multiple_of(qb * BQ, BQ)
        q_blk = q_ref[pl.ds(q_at, BQ), :]
        do_blk = don[pl.ds(q_at, BQ), :]
        len_row = len_ref[pl.ds(qb, 1), :]
        inverse = linv_ref[pl.ds(qb, 1), :]
        mixed = (do_blk.astype(f32) * onat_ref[pl.ds(q_at, BQ), :]).T
        delta = jnp.sum(mixed, axis=0, keepdims=True)
        acc[...] = jnp.zeros_like(acc)

        def tile(kb, masked):
            total = None
            for c in range(BK // SUB):
                k_at = pl.multiple_of(kb * BK + c * SUB, SUB)
                here = pl.ds(k_at, SUB)
                p = jnp.exp2(dot_nt(k_ref[here, :], q_blk)) * inverse
                if masked:
                    p = jnp.where(key_mask(len_row, q_at - k_at), p, 0.0)
                dp = dot_nt(v_ref[here, :], do_blk)
                ds = (p * (dp - delta)).astype(bf16)
                dv[here, :] += dot_nn(p.astype(bf16), do_blk)
                dk[here, :] += dot_nn(ds, q_blk)
                more = dot_tn(k_ref[here, :], ds)
                total = more if total is None else total + more
            acc[...] += total

        key_loops(bounds_ref, qb, q_at, tile)
        dq[pl.ds(q_at, BQ), :] = (acc[...] * SCORE_SCALE).T
        return 0

    lax.fori_loop(0, span // BQ, q_step, 0)
    dk[...] = dk[...] * (1.0 / LOG2_E)


def attend_back(klo, q, k, v, do, onat, linv, lens):
    span = q.shape[0]
    return pl.pallas_call(
        attend_back_kernel,
        in_specs=[pl.BlockSpec(memory_space=pltpu.SMEM)] + [vmem()] * 7,
        out_specs=[vmem()] * 3,
        out_shape=[jax.ShapeDtypeStruct((span, HD), f32)] * 3,
        scratch_shapes=[
            pltpu.VMEM((span, HD), bf16),
            pltpu.VMEM((HD, BQ), f32),
        ],
        compiler_params=pltpu.CompilerParams(vmem_limit_bytes=VMEM_BYTES),
        name="attend_back",
    )(klo, q, k, v, do, onat, linv, lens)


OUT_ROWS = 160
CHUNK_ROWS = 32
N_CHUNKS = 3
CHUNK = FF // N_CHUNKS
Q_WIDTH = H_Q * HD
HALF_OUT = (Q_WIDTH + FF) // 2
HALF_MID = 512
LEFT = HALF_OUT + HALF_MID


def middle_kernel(
    full_ref, mixed_ref, tok_ref, cot_ref, gain_ref, shuffle_ref, gate_ref, up_ref,
    out_ref, dres_ref, dob_ref, left_ref, wide_ref, dgain_ref,
    w_out, resid, mid_low, grad_mid, sems,
):
    step = pl.program_id(0)
    width = tok_ref.shape[1]

    def fetch(i):
        return pltpu.make_async_copy(
            full_ref.at[i, pl.ds(0, OUT_ROWS), :],
            w_out.at[pl.ds(i * OUT_ROWS, OUT_ROWS), :],
            sems.at[i],
        )

    n_fetch = full_ref.shape[0]
    n_first = -(-Q_WIDTH // OUT_ROWS)

    @pl.when(step == 0)
    def _():
        for i in range(n_fetch):
            fetch(i).start()
        for h in range(H_Q):
            left_ref[0, :, h * HD : (h + 1) * HD] = mixed_ref[h]
        for i in range(n_first):
            fetch(i).wait()
        residual = tok_ref[...].astype(f32) + dot_nn(
            left_ref[0, :, :Q_WIDTH], w_out[:Q_WIDTH, :]
        )
        resid[...] = residual
        out_ref[...] = residual
        normed = rms_norm(residual, gain_ref[...]).astype(bf16)
        low = dot_nn(normed, shuffle_ref[...]).astype(bf16)
        mid_low[...] = low
        for side in range(2):
            left_ref[side, :, HALF_OUT:] = low[:, side * HALF_MID : (side + 1) * HALF_MID]
        grad_mid[...] = jnp.zeros_like(grad_mid)
        for i in range(n_first, n_fetch):
            fetch(i).wait()

    for f in range(N_CHUNKS):

        @pl.when(step == f + 1)
        def _(f=f):
            at = Q_WIDTH + f * CHUNK
            gate_w = gate_ref[...].reshape(width, CHUNK)
            up_w = up_ref[...].reshape(width, CHUNK)
            gate = dot_nn(mid_low[...], gate_w)
            up = dot_nn(mid_low[...], up_w)
            sigmoid_gate = 1.0 / (1.0 + jnp.exp(-gate))
            activated = gate * sigmoid_gate
            hidden = (activated * up).astype(bf16)
            cut = min(max(HALF_OUT - at, 0), CHUNK)
            if cut > 0:
                left_ref[0, :, at : at + cut] = hidden[:, :cut]
            if cut < CHUNK:
                left_ref[1, :, at + cut - HALF_OUT : at + CHUNK - HALF_OUT] = hidden[:, cut:]
            down_w = w_out[at : at + CHUNK, :]
            out_ref[...] += dot_nn(hidden, down_w)
            grad_hidden = dot_nt(cot_ref[...], down_w)
            grad_up = (grad_hidden * activated).astype(bf16)
            grad_gate = (
                grad_hidden * up * sigmoid_gate * (1.0 + gate * (1.0 - sigmoid_gate))
            ).astype(bf16)
            wide_ref[:, f * CHUNK : (f + 1) * CHUNK] = grad_gate
            wide_ref[:, FF + f * CHUNK : FF + (f + 1) * CHUNK] = grad_up
            grad_mid[...] += dot_nt(grad_gate, gate_w) + dot_nt(grad_up, up_w)

    @pl.when(step == N_CHUNKS + 1)
    def _():
        grad = dot_nt(grad_mid[...].astype(bf16), shuffle_ref[...])
        part, terms = rms_back(resid[...], gain_ref[...], grad)
        dgain_ref[...] = jnp.sum(terms, axis=0, keepdims=True)
        dres = cot_ref[...].astype(f32) + part
        dres_ref[...] = dres
        low = dres.astype(bf16)
        wide_ref[:, 2 * FF :] = low
        for c in range(4):
            piece = dot_nt(low, w_out[c * 4 * HD : (c + 1) * 4 * HD, :]).astype(bf16)
            for h in range(4):
                dob_ref[4 * c + h] = piece[:, h * HD : (h + 1) * HD]


def middle(full, mixed, tok, cot, gain, shuffle):
    rows, width = tok.shape
    n_blocks = full.shape[0]
    first = OUT_ROWS // CHUNK_ROWS

    def chunk_of(i):
        return jnp.clip(i - 1, 0, N_CHUNKS - 1)

    def whole(shape):
        return pl.BlockSpec(shape, lambda i: (0,) * len(shape))

    chunk = (n_blocks, CHUNK_ROWS, CHUNK)
    return pl.pallas_call(
        middle_kernel,
        grid=(N_CHUNKS + 2,),
        in_specs=[
            pl.BlockSpec(memory_space=pl.ANY),
            whole((H_Q, rows, HD)),
            whole((rows, width)),
            whole((rows, width)),
            whole((1, width)),
            whole((width, width)),
            pl.BlockSpec(chunk, lambda i: (0, first + chunk_of(i), 0)),
            pl.BlockSpec(chunk, lambda i: (0, first + N_CHUNKS + chunk_of(i), 0)),
        ],
        out_specs=[
            whole((rows, width)),
            whole((rows, width)),
            whole((H_Q, rows, HD)),
            whole((2, rows, LEFT)),
            whole((rows, 2 * FF + width)),
            whole((1, width)),
        ],
        out_shape=[
            jax.ShapeDtypeStruct((rows, width), f32),
            jax.ShapeDtypeStruct((rows, width), f32),
            jax.ShapeDtypeStruct((H_Q, rows, HD), bf16),
            jax.ShapeDtypeStruct((2, rows, LEFT), bf16),
            jax.ShapeDtypeStruct((rows, 2 * FF + width), bf16),
            jax.ShapeDtypeStruct((1, width), f32),
        ],
        scratch_shapes=[
            pltpu.VMEM((Q_WIDTH + FF, width), bf16),
            pltpu.VMEM((rows, width), f32),
            pltpu.VMEM((rows, width), bf16),
            pltpu.VMEM((rows, width), f32),
            pltpu.SemaphoreType.DMA((n_blocks,)),
        ],
        compiler_params=pltpu.CompilerParams(vmem_limit_bytes=BIG_VMEM_BYTES),
        name="middle",
    )(full, mixed, tok, cot, gain, shuffle, full, full)


def grad_ffn_kernel(left_a, left_b, right_a, right_b, out_ref):
    total = dot_tn(left_a[...], right_a[...]) + dot_tn(left_b[...], right_b[...])
    out_ref[...] = total.astype(bf16).reshape(out_ref.shape)


def grad_ffn(lefts, wides, n_blocks):
    rows = lefts[0].shape[0]
    left = pl.BlockSpec((rows, HALF_MID), lambda i: (0, HALF_OUT // HALF_MID))
    right = pl.BlockSpec((rows, CHUNK), lambda i: (0, i))
    first = OUT_ROWS // CHUNK_ROWS
    height = OUT_ROWS + 2 * N_CHUNKS * CHUNK_ROWS
    return pl.pallas_call(
        grad_ffn_kernel,
        grid=(2 * N_CHUNKS,),
        in_specs=[left, left, right, right],
        out_specs=pl.BlockSpec((n_blocks, CHUNK_ROWS, CHUNK), lambda i: (0, first + i, 0)),
        out_shape=jax.ShapeDtypeStruct((n_blocks, height, CHUNK), bf16),
        compiler_params=pltpu.CompilerParams(vmem_limit_bytes=VMEM_BYTES),
        name="grad_ffn",
    )(*lefts, *wides)


def grad_out_kernel(core_ref, left_a, left_b, drb_a, drb_b, cot_a, cot_b, grads_ref, out_ref):
    step = pl.program_id(0)
    block = left_a.shape[1]
    both = Q_WIDTH // block
    cut = Q_WIDTH % block
    lower = core_ref[0] == 0

    def store(value):
        out_ref[...] = value.astype(bf16).reshape(out_ref.shape)

    @pl.when(lower & (step < both))
    def _():
        store(dot_tn(left_a[...], drb_a[...]) + dot_tn(left_b[...], drb_b[...]))

    @pl.when(lower & (step == both))
    def _():
        top = dot_tn(left_a[:, :cut], drb_a[...]) + dot_tn(left_b[:, :cut], drb_b[...])
        rest = dot_tn(left_a[:, cut:], cot_a[...]) + dot_tn(left_b[:, cut:], cot_b[...])
        store(jnp.concatenate([top, rest], axis=0))

    @pl.when(core_ref[0] == 1)
    def _():
        store(dot_tn(left_a[...], cot_a[...]) + dot_tn(left_b[...], cot_b[...]))


def grad_out(core, lefts, wides, cots, grads):
    rows, width = cots[0].shape
    blocks = 4
    left = pl.BlockSpec((rows, blocks * OUT_ROWS), lambda i, core: (0, i))
    drb = pl.BlockSpec((rows, width), lambda i, core: (0, 2 * N_CHUNKS))
    cot = pl.BlockSpec((rows, width), lambda i, core: (0, 0))
    return pl.pallas_call(
        grad_out_kernel,
        grid_spec=pltpu.PrefetchScalarGridSpec(
            num_scalar_prefetch=1,
            grid=(grads.shape[0] // blocks,),
            in_specs=[left, left, drb, drb, cot, cot, pl.BlockSpec(memory_space=pl.ANY)],
            out_specs=pl.BlockSpec((blocks, OUT_ROWS, width), lambda i, core: (i, 0, 0)),
        ),
        out_shape=jax.ShapeDtypeStruct(grads.shape, bf16),
        input_output_aliases={7: 0},
        compiler_params=pltpu.CompilerParams(vmem_limit_bytes=VMEM_BYTES),
        name="grad_out",
    )(core, *lefts, *wides, *cots, grads)


def adam_step(master, first_old, second_old, gradient, rate):
    first_new = BETA_ONE * first_old + (1.0 - BETA_ONE) * gradient
    second_new = BETA_TWO * second_old + (1.0 - BETA_TWO) * gradient * gradient
    first_hat = first_new / (1.0 - BETA_ONE**STEP)
    second_hat = second_new / (1.0 - BETA_TWO**STEP)
    master_new = master - rate * (
        first_hat / (jnp.sqrt(second_hat) + ADAM_EPS) + WEIGHT_DECAY * master
    )
    return (first_new, second_new, master_new)


def gathered(x):
    return lax.all_gather(x, AXIS_CYZ, axis=0, tiled=True)


def shift(x, axis, step):
    n = SIZES[axis]
    return lax.ppermute(x, axis, [(i, (i + step) % n) for i in range(n)])


def first_moves(x):
    first, second = x[None, :HALF], x[None, HALF:]
    pair = jnp.concatenate([first, shift(first, "xh", 1)], axis=0)
    ring = jnp.concatenate([second] + [shift(second, "y", b) for b in (1, 2, 3)], axis=0)
    return pair, ring


def second_moves(pair, ring, after):
    one = jnp.concatenate([pair] + [shift(pair, "y", b) for b in (1, 2, 3)], axis=0)
    two = jnp.concatenate([ring, shift(ring, "xh", 1)], axis=0)
    one, two, _ = lax.optimization_barrier((one, two, after))
    return [one, two, shift(one, "core", 1), shift(two, "core", 1)]


def places_of_groups():
    xh, y, core = (lax.axis_index(name) for name in CTX)
    places = []
    for other in range(2):
        for side in range(2):
            for i in range(GROUP):
                b, a = (i // 2, i % 2) if side == 0 else (i % 4, i // 4)
                dev = (((xh + a) % 2) * 4 + (y - b) % 4) * 2 + (core + other) % 2
                places.append(dev if side == 0 else 31 - dev)
    return jnp.stack(places).astype(jnp.int32)


def sum_over_core(near, far):
    return (near.astype(f32) + shift(far, "core", 1).astype(f32)).astype(bf16)


def first_sums(plane):
    one = plane[:GROUP].reshape((4, 2) + plane.shape[1:])
    two = plane[GROUP:].reshape((2, 4) + plane.shape[1:])
    two = (two[0].astype(f32) + shift(two[1], "xh", 1).astype(f32)).astype(bf16)
    one = sum((shift(one[b], "y", -b).astype(f32) for b in (1, 2, 3)), one[0].astype(f32))
    return one.astype(bf16), two


def second_sums(one, two):
    two = sum((shift(two[b], "y", -b).astype(f32) for b in (1, 2, 3)), two[0].astype(f32))
    one = one[0].astype(f32) + shift(one[1], "xh", 1).astype(f32)
    return jnp.concatenate([one, two], axis=0)


def gather_along_xl(x):
    xl = lax.axis_index("xl")
    other = shift(x, "xl", 1)
    return jnp.stack([jnp.where(xl == 0, x, other), jnp.where(xl == 0, other, x)])


def pick(v, i, n):
    return lax.dynamic_index_in_dim(v, lax.rem(i, n), 0, keepdims=False)


def sum_over_x(blocks):
    me = lax.axis_index(AXIS_X)
    n = blocks.shape[0]
    total = pick(blocks, me, n).astype(f32)
    for step in range(1, n):
        moves = [(i, (i + step) % n) for i in range(n)]
        total = total + lax.ppermute(pick(blocks, me + step, n), AXIS_X, moves).astype(f32)
    return total


def sum_at_owners(blocks):
    me = lax.axis_index(AXIS_X)
    n = blocks.shape[0]
    total = 0.0
    for step in range(n):
        moves = []
        for source, place in owner_pairs():
            moves.append((source, place - place % n + (place % n + step) % n))
        total = total + lax.ppermute(pick(blocks, me + step, n), EVERY, moves).astype(f32)
    return total


def natural_of_permuted(x):
    tail = x.shape[1:]
    x = x.reshape((2, 4, 4, 2, 2) + tail)
    x = x.transpose((3, 1, 0, 4, 2) + tuple(range(5, 5 + len(tail))))
    return x.reshape((128,) + tail)


def owner_pairs():
    pairs = []
    for n in range(128):
        z = n % 4
        xl = (n // 4) % 2
        core = (n // 8) % 2
        y = (n // 16) % 4
        xh = n // 64
        pairs.append((n, (((core * 4 + y) * 4 + z) * 2 + xh) * 2 + xl))
    return pairs


def body(
    tokens,
    cotangent,
    segments,
    positions,
    pad_mask,
    w_in,
    w_out,
    gains,
    first_in,
    first_out,
    first_gains,
    second_in,
    second_out,
    second_gains,
):
    rows = tokens.shape[1]
    width = tokens.shape[2]
    span = segments.shape[1]
    half = rows // 2
    n_ctx = span // rows
    q_width = H_Q * HD
    kv_width = H_KV * HD
    attn_cols = q_width + 2 * kv_width
    owned = w_in.shape[0]
    owned_gains = gains.shape[0]

    n_x = 4
    low_in = w_in.astype(bf16)
    n_dev = width // owned

    own_head = jnp.concatenate(
        [
            low_in[:, :q_width].reshape(owned, H_Q, HD),
            jnp.repeat(low_in[:, q_width : q_width + kv_width].reshape(owned, H_KV, HD), 2, axis=1),
            jnp.repeat(low_in[:, q_width + kv_width : attn_cols].reshape(owned, H_KV, HD), 2, axis=1),
            jnp.broadcast_to(
                jnp.pad(gains.astype(bf16)[None, None], ((0, owned - 1), (0, 0), (0, HD - owned_gains))),
                (owned, H_Q, HD),
            ),
        ],
        axis=2,
    ).transpose(1, 0, 2)
    pair, ring = first_moves(tokens[0])
    head = lax.all_to_all(own_head, CTX, 0, 0, tiled=True)
    pairs = owner_pairs()
    own_out = lax.ppermute(w_out.astype(bf16), EVERY, [(p, n) for n, p in pairs])
    head, pair, ring, own_out = lax.optimization_barrier((head, pair, ring, own_out))
    own_ffn = low_in[:, attn_cols:].reshape(owned, 2 * N_CHUNKS, CHUNK)
    own_ffn = own_ffn.transpose(1, 0, 2).reshape(2 * N_CHUNKS * owned, CHUNK)
    own_rest = jnp.concatenate([own_out, own_ffn], axis=0)
    own_rest = lax.all_gather(own_rest, AXIS_X, axis=0, tiled=False)
    segments, pad_mask, own_rest, pair, ring = lax.optimization_barrier(
        (segments, pad_mask, own_rest, pair, ring)
    )
    n_out = w_out.shape[0]
    part_out = own_rest[:, :n_out].reshape(n_x * n_out, width)
    part_ffn = own_rest[:, n_out:].reshape(n_x, 2 * N_CHUNKS, owned, CHUNK).transpose(1, 0, 2, 3)
    part_ffn = part_ffn.reshape(2 * N_CHUNKS * CHUNK_ROWS, CHUNK)
    full = gathered(jnp.concatenate([part_out, part_ffn], axis=0)[None])

    order = natural_of_permuted(jnp.arange(width, dtype=jnp.int32).reshape(n_dev, owned)).reshape(-1)
    shuffle = (order[:, None] == jnp.arange(width, dtype=jnp.int32)[None, :]).astype(bf16)

    def natural(x):
        x = x.reshape(n_ctx, 2, half)
        return jnp.concatenate([x[:, 0], x[::-1, 1]], axis=0)

    halves = jnp.arange(HD // 2, dtype=f32)
    inverse = ROPE_BASE ** (-2.0 * halves / HD)
    cos, sin, lens = tables(
        natural(segments[0]), natural(pad_mask[0]), jnp.concatenate([inverse, inverse])[None]
    )
    first_key = (jnp.arange(span, dtype=jnp.int32).reshape(lens.shape) - lens).reshape(span // BQ, BQ)
    klo = jnp.stack(
        [jnp.min(first_key, axis=1) // BK, (jnp.max(first_key, axis=1) + BK - 1) // BK]
    )
    lens = lens.reshape(span // BQ, BQ)

    head, _ = lax.optimization_barrier((head, lens))
    head = lax.all_gather(head, "z", axis=0, tiled=False)
    groups = second_moves(pair, ring, (cos, klo, lens, head))
    head = gather_along_xl(head).transpose(2, 0, 1, 3, 4)
    gain_vals = head[:, :, :, 0, HEAD_COLS : HEAD_COLS + owned_gains].reshape(-1).astype(f32)
    w_head = head[..., :HEAD_COLS].reshape(width, HEAD_COLS)
    gain_one = gain_vals[:width]
    gain_two = gain_vals[width : 2 * width]
    gain_query = gain_vals[2 * width : 2 * width + HD].reshape(1, HD)
    gain_key = gain_vals[2 * width + HD :].reshape(1, HD)
    w_scaled = (w_head.astype(f32) * gain_one[:, None]).astype(bf16)

    place = places_of_groups()
    q, k, v, query_raw, key_raw, inv = project(
        place, groups, w_scaled, cos, sin, gain_query, gain_key
    )
    o_send, o_nat, l_inv = attend(klo, q, k, v, lens, rows)
    mixed = lax.all_to_all(o_send, CTX, 0, 0, tiled=True)

    output, grad_residual, do_send, left, wide, gain_two_terms = middle(
        full, mixed, tokens[0], cotangent[0], gain_two.reshape(1, width), shuffle
    )
    core = lax.axis_index("core")
    lefts = (pick(left, core, 2), shift(pick(left, core + 1, 2), "core", 1))
    wides = (wide, shift(wide, "core", 1))
    cots = (cotangent[0], shift(cotangent[0], "core", 1))
    grads = grad_ffn(lefts, wides, full.shape[0] // 2)
    grads = grad_out(core.astype(jnp.int32).reshape(1), lefts, wides, cots, grads)
    do = lax.all_to_all(do_send, CTX, 0, 0, tiled=True)
    do, grads = lax.optimization_barrier((do, grads))
    grads = grads.reshape(-1, width)
    grads = lax.psum_scatter(grads, AXIS_YZ, scatter_dimension=0, tiled=True)

    head_grads = attend_back(klo, q, k, v, do, o_nat, l_inv, lens)
    da_near, da_far, dw_head, gain_qk = project_back(
        place, groups, head_grads, (query_raw, key_raw, inv), cos, sin, gain_query, gain_key, w_head
    )

    gain_one_grad = jnp.sum(dw_head * w_head.astype(f32), axis=1)
    grad_gains = jnp.concatenate([gain_one_grad, gain_two_terms[0], gain_qk[0], gain_qk[1]])
    grad_gains = jnp.pad(
        grad_gains.reshape(n_dev, 1, owned_gains), ((0, 0), (0, owned - 1), (0, HD - owned_gains))
    )
    dw_head = (dw_head * gain_one[:, None]).reshape(n_dev, owned, HEAD_COLS)
    dw_head = jnp.concatenate([dw_head, grad_gains], axis=2).astype(bf16)
    dw_head = dw_head.reshape(n_ctx, n_dev // n_ctx, owned, PAD_COLS).transpose(1, 0, 2, 3)
    plane = sum_over_core(da_near, da_far)
    one, two = first_sums(plane)
    dw_head = lax.all_to_all(dw_head, SHARD, 0, 0, tiled=True)
    dw_head = jnp.sum(dw_head.astype(f32), axis=0).astype(bf16)

    out_part = grads[:OUT_ROWS].reshape(n_x, OUT_ROWS // n_x, width)
    ffn_part = grads[OUT_ROWS:].reshape(2 * N_CHUNKS, n_x, owned, CHUNK)
    ffn_part = ffn_part.transpose(1, 0, 2, 3).reshape(n_x, 2 * N_CHUNKS * owned, CHUNK)
    owned_out = sum_at_owners(out_part)
    owned_ffn = sum_over_x(ffn_part).reshape(2 * N_CHUNKS, owned, CHUNK)
    one, two, owned_out, owned_ffn = lax.optimization_barrier((one, two, owned_out, owned_ffn))

    dw_head, _, _ = lax.optimization_barrier((dw_head, one, two))
    dw_head = lax.all_to_all(dw_head, CTX, 0, 0, tiled=True).astype(f32)
    owned_gain_grad = jnp.sum(dw_head[:, 0, HEAD_COLS : HEAD_COLS + owned_gains], axis=0)

    grad_a = second_sums(one, two)
    inputs = tokens[0].astype(f32)
    input_grad = grad_residual + rms_back(inputs, gain_one, grad_a)[0]

    def columns(x):
        return x.transpose(1, 0, 2).reshape(owned, -1)

    def over_pair(x):
        return columns(jnp.sum(x.reshape(H_KV, 2, owned, HD), axis=1))

    owned_in = jnp.concatenate(
        [
            columns(dw_head[:, :, :HD]),
            over_pair(dw_head[:, :, HD : 2 * HD]),
            over_pair(dw_head[:, :, 2 * HD : HEAD_COLS]),
            columns(owned_ffn),
        ],
        axis=1,
    )
    new_first_in, new_second_in, new_master_in = adam_step(
        w_in, first_in, second_in, owned_in, RATE_MATRIX
    )
    new_first_out, new_second_out, new_master_out = adam_step(
        w_out, first_out, second_out, owned_out, RATE_MATRIX
    )
    new_first_gains, new_second_gains, new_master_gains = adam_step(
        gains, first_gains, second_gains, owned_gain_grad, RATE_GAIN
    )
    return (
        output[None],
        input_grad[None],
        new_first_in,
        new_first_out,
        new_first_gains,
        new_second_in,
        new_second_out,
        new_second_gains,
        new_master_in,
        new_master_out,
        new_master_gains,
        new_master_in.astype(bf16),
        new_master_out.astype(bf16),
    )


def solution(mesh):
    cut = Mesh(mesh.devices.reshape(tuple(SIZES[name] for name in EVERY)), EVERY)
    weights = P(EVERY, None)
    vector = P(EVERY)
    acts = P(SHARD, CTX, None)
    in_specs = (
        acts,
        acts,
        P(SHARD, None),
        P(SHARD, CTX),
        P(SHARD, None),
    ) + (weights, weights, vector) * 3
    out_specs = (acts, acts) + (weights, weights, vector) * 3 + (weights, weights)
    return jax.shard_map(body, mesh=cut, in_specs=in_specs, out_specs=out_specs, check_vma=False)
```

```python
import functools
import math

import jax
import jax.numpy as jnp
from jax import lax
from jax.experimental import pallas as pl
from jax.experimental.pallas import tpu as pltpu
from jax.sharding import Mesh
from jax.sharding import PartitionSpec as P

H_Q = 16
H_KV = 8
HD = 128
FF = 3072
STEP = 5

NORM_EPS = 1e-06
ROPE_BASE = 1000000.0
BETA_ONE = 0.5
BETA_TWO = 0.5
ADAM_EPS = 1e-08
WEIGHT_DECAY = 0.1
RATE_MATRIX = 0.03
RATE_GAIN = 0.25

CTX = ("xh", "y", "core")
SHARD = ("xl", "z")
EVERY = CTX + SHARD
AXIS_X = ("xh", "xl")
AXIS_YZ = ("y", "z")
AXIS_CYZ = ("core", "y", "z")
SIZES = {"xh": 2, "y": 4, "core": 2, "xl": 2, "z": 4}

LOG2_E = 1.4426950408889634
SCORE_SCALE = 1.0 / math.sqrt(HD)
BQ = 512
BK = 512
SUB = 256
VMEM_BYTES = 48 * 1024 * 1024
BIG_VMEM_BYTES = 60 * 1024 * 1024

bf16 = jnp.bfloat16
f32 = jnp.float32


def rms_norm(values, weight):
    return values * lax.rsqrt(jnp.mean(values * values, axis=-1, keepdims=True) + NORM_EPS) * weight


def rms_back(values, weight, upstream):
    inverse = lax.rsqrt(jnp.mean(values * values, axis=-1, keepdims=True) + NORM_EPS)
    normed = values * inverse
    scaled = upstream * weight
    grad_values = inverse * (scaled - normed * jnp.mean(scaled * normed, axis=-1, keepdims=True))
    return (grad_values, upstream * normed)


def dot_nt(a, b):
    return lax.dot_general(a, b, (((1,), (1,)), ((), ())), preferred_element_type=f32)


def dot_tn(a, b):
    return lax.dot_general(a, b, (((0,), (0,)), ((), ())), preferred_element_type=f32)


def dot_nn(a, b):
    return lax.dot_general(a, b, (((1,), (0,)), ((), ())), preferred_element_type=f32)


LAST_DOC = 13


def tables_kernel(docs_ref, live_ref, freq_ref, cos_ref, sin_ref, lens_ref):
    docs = docs_ref[...]
    shape = docs.shape
    start = jnp.zeros(shape, f32)
    for number in range(1, LAST_DOC + 1):
        before = jnp.sum(jnp.where(docs < number, 1.0, 0.0))
        start = jnp.where(docs == number, before, start)
    at = lax.broadcasted_iota(jnp.int32, shape, 0) * shape[1] + lax.broadcasted_iota(
        jnp.int32, shape, 1
    )
    within = at.astype(f32) - start
    lens_ref[...] = jnp.where(live_ref[...] == 1, within.astype(jnp.int32), 0)

    left = lax.broadcasted_iota(jnp.int32, (HD, HD), 1) < HD // 2
    for i in range(0, shape[0], 2):
        cols = [jnp.broadcast_to(within[i + n : i + n + 1, :], (HD, HD)).T for n in range(2)]
        angle = jnp.where(left, cols[0], cols[1]) * freq_ref[...]
        for ref, values, flip in ((cos_ref, jnp.cos(angle), False), (sin_ref, jnp.sin(angle), True)):
            turned = pltpu.roll(values, HD // 2, 1)
            for n in range(2):
                lower, upper = (values, turned) if n == 0 else (turned, values)
                ref[(i + n) * HD : (i + n + 1) * HD, :] = jnp.where(
                    left, -lower if flip else lower, upper
                )


def tables(docs, live, freq):
    span = docs.size
    table = jax.ShapeDtypeStruct((span, HD), f32)
    return pl.pallas_call(
        tables_kernel,
        in_specs=[vmem()] * 3,
        out_specs=[vmem()] * 3,
        out_shape=[table, table, jax.ShapeDtypeStruct(docs.shape, jnp.int32)],
        compiler_params=pltpu.CompilerParams(vmem_limit_bytes=VMEM_BYTES),
        cost_estimate=pl.CostEstimate(
            flops=100 * span * HD, bytes_accessed=3 * span * HD * 4, transcendentals=span * HD
        ),
        name="tables",
    )(docs, live, freq)


N_GROUPS = 4
GROUP = 8
HALF = 128
STEP_BLOCKS = 4
STEPS = GROUP // STEP_BLOCKS
HEAD_COLS = 3 * HD
PAD_COLS = 4 * HD


def block_spec(width, first, count):
    return pl.BlockSpec(
        (STEP_BLOCKS, HALF, width), lambda i, place: (jnp.clip(i - first, 0, count - 1), 0, 0)
    )


def group_specs(width):
    return [block_spec(width, k * STEPS, STEPS) for k in range(N_GROUPS)]


def fixed(shape):
    return pl.BlockSpec(shape, lambda i, place: (0,) * len(shape))


def rows_of(place_ref, step, i):
    return pl.ds(pl.multiple_of(place_ref[step * STEP_BLOCKS + i] * HALF, HALF), HALF)


def head_mean(x):
    return lax.dot_general(
        x.astype(bf16),
        jnp.full((HD, HD), 1.0 / HD, bf16),
        (((1,), (0,)), ((), ())),
        preferred_element_type=f32,
    )


def project_kernel(
    place_ref, x0, x1, x2, x3, w_ref, cos_ref, sin_ref, gq_ref, gk_ref,
    q_ref, k_ref, v_ref, qraw_ref, kraw_ref, inv_ref,
):
    step = pl.program_id(0)

    def run(x):
        wide = x.astype(f32)
        inverse = lax.rsqrt(jnp.mean(wide * wide, axis=-1, keepdims=True) + NORM_EPS)
        prod = dot_nn(x, w_ref[...]) * inverse
        for i in range(STEP_BLOCKS):
            at = rows_of(place_ref, step, i)
            part = slice(i * HALF, (i + 1) * HALF)
            cos = cos_ref[at, :]
            sin = sin_ref[at, :]

            def roped(raw, gain, cos=cos, sin=sin):
                normed = raw * lax.rsqrt(head_mean(raw * raw) + NORM_EPS) * gain
                return normed * cos + pltpu.roll(normed, HD // 2, 1) * sin

            query = prod[part, :HD]
            key = prod[part, HD : 2 * HD]
            inv_ref[at, :] = jnp.broadcast_to(inverse[part], (HALF, HD)).astype(bf16)
            qraw_ref[at, :] = query.astype(bf16)
            kraw_ref[at, :] = key.astype(bf16)
            q_ref[at, :] = (roped(query, gq_ref[...]) * (SCORE_SCALE * LOG2_E)).astype(bf16)
            k_ref[at, :] = roped(key, gk_ref[...]).astype(bf16)
            v_ref[at, :] = prod[part, 2 * HD :].astype(bf16)

    for k, x_ref in enumerate((x0, x1, x2, x3)):

        @pl.when(step // STEPS == k)
        def _(x_ref=x_ref):
            run(x_ref[...].reshape(STEP_BLOCKS * HALF, x_ref.shape[2]))


def project(place, groups, w, cos, sin, gq, gk):
    width = w.shape[0]
    span = cos.shape[0]
    low = jax.ShapeDtypeStruct((span, HD), bf16)
    whole = fixed((span, HD))
    return pl.pallas_call(
        project_kernel,
        grid_spec=pltpu.PrefetchScalarGridSpec(
            num_scalar_prefetch=1,
            grid=(N_GROUPS * STEPS,),
            in_specs=group_specs(width)
            + [fixed((width, HEAD_COLS)), whole, whole, fixed((1, HD)), fixed((1, HD))],
            out_specs=[whole] * 6,
        ),
        out_shape=[low] * 6,
        compiler_params=pltpu.CompilerParams(vmem_limit_bytes=VMEM_BYTES),
        name="project",
    )(place, *groups, w, cos, sin, gq, gk)


def project_back_kernel(
    place_ref, x0, x1, x2, x3, dq_ref, dk_ref, dv_ref, qraw_ref, kraw_ref, inv_ref, cos_ref, sin_ref,
    gq_ref, gk_ref, w_ref, near_ref, far_ref, dw_ref, dg_ref, grads, scaled,
):
    step = pl.program_id(0)

    @pl.when(step == 0)
    def _():
        dw_ref[...] = jnp.zeros_like(dw_ref)
        dg_ref[...] = jnp.zeros_like(dg_ref)

    def run(x, da_ref):
        q_sum = jnp.zeros((1, HD), f32)
        k_sum = jnp.zeros((1, HD), f32)
        for i in range(STEP_BLOCKS):
            at = rows_of(place_ref, step, i)
            part = slice(i * HALF, (i + 1) * HALF)
            cos = cos_ref[at, :]
            sin = sin_ref[at, :]

            def back(raw, gain, grad, cos=cos, sin=sin):
                unrot = grad * cos + pltpu.roll(grad * sin, HD // 2, 1)
                inv_rms = lax.rsqrt(head_mean(raw * raw) + NORM_EPS)
                normed = raw * inv_rms
                scaled_up = unrot * gain
                grad = inv_rms * (scaled_up - normed * head_mean(scaled_up * normed))
                return grad, unrot * normed

            grad_q, q_terms = back(qraw_ref[at, :].astype(f32), gq_ref[...], dq_ref[at, :])
            grad_k, k_terms = back(kraw_ref[at, :].astype(f32), gk_ref[...], dk_ref[at, :])
            inverse = inv_ref[at, :].astype(f32)
            for c, grad in enumerate((grad_q, grad_k, dv_ref[at, :])):
                grads[part, c * HD : (c + 1) * HD] = grad.astype(bf16)
                scaled[part, c * HD : (c + 1) * HD] = (grad * inverse).astype(bf16)
            q_sum = q_sum + jnp.sum(q_terms, axis=0, keepdims=True)
            k_sum = k_sum + jnp.sum(k_terms, axis=0, keepdims=True)
        da_ref[...] = dot_nt(grads[...], w_ref[...]).astype(bf16).reshape(da_ref.shape)
        dw_ref[...] += dot_tn(x, scaled[...])
        dg_ref[0:1, :] += q_sum
        dg_ref[1:2, :] += k_sum

    for k, x_ref in enumerate((x0, x1, x2, x3)):

        @pl.when(step // STEPS == k)
        def _(k=k, x_ref=x_ref):
            da_ref = near_ref if k < N_GROUPS // 2 else far_ref
            run(x_ref[...].reshape(STEP_BLOCKS * HALF, x_ref.shape[2]), da_ref)


def project_back(place, groups, grads, raws, cos, sin, gq, gk, w):
    width = w.shape[0]
    span = cos.shape[0]
    whole = fixed((span, HD))
    n_half = N_GROUPS // 2
    da = jax.ShapeDtypeStruct((n_half * GROUP, HALF, width), bf16)
    return pl.pallas_call(
        project_back_kernel,
        grid_spec=pltpu.PrefetchScalarGridSpec(
            num_scalar_prefetch=1,
            grid=(N_GROUPS * STEPS,),
            in_specs=group_specs(width)
            + [whole] * 8
            + [fixed((1, HD)), fixed((1, HD)), fixed((width, HEAD_COLS))],
            out_specs=[
                block_spec(width, 0, n_half * STEPS),
                block_spec(width, n_half * STEPS, n_half * STEPS),
                fixed((width, HEAD_COLS)),
                fixed((8, HD)),
            ],
            scratch_shapes=[
                pltpu.VMEM((STEP_BLOCKS * HALF, HEAD_COLS), bf16),
                pltpu.VMEM((STEP_BLOCKS * HALF, HEAD_COLS), bf16),
            ],
        ),
        out_shape=[
            da,
            da,
            jax.ShapeDtypeStruct((width, HEAD_COLS), f32),
            jax.ShapeDtypeStruct((8, HD), f32),
        ],
        compiler_params=pltpu.CompilerParams(vmem_limit_bytes=BIG_VMEM_BYTES),
        name="project_back",
    )(place, *groups, *grads, *raws, cos, sin, gq, gk, w)


def dealt_slot(place, n_dev):
    if place < n_dev:
        return place, 0
    return 2 * n_dev - 1 - place, 1


def key_mask(len_row, offset):
    ahead = (
        lax.broadcasted_iota(jnp.int32, (SUB, BQ), 1)
        - lax.broadcasted_iota(jnp.int32, (SUB, BQ), 0)
        + offset
    )
    return (ahead >= 0) & (ahead <= len_row)


def key_loops(bounds_ref, qb, q_at, tile):
    low = bounds_ref[0, qb]
    high = (q_at + BQ - 1) // BK + 1
    first = jnp.minimum(bounds_ref[1, qb], high)
    last = jnp.maximum((q_at + 1) // BK, first)

    def run(masked):
        def step(kb, _):
            tile(kb, masked)
            return 0

        return step

    lax.fori_loop(low, first, run(True), 0)
    lax.fori_loop(first, last, run(False), 0)
    lax.fori_loop(last, high, run(True), 0)


def attend_kernel(
    bounds_ref, q_ref, k_ref, v_ref, len_ref, osend_ref, onat_ref, linv_ref, acc, total
):
    n_dev, rows, _ = osend_ref.shape
    half = rows // 2
    span = q_ref.shape[0]
    def q_step(qb, _):
        q_at = pl.multiple_of(qb * BQ, BQ)
        q_blk = q_ref[pl.ds(q_at, BQ), :]
        len_row = len_ref[pl.ds(qb, 1), :]
        acc[...] = jnp.zeros_like(acc)
        total[...] = jnp.zeros_like(total)

        def tile(kb, masked):
            mixed = None
            summed = None
            for c in range(BK // SUB):
                k_at = pl.multiple_of(kb * BK + c * SUB, SUB)
                p = jnp.exp2(dot_nt(k_ref[pl.ds(k_at, SUB), :], q_blk))
                if masked:
                    p = jnp.where(key_mask(len_row, q_at - k_at), p, 0.0)
                part = jnp.sum(p.reshape(SUB // 8, 8, BQ), axis=0)
                more = dot_tn(v_ref[pl.ds(k_at, SUB), :], p.astype(bf16))
                summed = part if summed is None else summed + part
                mixed = more if mixed is None else mixed + more
            acc[...] += mixed
            total[...] += summed

        key_loops(bounds_ref, qb, q_at, tile)
        inverse = 1.0 / jnp.sum(total[...], axis=0, keepdims=True)
        linv_ref[pl.ds(qb, 1), :] = inverse
        onat_ref[pl.ds(q_at, BQ), :] = (acc[...] * inverse).T
        return 0

    lax.fori_loop(0, span // BQ, q_step, 0)
    for place in range(2 * n_dev):
        dev, side = dealt_slot(place, n_dev)
        osend_ref[dev, side * half : (side + 1) * half, :] = onat_ref[
            place * half : (place + 1) * half, :
        ].astype(bf16)


def vmem():
    return pl.BlockSpec(memory_space=pltpu.VMEM)


def attend(klo, q, k, v, lens, rows):
    span = q.shape[0]
    return pl.pallas_call(
        attend_kernel,
        in_specs=[pl.BlockSpec(memory_space=pltpu.SMEM)] + [vmem()] * 4,
        out_specs=[vmem(), vmem(), vmem()],
        out_shape=[
            jax.ShapeDtypeStruct((span // rows, rows, HD), bf16),
            jax.ShapeDtypeStruct((span, HD), f32),
            jax.ShapeDtypeStruct((span // BQ, BQ), f32),
        ],
        scratch_shapes=[
            pltpu.VMEM((HD, BQ), f32),
            pltpu.VMEM((8, BQ), f32),
        ],
        compiler_params=pltpu.CompilerParams(vmem_limit_bytes=VMEM_BYTES),
        name="attend",
    )(klo, q, k, v, lens)


def attend_back_kernel(
    bounds_ref, q_ref, k_ref, v_ref, do_ref, onat_ref, linv_ref, len_ref, dq, dk, dv, don, acc
):
    n_dev, rows, _ = do_ref.shape
    half = rows // 2
    span = q_ref.shape[0]
    for place in range(2 * n_dev):
        dev, side = dealt_slot(place, n_dev)
        to = slice(place * half, (place + 1) * half)
        don[to, :] = do_ref[dev, side * half : (side + 1) * half, :]
    dk[...] = jnp.zeros_like(dk)
    dv[...] = jnp.zeros_like(dv)

    def q_step(qb, _):
        q_at = pl.multiple_of(qb * BQ, BQ)
        q_blk = q_ref[pl.ds(q_at, BQ), :]
        do_blk = don[pl.ds(q_at, BQ), :]
        len_row = len_ref[pl.ds(qb, 1), :]
        inverse = linv_ref[pl.ds(qb, 1), :]
        mixed = (do_blk.astype(f32) * onat_ref[pl.ds(q_at, BQ), :]).T
        delta = jnp.sum(mixed, axis=0, keepdims=True)
        acc[...] = jnp.zeros_like(acc)

        def tile(kb, masked):
            total = None
            for c in range(BK // SUB):
                k_at = pl.multiple_of(kb * BK + c * SUB, SUB)
                here = pl.ds(k_at, SUB)
                p = jnp.exp2(dot_nt(k_ref[here, :], q_blk)) * inverse
                if masked:
                    p = jnp.where(key_mask(len_row, q_at - k_at), p, 0.0)
                dp = dot_nt(v_ref[here, :], do_blk)
                ds = (p * (dp - delta)).astype(bf16)
                dv[here, :] += dot_nn(p.astype(bf16), do_blk)
                dk[here, :] += dot_nn(ds, q_blk)
                more = dot_tn(k_ref[here, :], ds)
                total = more if total is None else total + more
            acc[...] += total

        key_loops(bounds_ref, qb, q_at, tile)
        dq[pl.ds(q_at, BQ), :] = (acc[...] * SCORE_SCALE).T
        return 0

    lax.fori_loop(0, span // BQ, q_step, 0)
    dk[...] = dk[...] * (1.0 / LOG2_E)


def attend_back(klo, q, k, v, do, onat, linv, lens):
    span = q.shape[0]
    return pl.pallas_call(
        attend_back_kernel,
        in_specs=[pl.BlockSpec(memory_space=pltpu.SMEM)] + [vmem()] * 7,
        out_specs=[vmem()] * 3,
        out_shape=[jax.ShapeDtypeStruct((span, HD), f32)] * 3,
        scratch_shapes=[
            pltpu.VMEM((span, HD), bf16),
            pltpu.VMEM((HD, BQ), f32),
        ],
        compiler_params=pltpu.CompilerParams(vmem_limit_bytes=VMEM_BYTES),
        name="attend_back",
    )(klo, q, k, v, do, onat, linv, lens)


OUT_ROWS = 160
CHUNK_ROWS = 32
N_CHUNKS = 3
CHUNK = FF // N_CHUNKS
Q_WIDTH = H_Q * HD
HALF_OUT = (Q_WIDTH + FF) // 2
HALF_MID = 512
LEFT = HALF_OUT + HALF_MID


def middle_kernel(
    full_ref, mixed_ref, tok_ref, cot_ref, gain_ref, shuffle_ref, gate_ref, up_ref,
    out_ref, dres_ref, dob_ref, left_ref, wide_ref, dgain_ref,
    w_out, resid, mid_low, grad_mid, sems,
):
    step = pl.program_id(0)
    width = tok_ref.shape[1]

    def fetch(i):
        return pltpu.make_async_copy(
            full_ref.at[i, pl.ds(0, OUT_ROWS), :],
            w_out.at[pl.ds(i * OUT_ROWS, OUT_ROWS), :],
            sems.at[i],
        )

    n_fetch = full_ref.shape[0]
    n_first = -(-Q_WIDTH // OUT_ROWS)

    @pl.when(step == 0)
    def _():
        for i in range(n_fetch):
            fetch(i).start()
        for h in range(H_Q):
            left_ref[0, :, h * HD : (h + 1) * HD] = mixed_ref[h]
        for i in range(n_first):
            fetch(i).wait()
        residual = tok_ref[...].astype(f32) + dot_nn(
            left_ref[0, :, :Q_WIDTH], w_out[:Q_WIDTH, :]
        )
        resid[...] = residual
        out_ref[...] = residual
        normed = rms_norm(residual, gain_ref[...]).astype(bf16)
        low = dot_nn(normed, shuffle_ref[...]).astype(bf16)
        mid_low[...] = low
        for side in range(2):
            left_ref[side, :, HALF_OUT:] = low[:, side * HALF_MID : (side + 1) * HALF_MID]
        grad_mid[...] = jnp.zeros_like(grad_mid)
        for i in range(n_first, n_fetch):
            fetch(i).wait()

    for f in range(N_CHUNKS):

        @pl.when(step == f + 1)
        def _(f=f):
            at = Q_WIDTH + f * CHUNK
            gate_w = gate_ref[...].reshape(width, CHUNK)
            up_w = up_ref[...].reshape(width, CHUNK)
            gate = dot_nn(mid_low[...], gate_w)
            up = dot_nn(mid_low[...], up_w)
            sigmoid_gate = 1.0 / (1.0 + jnp.exp(-gate))
            activated = gate * sigmoid_gate
            hidden = (activated * up).astype(bf16)
            cut = min(max(HALF_OUT - at, 0), CHUNK)
            if cut > 0:
                left_ref[0, :, at : at + cut] = hidden[:, :cut]
            if cut < CHUNK:
                left_ref[1, :, at + cut - HALF_OUT : at + CHUNK - HALF_OUT] = hidden[:, cut:]
            down_w = w_out[at : at + CHUNK, :]
            out_ref[...] += dot_nn(hidden, down_w)
            grad_hidden = dot_nt(cot_ref[...], down_w)
            grad_up = (grad_hidden * activated).astype(bf16)
            grad_gate = (
                grad_hidden * up * sigmoid_gate * (1.0 + gate * (1.0 - sigmoid_gate))
            ).astype(bf16)
            wide_ref[:, f * CHUNK : (f + 1) * CHUNK] = grad_gate
            wide_ref[:, FF + f * CHUNK : FF + (f + 1) * CHUNK] = grad_up
            grad_mid[...] += dot_nt(grad_gate, gate_w) + dot_nt(grad_up, up_w)

    @pl.when(step == N_CHUNKS + 1)
    def _():
        grad = dot_nt(grad_mid[...].astype(bf16), shuffle_ref[...])
        part, terms = rms_back(resid[...], gain_ref[...], grad)
        dgain_ref[...] = jnp.sum(terms, axis=0, keepdims=True)
        dres = cot_ref[...].astype(f32) + part
        dres_ref[...] = dres
        low = dres.astype(bf16)
        wide_ref[:, 2 * FF :] = low
        for c in range(4):
            piece = dot_nt(low, w_out[c * 4 * HD : (c + 1) * 4 * HD, :]).astype(bf16)
            for h in range(4):
                dob_ref[4 * c + h] = piece[:, h * HD : (h + 1) * HD]


def middle(full, mixed, tok, cot, gain, shuffle):
    rows, width = tok.shape
    n_blocks = full.shape[0]
    first = OUT_ROWS // CHUNK_ROWS

    def chunk_of(i):
        return jnp.clip(i - 1, 0, N_CHUNKS - 1)

    def whole(shape):
        return pl.BlockSpec(shape, lambda i: (0,) * len(shape))

    chunk = (n_blocks, CHUNK_ROWS, CHUNK)
    return pl.pallas_call(
        middle_kernel,
        grid=(N_CHUNKS + 2,),
        in_specs=[
            pl.BlockSpec(memory_space=pl.ANY),
            whole((H_Q, rows, HD)),
            whole((rows, width)),
            whole((rows, width)),
            whole((1, width)),
            whole((width, width)),
            pl.BlockSpec(chunk, lambda i: (0, first + chunk_of(i), 0)),
            pl.BlockSpec(chunk, lambda i: (0, first + N_CHUNKS + chunk_of(i), 0)),
        ],
        out_specs=[
            whole((rows, width)),
            whole((rows, width)),
            whole((H_Q, rows, HD)),
            whole((2, rows, LEFT)),
            whole((rows, 2 * FF + width)),
            whole((1, width)),
        ],
        out_shape=[
            jax.ShapeDtypeStruct((rows, width), f32),
            jax.ShapeDtypeStruct((rows, width), f32),
            jax.ShapeDtypeStruct((H_Q, rows, HD), bf16),
            jax.ShapeDtypeStruct((2, rows, LEFT), bf16),
            jax.ShapeDtypeStruct((rows, 2 * FF + width), bf16),
            jax.ShapeDtypeStruct((1, width), f32),
        ],
        scratch_shapes=[
            pltpu.VMEM((Q_WIDTH + FF, width), bf16),
            pltpu.VMEM((rows, width), f32),
            pltpu.VMEM((rows, width), bf16),
            pltpu.VMEM((rows, width), f32),
            pltpu.SemaphoreType.DMA((n_blocks,)),
        ],
        compiler_params=pltpu.CompilerParams(vmem_limit_bytes=BIG_VMEM_BYTES),
        name="middle",
    )(full, mixed, tok, cot, gain, shuffle, full, full)


def grad_ffn_kernel(left_a, left_b, right_a, right_b, out_ref):
    total = dot_tn(left_a[...], right_a[...]) + dot_tn(left_b[...], right_b[...])
    out_ref[...] = total.astype(bf16).reshape(out_ref.shape)


def grad_ffn(lefts, wides, n_blocks):
    rows = lefts[0].shape[0]
    left = pl.BlockSpec((rows, HALF_MID), lambda i: (0, HALF_OUT // HALF_MID))
    right = pl.BlockSpec((rows, CHUNK), lambda i: (0, i))
    first = OUT_ROWS // CHUNK_ROWS
    height = OUT_ROWS + 2 * N_CHUNKS * CHUNK_ROWS
    return pl.pallas_call(
        grad_ffn_kernel,
        grid=(2 * N_CHUNKS,),
        in_specs=[left, left, right, right],
        out_specs=pl.BlockSpec((n_blocks, CHUNK_ROWS, CHUNK), lambda i: (0, first + i, 0)),
        out_shape=jax.ShapeDtypeStruct((n_blocks, height, CHUNK), bf16),
        compiler_params=pltpu.CompilerParams(vmem_limit_bytes=VMEM_BYTES),
        name="grad_ffn",
    )(*lefts, *wides)


def grad_out_kernel(core_ref, left_a, left_b, drb_a, drb_b, cot_a, cot_b, grads_ref, out_ref):
    step = pl.program_id(0)
    block = left_a.shape[1]
    both = Q_WIDTH // block
    cut = Q_WIDTH % block
    lower = core_ref[0] == 0

    def store(value):
        out_ref[...] = value.astype(bf16).reshape(out_ref.shape)

    @pl.when(lower & (step < both))
    def _():
        store(dot_tn(left_a[...], drb_a[...]) + dot_tn(left_b[...], drb_b[...]))

    @pl.when(lower & (step == both))
    def _():
        top = dot_tn(left_a[:, :cut], drb_a[...]) + dot_tn(left_b[:, :cut], drb_b[...])
        rest = dot_tn(left_a[:, cut:], cot_a[...]) + dot_tn(left_b[:, cut:], cot_b[...])
        store(jnp.concatenate([top, rest], axis=0))

    @pl.when(core_ref[0] == 1)
    def _():
        store(dot_tn(left_a[...], cot_a[...]) + dot_tn(left_b[...], cot_b[...]))


def grad_out(core, lefts, wides, cots, grads):
    rows, width = cots[0].shape
    blocks = 4
    left = pl.BlockSpec((rows, blocks * OUT_ROWS), lambda i, core: (0, i))
    drb = pl.BlockSpec((rows, width), lambda i, core: (0, 2 * N_CHUNKS))
    cot = pl.BlockSpec((rows, width), lambda i, core: (0, 0))
    return pl.pallas_call(
        grad_out_kernel,
        grid_spec=pltpu.PrefetchScalarGridSpec(
            num_scalar_prefetch=1,
            grid=(grads.shape[0] // blocks,),
            in_specs=[left, left, drb, drb, cot, cot, pl.BlockSpec(memory_space=pl.ANY)],
            out_specs=pl.BlockSpec((blocks, OUT_ROWS, width), lambda i, core: (i, 0, 0)),
        ),
        out_shape=jax.ShapeDtypeStruct(grads.shape, bf16),
        input_output_aliases={7: 0},
        compiler_params=pltpu.CompilerParams(vmem_limit_bytes=VMEM_BYTES),
        name="grad_out",
    )(core, *lefts, *wides, *cots, grads)


def adam_step(master, first_old, second_old, gradient, rate):
    first_new = BETA_ONE * first_old + (1.0 - BETA_ONE) * gradient
    second_new = BETA_TWO * second_old + (1.0 - BETA_TWO) * gradient * gradient
    first_hat = first_new / (1.0 - BETA_ONE**STEP)
    second_hat = second_new / (1.0 - BETA_TWO**STEP)
    master_new = master - rate * (
        first_hat / (jnp.sqrt(second_hat) + ADAM_EPS) + WEIGHT_DECAY * master
    )
    return (first_new, second_new, master_new)


def gathered(x):
    return lax.all_gather(x, AXIS_CYZ, axis=0, tiled=True)


def shift(x, axis, step):
    n = SIZES[axis]
    return lax.ppermute(x, axis, [(i, (i + step) % n) for i in range(n)])


def first_moves(x):
    first, second = x[None, :HALF], x[None, HALF:]
    pair = jnp.concatenate([first, shift(first, "xh", 1)], axis=0)
    ring = jnp.concatenate([second] + [shift(second, "y", b) for b in (1, 2, 3)], axis=0)
    return pair, ring


def second_moves(pair, ring, after):
    one = jnp.concatenate([pair] + [shift(pair, "y", b) for b in (1, 2, 3)], axis=0)
    two = jnp.concatenate([ring, shift(ring, "xh", 1)], axis=0)
    one, two, after = lax.optimization_barrier((one, two, after))
    return [one, two, shift(one, "core", 1), shift(two, "core", 1)], after


def places_of_groups():
    xh, y, core = (lax.axis_index(name) for name in CTX)
    places = []
    for other in range(2):
        for side in range(2):
            for i in range(GROUP):
                b, a = (i // 2, i % 2) if side == 0 else (i % 4, i // 4)
                dev = (((xh + a) % 2) * 4 + (y - b) % 4) * 2 + (core + other) % 2
                places.append(dev if side == 0 else 31 - dev)
    return jnp.stack(places).astype(jnp.int32)


def sum_over_core(near, far):
    return (near.astype(f32) + shift(far, "core", 1).astype(f32)).astype(bf16)


def first_sums(plane):
    one = plane[:GROUP].reshape((4, 2) + plane.shape[1:])
    two = plane[GROUP:].reshape((2, 4) + plane.shape[1:])
    two = (two[0].astype(f32) + shift(two[1], "xh", 1).astype(f32)).astype(bf16)
    one = sum((shift(one[b], "y", -b).astype(f32) for b in (1, 2, 3)), one[0].astype(f32))
    return one.astype(bf16), two


def second_sums(one, two):
    two = sum((shift(two[b], "y", -b).astype(f32) for b in (1, 2, 3)), two[0].astype(f32))
    one = one[0].astype(f32) + shift(one[1], "xh", 1).astype(f32)
    return jnp.concatenate([one, two], axis=0)


def both_along_xl(x, other):
    xl = lax.axis_index("xl")
    return jnp.stack([jnp.where(xl == 0, x, other), jnp.where(xl == 0, other, x)])


def pick(v, i, n):
    return lax.dynamic_index_in_dim(v, lax.rem(i, n), 0, keepdims=False)


def sum_over_x(blocks):
    me = lax.axis_index(AXIS_X)
    n = blocks.shape[0]
    total = pick(blocks, me, n).astype(f32)
    for step in range(1, n):
        moves = [(i, (i + step) % n) for i in range(n)]
        total = total + lax.ppermute(pick(blocks, me + step, n), AXIS_X, moves).astype(f32)
    return total


def sum_at_owners(blocks):
    me = lax.axis_index(AXIS_X)
    n = blocks.shape[0]
    total = 0.0
    for step in range(n):
        moves = []
        for source, place in owner_pairs():
            moves.append((source, place - place % n + (place % n + step) % n))
        total = total + lax.ppermute(pick(blocks, me + step, n), EVERY, moves).astype(f32)
    return total


def natural_of_permuted(x):
    tail = x.shape[1:]
    x = x.reshape((2, 4, 4, 2, 2) + tail)
    x = x.transpose((3, 1, 0, 4, 2) + tuple(range(5, 5 + len(tail))))
    return x.reshape((128,) + tail)


def owner_pairs():
    pairs = []
    for n in range(128):
        z = n % 4
        xl = (n // 4) % 2
        core = (n // 8) % 2
        y = (n // 16) % 4
        xh = n // 64
        pairs.append((n, (((core * 4 + y) * 4 + z) * 2 + xh) * 2 + xl))
    return pairs


def body(
    tokens,
    cotangent,
    segments,
    positions,
    pad_mask,
    w_in,
    w_out,
    gains,
    first_in,
    first_out,
    first_gains,
    second_in,
    second_out,
    second_gains,
):
    rows = tokens.shape[1]
    width = tokens.shape[2]
    span = segments.shape[1]
    half = rows // 2
    n_ctx = span // rows
    q_width = H_Q * HD
    kv_width = H_KV * HD
    attn_cols = q_width + 2 * kv_width
    owned = w_in.shape[0]
    owned_gains = gains.shape[0]

    n_x = 4
    low_in = w_in.astype(bf16)
    n_dev = width // owned

    own_head = jnp.concatenate(
        [
            low_in[:, :q_width].reshape(owned, H_Q, HD),
            jnp.repeat(low_in[:, q_width : q_width + kv_width].reshape(owned, H_KV, HD), 2, axis=1),
            jnp.repeat(low_in[:, q_width + kv_width : attn_cols].reshape(owned, H_KV, HD), 2, axis=1),
            jnp.broadcast_to(
                jnp.pad(gains.astype(bf16)[None, None], ((0, owned - 1), (0, 0), (0, HD - owned_gains))),
                (owned, H_Q, HD),
            ),
        ],
        axis=2,
    ).transpose(1, 0, 2)
    pair, ring = first_moves(tokens[0])
    head = lax.all_to_all(own_head, CTX, 0, 0, tiled=True)
    pairs = owner_pairs()
    own_out = lax.ppermute(w_out.astype(bf16), EVERY, [(p, n) for n, p in pairs])
    head, pair, ring, own_out = lax.optimization_barrier((head, pair, ring, own_out))
    own_ffn = low_in[:, attn_cols:].reshape(owned, 2 * N_CHUNKS, CHUNK)
    own_ffn = own_ffn.transpose(1, 0, 2).reshape(2 * N_CHUNKS * owned, CHUNK)
    own_rest = jnp.concatenate([own_out, own_ffn], axis=0)
    own_rest = lax.all_gather(own_rest, AXIS_X, axis=0, tiled=False)
    segments, pad_mask, own_rest, pair, ring = lax.optimization_barrier(
        (segments, pad_mask, own_rest, pair, ring)
    )
    n_out = w_out.shape[0]
    part_out = own_rest[:, :n_out].reshape(n_x * n_out, width)
    part_ffn = own_rest[:, n_out:].reshape(n_x, 2 * N_CHUNKS, owned, CHUNK).transpose(1, 0, 2, 3)
    part_ffn = part_ffn.reshape(2 * N_CHUNKS * CHUNK_ROWS, CHUNK)
    full = gathered(jnp.concatenate([part_out, part_ffn], axis=0)[None])

    order = natural_of_permuted(jnp.arange(width, dtype=jnp.int32).reshape(n_dev, owned)).reshape(-1)
    shuffle = (order[:, None] == jnp.arange(width, dtype=jnp.int32)[None, :]).astype(bf16)

    def natural(x):
        x = x.reshape(n_ctx, 2, half)
        return jnp.concatenate([x[:, 0], x[::-1, 1]], axis=0)

    halves = jnp.arange(HD // 2, dtype=f32)
    inverse = ROPE_BASE ** (-2.0 * halves / HD)
    cos, sin, lens = tables(
        natural(segments[0]), natural(pad_mask[0]), jnp.concatenate([inverse, inverse])[None]
    )
    first_key = (jnp.arange(span, dtype=jnp.int32).reshape(lens.shape) - lens).reshape(span // BQ, BQ)
    klo = jnp.stack(
        [jnp.min(first_key, axis=1) // BK, (jnp.max(first_key, axis=1) + BK - 1) // BK]
    )
    lens = lens.reshape(span // BQ, BQ)

    head, _ = lax.optimization_barrier((head, lens))
    head = lax.all_gather(head, "z", axis=0, tiled=False)
    other = shift(head, "xl", 1)
    groups, (cos, klo, lens, head, other) = second_moves(
        pair, ring, (cos, klo, lens, head, other)
    )
    head = both_along_xl(head, other).transpose(2, 0, 1, 3, 4)
    gain_vals = head[:, :, :, 0, HEAD_COLS : HEAD_COLS + owned_gains].reshape(-1).astype(f32)
    w_head = head[..., :HEAD_COLS].reshape(width, HEAD_COLS)
    gain_one = gain_vals[:width]
    gain_two = gain_vals[width : 2 * width]
    gain_query = gain_vals[2 * width : 2 * width + HD].reshape(1, HD)
    gain_key = gain_vals[2 * width + HD :].reshape(1, HD)
    w_scaled = (w_head.astype(f32) * gain_one[:, None]).astype(bf16)

    place = places_of_groups()
    q, k, v, query_raw, key_raw, inv = project(
        place, groups, w_scaled, cos, sin, gain_query, gain_key
    )
    o_send, o_nat, l_inv = attend(klo, q, k, v, lens, rows)
    mixed = lax.all_to_all(o_send, CTX, 0, 0, tiled=True)

    output, grad_residual, do_send, left, wide, gain_two_terms = middle(
        full, mixed, tokens[0], cotangent[0], gain_two.reshape(1, width), shuffle
    )
    core = lax.axis_index("core")
    lefts = (pick(left, core, 2), shift(pick(left, core + 1, 2), "core", 1))
    wides = (wide, shift(wide, "core", 1))
    cots = (cotangent[0], shift(cotangent[0], "core", 1))
    grads = grad_ffn(lefts, wides, full.shape[0] // 2)
    grads = grad_out(core.astype(jnp.int32).reshape(1), lefts, wides, cots, grads)
    do = lax.all_to_all(do_send, CTX, 0, 0, tiled=True)
    do, grads = lax.optimization_barrier((do, grads))
    grads = grads.reshape(-1, width)
    grads = lax.psum_scatter(grads, AXIS_YZ, scatter_dimension=0, tiled=True)

    head_grads = attend_back(klo, q, k, v, do, o_nat, l_inv, lens)
    da_near, da_far, dw_head, gain_qk = project_back(
        place, groups, head_grads, (query_raw, key_raw, inv), cos, sin, gain_query, gain_key, w_head
    )

    gain_one_grad = jnp.sum(dw_head * w_head.astype(f32), axis=1)
    grad_gains = jnp.concatenate([gain_one_grad, gain_two_terms[0], gain_qk[0], gain_qk[1]])
    grad_gains = jnp.pad(
        grad_gains.reshape(n_dev, 1, owned_gains), ((0, 0), (0, owned - 1), (0, HD - owned_gains))
    )
    dw_head = (dw_head * gain_one[:, None]).reshape(n_dev, owned, HEAD_COLS)
    dw_head = jnp.concatenate([dw_head, grad_gains], axis=2).astype(bf16)
    dw_head = dw_head.reshape(n_ctx, n_dev // n_ctx, owned, PAD_COLS).transpose(1, 0, 2, 3)
    plane = sum_over_core(da_near, da_far)
    one, two = first_sums(plane)
    dw_head = lax.all_to_all(dw_head, SHARD, 0, 0, tiled=True)
    dw_head = jnp.sum(dw_head.astype(f32), axis=0).astype(bf16)

    out_part = grads[:OUT_ROWS].reshape(n_x, OUT_ROWS // n_x, width)
    ffn_part = grads[OUT_ROWS:].reshape(2 * N_CHUNKS, n_x, owned, CHUNK)
    ffn_part = ffn_part.transpose(1, 0, 2, 3).reshape(n_x, 2 * N_CHUNKS * owned, CHUNK)
    owned_out = sum_at_owners(out_part)
    owned_ffn = sum_over_x(ffn_part).reshape(2 * N_CHUNKS, owned, CHUNK)
    one, two, owned_out, owned_ffn = lax.optimization_barrier((one, two, owned_out, owned_ffn))

    dw_head, _, _ = lax.optimization_barrier((dw_head, one, two))
    dw_head = lax.all_to_all(dw_head, CTX, 0, 0, tiled=True).astype(f32)
    owned_gain_grad = jnp.sum(dw_head[:, 0, HEAD_COLS : HEAD_COLS + owned_gains], axis=0)

    grad_a = second_sums(one, two)
    inputs = tokens[0].astype(f32)
    input_grad = grad_residual + rms_back(inputs, gain_one, grad_a)[0]

    def columns(x):
        return x.transpose(1, 0, 2).reshape(owned, -1)

    def over_pair(x):
        return columns(jnp.sum(x.reshape(H_KV, 2, owned, HD), axis=1))

    owned_in = jnp.concatenate(
        [
            columns(dw_head[:, :, :HD]),
            over_pair(dw_head[:, :, HD : 2 * HD]),
            over_pair(dw_head[:, :, 2 * HD : HEAD_COLS]),
            columns(owned_ffn),
        ],
        axis=1,
    )
    new_first_in, new_second_in, new_master_in = adam_step(
        w_in, first_in, second_in, owned_in, RATE_MATRIX
    )
    new_first_out, new_second_out, new_master_out = adam_step(
        w_out, first_out, second_out, owned_out, RATE_MATRIX
    )
    new_first_gains, new_second_gains, new_master_gains = adam_step(
        gains, first_gains, second_gains, owned_gain_grad, RATE_GAIN
    )
    return (
        output[None],
        input_grad[None],
        new_first_in,
        new_first_out,
        new_first_gains,
        new_second_in,
        new_second_out,
        new_second_gains,
        new_master_in,
        new_master_out,
        new_master_gains,
        new_master_in.astype(bf16),
        new_master_out.astype(bf16),
    )


def solution(mesh):
    cut = Mesh(mesh.devices.reshape(tuple(SIZES[name] for name in EVERY)), EVERY)
    weights = P(EVERY, None)
    vector = P(EVERY)
    acts = P(SHARD, CTX, None)
    in_specs = (
        acts,
        acts,
        P(SHARD, None),
        P(SHARD, CTX),
        P(SHARD, None),
    ) + (weights, weights, vector) * 3
    out_specs = (acts, acts) + (weights, weights, vector) * 3 + (weights, weights)
    return jax.shard_map(body, mesh=cut, in_specs=in_specs, out_specs=out_specs, check_vma=False)
```

```python
import functools
import math

import jax
import jax.numpy as jnp
from jax import lax
from jax.experimental import pallas as pl
from jax.experimental.pallas import tpu as pltpu
from jax.sharding import Mesh
from jax.sharding import PartitionSpec as P

H_Q = 16
H_KV = 8
HD = 128
FF = 3072
STEP = 5

NORM_EPS = 1e-06
ROPE_BASE = 1000000.0
BETA_ONE = 0.5
BETA_TWO = 0.5
ADAM_EPS = 1e-08
WEIGHT_DECAY = 0.1
RATE_MATRIX = 0.03
RATE_GAIN = 0.25

CTX = ("xh", "y", "core")
SHARD = ("xl", "z")
EVERY = CTX + SHARD
AXIS_X = ("xh", "xl")
AXIS_YZ = ("y", "z")
AXIS_CYZ = ("core", "y", "z")
SIZES = {"xh": 2, "y": 4, "core": 2, "xl": 2, "z": 4}

LOG2_E = 1.4426950408889634
SCORE_SCALE = 1.0 / math.sqrt(HD)
BQ = 512
BK = 512
SUB = 256
VMEM_BYTES = 48 * 1024 * 1024
BIG_VMEM_BYTES = 60 * 1024 * 1024

bf16 = jnp.bfloat16
f32 = jnp.float32


def rms_norm(values, weight):
    return values * lax.rsqrt(jnp.mean(values * values, axis=-1, keepdims=True) + NORM_EPS) * weight


def rms_back(values, weight, upstream):
    inverse = lax.rsqrt(jnp.mean(values * values, axis=-1, keepdims=True) + NORM_EPS)
    normed = values * inverse
    scaled = upstream * weight
    grad_values = inverse * (scaled - normed * jnp.mean(scaled * normed, axis=-1, keepdims=True))
    return (grad_values, upstream * normed)


def dot_nt(a, b):
    return lax.dot_general(a, b, (((1,), (1,)), ((), ())), preferred_element_type=f32)


def dot_tn(a, b):
    return lax.dot_general(a, b, (((0,), (0,)), ((), ())), preferred_element_type=f32)


def dot_nn(a, b):
    return lax.dot_general(a, b, (((1,), (0,)), ((), ())), preferred_element_type=f32)


LAST_DOC = 13


def tables_kernel(docs_ref, live_ref, freq_ref, cos_ref, sin_ref, lens_ref):
    docs = docs_ref[...]
    shape = docs.shape
    start = jnp.zeros(shape, f32)
    for number in range(1, LAST_DOC + 1):
        before = jnp.sum(jnp.where(docs < number, 1.0, 0.0))
        start = jnp.where(docs == number, before, start)
    at = lax.broadcasted_iota(jnp.int32, shape, 0) * shape[1] + lax.broadcasted_iota(
        jnp.int32, shape, 1
    )
    within = at.astype(f32) - start
    lens_ref[...] = jnp.where(live_ref[...] == 1, within.astype(jnp.int32), 0)

    left = lax.broadcasted_iota(jnp.int32, (HD, HD), 1) < HD // 2
    for i in range(0, shape[0], 2):
        cols = [jnp.broadcast_to(within[i + n : i + n + 1, :], (HD, HD)).T for n in range(2)]
        angle = jnp.where(left, cols[0], cols[1]) * freq_ref[...]
        for ref, values, flip in ((cos_ref, jnp.cos(angle), False), (sin_ref, jnp.sin(angle), True)):
            turned = pltpu.roll(values, HD // 2, 1)
            for n in range(2):
                lower, upper = (values, turned) if n == 0 else (turned, values)
                ref[(i + n) * HD : (i + n + 1) * HD, :] = jnp.where(
                    left, -lower if flip else lower, upper
                )


def tables(docs, live, freq):
    span = docs.size
    table = jax.ShapeDtypeStruct((span, HD), f32)
    return pl.pallas_call(
        tables_kernel,
        in_specs=[vmem()] * 3,
        out_specs=[vmem()] * 3,
        out_shape=[table, table, jax.ShapeDtypeStruct(docs.shape, jnp.int32)],
        compiler_params=pltpu.CompilerParams(vmem_limit_bytes=VMEM_BYTES),
        cost_estimate=pl.CostEstimate(
            flops=100 * span * HD, bytes_accessed=3 * span * HD * 4, transcendentals=span * HD
        ),
        name="tables",
    )(docs, live, freq)


N_GROUPS = 4
GROUP = 8
HALF = 128
STEP_BLOCKS = 4
STEPS = GROUP // STEP_BLOCKS
HEAD_COLS = 3 * HD
PAD_COLS = 4 * HD


def block_spec(width, first, count):
    return pl.BlockSpec(
        (STEP_BLOCKS, HALF, width), lambda i, place: (jnp.clip(i - first, 0, count - 1), 0, 0)
    )


def group_specs(width):
    return [block_spec(width, k * STEPS, STEPS) for k in range(N_GROUPS)]


def fixed(shape):
    return pl.BlockSpec(shape, lambda i, place: (0,) * len(shape))


def rows_of(place_ref, step, i):
    return pl.ds(pl.multiple_of(place_ref[step * STEP_BLOCKS + i] * HALF, HALF), HALF)


def head_mean(x):
    return lax.dot_general(
        x.astype(bf16),
        jnp.full((HD, HD), 1.0 / HD, bf16),
        (((1,), (0,)), ((), ())),
        preferred_element_type=f32,
    )


def project_kernel(
    place_ref, x0, x1, x2, x3, w_ref, cos_ref, sin_ref, gq_ref, gk_ref,
    q_ref, k_ref, v_ref, qraw_ref, kraw_ref, inv_ref,
):
    step = pl.program_id(0)

    def run(x):
        wide = x.astype(f32)
        inverse = lax.rsqrt(jnp.mean(wide * wide, axis=-1, keepdims=True) + NORM_EPS)
        prod = dot_nn(x, w_ref[...]) * inverse
        for i in range(STEP_BLOCKS):
            at = rows_of(place_ref, step, i)
            part = slice(i * HALF, (i + 1) * HALF)
            cos = cos_ref[at, :]
            sin = sin_ref[at, :]

            def roped(raw, gain, cos=cos, sin=sin):
                normed = raw * lax.rsqrt(head_mean(raw * raw) + NORM_EPS) * gain
                return normed * cos + pltpu.roll(normed, HD // 2, 1) * sin

            query = prod[part, :HD]
            key = prod[part, HD : 2 * HD]
            inv_ref[at, :] = jnp.broadcast_to(inverse[part], (HALF, HD)).astype(bf16)
            qraw_ref[at, :] = query.astype(bf16)
            kraw_ref[at, :] = key.astype(bf16)
            q_ref[at, :] = (roped(query, gq_ref[...]) * (SCORE_SCALE * LOG2_E)).astype(bf16)
            k_ref[at, :] = roped(key, gk_ref[...]).astype(bf16)
            v_ref[at, :] = prod[part, 2 * HD :].astype(bf16)

    for k, x_ref in enumerate((x0, x1, x2, x3)):

        @pl.when(step // STEPS == k)
        def _(x_ref=x_ref):
            run(x_ref[...].reshape(STEP_BLOCKS * HALF, x_ref.shape[2]))


def project(place, groups, w, cos, sin, gq, gk):
    width = w.shape[0]
    span = cos.shape[0]
    low = jax.ShapeDtypeStruct((span, HD), bf16)
    whole = fixed((span, HD))
    return pl.pallas_call(
        project_kernel,
        grid_spec=pltpu.PrefetchScalarGridSpec(
            num_scalar_prefetch=1,
            grid=(N_GROUPS * STEPS,),
            in_specs=group_specs(width)
            + [fixed((width, HEAD_COLS)), whole, whole, fixed((1, HD)), fixed((1, HD))],
            out_specs=[whole] * 6,
        ),
        out_shape=[low] * 6,
        compiler_params=pltpu.CompilerParams(vmem_limit_bytes=VMEM_BYTES),
        name="project",
    )(place, *groups, w, cos, sin, gq, gk)


def project_back_kernel(
    place_ref, x0, x1, x2, x3, dq_ref, dk_ref, dv_ref, qraw_ref, kraw_ref, inv_ref, cos_ref, sin_ref,
    gq_ref, gk_ref, w_ref, near_ref, far_ref, dw_ref, dg_ref, grads, scaled,
):
    step = pl.program_id(0)

    @pl.when(step == 0)
    def _():
        dw_ref[...] = jnp.zeros_like(dw_ref)
        dg_ref[...] = jnp.zeros_like(dg_ref)

    def run(x, da_ref):
        q_sum = jnp.zeros((1, HD), f32)
        k_sum = jnp.zeros((1, HD), f32)
        for i in range(STEP_BLOCKS):
            at = rows_of(place_ref, step, i)
            part = slice(i * HALF, (i + 1) * HALF)
            cos = cos_ref[at, :]
            sin = sin_ref[at, :]

            def back(raw, gain, grad, cos=cos, sin=sin):
                unrot = grad * cos + pltpu.roll(grad * sin, HD // 2, 1)
                inv_rms = lax.rsqrt(head_mean(raw * raw) + NORM_EPS)
                normed = raw * inv_rms
                scaled_up = unrot * gain
                grad = inv_rms * (scaled_up - normed * head_mean(scaled_up * normed))
                return grad, unrot * normed

            grad_q, q_terms = back(qraw_ref[at, :].astype(f32), gq_ref[...], dq_ref[at, :])
            grad_k, k_terms = back(kraw_ref[at, :].astype(f32), gk_ref[...], dk_ref[at, :])
            inverse = inv_ref[at, :].astype(f32)
            for c, grad in enumerate((grad_q, grad_k, dv_ref[at, :])):
                grads[part, c * HD : (c + 1) * HD] = grad.astype(bf16)
                scaled[part, c * HD : (c + 1) * HD] = (grad * inverse).astype(bf16)
            q_sum = q_sum + jnp.sum(q_terms, axis=0, keepdims=True)
            k_sum = k_sum + jnp.sum(k_terms, axis=0, keepdims=True)
        da_ref[...] = dot_nt(grads[...], w_ref[...]).astype(bf16).reshape(da_ref.shape)
        dw_ref[...] += dot_tn(x, scaled[...])
        dg_ref[0:1, :] += q_sum
        dg_ref[1:2, :] += k_sum

    for k, x_ref in enumerate((x0, x1, x2, x3)):

        @pl.when(step // STEPS == k)
        def _(k=k, x_ref=x_ref):
            da_ref = near_ref if k < N_GROUPS // 2 else far_ref
            run(x_ref[...].reshape(STEP_BLOCKS * HALF, x_ref.shape[2]), da_ref)


def project_back(place, groups, grads, raws, cos, sin, gq, gk, w):
    width = w.shape[0]
    span = cos.shape[0]
    whole = fixed((span, HD))
    n_half = N_GROUPS // 2
    da = jax.ShapeDtypeStruct((n_half * GROUP, HALF, width), bf16)
    return pl.pallas_call(
        project_back_kernel,
        grid_spec=pltpu.PrefetchScalarGridSpec(
            num_scalar_prefetch=1,
            grid=(N_GROUPS * STEPS,),
            in_specs=group_specs(width)
            + [whole] * 8
            + [fixed((1, HD)), fixed((1, HD)), fixed((width, HEAD_COLS))],
            out_specs=[
                block_spec(width, 0, n_half * STEPS),
                block_spec(width, n_half * STEPS, n_half * STEPS),
                fixed((width, HEAD_COLS)),
                fixed((8, HD)),
            ],
            scratch_shapes=[
                pltpu.VMEM((STEP_BLOCKS * HALF, HEAD_COLS), bf16),
                pltpu.VMEM((STEP_BLOCKS * HALF, HEAD_COLS), bf16),
            ],
        ),
        out_shape=[
            da,
            da,
            jax.ShapeDtypeStruct((width, HEAD_COLS), f32),
            jax.ShapeDtypeStruct((8, HD), f32),
        ],
        compiler_params=pltpu.CompilerParams(vmem_limit_bytes=BIG_VMEM_BYTES),
        name="project_back",
    )(place, *groups, *grads, *raws, cos, sin, gq, gk, w)


def dealt_slot(place, n_dev):
    if place < n_dev:
        return place, 0
    return 2 * n_dev - 1 - place, 1


def key_mask(len_row, offset):
    ahead = (
        lax.broadcasted_iota(jnp.int32, (SUB, BQ), 1)
        - lax.broadcasted_iota(jnp.int32, (SUB, BQ), 0)
        + offset
    )
    return (ahead >= 0) & (ahead <= len_row)


def key_loops(bounds_ref, qb, q_at, tile):
    low = bounds_ref[0, qb]
    high = (q_at + BQ - 1) // BK + 1
    first = jnp.minimum(bounds_ref[1, qb], high)
    last = jnp.maximum((q_at + 1) // BK, first)

    def run(masked):
        def step(kb, _):
            tile(kb, masked)
            return 0

        return step

    lax.fori_loop(low, first, run(True), 0)
    lax.fori_loop(first, last, run(False), 0)
    lax.fori_loop(last, high, run(True), 0)


def attend_kernel(
    bounds_ref, q_ref, k_ref, v_ref, len_ref, osend_ref, onat_ref, linv_ref, acc, total
):
    n_dev, rows, _ = osend_ref.shape
    half = rows // 2
    span = q_ref.shape[0]
    def q_step(qb, _):
        q_at = pl.multiple_of(qb * BQ, BQ)
        q_blk = q_ref[pl.ds(q_at, BQ), :]
        len_row = len_ref[pl.ds(qb, 1), :]
        acc[...] = jnp.zeros_like(acc)
        total[...] = jnp.zeros_like(total)

        def tile(kb, masked):
            mixed = None
            summed = None
            for c in range(BK // SUB):
                k_at = pl.multiple_of(kb * BK + c * SUB, SUB)
                p = jnp.exp2(dot_nt(k_ref[pl.ds(k_at, SUB), :], q_blk))
                if masked:
                    p = jnp.where(key_mask(len_row, q_at - k_at), p, 0.0)
                part = jnp.sum(p.reshape(SUB // 8, 8, BQ), axis=0)
                more = dot_tn(v_ref[pl.ds(k_at, SUB), :], p.astype(bf16))
                summed = part if summed is None else summed + part
                mixed = more if mixed is None else mixed + more
            acc[...] += mixed
            total[...] += summed

        key_loops(bounds_ref, qb, q_at, tile)
        inverse = 1.0 / jnp.sum(total[...], axis=0, keepdims=True)
        linv_ref[pl.ds(qb, 1), :] = inverse
        onat_ref[pl.ds(q_at, BQ), :] = (acc[...] * inverse).T
        return 0

    lax.fori_loop(0, span // BQ, q_step, 0)
    for place in range(2 * n_dev):
        dev, side = dealt_slot(place, n_dev)
        osend_ref[dev, side * half : (side + 1) * half, :] = onat_ref[
            place * half : (place + 1) * half, :
        ].astype(bf16)


def vmem():
    return pl.BlockSpec(memory_space=pltpu.VMEM)


def attend(klo, q, k, v, lens, rows):
    span = q.shape[0]
    return pl.pallas_call(
        attend_kernel,
        in_specs=[pl.BlockSpec(memory_space=pltpu.SMEM)] + [vmem()] * 4,
        out_specs=[vmem(), vmem(), vmem()],
        out_shape=[
            jax.ShapeDtypeStruct((span // rows, rows, HD), bf16),
            jax.ShapeDtypeStruct((span, HD), f32),
            jax.ShapeDtypeStruct((span // BQ, BQ), f32),
        ],
        scratch_shapes=[
            pltpu.VMEM((HD, BQ), f32),
            pltpu.VMEM((8, BQ), f32),
        ],
        compiler_params=pltpu.CompilerParams(vmem_limit_bytes=VMEM_BYTES),
        name="attend",
    )(klo, q, k, v, lens)


def attend_back_kernel(
    bounds_ref, q_ref, k_ref, v_ref, do_ref, onat_ref, linv_ref, len_ref, dq, dk, dv, don, acc
):
    n_dev, rows, _ = do_ref.shape
    half = rows // 2
    span = q_ref.shape[0]
    for place in range(2 * n_dev):
        dev, side = dealt_slot(place, n_dev)
        to = slice(place * half, (place + 1) * half)
        don[to, :] = do_ref[dev, side * half : (side + 1) * half, :]
    dk[...] = jnp.zeros_like(dk)
    dv[...] = jnp.zeros_like(dv)

    def q_step(qb, _):
        q_at = pl.multiple_of(qb * BQ, BQ)
        q_blk = q_ref[pl.ds(q_at, BQ), :]
        do_blk = don[pl.ds(q_at, BQ), :]
        len_row = len_ref[pl.ds(qb, 1), :]
        inverse = linv_ref[pl.ds(qb, 1), :]
        mixed = (do_blk.astype(f32) * onat_ref[pl.ds(q_at, BQ), :]).T
        delta = jnp.sum(mixed, axis=0, keepdims=True)
        acc[...] = jnp.zeros_like(acc)

        def tile(kb, masked):
            total = None
            for c in range(BK // SUB):
                k_at = pl.multiple_of(kb * BK + c * SUB, SUB)
                here = pl.ds(k_at, SUB)
                p = jnp.exp2(dot_nt(k_ref[here, :], q_blk)) * inverse
                if masked:
                    p = jnp.where(key_mask(len_row, q_at - k_at), p, 0.0)
                dp = dot_nt(v_ref[here, :], do_blk)
                ds = (p * (dp - delta)).astype(bf16)
                dv[here, :] += dot_nn(p.astype(bf16), do_blk)
                dk[here, :] += dot_nn(ds, q_blk)
                more = dot_tn(k_ref[here, :], ds)
                total = more if total is None else total + more
            acc[...] += total

        key_loops(bounds_ref, qb, q_at, tile)
        dq[pl.ds(q_at, BQ), :] = (acc[...] * SCORE_SCALE).T
        return 0

    lax.fori_loop(0, span // BQ, q_step, 0)
    dk[...] = dk[...] * (1.0 / LOG2_E)


def attend_back(klo, q, k, v, do, onat, linv, lens):
    span = q.shape[0]
    return pl.pallas_call(
        attend_back_kernel,
        in_specs=[pl.BlockSpec(memory_space=pltpu.SMEM)] + [vmem()] * 7,
        out_specs=[vmem()] * 3,
        out_shape=[jax.ShapeDtypeStruct((span, HD), f32)] * 3,
        scratch_shapes=[
            pltpu.VMEM((span, HD), bf16),
            pltpu.VMEM((HD, BQ), f32),
        ],
        compiler_params=pltpu.CompilerParams(vmem_limit_bytes=VMEM_BYTES),
        name="attend_back",
    )(klo, q, k, v, do, onat, linv, lens)


OUT_ROWS = 160
CHUNK_ROWS = 32
N_CHUNKS = 3
CHUNK = FF // N_CHUNKS
Q_WIDTH = H_Q * HD
HALF_OUT = (Q_WIDTH + FF) // 2
HALF_MID = 512
LEFT = HALF_OUT + HALF_MID


def middle_kernel(
    full_ref, mixed_ref, tok_ref, cot_ref, gain_ref, shuffle_ref, gate_ref, up_ref,
    out_ref, dres_ref, dob_ref, left_ref, wide_ref, dgain_ref,
    w_out, resid, mid_low, grad_mid, sems,
):
    step = pl.program_id(0)
    width = tok_ref.shape[1]

    def fetch(i):
        return pltpu.make_async_copy(
            full_ref.at[i, pl.ds(0, OUT_ROWS), :],
            w_out.at[pl.ds(i * OUT_ROWS, OUT_ROWS), :],
            sems.at[i],
        )

    n_fetch = full_ref.shape[0]
    n_first = -(-Q_WIDTH // OUT_ROWS)

    @pl.when(step == 0)
    def _():
        for i in range(n_fetch):
            fetch(i).start()
        for h in range(H_Q):
            left_ref[0, :, h * HD : (h + 1) * HD] = mixed_ref[h]
        for i in range(n_first):
            fetch(i).wait()
        residual = tok_ref[...].astype(f32) + dot_nn(
            left_ref[0, :, :Q_WIDTH], w_out[:Q_WIDTH, :]
        )
        resid[...] = residual
        out_ref[...] = residual
        normed = rms_norm(residual, gain_ref[...]).astype(bf16)
        low = dot_nn(normed, shuffle_ref[...]).astype(bf16)
        mid_low[...] = low
        for side in range(2):
            left_ref[side, :, HALF_OUT:] = low[:, side * HALF_MID : (side + 1) * HALF_MID]
        grad_mid[...] = jnp.zeros_like(grad_mid)
        for i in range(n_first, n_fetch):
            fetch(i).wait()

    for f in range(N_CHUNKS):

        @pl.when(step == f + 1)
        def _(f=f):
            at = Q_WIDTH + f * CHUNK
            gate_w = gate_ref[...].reshape(width, CHUNK)
            up_w = up_ref[...].reshape(width, CHUNK)
            gate = dot_nn(mid_low[...], gate_w)
            up = dot_nn(mid_low[...], up_w)
            sigmoid_gate = 1.0 / (1.0 + jnp.exp(-gate))
            activated = gate * sigmoid_gate
            hidden = (activated * up).astype(bf16)
            cut = min(max(HALF_OUT - at, 0), CHUNK)
            if cut > 0:
                left_ref[0, :, at : at + cut] = hidden[:, :cut]
            if cut < CHUNK:
                left_ref[1, :, at + cut - HALF_OUT : at + CHUNK - HALF_OUT] = hidden[:, cut:]
            down_w = w_out[at : at + CHUNK, :]
            out_ref[...] += dot_nn(hidden, down_w)
            grad_hidden = dot_nt(cot_ref[...], down_w)
            grad_up = (grad_hidden * activated).astype(bf16)
            grad_gate = (
                grad_hidden * up * sigmoid_gate * (1.0 + gate * (1.0 - sigmoid_gate))
            ).astype(bf16)
            wide_ref[:, f * CHUNK : (f + 1) * CHUNK] = grad_gate
            wide_ref[:, FF + f * CHUNK : FF + (f + 1) * CHUNK] = grad_up
            grad_mid[...] += dot_nt(grad_gate, gate_w) + dot_nt(grad_up, up_w)

    @pl.when(step == N_CHUNKS + 1)
    def _():
        grad = dot_nt(grad_mid[...].astype(bf16), shuffle_ref[...])
        part, terms = rms_back(resid[...], gain_ref[...], grad)
        dgain_ref[...] = jnp.sum(terms, axis=0, keepdims=True)
        dres = cot_ref[...].astype(f32) + part
        dres_ref[...] = dres
        low = dres.astype(bf16)
        wide_ref[:, 2 * FF :] = low
        for c in range(4):
            piece = dot_nt(low, w_out[c * 4 * HD : (c + 1) * 4 * HD, :]).astype(bf16)
            for h in range(4):
                dob_ref[4 * c + h] = piece[:, h * HD : (h + 1) * HD]


def middle(full, mixed, tok, cot, gain, shuffle):
    rows, width = tok.shape
    n_blocks = full.shape[0]
    first = OUT_ROWS // CHUNK_ROWS

    def chunk_of(i):
        return jnp.clip(i - 1, 0, N_CHUNKS - 1)

    def whole(shape):
        return pl.BlockSpec(shape, lambda i: (0,) * len(shape))

    chunk = (n_blocks, CHUNK_ROWS, CHUNK)
    return pl.pallas_call(
        middle_kernel,
        grid=(N_CHUNKS + 2,),
        in_specs=[
            pl.BlockSpec(memory_space=pl.ANY),
            whole((H_Q, rows, HD)),
            whole((rows, width)),
            whole((rows, width)),
            whole((1, width)),
            whole((width, width)),
            pl.BlockSpec(chunk, lambda i: (0, first + chunk_of(i), 0)),
            pl.BlockSpec(chunk, lambda i: (0, first + N_CHUNKS + chunk_of(i), 0)),
        ],
        out_specs=[
            whole((rows, width)),
            whole((rows, width)),
            whole((H_Q, rows, HD)),
            whole((2, rows, LEFT)),
            whole((rows, 2 * FF + width)),
            whole((1, width)),
        ],
        out_shape=[
            jax.ShapeDtypeStruct((rows, width), f32),
            jax.ShapeDtypeStruct((rows, width), f32),
            jax.ShapeDtypeStruct((H_Q, rows, HD), bf16),
            jax.ShapeDtypeStruct((2, rows, LEFT), bf16),
            jax.ShapeDtypeStruct((rows, 2 * FF + width), bf16),
            jax.ShapeDtypeStruct((1, width), f32),
        ],
        scratch_shapes=[
            pltpu.VMEM((Q_WIDTH + FF, width), bf16),
            pltpu.VMEM((rows, width), f32),
            pltpu.VMEM((rows, width), bf16),
            pltpu.VMEM((rows, width), f32),
            pltpu.SemaphoreType.DMA((n_blocks,)),
        ],
        compiler_params=pltpu.CompilerParams(vmem_limit_bytes=BIG_VMEM_BYTES),
        name="middle",
    )(full, mixed, tok, cot, gain, shuffle, full, full)


def grad_ffn_kernel(left_a, left_b, right_a, right_b, out_ref):
    total = dot_tn(left_a[...], right_a[...]) + dot_tn(left_b[...], right_b[...])
    out_ref[...] = total.astype(bf16).reshape(out_ref.shape)


def grad_ffn(lefts, wides, n_blocks):
    rows = lefts[0].shape[0]
    left = pl.BlockSpec((rows, HALF_MID), lambda i: (0, HALF_OUT // HALF_MID))
    right = pl.BlockSpec((rows, CHUNK), lambda i: (0, i))
    first = OUT_ROWS // CHUNK_ROWS
    height = OUT_ROWS + 2 * N_CHUNKS * CHUNK_ROWS
    return pl.pallas_call(
        grad_ffn_kernel,
        grid=(2 * N_CHUNKS,),
        in_specs=[left, left, right, right],
        out_specs=pl.BlockSpec((n_blocks, CHUNK_ROWS, CHUNK), lambda i: (0, first + i, 0)),
        out_shape=jax.ShapeDtypeStruct((n_blocks, height, CHUNK), bf16),
        compiler_params=pltpu.CompilerParams(vmem_limit_bytes=VMEM_BYTES),
        name="grad_ffn",
    )(*lefts, *wides)


def grad_out_kernel(core_ref, left_a, left_b, drb_a, drb_b, cot_a, cot_b, grads_ref, out_ref):
    step = pl.program_id(0)
    block = left_a.shape[1]
    both = Q_WIDTH // block
    cut = Q_WIDTH % block
    lower = core_ref[0] == 0

    def store(value):
        out_ref[...] = value.astype(bf16).reshape(out_ref.shape)

    @pl.when(lower & (step < both))
    def _():
        store(dot_tn(left_a[...], drb_a[...]) + dot_tn(left_b[...], drb_b[...]))

    @pl.when(lower & (step == both))
    def _():
        top = dot_tn(left_a[:, :cut], drb_a[...]) + dot_tn(left_b[:, :cut], drb_b[...])
        rest = dot_tn(left_a[:, cut:], cot_a[...]) + dot_tn(left_b[:, cut:], cot_b[...])
        store(jnp.concatenate([top, rest], axis=0))

    @pl.when(core_ref[0] == 1)
    def _():
        store(dot_tn(left_a[...], cot_a[...]) + dot_tn(left_b[...], cot_b[...]))


def grad_out(core, lefts, wides, cots, grads):
    rows, width = cots[0].shape
    blocks = 4
    left = pl.BlockSpec((rows, blocks * OUT_ROWS), lambda i, core: (0, i))
    drb = pl.BlockSpec((rows, width), lambda i, core: (0, 2 * N_CHUNKS))
    cot = pl.BlockSpec((rows, width), lambda i, core: (0, 0))
    return pl.pallas_call(
        grad_out_kernel,
        grid_spec=pltpu.PrefetchScalarGridSpec(
            num_scalar_prefetch=1,
            grid=(grads.shape[0] // blocks,),
            in_specs=[left, left, drb, drb, cot, cot, pl.BlockSpec(memory_space=pl.ANY)],
            out_specs=pl.BlockSpec((blocks, OUT_ROWS, width), lambda i, core: (i, 0, 0)),
        ),
        out_shape=jax.ShapeDtypeStruct(grads.shape, bf16),
        input_output_aliases={7: 0},
        compiler_params=pltpu.CompilerParams(vmem_limit_bytes=VMEM_BYTES),
        name="grad_out",
    )(core, *lefts, *wides, *cots, grads)


def adam_step(master, first_old, second_old, gradient, rate):
    first_new = BETA_ONE * first_old + (1.0 - BETA_ONE) * gradient
    second_new = BETA_TWO * second_old + (1.0 - BETA_TWO) * gradient * gradient
    first_hat = first_new / (1.0 - BETA_ONE**STEP)
    second_hat = second_new / (1.0 - BETA_TWO**STEP)
    master_new = master - rate * (
        first_hat / (jnp.sqrt(second_hat) + ADAM_EPS) + WEIGHT_DECAY * master
    )
    return (first_new, second_new, master_new)


def gathered(x):
    return lax.all_gather(x, AXIS_CYZ, axis=0, tiled=True)


def shift(x, axis, step):
    n = SIZES[axis]
    return lax.ppermute(x, axis, [(i, (i + step) % n) for i in range(n)])


def first_moves(x):
    first, second = x[None, :HALF], x[None, HALF:]
    pair = jnp.concatenate([first, shift(first, "xh", 1)], axis=0)
    ring = jnp.concatenate([second] + [shift(second, "y", b) for b in (1, 2, 3)], axis=0)
    return pair, ring


def second_moves(pair, ring, after):
    one = jnp.concatenate([pair] + [shift(pair, "y", b) for b in (1, 2, 3)], axis=0)
    two = jnp.concatenate([ring, shift(ring, "xh", 1)], axis=0)
    one, two, after = lax.optimization_barrier((one, two, after))
    return [one, two, shift(one, "core", 1), shift(two, "core", 1)], after


def places_of_groups():
    xh, y, core = (lax.axis_index(name) for name in CTX)
    places = []
    for other in range(2):
        for side in range(2):
            for i in range(GROUP):
                b, a = (i // 2, i % 2) if side == 0 else (i % 4, i // 4)
                dev = (((xh + a) % 2) * 4 + (y - b) % 4) * 2 + (core + other) % 2
                places.append(dev if side == 0 else 31 - dev)
    return jnp.stack(places).astype(jnp.int32)


def sum_over_core(near, far):
    return (near.astype(f32) + shift(far, "core", 1).astype(f32)).astype(bf16)


def first_sums(plane):
    one = plane[:GROUP].reshape((4, 2) + plane.shape[1:])
    two = plane[GROUP:].reshape((2, 4) + plane.shape[1:])
    two = (two[0].astype(f32) + shift(two[1], "xh", 1).astype(f32)).astype(bf16)
    one = sum((shift(one[b], "y", -b).astype(f32) for b in (1, 2, 3)), one[0].astype(f32))
    return one.astype(bf16), two


def second_sums(one, two):
    two = sum((shift(two[b], "y", -b).astype(f32) for b in (1, 2, 3)), two[0].astype(f32))
    one = one[0].astype(f32) + shift(one[1], "xh", 1).astype(f32)
    return jnp.concatenate([one, two], axis=0)


def both_along_xl(x, other):
    xl = lax.axis_index("xl")
    return jnp.stack([jnp.where(xl == 0, x, other), jnp.where(xl == 0, other, x)])


def pick(v, i, n):
    return lax.dynamic_index_in_dim(v, lax.rem(i, n), 0, keepdims=False)


def sum_over_x(blocks):
    me = lax.axis_index(AXIS_X)
    n = blocks.shape[0]
    total = pick(blocks, me, n).astype(f32)
    for step in range(1, n):
        moves = [(i, (i + step) % n) for i in range(n)]
        total = total + lax.ppermute(pick(blocks, me + step, n), AXIS_X, moves).astype(f32)
    return total


def sum_at_owners(blocks):
    me = lax.axis_index(AXIS_X)
    n = blocks.shape[0]
    total = 0.0
    for step in range(n):
        moves = []
        for source, place in owner_pairs():
            moves.append((source, place - place % n + (place % n + step) % n))
        total = total + lax.ppermute(pick(blocks, me + step, n), EVERY, moves).astype(f32)
    return total


def natural_of_permuted(x):
    tail = x.shape[1:]
    x = x.reshape((2, 4, 4, 2, 2) + tail)
    x = x.transpose((3, 1, 0, 4, 2) + tuple(range(5, 5 + len(tail))))
    return x.reshape((128,) + tail)


def owner_pairs():
    pairs = []
    for n in range(128):
        z = n % 4
        xl = (n // 4) % 2
        core = (n // 8) % 2
        y = (n // 16) % 4
        xh = n // 64
        pairs.append((n, (((core * 4 + y) * 4 + z) * 2 + xh) * 2 + xl))
    return pairs


def body(
    tokens,
    cotangent,
    segments,
    positions,
    pad_mask,
    w_in,
    w_out,
    gains,
    first_in,
    first_out,
    first_gains,
    second_in,
    second_out,
    second_gains,
):
    rows = tokens.shape[1]
    width = tokens.shape[2]
    span = segments.shape[1]
    half = rows // 2
    n_ctx = span // rows
    q_width = H_Q * HD
    kv_width = H_KV * HD
    attn_cols = q_width + 2 * kv_width
    owned = w_in.shape[0]
    owned_gains = gains.shape[0]

    n_x = 4
    low_in = w_in.astype(bf16)
    n_dev = width // owned

    own_head = jnp.concatenate(
        [
            low_in[:, :q_width].reshape(owned, H_Q, HD),
            jnp.repeat(low_in[:, q_width : q_width + kv_width].reshape(owned, H_KV, HD), 2, axis=1),
            jnp.repeat(low_in[:, q_width + kv_width : attn_cols].reshape(owned, H_KV, HD), 2, axis=1),
            jnp.broadcast_to(
                jnp.pad(gains.astype(bf16)[None, None], ((0, owned - 1), (0, 0), (0, HD - owned_gains))),
                (owned, H_Q, HD),
            ),
        ],
        axis=2,
    ).transpose(1, 0, 2)
    pair, ring = first_moves(tokens[0])
    head = lax.all_to_all(own_head, CTX, 0, 0, tiled=True)
    pairs = owner_pairs()
    own_out = lax.ppermute(w_out.astype(bf16), EVERY, [(p, n) for n, p in pairs])
    head, pair, ring, own_out = lax.optimization_barrier((head, pair, ring, own_out))
    own_ffn = low_in[:, attn_cols:].reshape(owned, 2 * N_CHUNKS, CHUNK)
    own_ffn = own_ffn.transpose(1, 0, 2).reshape(2 * N_CHUNKS * owned, CHUNK)
    own_rest = jnp.concatenate([own_out, own_ffn], axis=0)
    own_rest = lax.all_gather(own_rest, AXIS_X, axis=0, tiled=False)
    segments, pad_mask, own_rest, pair, ring = lax.optimization_barrier(
        (segments, pad_mask, own_rest, pair, ring)
    )
    n_out = w_out.shape[0]
    part_out = own_rest[:, :n_out].reshape(n_x * n_out, width)
    part_ffn = own_rest[:, n_out:].reshape(n_x, 2 * N_CHUNKS, owned, CHUNK).transpose(1, 0, 2, 3)
    part_ffn = part_ffn.reshape(2 * N_CHUNKS * CHUNK_ROWS, CHUNK)
    full = gathered(jnp.concatenate([part_out, part_ffn], axis=0)[None])

    order = natural_of_permuted(jnp.arange(width, dtype=jnp.int32).reshape(n_dev, owned)).reshape(-1)
    shuffle = (order[:, None] == jnp.arange(width, dtype=jnp.int32)[None, :]).astype(bf16)

    def natural(x):
        x = x.reshape(n_ctx, 2, half)
        return jnp.concatenate([x[:, 0], x[::-1, 1]], axis=0)

    halves = jnp.arange(HD // 2, dtype=f32)
    inverse = ROPE_BASE ** (-2.0 * halves / HD)
    cos, sin, lens = tables(
        natural(segments[0]), natural(pad_mask[0]), jnp.concatenate([inverse, inverse])[None]
    )
    first_key = (jnp.arange(span, dtype=jnp.int32).reshape(lens.shape) - lens).reshape(span // BQ, BQ)
    klo = jnp.stack(
        [jnp.min(first_key, axis=1) // BK, (jnp.max(first_key, axis=1) + BK - 1) // BK]
    )
    lens = lens.reshape(span // BQ, BQ)

    head, _ = lax.optimization_barrier((head, lens))
    head = lax.all_gather(head, "z", axis=0, tiled=False)
    other = shift(head, "xl", 1)
    groups, (cos, klo, lens, head, other) = second_moves(
        pair, ring, (cos, klo, lens, head, other)
    )
    head = both_along_xl(head, other).transpose(2, 0, 1, 3, 4)
    gain_vals = head[:, :, :, 0, HEAD_COLS : HEAD_COLS + owned_gains].reshape(-1).astype(f32)
    w_head = head[..., :HEAD_COLS].reshape(width, HEAD_COLS)
    gain_one = gain_vals[:width]
    gain_two = gain_vals[width : 2 * width]
    gain_query = gain_vals[2 * width : 2 * width + HD].reshape(1, HD)
    gain_key = gain_vals[2 * width + HD :].reshape(1, HD)
    w_scaled = (w_head.astype(f32) * gain_one[:, None]).astype(bf16)

    place = places_of_groups()
    q, k, v, query_raw, key_raw, inv = project(
        place, groups, w_scaled, cos, sin, gain_query, gain_key
    )
    o_send, o_nat, l_inv = attend(klo, q, k, v, lens, rows)
    mixed = lax.all_to_all(o_send, CTX, 0, 0, tiled=True)

    output, grad_residual, do_send, left, wide, gain_two_terms = middle(
        full, mixed, tokens[0], cotangent[0], gain_two.reshape(1, width), shuffle
    )
    core = lax.axis_index("core")
    lefts = (pick(left, core, 2), shift(pick(left, core + 1, 2), "core", 1))
    wides = (wide, shift(wide, "core", 1))
    cots = (cotangent[0], shift(cotangent[0], "core", 1))
    grads = grad_ffn(lefts, wides, full.shape[0] // 2)
    grads = grad_out(core.astype(jnp.int32).reshape(1), lefts, wides, cots, grads)
    do = lax.all_to_all(do_send, CTX, 0, 0, tiled=True)
    do, grads = lax.optimization_barrier((do, grads))
    grads = grads.reshape(-1, width)
    grads = lax.psum_scatter(grads, AXIS_YZ, scatter_dimension=0, tiled=True)

    head_grads = attend_back(klo, q, k, v, do, o_nat, l_inv, lens)
    da_near, da_far, dw_head, gain_qk = project_back(
        place, groups, head_grads, (query_raw, key_raw, inv), cos, sin, gain_query, gain_key, w_head
    )

    gain_one_grad = jnp.sum(dw_head * w_head.astype(f32), axis=1)
    grad_gains = jnp.concatenate([gain_one_grad, gain_two_terms[0], gain_qk[0], gain_qk[1]])
    grad_gains = jnp.pad(
        grad_gains.reshape(n_dev, 1, owned_gains), ((0, 0), (0, owned - 1), (0, HD - owned_gains))
    )
    dw_head = (dw_head * gain_one[:, None]).reshape(n_dev, owned, HEAD_COLS)
    dw_head = jnp.concatenate([dw_head, grad_gains], axis=2).astype(bf16)
    dw_head = dw_head.reshape(n_ctx, n_dev // n_ctx, owned, PAD_COLS).transpose(1, 0, 2, 3)
    plane = sum_over_core(da_near, da_far)
    one, two = first_sums(plane)
    dw_head, _ = lax.optimization_barrier((dw_head, plane))
    dw_head = lax.all_to_all(dw_head, SHARD, 0, 0, tiled=True)
    dw_head = jnp.sum(dw_head.astype(f32), axis=0).astype(bf16)

    out_part = grads[:OUT_ROWS].reshape(n_x, OUT_ROWS // n_x, width)
    ffn_part = grads[OUT_ROWS:].reshape(2 * N_CHUNKS, n_x, owned, CHUNK)
    ffn_part = ffn_part.transpose(1, 0, 2, 3).reshape(n_x, 2 * N_CHUNKS * owned, CHUNK)
    owned_out = sum_at_owners(out_part)
    owned_ffn = sum_over_x(ffn_part).reshape(2 * N_CHUNKS, owned, CHUNK)
    one, two, owned_out, owned_ffn = lax.optimization_barrier((one, two, owned_out, owned_ffn))

    dw_head = lax.all_to_all(dw_head, CTX, 0, 0, tiled=True).astype(f32)
    owned_gain_grad = jnp.sum(dw_head[:, 0, HEAD_COLS : HEAD_COLS + owned_gains], axis=0)

    grad_a = second_sums(one, two)
    inputs = tokens[0].astype(f32)
    input_grad = grad_residual + rms_back(inputs, gain_one, grad_a)[0]

    def columns(x):
        return x.transpose(1, 0, 2).reshape(owned, -1)

    def over_pair(x):
        return columns(jnp.sum(x.reshape(H_KV, 2, owned, HD), axis=1))

    owned_in = jnp.concatenate(
        [
            columns(dw_head[:, :, :HD]),
            over_pair(dw_head[:, :, HD : 2 * HD]),
            over_pair(dw_head[:, :, 2 * HD : HEAD_COLS]),
            columns(owned_ffn),
        ],
        axis=1,
    )
    new_first_in, new_second_in, new_master_in = adam_step(
        w_in, first_in, second_in, owned_in, RATE_MATRIX
    )
    new_first_out, new_second_out, new_master_out = adam_step(
        w_out, first_out, second_out, owned_out, RATE_MATRIX
    )
    new_first_gains, new_second_gains, new_master_gains = adam_step(
        gains, first_gains, second_gains, owned_gain_grad, RATE_GAIN
    )
    return (
        output[None],
        input_grad[None],
        new_first_in,
        new_first_out,
        new_first_gains,
        new_second_in,
        new_second_out,
        new_second_gains,
        new_master_in,
        new_master_out,
        new_master_gains,
        new_master_in.astype(bf16),
        new_master_out.astype(bf16),
    )


def solution(mesh):
    cut = Mesh(mesh.devices.reshape(tuple(SIZES[name] for name in EVERY)), EVERY)
    weights = P(EVERY, None)
    vector = P(EVERY)
    acts = P(SHARD, CTX, None)
    in_specs = (
        acts,
        acts,
        P(SHARD, None),
        P(SHARD, CTX),
        P(SHARD, None),
    ) + (weights, weights, vector) * 3
    out_specs = (acts, acts) + (weights, weights, vector) * 3 + (weights, weights)
    return jax.shard_map(body, mesh=cut, in_specs=in_specs, out_specs=out_specs, check_vma=False)
```
